32 devices in a mesh: dp: 16 (over z, y, x), blk: 2 (over core).
Axes of the slice: x: 2, y: 2, z: 4, core: 2. Of those that a mesh axis runs over, the one named last changes fastest.
Arguments:
- tokens: bfloat16 [16384, 1024], P(('dp', 'blk')), may hold values from -6 to 6
- positions: int32 [16384], P(('dp', 'blk')), may hold values from 0 to 1023, as said below
- row_ids: int32 [16384], P(('dp', 'blk')), may hold values from 0 to 1, as said below
- alibi_slope: float32 [16], replicated, may hold values from 0 to 1, as said below
- ln1_gain: float32 [1024], P('dp'), may hold values from 0.1 to 1.9
- ln1_bias: float32 [1024], P('dp'), may hold values from -4 to 4
- qkv_weight: float32 [1024, 3072], P('dp'), may hold values from -0.1875 to 0.1875
- query_bias: float32 [1024], P('dp'), may hold values from -4 to 4
- value_bias: float32 [1024], P('dp'), may hold values from -4 to 4
- out_weight: float32 [1024, 1024], P('dp'), may hold values from -0.75 to 0.75
- out_bias: float32 [1024], P('dp'), may hold values from -4 to 4
- ln2_gain: float32 [1024], P('dp'), may hold values from 0.1 to 1.9
- ln2_bias: float32 [1024], P('dp'), may hold values from -4 to 4
- fc_weight: float32 [1024, 4096], P('dp'), may hold values from -0.1875 to 0.1875
- fc_bias: float32 [4096], P('dp'), may hold values from -4 to 4
- proj_weight: float32 [4096, 1024], P('dp'), may hold values from -0.09375 to 0.09375
- proj_bias: float32 [1024], P('dp'), may hold values from -4 to 4
- out_grad: bfloat16 [16384, 1024], P(('dp', 'blk')), may hold values from -6 to 6
Outputs:
- layer_output: bfloat16 [16384, 1024], P(('dp', 'blk'))
- input_grad: float32 [16384, 1024], P(('dp', 'blk'))
- ln1_gain_grad: float32 [1024], P('dp')
- ln1_bias_grad: float32 [1024], P('dp')
- qkv_weight_grad: float32 [1024, 3072], P('dp')
- query_bias_grad: float32 [1024], P('dp')
- value_bias_grad: float32 [1024], P('dp')
- out_weight_grad: float32 [1024, 1024], P('dp')
- out_bias_grad: float32 [1024], P('dp')
- ln2_gain_grad: float32 [1024], P('dp')
- ln2_bias_grad: float32 [1024], P('dp')
- fc_weight_grad: float32 [1024, 4096], P('dp')
- fc_bias_grad: float32 [4096], P('dp')
- proj_weight_grad: float32 [4096, 1024], P('dp')
- proj_bias_grad: float32 [1024], P('dp')
The draws below stay inside these ranges and needn't reach their ends.
Inputs may be any that keep to these rules, and one draw needn't show every extreme that they name: Within each group of 1024 consecutive tokens, every row holds each position from 0 to its length - 1 exactly once, and the positions of one row rise with the token's index; some group holds a single row of 1024 tokens. `row_ids`: each group holds one or two rows, numbered within the group; every row of a group has tokens on every device of its group, and within each device's 512 tokens those of row 0 come first; some group holds two rows. `alibi_slope`: Positive.
All inputs are finite; a program needn't handle non-finite values.
Results may differ from the reference program's by a relative error of at most 0.02.
Values may be sent and summed in bfloat16 or wider, within the bound.
A program may use at most 256 MiB of HBM per device.

```python
import math
import jax
import jax.numpy as jnp
from jax import lax

D = 1024
HEADS = 16
FF = 4096
TOK_DEV = 512
GROUP = 1024
TOKENS = 16384
N_DP = 16


def place_tokens(key):
    key_long, key_first, key_other, key_split = jax.random.split(key, 4)
    single = jax.random.randint(key_long, (N_DP,), 0, 3) == 0
    first_long = jax.random.randint(key_first, (), 0, N_DP)
    first_pair = (first_long + 1 + jax.random.randint(key_other, (), 0, N_DP - 1)) % N_DP
    groups = jnp.arange(N_DP)
    single = (single | (groups == first_long)) & (groups != first_pair)
    devices_group = GROUP // TOK_DEV
    split_count = jax.random.randint(key_split, (N_DP, devices_group), 1, TOK_DEV).astype(jnp.int32)
    before_count = (jnp.cumsum(split_count, axis=1) - split_count).astype(jnp.int32)
    inside = jnp.arange(GROUP).astype(jnp.int32)
    device = inside // TOK_DEV
    offset = inside % TOK_DEV
    split_here = split_count[:, device]
    before_here = before_count[:, device]
    first_row = offset[None, :] < split_here
    pair_pos = jnp.where(first_row, before_here + offset[None, :], device[None, :] * TOK_DEV - before_here + offset[None, :] - split_here)
    pair_row = jnp.where(first_row, 0, 1)
    place = jnp.where(single[:, None], inside[None, :], pair_pos).reshape(-1)
    rows = jnp.where(single[:, None], 0, pair_row).reshape(-1)
    return (place.astype(jnp.int32), rows.astype(jnp.int32))


def draw_positions(key, part):
    place, rows = place_tokens(key)
    return place


def draw_row_ids(key, part):
    place, rows = place_tokens(key)
    return rows


def draw_alibi_slope(key, part):
    key = jax.random.fold_in(key, 5)
    key_kind, key_slow, key_fast = jax.random.split(key, 3)
    slow_share = 0.5
    slow = jax.random.uniform(key_kind, (HEADS,)) < slow_share
    slow_rate = jnp.exp(jax.random.uniform(key_slow, (HEADS,), minval=math.log(0.2 / GROUP), maxval=math.log(3.0 / GROUP)))
    fast_lo = max(0.02, 6.0 / GROUP)
    fast_hi = max(0.06, 16.0 / GROUP)
    fast_rate = jnp.exp(jax.random.uniform(key_fast, (HEADS,), minval=math.log(fast_lo), maxval=math.log(fast_hi)))
    return jnp.where(slow, slow_rate, fast_rate).astype(jnp.float32)


def spiked(entries, rng, source, target, parts, factor):
    def block_of(position):
        return (jnp.arange(entries.shape[position]) // (entries.shape[position] // parts)).reshape((-1,) + (1,) * (entries.ndim - 1 - position))

    near = jax.random.permutation(rng, parts)[block_of(target)]
    second = (block_of(target) + parts // 2) % parts
    return jnp.where((block_of(source) == near) | (block_of(source) == second), factor * entries, entries)


def level_of(rng, dims, pieces, smallest, largest):
    level, own = 1.0, jax.random.fold_in(rng, 6)
    for axis_at, shards_of in pieces:
        steps = jnp.exp(jax.random.uniform(jax.random.fold_in(own, axis_at), (shards_of,), jnp.float32, smallest / len(pieces), largest / len(pieces)))
        level = level * jnp.repeat(steps, dims[axis_at] // shards_of).reshape([-1 if axis == axis_at else 1 for axis in range(len(dims))])
    return level


def noise(own_key, dims, deviation, reach, pieces=(), kind=jnp.bfloat16):
    values = deviation * jax.random.normal(own_key, dims, jnp.float32)
    if pieces:
        values = values * level_of(own_key, dims, pieces, -0.22, 0.18)
    return jnp.clip(values, -reach, reach).astype(kind)


def heavy_noise(rng, shape, scale, most, cuts, heavy, held_as=jnp.bfloat16):
    values = scale * jax.random.normal(rng, shape, jnp.float32)
    if cuts:
        values = values * level_of(rng, shape, cuts, -0.22, 0.18)
    return jnp.clip(spiked(values, jax.random.fold_in(rng, 3), *heavy), -most, most).astype(held_as)


def setup_inputs(seed: int = 0) -> dict:
    seeds = jax.random.split(jax.random.key(seed), 19)
    tokens = heavy_noise(seeds[0], (TOKENS, D), 1.0, 6.0, ((0, 32),), (0, 1, 32, 2.75))
    positions = draw_positions(jax.random.fold_in(seeds[18], 71), 0)
    row_ids = draw_row_ids(jax.random.fold_in(seeds[18], 71), 0)
    alibi_slope = draw_alibi_slope(jax.random.fold_in(seeds[18], 71), 0)
    ln1_gain = jnp.clip(1.0 + 0.18 * jax.random.normal(seeds[4], (D,), jnp.float32), 0.1, 1.9)
    ln1_bias = noise(seeds[5], (D,), 0.3, 4.0, ((0, 16),), jnp.float32)
    qkv_weight = noise(seeds[6], (D, 3 * D), D ** -0.5, 0.1875, ((0, 16),), jnp.float32)
    query_bias = noise(seeds[7], (D,), 0.3, 4.0, ((0, 16),), jnp.float32)
    value_bias = noise(seeds[8], (D,), 0.3, 4.0, ((0, 16),), jnp.float32)
    out_weight = noise(seeds[9], (D, D), (D // 16) ** -0.5, 0.75, ((0, 16),), jnp.float32)
    out_bias = noise(seeds[10], (D,), 0.3, 4.0, ((0, 16),), jnp.float32)
    ln2_gain = jnp.clip(1.0 + 0.18 * jax.random.normal(seeds[11], (D,), jnp.float32), 0.1, 1.9)
    ln2_bias = noise(seeds[12], (D,), 0.3, 4.0, ((0, 16),), jnp.float32)
    fc_weight = noise(seeds[13], (D, FF), D ** -0.5, 0.1875, ((0, 16),), jnp.float32)
    fc_bias = noise(seeds[14], (FF,), 0.3, 4.0, ((0, 16),), jnp.float32)
    proj_weight = noise(seeds[15], (FF, D), FF ** -0.5, 0.09375, ((0, 16),), jnp.float32)
    proj_bias = noise(seeds[16], (D,), 0.3, 4.0, ((0, 16),), jnp.float32)
    out_grad = noise(seeds[17], (TOKENS, D), 1.0, 6.0, ((0, 32),))
    return dict(tokens=tokens, positions=positions, row_ids=row_ids, alibi_slope=alibi_slope, ln1_gain=ln1_gain, ln1_bias=ln1_bias, qkv_weight=qkv_weight, query_bias=query_bias, value_bias=value_bias, out_weight=out_weight, out_bias=out_bias, ln2_gain=ln2_gain, ln2_bias=ln2_bias, fc_weight=fc_weight, fc_bias=fc_bias, proj_weight=proj_weight, proj_bias=proj_bias, out_grad=out_grad)


@jax.custom_vjp
def low(v):
    return lax.optimization_barrier(v.astype(jnp.bfloat16)).astype(jnp.float32)

@jax.custom_vjp
def low_back(v):
    return v

def low_keep(v):
    return (low(v), None)

def low_pass(kept, grad):
    return (grad,)

def back_keep(v):
    return (v, None)

def back_low(kept, grad):
    return (low(grad),)
low.defvjp(low_keep, low_pass)
low_back.defvjp(back_keep, back_low)
EPSILON = 1e-05
NEG_LARGE = -1e+30
HIGHEST = lax.Precision.HIGHEST

def layer_norm(inputs, gain_vec, bias_vec):
    row_mean = lax.optimization_barrier(jnp.mean(inputs, axis=-1, keepdims=True))
    centred = inputs - row_mean
    spread = lax.optimization_barrier(jnp.mean(centred * centred, axis=-1, keepdims=True))
    return centred * lax.rsqrt(spread + EPSILON) * gain_vec + bias_vec

def product(left, right):
    return jnp.dot(left, right, precision=HIGHEST, preferred_element_type=jnp.float32)

def attend_group(query_all, key_all, value_all, group_pos, group_rows, slopes):
    group_len = query_all.shape[0]
    head_size = query_all.shape[2]
    scale = 1.0 / math.sqrt(head_size)
    width = math.gcd(group_len, 512)

    def one_block(block_index):
        offset = (block_index * width).astype(jnp.int32)
        query_block = lax.dynamic_slice_in_dim(query_all, offset, width, 0)
        query_pos = lax.dynamic_slice_in_dim(group_pos, offset, width, 0)
        query_row = lax.dynamic_slice_in_dim(group_rows, offset, width, 0)
        distance = (query_pos[:, None] - group_pos[None, :]).astype(jnp.float32)
        scores = jnp.einsum('qhe,khe->hqk', query_block, key_all, precision=HIGHEST) * scale
        scores = low_back(scores - slopes[:, None, None] * distance[None])
        visible = (query_row[:, None] == group_rows[None, :]) & (group_pos[None, :] <= query_pos[:, None])
        scores = jnp.where(visible[None], scores, NEG_LARGE)
        top_score = lax.optimization_barrier(jnp.max(scores, axis=-1, keepdims=True))
        weights = jnp.where(visible[None], jnp.exp(scores - top_score), 0.0)
        probs = weights / lax.optimization_barrier(jnp.sum(weights, axis=-1, keepdims=True))
        return jnp.einsum('hqk,khe->qhe', low(probs), value_all, precision=HIGHEST)
    blocks = lax.map(jax.checkpoint(one_block), jnp.arange(group_len // width, dtype=jnp.int32))
    return blocks.reshape(group_len, -1)

def group_forward(inputs, group_pos, group_rows, slopes, params):
    gain_one, bias_one, weight_qkv, bias_query, bias_value, weight_out, bias_out, gain_two, bias_two, weight_fc, bias_fc, weight_proj, bias_proj = params
    width = inputs.shape[1]
    heads = slopes.shape[0]
    head_size = width // heads
    normed = low(layer_norm(inputs, gain_one, bias_one))
    mixed = product(normed, weight_qkv)
    queries = low(low_back(mixed[:, :width] + bias_query))
    keys_all = low(low_back(mixed[:, width:2 * width]))
    values_all = low(low_back(mixed[:, 2 * width:] + bias_value))
    shape_heads = (inputs.shape[0], heads, head_size)
    attended = attend_group(queries.reshape(shape_heads), keys_all.reshape(shape_heads), values_all.reshape(shape_heads), group_pos, group_rows, slopes)
    attended = low(low_back(attended))
    branch = low_back(product(attended, weight_out) + bias_out)
    middle = inputs + branch
    normed_two = low(layer_norm(middle, gain_two, bias_two))
    hidden_pre = low_back(product(normed_two, weight_fc) + bias_fc)
    hidden = low(jax.nn.gelu(hidden_pre, approximate=True))
    return middle + product(hidden, weight_proj) + bias_proj

def reference(tokens, positions, row_ids, alibi_slope, ln1_gain, ln1_bias, qkv_weight, query_bias, value_bias, out_weight, out_bias, ln2_gain, ln2_bias, fc_weight, fc_bias, proj_weight, proj_bias, out_grad):
    width = tokens.shape[1]
    params = (ln1_gain, ln1_bias, qkv_weight, query_bias, value_bias, out_weight, out_bias, ln2_gain, ln2_bias, fc_weight, fc_bias, proj_weight, proj_bias)
    inputs = tokens.astype(jnp.float32)

    def forward(layer_in, layer_params):
        rounded = tuple((low(member) for member in layer_params))

        def one_group(group_args):
            group_in, group_pos, group_rows = group_args
            return group_forward(group_in, group_pos, group_rows, alibi_slope, rounded)
        grouped = (layer_in.reshape(-1, GROUP, width), positions.reshape(-1, GROUP), row_ids.reshape(-1, GROUP))
        return lax.map(jax.checkpoint(one_group), grouped).reshape(-1, width)
    result, backward = jax.vjp(forward, inputs, params)
    grad_in, grads = backward(out_grad.astype(jnp.float32))
    return (result.astype(jnp.bfloat16), grad_in, grads[0], grads[1], grads[2], grads[3], grads[4], grads[5], grads[6], grads[7], grads[8], grads[9], grads[10], grads[11], grads[12])
```

```python
import functools
import math

import jax
import jax.numpy as jnp
from jax import lax
from jax.experimental import pallas as pl
from jax.experimental.pallas import tpu as pltpu
from jax.sharding import PartitionSpec as P

EPSILON = 1e-05
MASKED = -1e30
BF16 = jnp.bfloat16
F32 = jnp.float32
MESH = pl.DeviceIdType.MESH
PLANE = 4
LANES = 128
VMEM_BYTES = 58 * 2**20


def matmul(left, right):
    return jnp.dot(left, right, preferred_element_type=F32)


def matmul_tn(left, right):
    return lax.dot_general(left, right, (((0,), (0,)), ((), ())), preferred_element_type=F32)


def matmul_nt(left, right):
    return lax.dot_general(left, right, (((1,), (1,)), ((), ())), preferred_element_type=F32)


def layer_norm(inputs, gain_vec, bias_vec):
    row_mean = jnp.mean(inputs, axis=-1, keepdims=True)
    centred = inputs - row_mean
    spread = jnp.mean(centred * centred, axis=-1, keepdims=True)
    return centred * lax.rsqrt(spread + EPSILON) * gain_vec + bias_vec


class Place:
    def __init__(self, n_dp, n_blk):
        self.n_dp, self.n_blk, self.length = n_dp, n_blk, n_dp // PLANE
        self.dp, self.c = lax.axis_index("dp"), lax.axis_index("blk")
        self.z, self.p = self.dp // PLANE, lax.rem(self.dp, PLANE)
        side, row = lax.rem(self.p, 2), self.p // 2
        self.flip_x, self.flip_y = self.p + 1 - 2 * side, self.p + 2 - 4 * row
        self.diag = PLANE - 1 - self.p

    def routes(self, zz):
        odd = lax.rem(zz, 2)
        return (
            self.flip_x * (1 - odd) + self.flip_y * odd,
            self.flip_x * odd + self.flip_y * (1 - odd),
        )

    def at(self, zz, pp):
        return (zz * PLANE + pp, self.c)

    def sibling(self, k):
        return (self.dp, lax.rem(self.c + k, self.n_blk))

    def greet(self):
        barrier = pltpu.get_barrier_semaphore()

        def hello(device):
            pl.semaphore_signal(barrier, inc=1, device_id=device, device_id_type=MESH)

        hello(self.at(self.z, self.flip_x))
        hello(self.at(self.z, self.flip_y))
        for k in range(1, self.n_blk):
            hello(self.sibling(k))
        pl.when(self.z > 0)(lambda: hello(self.at(self.z - 1, self.p)))
        pl.when(self.z < self.length - 1)(lambda: hello(self.at(self.z + 1, self.p)))
        ends = jnp.minimum(self.z, 1) + jnp.minimum(self.length - 1 - self.z, 1)
        pl.semaphore_wait(barrier, 1 + self.n_blk + ends)


def remote(src, dst, send_sem, recv_sem, device):
    return pltpu.make_async_remote_copy(
        src_ref=src,
        dst_ref=dst,
        send_sem=send_sem,
        recv_sem=recv_sem,
        device_id=device,
        device_id_type=MESH,
    )


class Gather:
    def __init__(self, place, unit, own, chunk, send, recv, local):
        self.place, self.own, self.chunk = place, own, chunk
        self.send = lambda kind, zz: send.at[unit, kind, zz]
        self.recv = lambda slot: recv.at[unit, slot]
        self.local = local.at[unit]

    def copy(self, src, slot, kind, zz, device):
        return remote(src, self.chunk(slot), self.send(kind, zz), self.recv(slot), device)

    def arrived(self, slot):
        piece = self.chunk(slot)
        remote(piece, piece, self.send(0, 0), self.recv(slot), self.place.sibling(1)).wait_recv()

    def start(self):
        pc = self.place
        keep = pltpu.make_async_copy(self.own, self.chunk(pc.dp), self.local)
        keep.start()

        def to(kind, device):
            self.copy(self.own, pc.dp, kind, pc.z, device).start()

        pl.when(pc.z < pc.length - 1)(lambda: to(3, pc.at(pc.z + 1, pc.p)))
        pl.when(pc.z > 0)(lambda: to(4, pc.at(pc.z - 1, pc.p)))
        to(0, pc.at(pc.z, pc.flip_x))
        to(1, pc.at(pc.z, pc.flip_y))

    def along(self, s):
        pc = self.place

        def pass_on(zz, more, onward):
            slot = zz * PLANE + pc.p
            self.arrived(slot)
            piece = self.chunk(slot)
            pl.when(more)(lambda: self.copy(piece, slot, 3, zz, pc.at(onward, pc.p)).start())
            self.copy(piece, slot, 0, zz, pc.at(pc.z, pc.flip_x)).start()
            self.copy(piece, slot, 1, zz, pc.at(pc.z, pc.flip_y)).start()

        pl.when(pc.z >= s)(lambda: pass_on(pc.z - s, pc.z < pc.length - 1, pc.z + 1))
        pl.when(pc.z + s < pc.length)(lambda: pass_on(pc.z + s, pc.z > 0, pc.z - 1))

    def across(self):
        pc = self.place

        @pl.loop(0, pc.length)
        def _(zz):
            near, far = pc.routes(zz)
            slot = zz * PLANE + near
            self.arrived(slot)
            self.copy(self.chunk(slot), slot, 2, zz, pc.at(pc.z, far)).start()

    def finish(self):
        pc = self.place
        pltpu.make_async_copy(self.own, self.chunk(pc.dp), self.local).wait()

        @pl.loop(0, pc.length)
        def _(zz):
            near, far = pc.routes(zz)
            self.arrived(zz * PLANE + far)
            self.arrived(zz * PLANE + pc.diag)

    def drain(self):
        pc = self.place
        piece = self.chunk(pc.dp)

        def sent(kind, zz):
            remote(piece, piece, self.send(kind, zz), self.recv(0), pc.sibling(1)).wait_send()

        @pl.loop(0, pc.length)
        def _(zz):
            sent(0, zz)
            sent(1, zz)
            sent(2, zz)
            pl.when((zz <= pc.z) & (pc.z < pc.length - 1))(lambda: sent(3, zz))
            pl.when((zz > pc.z) & (pc.z > 0))(lambda: sent(3, zz))

        pl.when(pc.z > 0)(lambda: sent(4, pc.z))


def gather_kernel(
    n_dp, n_blk, qkv, out, fc, proj, small, all_qkv, all_out, all_fc, all_proj, all_small, send, recv, local, side
):
    pc = Place(n_dp, n_blk)
    pc.greet()
    wide = out.shape[1]
    mine = pl.ds(pl.multiple_of(pc.c * wide, LANES), wide)
    parts = [
        (small, lambda slot: all_small.at[slot]),
        (qkv, lambda slot: all_qkv.at[slot]),
        (out, lambda slot: all_out.at[slot, :, mine]),
        (fc, lambda slot: all_fc.at[slot]),
        (proj, lambda slot: all_proj.at[slot]),
    ]
    units = [Gather(pc, i, own, chunk, send, recv, local) for i, (own, chunk) in enumerate(parts)]
    units[0].start()
    units[1].start()
    for i in range(5):
        for s in range(1, pc.length):
            units[i].along(s)
        if i + 2 < 5:
            units[i + 2].start()
        if i > 0:
            units[i - 1].across()
        if i > 1:
            units[i - 2].finish()
    units[4].across()
    side_copies = []
    piece = all_out.at[:, :, mine]
    for k in range(1, n_blk):
        copy = remote(piece, piece, side.at[0, k], side.at[1, k], pc.sibling(k))
        copy.start()
        side_copies.append(copy)
    units[3].finish()
    units[4].finish()
    for copy in side_copies:
        copy.wait()
    for unit in units:
        unit.drain()


class Scatter:
    def __init__(self, place, unit, chunk, bufs, send, recv):
        self.place, self.chunk = place, chunk
        self.diag, self.near, self.far, self.up, self.down = bufs
        self.send = lambda kind, zz: send.at[unit, kind, zz]
        self.recv = lambda kind, zz: recv.at[unit, kind, zz]

    def copy(self, src, dst, kind, zz, device):
        return remote(src, dst.at[zz], self.send(kind, zz), self.recv(kind, zz), device)

    def arrived(self, buf, kind, zz):
        self.copy(buf.at[zz], buf, kind, zz, self.place.sibling(1)).wait_recv()

    def start(self):
        pc = self.place

        @pl.loop(0, pc.length)
        def _(zz):
            near, far = pc.routes(zz)
            to = pc.at(pc.z, near)
            self.copy(self.chunk(zz * PLANE + pc.diag), self.diag, 0, zz, to).start()
            self.copy(self.chunk(zz * PLANE + near), self.near, 1, zz, to).start()

    def middle(self):
        pc = self.place

        @pl.loop(0, pc.length)
        def _(zz):
            near, far = pc.routes(zz)
            self.arrived(self.diag, 0, zz)
            total = self.diag[zz].astype(F32) + self.chunk(zz * PLANE + far)[...].astype(F32)
            self.diag[zz] = total.astype(BF16)
            self.copy(self.diag.at[zz], self.far, 2, zz, pc.at(pc.z, far)).start()

    def settle(self):
        pc = self.place

        @pl.loop(0, pc.length)
        def _(zz):
            self.arrived(self.near, 1, zz)
            self.arrived(self.far, 2, zz)
            total = self.near[zz].astype(F32) + self.far[zz].astype(F32)
            total += self.chunk(zz * PLANE + pc.p)[...].astype(F32)
            self.near[zz] = total.astype(BF16)

    def along(self, s):
        pc = self.place

        def pass_on(zz, buf, kind, more, onward):
            @pl.when(more)
            def _():
                self.arrived(buf, kind, zz)
                total = self.near[zz].astype(F32) + buf[zz].astype(F32)
                self.near[zz] = total.astype(BF16)

            self.copy(self.near.at[zz], buf, kind, zz, pc.at(onward, pc.p)).start()

        pl.when(pc.z + s < pc.length)(lambda: pass_on(pc.z + s, self.up, 3, pc.z > 0, pc.z + 1))
        pl.when(pc.z >= s)(
            lambda: pass_on(pc.z - s, self.down, 4, pc.z < pc.length - 1, pc.z - 1)
        )

    def finish(self, total):
        pc = self.place
        total[...] = self.near[pc.z].astype(F32)

        def more(buf, kind):
            self.arrived(buf, kind, pc.z)
            total[...] += buf[pc.z].astype(F32)

        pl.when(pc.z > 0)(lambda: more(self.up, 3))
        pl.when(pc.z < pc.length - 1)(lambda: more(self.down, 4))

    def drain(self):
        pc = self.place

        def sent(kind, zz):
            self.copy(self.near.at[zz], self.near, kind, zz, pc.sibling(1)).wait_send()

        @pl.loop(0, pc.length)
        def _(zz):
            sent(0, zz)
            sent(1, zz)
            sent(2, zz)
            pl.when(zz > pc.z)(lambda: sent(3, zz))
            pl.when(zz < pc.z)(lambda: sent(4, zz))


def scatter_kernel(n_dp, n_blk, *refs):
    grads, outs, rest = refs[:4], refs[4:8], refs[8:]
    bufs, totals, rest = rest[:20], rest[20:24], rest[24:]
    side_buf, send, recv, side, last = rest
    proj, fc, out, qkv = grads
    pc = Place(n_dp, n_blk)
    pc.greet()
    wide = out.shape[2] // n_blk

    def columns(core):
        return pl.ds(pl.multiple_of(core * wide, LANES), wide)

    chunks = [
        lambda slot: proj.at[slot],
        lambda slot: fc.at[slot],
        lambda slot: side_buf.at[0, slot],
        lambda slot: qkv.at[slot],
    ]
    units = [
        Scatter(pc, i, chunks[i], bufs[5 * i : 5 * i + 5], send, recv) for i in range(4)
    ]
    units[0].start()
    units[1].start()
    side_copies = []
    for k in range(1, n_blk):
        dev = pc.sibling(k)
        copy = remote(
            out.at[:, :, columns(dev[1])], side_buf.at[k], side.at[0, k], side.at[1, k], dev
        )
        copy.start()
        side_copies.append(copy)

    def side_sum():
        for copy in side_copies:
            copy.wait()

        @pl.loop(0, n_dp)
        def _(slot):
            total = out[slot, :, columns(pc.c)].astype(F32)
            for k in range(1, n_blk):
                total += side_buf[k, slot].astype(F32)
            side_buf[0, slot] = total.astype(BF16)

    pending = []

    def spread(i):
        units[i].finish(totals[i])
        total = totals[i]
        pieces = [(total, outs[i].at[pc.c])]
        for j, (src, dst) in enumerate(pieces):
            keep = pltpu.make_async_copy(src, dst, last.at[i, 0, 0])
            keep.start()
            pending.append(keep)
            for k in range(1, n_blk):
                copy = remote(src, dst, last.at[i, 0, k], last.at[i, 1, k], pc.sibling(k))
                copy.start()
                pending.append(copy)

    units[0].middle()
    side_sum()
    units[2].start()
    units[1].middle()
    units[3].start()
    units[0].settle()
    for s in range(pc.length - 1, 0, -1):
        units[0].along(s)
    units[2].middle()
    units[1].settle()
    for s in range(pc.length - 1, 0, -1):
        units[1].along(s)
    spread(0)
    units[3].middle()
    units[2].settle()
    for s in range(pc.length - 1, 0, -1):
        units[2].along(s)
    units[3].settle()
    for s in range(pc.length - 1, 0, -1):
        units[3].along(s)
    spread(1)
    spread(2)
    spread(3)
    for copy in pending:
        copy.wait()
    for unit in units:
        unit.drain()


def gather_weights(n_dp, n_blk, qkv, out, fc, proj, small):
    shards = (qkv, out, fc, proj, small)
    shapes = [
        jax.ShapeDtypeStruct((n_dp, a.shape[0], a.shape[1] * (n_blk if a is out else 1)), BF16)
        for a in shards
    ]
    length = n_dp // PLANE
    hbm = pl.BlockSpec(memory_space=pl.ANY)
    return pl.pallas_call(
        functools.partial(gather_kernel, n_dp, n_blk),
        out_shape=shapes,
        in_specs=[hbm] * 5,
        out_specs=[hbm] * 5,
        scratch_shapes=[
            pltpu.SemaphoreType.DMA((5, 5, length)),
            pltpu.SemaphoreType.DMA((5, n_dp)),
            pltpu.SemaphoreType.DMA((5,)),
            pltpu.SemaphoreType.DMA((2, n_blk)),
        ],
        compiler_params=pltpu.CompilerParams(
            collective_id=0, has_side_effects=True, vmem_limit_bytes=VMEM_BYTES
        ),
    )(*shards)


def scatter_grads(n_dp, n_blk, proj, fc, out, qkv):
    length = n_dp // PLANE
    grads = (proj, fc, out, qkv)
    sizes = [a.shape[1:] for a in grads]
    sizes[2] = (sizes[2][0], sizes[2][1] // n_blk)
    vmem = pl.BlockSpec(memory_space=pltpu.VMEM)
    scratch = [pltpu.VMEM((length,) + size, BF16) for size in sizes for _ in range(5)]
    scratch += [pltpu.VMEM(size, F32) for size in sizes]
    scratch += [
        pltpu.VMEM((n_blk, n_dp) + sizes[2], BF16),
        pltpu.SemaphoreType.DMA((4, 5, length)),
        pltpu.SemaphoreType.DMA((4, 5, length)),
        pltpu.SemaphoreType.DMA((2, n_blk)),
        pltpu.SemaphoreType.DMA((4, 2, n_blk)),
    ]
    return pl.pallas_call(
        functools.partial(scatter_kernel, n_dp, n_blk),
        out_shape=[jax.ShapeDtypeStruct((n_blk,) + size, F32) for size in sizes],
        in_specs=[vmem] * 4,
        out_specs=[pl.BlockSpec(memory_space=pl.ANY)] * 4,
        scratch_shapes=scratch,
        compiler_params=pltpu.CompilerParams(
            collective_id=1, has_side_effects=True, vmem_limit_bytes=VMEM_BYTES
        ),
    )(*grads)


def lane_split(value, lane, first, base):
    for i in range(3):
        term = value.astype(BF16)
        base = jnp.where(lane == first + i, term, base)
        value = value - term.astype(F32)
    return base


def causal_tail(scores, block, axis, masked):
    key_axis, query_axis = (0, 1) if axis == 0 else (1, 0)
    tail_shape = (block, block)
    keep = lax.broadcasted_iota(jnp.int32, tail_shape, key_axis) <= lax.broadcasted_iota(
        jnp.int32, tail_shape, query_axis
    )
    size = scores.shape[axis]
    if size == block:
        return jnp.where(keep, scores, masked)
    head = lax.slice_in_dim(scores, 0, size - block, axis=axis)
    tail = jnp.where(keep, lax.slice_in_dim(scores, size - block, size, axis=axis), masked)
    return jnp.concatenate([head, tail], axis=axis)


def causal_all(scores, offset, axis, masked):
    key_axis, query_axis = (0, 1) if axis == 0 else (1, 0)
    keep = (
        lax.broadcasted_iota(jnp.int32, scores.shape, key_axis)
        <= lax.broadcasted_iota(jnp.int32, scores.shape, query_axis) + offset
    )
    return jnp.where(keep, scores, masked)


def query_blocks(total, block, run):
    count = total // block
    if count <= 4:
        for b in range(count):
            run(
                b * block,
                (b + 1) * block,
                lambda scores, axis, masked: causal_tail(scores, block, axis, masked),
            )
    else:

        @pl.loop(0, count)
        def _(b):
            first = pl.multiple_of(b * block, block)
            run(first, total, lambda scores, axis, masked: causal_all(scores, first, axis, masked))


def attend_kernel(block, scale, q_ref, k_ref, v_ref, key_aug, query_aug, slope_ref, out_ref, qx_ref):
    total = q_ref.shape[0]
    half = LANES // 2
    lane = lax.broadcasted_iota(jnp.int32, (1, LANES), 1)

    def run(first, keys, mask):
        rows = pl.ds(first, block)
        result = None
        for hh in range(2):
            own = (lane < half) if hh == 0 else (lane >= half)
            base = half * (1 - hh)
            aug = query_aug[rows, :] + slope_ref[0, hh : hh + 1, :]
            query = jnp.where(own, q_ref[rows, :] * BF16(scale), aug)
            key = jnp.where(own, k_ref[0:keys, :], key_aug[0:keys, :])
            value = jnp.where(own, v_ref[0:keys, :], BF16(1))
            scores = mask(matmul_nt(query, key), 1, MASKED)
            top = jnp.max(scores, axis=1, keepdims=True)
            weights = jnp.exp(scores - top).astype(BF16)
            sums = matmul(weights, value)
            log_total = top + jnp.log(sums[:, base : base + 1])
            qx_ref[0, hh, rows, :] = lane_split(-log_total, lane, base + 8, query)
            part = sums / pltpu.roll(sums, half, 1)
            result = part if hh == 0 else jnp.where(own, part, result)
        out_ref[rows, :] = result.astype(BF16)

    query_blocks(total, block, run)


def attend_back_kernel(
    block, scale, qx_ref, k_ref, v_ref, key_aug, out_ref, grad_ref, dq_ref, dk_ref, dv_ref, dk_acc, dv_acc
):
    total = k_ref.shape[0]
    half = LANES // 2
    lane = lax.broadcasted_iota(jnp.int32, (1, LANES), 1)
    dk_acc[...] = jnp.zeros_like(dk_acc)
    dv_acc[...] = jnp.zeros_like(dv_acc)

    def run(first, keys, mask):
        rows = pl.ds(first, block)
        grad = grad_ref[rows, :]
        product = grad.astype(F32) * out_ref[rows, :].astype(F32)
        dq = None
        dk = None
        dv = None
        for hh in range(2):
            own = (lane < half) if hh == 0 else (lane >= half)
            base = half * (1 - hh)
            query = qx_ref[0, hh, rows, :]
            key = jnp.where(own, k_ref[0:keys, :], key_aug[0:keys, :])
            delta = jnp.sum(jnp.where(own, product, 0.0), axis=1, keepdims=True)
            grad_own = jnp.where(own, grad, BF16(0))
            grad_aug = lane_split(-delta, lane, base, grad_own)
            value = jnp.where(own, v_ref[0:keys, :], BF16(1))
            weights = mask(jnp.exp(matmul_nt(key, query)), 0, 0.0)
            change = (weights * matmul_nt(value, grad_aug)).astype(BF16)
            key_own = jnp.where(own, key, BF16(0))
            query_own = jnp.where(own, query, BF16(0))
            dv_part = matmul(weights.astype(BF16), grad_own)
            dk_part = matmul(change, query_own)
            dq_part = matmul_tn(change, key_own)
            dv = dv_part if hh == 0 else dv + dv_part
            dk = dk_part if hh == 0 else dk + dk_part
            dq = dq_part if hh == 0 else dq + dq_part
        dq_ref[rows, :] = (dq * scale).astype(BF16)
        dk_acc[0:keys, :] += dk
        dv_acc[0:keys, :] += dv

    query_blocks(total, block, run)
    dk_ref[...] = dk_acc[...].astype(BF16)
    dv_ref[...] = dv_acc[...].astype(BF16)


def columns_spec(rows, first):
    return pl.BlockSpec((rows, LANES), lambda j: (0, first + j))


def attend(qkv, key_aug, query_aug, slope_aug, scale):
    total, wide = qkv.shape[0], qkv.shape[1] // 3
    pairs = wide // LANES
    block = math.gcd(total, 256)
    whole = pl.BlockSpec((total, LANES), lambda j: (0, 0))
    return pl.pallas_call(
        functools.partial(attend_kernel, block, scale),
        grid=(pairs,),
        out_shape=[
            jax.ShapeDtypeStruct((total, wide), BF16),
            jax.ShapeDtypeStruct((pairs, 2, total, LANES), BF16),
        ],
        in_specs=[
            columns_spec(total, 0),
            columns_spec(total, pairs),
            columns_spec(total, 2 * pairs),
            whole,
            whole,
            pl.BlockSpec((1, 2, LANES), lambda j: (j, 0, 0)),
        ],
        out_specs=[
            columns_spec(total, 0),
            pl.BlockSpec((1, 2, total, LANES), lambda j: (j, 0, 0, 0)),
        ],
        compiler_params=pltpu.CompilerParams(vmem_limit_bytes=VMEM_BYTES),
    )(qkv, qkv, qkv, key_aug, query_aug, slope_aug)


def attend_back(query_ext, qkv, key_aug, attended, grad, scale):
    total, wide = attended.shape
    pairs = wide // LANES
    block = math.gcd(total, 256)
    whole = pl.BlockSpec((total, LANES), lambda j: (0, 0))
    out = jax.ShapeDtypeStruct((total, wide), BF16)
    return pl.pallas_call(
        functools.partial(attend_back_kernel, block, scale),
        grid=(pairs,),
        out_shape=[out] * 3,
        in_specs=[
            pl.BlockSpec((1, 2, total, LANES), lambda j: (j, 0, 0, 0)),
            columns_spec(total, pairs),
            columns_spec(total, 2 * pairs),
            whole,
            columns_spec(total, 0),
            columns_spec(total, 0),
        ],
        out_specs=[columns_spec(total, 0)] * 3,
        scratch_shapes=[pltpu.VMEM((total, LANES), F32)] * 2,
        compiler_params=pltpu.CompilerParams(vmem_limit_bytes=VMEM_BYTES),
    )(query_ext, qkv, qkv, key_aug, attended, grad)


def attention_terms(positions, rows, slopes, n_blk, c):
    high = (positions // 256) * 256
    low = positions - high
    first = rows == 0
    one = jnp.ones_like(positions)
    zero = jnp.zeros_like(positions)

    def table(columns):
        cols = jnp.stack([col.astype(F32) for col in columns], axis=1)
        cols = jnp.pad(cols, ((0, 0), (0, LANES // 2 - len(columns))))
        return jnp.concatenate([cols, cols], axis=1).astype(BF16)

    key_aug = table([high, high, high, low, low, low, first, ~first, one, one, one])
    other = jnp.where(first, 0.0, MASKED)
    query_aug = table([zero] * 6 + [other, jnp.where(first, MASKED, 0.0)])
    heads = slopes.shape[0] // n_blk
    mine = lax.dynamic_slice_in_dim(slopes, c * heads, heads, 0)
    parts = []
    left = mine
    for _ in range(3):
        term = lax.reduce_precision(left, 8, 7)
        parts.append(term)
        left = left - term
    cols = jnp.stack(parts + parts, axis=1)
    cols = jnp.pad(cols, ((0, 0), (0, LANES // 2 - 6)))
    slope_aug = jnp.concatenate([cols, cols], axis=1).astype(BF16).reshape(heads // 2, 2, LANES)
    keep = (jnp.arange(LANES) // (LANES // 2))[None, None, :] == 1 - jnp.arange(2)[None, :, None]
    return key_aug, query_aug, jnp.where(keep, slope_aug, 0)


def body(
    n_dp,
    n_blk,
    tokens,
    positions,
    row_ids,
    alibi_slope,
    ln1_gain,
    ln1_bias,
    qkv_weight,
    query_bias,
    value_bias,
    out_weight,
    out_bias,
    ln2_gain,
    ln2_bias,
    fc_weight,
    fc_bias,
    proj_weight,
    proj_bias,
    out_grad,
):
    local, width = tokens.shape
    heads = alibi_slope.shape[0]
    hidden_all = fc_weight.shape[1]
    scale = 1.0 / math.sqrt(width // heads)
    c = lax.axis_index("blk")
    dp = lax.axis_index("dp")
    wide = width // n_blk
    shard = width // n_dp
    piece = hidden_all // (n_dp * n_blk)
    total = n_blk * local

    def swap(a):
        return lax.ppermute(a, "blk", [(0, 1), (1, 0)])

    def blk_gather(a):
        if n_blk != 2:
            return lax.all_gather(a, "blk", axis=0, tiled=True)
        other = swap(a)
        return jnp.where(
            c == 0, jnp.concatenate([a, other], 0), jnp.concatenate([other, a], 0)
        )

    def blk_sum(a):
        if n_blk != 2:
            return lax.psum_scatter(a.astype(BF16), "blk", scatter_dimension=0, tiled=True).astype(F32)
        own = lax.dynamic_slice_in_dim(a, c * local, local, 0)
        other = lax.dynamic_slice_in_dim(a, (1 - c) * local, local, 0)
        return own + swap(other.astype(BF16)).astype(F32)

    def to_tokens(a):
        if n_blk != 2:
            moved = lax.all_to_all(a.reshape(n_blk, local, wide), "blk", 0, 0)
            return jnp.transpose(moved, (1, 0, 2)).reshape(local, width)
        own = lax.dynamic_slice_in_dim(a, c * local, local, 0)
        other = swap(lax.dynamic_slice_in_dim(a, (1 - c) * local, local, 0))
        return jnp.where(
            c == 0, jnp.concatenate([own, other], 1), jnp.concatenate([other, own], 1)
        )

    def to_heads(a):
        if n_blk != 2:
            moved = lax.all_to_all(
                jnp.transpose(a.reshape(local, n_blk, wide), (1, 0, 2)), "blk", 0, 0
            )
            return moved.reshape(total, wide)
        own = lax.dynamic_slice_in_dim(a, c * wide, wide, 1)
        other = swap(lax.dynamic_slice_in_dim(a, (1 - c) * wide, wide, 1))
        return jnp.where(
            c == 0, jnp.concatenate([own, other], 0), jnp.concatenate([other, own], 0)
        )

    def mine(a, axis, size):
        return lax.dynamic_slice_in_dim(a, c * size, size, axis)

    qkv_own = jnp.concatenate(
        [mine(qkv_weight[:, i * width : (i + 1) * width], 1, wide) for i in range(3)], 1
    ).astype(BF16)
    out_own = mine(out_weight, 1, wide).astype(BF16)
    fc_own = mine(fc_weight.reshape(shard, n_dp, n_blk, piece), 2, 1).reshape(shard, n_dp * piece)
    proj_own = mine(proj_weight, 0, piece)
    vectors = [ln1_gain, ln1_bias, query_bias, value_bias, out_bias, ln2_gain, ln2_bias, proj_bias]
    vectors.append(mine(fc_bias, 0, piece))
    small = jnp.stack(
        [
            lax.dynamic_update_slice_in_dim(
                jnp.zeros((LANES,), F32), vec, lax.rem(dp * vec.shape[0], LANES), 0
            )
            for vec in vectors
        ]
    )
    small = jnp.pad(small, ((0, 16 - len(vectors)), (0, 0))).astype(BF16)
    full_qkv, full_out, full_fc, full_proj, full_small = gather_weights(
        n_dp, n_blk, qkv_own, out_own, fc_own.astype(BF16), proj_own.astype(BF16), small
    )
    weight_qkv = full_qkv.reshape(width, 3 * wide)
    weight_out = full_out.reshape(width, width)
    weight_fc = full_fc.reshape(width, n_dp * piece)
    weight_proj = full_proj.reshape(n_dp * piece, width)
    spread = full_small.astype(F32)

    def vector(i):
        size = vectors[i].shape[0]
        per = LANES // size
        rows = jnp.sum(spread[:, i].reshape(n_dp // per, per, LANES), axis=1)
        return rows.reshape(n_dp * size)

    gain_one, bias_one, bias_query, bias_value, bias_out, gain_two, bias_two, bias_proj, bias_fc = (
        vector(i) for i in range(len(vectors))
    )
    place = blk_gather(jnp.stack([positions, row_ids], axis=1))
    key_aug, query_aug, slope_aug = attention_terms(
        place[:, 0], place[:, 1], alibi_slope, n_blk, c
    )
    inputs = tokens.astype(F32)
    every_token = blk_gather(tokens).astype(F32)
    every_grad = blk_gather(out_grad)
    normed = layer_norm(every_token, gain_one, bias_one).astype(BF16)
    bias_qkv = jnp.concatenate(
        [mine(bias_query, 0, wide), jnp.zeros((wide,), F32), mine(bias_value, 0, wide)]
    )
    mixed = (matmul(normed, weight_qkv) + bias_qkv).astype(BF16)
    attended_heads, query_ext = attend(mixed, key_aug, query_aug, slope_aug, scale)
    attended = to_tokens(attended_heads)
    middle = inputs + matmul(attended, weight_out) + bias_out
    normed_two = layer_norm(middle, gain_two, bias_two).astype(BF16)
    every_two = blk_gather(normed_two)
    hidden_pre = matmul(every_two, weight_fc) + bias_fc
    hidden_vals, gelu_back = jax.vjp(
        functools.partial(jax.nn.gelu, approximate=True), hidden_pre
    )
    hidden = hidden_vals.astype(BF16)
    layer_output = (middle + blk_sum(matmul(hidden, weight_proj)) + bias_proj).astype(BF16)
    grad_top = out_grad.astype(F32)
    grad_proj_weight = matmul_tn(hidden, every_grad).astype(BF16)
    grad_proj_bias = jnp.sum(grad_top, axis=0)
    (grad_pre,) = gelu_back(matmul_nt(every_grad, weight_proj))
    grad_pre = grad_pre.astype(BF16)
    grad_fc_weight = matmul_tn(every_two, grad_pre).astype(BF16)
    grad_fc_bias = jnp.sum(grad_pre.astype(F32), axis=0)
    grad_normed_two = blk_sum(matmul_nt(grad_pre, weight_fc))
    _, norm_two_back = jax.vjp(layer_norm, middle, gain_two, bias_two)
    grad_mid_norm, grad_gain_two, grad_bias_two = norm_two_back(grad_normed_two)
    grad_middle = grad_top + grad_mid_norm
    grad_branch = grad_middle.astype(BF16)
    grad_out_weight = matmul_tn(attended, grad_branch).astype(BF16)
    grad_out_bias = jnp.sum(grad_branch.astype(F32), axis=0)
    grad_heads = to_heads(matmul_nt(grad_branch, weight_out).astype(BF16))
    grad_mixed = jnp.concatenate(
        attend_back(query_ext, mixed, key_aug, attended_heads, grad_heads, scale), axis=1
    )
    grad_qkv_weight = matmul_tn(normed, grad_mixed).astype(BF16)
    sums = jnp.sum(grad_mixed.astype(F32), axis=0)
    grad_normed = blk_sum(matmul_nt(grad_mixed, weight_qkv))
    _, norm_one_back = jax.vjp(layer_norm, inputs, gain_one, bias_one)
    grad_in_norm, grad_gain_one, grad_bias_one = norm_one_back(grad_normed)
    input_grad = grad_middle + grad_in_norm

    proj_sum, fc_sum, out_sum, qkv_sum = scatter_grads(
        n_dp,
        n_blk,
        grad_proj_weight.reshape(n_dp, piece, width),
        grad_fc_weight.reshape(n_dp, shard, n_dp * piece),
        grad_out_weight.reshape(n_dp, shard, width),
        grad_qkv_weight.reshape(n_dp, shard, 3 * wide),
    )

    def spread_out(vec, size):
        parts = vec.reshape(-1, 1, size)
        return jnp.where((jnp.arange(n_blk) == c)[None, :, None], parts, 0.0).reshape(-1)

    small_grads = [
        grad_gain_one,
        grad_bias_one,
        spread_out(sums[:wide], wide),
        spread_out(sums[2 * wide :], wide),
        grad_out_bias,
        grad_gain_two,
        grad_bias_two,
        grad_proj_bias,
        spread_out(grad_fc_bias, piece),
    ]
    small_sum = lax.psum(jnp.concatenate(small_grads), ("dp", "blk"))
    finals = []
    at = 0
    for vec in small_grads:
        size = vec.shape[0]
        finals.append(lax.dynamic_slice_in_dim(small_sum, at + dp * (size // n_dp), size // n_dp, 0))
        at += size
    g_gain1, g_bias1, g_query, g_value, g_out, g_gain2, g_bias2, g_proj, g_fc = finals
    final_qkv = jnp.transpose(qkv_sum.reshape(n_blk, shard, 3, wide), (1, 2, 0, 3))
    final_fc = jnp.transpose(fc_sum.reshape(n_blk, shard, n_dp, piece), (1, 2, 0, 3))
    return (
        layer_output,
        input_grad,
        g_gain1,
        g_bias1,
        final_qkv.reshape(shard, 3 * width),
        g_query,
        g_value,
        jnp.transpose(out_sum, (1, 0, 2)).reshape(shard, width),
        g_out,
        g_gain2,
        g_bias2,
        final_fc.reshape(shard, hidden_all),
        g_fc,
        proj_sum.reshape(n_blk * piece, width),
        g_proj,
    )


def solution(mesh):
    both, rows, one = P(("dp", "blk"), None), P("dp", None), P("dp")
    tokens = P(("dp", "blk"))
    in_specs = (both, tokens, tokens, P(), one, one, rows, one, one, rows, one, one, one, rows, one, rows, one, both)
    out_specs = (both, both, one, one, rows, one, one, rows, one, one, one, rows, one, rows, one)
    return jax.shard_map(
        functools.partial(body, mesh.shape["dp"], mesh.shape["blk"]),
        mesh=mesh,
        in_specs=in_specs,
        out_specs=out_specs,
        check_vma=False,
    )
```

```python
import functools
import math

import jax
import jax.numpy as jnp
from jax import lax
from jax.experimental import pallas as pl
from jax.experimental.pallas import tpu as pltpu
from jax.sharding import PartitionSpec as P

EPSILON = 1e-05
MASKED = -1e30
BF16 = jnp.bfloat16
F32 = jnp.float32
MESH = pl.DeviceIdType.MESH
PLANE = 4
LANES = 128
VMEM_BYTES = 58 * 2**20


def matmul(left, right):
    return jnp.dot(left, right, preferred_element_type=F32)


def matmul_tn(left, right):
    return lax.dot_general(left, right, (((0,), (0,)), ((), ())), preferred_element_type=F32)


def matmul_nt(left, right):
    return lax.dot_general(left, right, (((1,), (1,)), ((), ())), preferred_element_type=F32)


def layer_norm(inputs, gain_vec, bias_vec):
    row_mean = jnp.mean(inputs, axis=-1, keepdims=True)
    centred = inputs - row_mean
    spread = jnp.mean(centred * centred, axis=-1, keepdims=True)
    return centred * lax.rsqrt(spread + EPSILON) * gain_vec + bias_vec


class Place:
    def __init__(self, n_dp, n_blk):
        self.n_dp, self.n_blk, self.length = n_dp, n_blk, n_dp // PLANE
        self.dp, self.c = lax.axis_index("dp"), lax.axis_index("blk")
        self.z, self.p = self.dp // PLANE, lax.rem(self.dp, PLANE)
        side, row = lax.rem(self.p, 2), self.p // 2
        self.flip_x, self.flip_y = self.p + 1 - 2 * side, self.p + 2 - 4 * row
        self.diag = PLANE - 1 - self.p

    def routes(self, zz):
        odd = lax.rem(zz, 2)
        return (
            self.flip_x * (1 - odd) + self.flip_y * odd,
            self.flip_x * odd + self.flip_y * (1 - odd),
        )

    def at(self, zz, pp):
        return (zz * PLANE + pp, self.c)

    def sibling(self, k):
        return (self.dp, lax.rem(self.c + k, self.n_blk))

    def greet(self):
        barrier = pltpu.get_barrier_semaphore()

        def hello(device):
            pl.semaphore_signal(barrier, inc=1, device_id=device, device_id_type=MESH)

        hello(self.at(self.z, self.flip_x))
        hello(self.at(self.z, self.flip_y))
        for k in range(1, self.n_blk):
            hello(self.sibling(k))
        pl.when(self.z > 0)(lambda: hello(self.at(self.z - 1, self.p)))
        pl.when(self.z < self.length - 1)(lambda: hello(self.at(self.z + 1, self.p)))
        ends = jnp.minimum(self.z, 1) + jnp.minimum(self.length - 1 - self.z, 1)
        pl.semaphore_wait(barrier, 1 + self.n_blk + ends)


def remote(src, dst, send_sem, recv_sem, device):
    return pltpu.make_async_remote_copy(
        src_ref=src,
        dst_ref=dst,
        send_sem=send_sem,
        recv_sem=recv_sem,
        device_id=device,
        device_id_type=MESH,
    )


class Gather:
    def __init__(self, place, unit, own, chunk, send, recv, local):
        self.place, self.own, self.chunk = place, own, chunk
        self.send = lambda kind, zz: send.at[unit, kind, zz]
        self.recv = lambda slot: recv.at[unit, slot]
        self.local = local.at[unit]

    def copy(self, src, slot, kind, zz, device):
        return remote(src, self.chunk(slot), self.send(kind, zz), self.recv(slot), device)

    def arrived(self, slot):
        piece = self.chunk(slot)
        remote(piece, piece, self.send(0, 0), self.recv(slot), self.place.sibling(1)).wait_recv()

    def start(self):
        pc = self.place
        keep = pltpu.make_async_copy(self.own, self.chunk(pc.dp), self.local)
        keep.start()

        def to(kind, device):
            self.copy(self.own, pc.dp, kind, pc.z, device).start()

        pl.when(pc.z < pc.length - 1)(lambda: to(3, pc.at(pc.z + 1, pc.p)))
        pl.when(pc.z > 0)(lambda: to(4, pc.at(pc.z - 1, pc.p)))
        to(0, pc.at(pc.z, pc.flip_x))
        to(1, pc.at(pc.z, pc.flip_y))

    def along(self, s):
        pc = self.place

        def pass_on(zz, more, onward):
            slot = zz * PLANE + pc.p
            self.arrived(slot)
            piece = self.chunk(slot)
            pl.when(more)(lambda: self.copy(piece, slot, 3, zz, pc.at(onward, pc.p)).start())
            self.copy(piece, slot, 0, zz, pc.at(pc.z, pc.flip_x)).start()
            self.copy(piece, slot, 1, zz, pc.at(pc.z, pc.flip_y)).start()

        pl.when(pc.z >= s)(lambda: pass_on(pc.z - s, pc.z < pc.length - 1, pc.z + 1))
        pl.when(pc.z + s < pc.length)(lambda: pass_on(pc.z + s, pc.z > 0, pc.z - 1))

    def across(self):
        pc = self.place

        @pl.loop(0, pc.length)
        def _(zz):
            near, far = pc.routes(zz)
            slot = zz * PLANE + near
            self.arrived(slot)
            self.copy(self.chunk(slot), slot, 2, zz, pc.at(pc.z, far)).start()

    def finish(self):
        pc = self.place
        pltpu.make_async_copy(self.own, self.chunk(pc.dp), self.local).wait()

        @pl.loop(0, pc.length)
        def _(zz):
            near, far = pc.routes(zz)
            self.arrived(zz * PLANE + far)
            self.arrived(zz * PLANE + pc.diag)

    def drain(self):
        pc = self.place
        piece = self.chunk(pc.dp)

        def sent(kind, zz):
            remote(piece, piece, self.send(kind, zz), self.recv(0), pc.sibling(1)).wait_send()

        @pl.loop(0, pc.length)
        def _(zz):
            sent(0, zz)
            sent(1, zz)
            sent(2, zz)
            pl.when((zz <= pc.z) & (pc.z < pc.length - 1))(lambda: sent(3, zz))
            pl.when((zz > pc.z) & (pc.z > 0))(lambda: sent(3, zz))

        pl.when(pc.z > 0)(lambda: sent(4, pc.z))


def gather_kernel(
    n_dp, n_blk, qkv, out, fc, proj, small, all_qkv, all_out, all_fc, all_proj, all_small, send, recv, local, side
):
    pc = Place(n_dp, n_blk)
    pc.greet()
    wide = out.shape[1]
    mine = pl.ds(pl.multiple_of(pc.c * wide, LANES), wide)
    parts = [
        (small, lambda slot: all_small.at[slot]),
        (qkv, lambda slot: all_qkv.at[slot]),
        (out, lambda slot: all_out.at[slot, :, mine]),
        (fc, lambda slot: all_fc.at[slot]),
        (proj, lambda slot: all_proj.at[slot]),
    ]
    units = [Gather(pc, i, own, chunk, send, recv, local) for i, (own, chunk) in enumerate(parts)]
    units[0].start()
    units[1].start()
    for i in range(5):
        for s in range(1, pc.length):
            units[i].along(s)
        if i + 2 < 5:
            units[i + 2].start()
        if i > 0:
            units[i - 1].across()
        if i > 1:
            units[i - 2].finish()
    units[4].across()
    side_copies = []
    piece = all_out.at[:, :, mine]
    for k in range(1, n_blk):
        copy = remote(piece, piece, side.at[0, k], side.at[1, k], pc.sibling(k))
        copy.start()
        side_copies.append(copy)
    units[3].finish()
    units[4].finish()
    for copy in side_copies:
        copy.wait()
    for unit in units:
        unit.drain()


class Scatter:
    def __init__(self, place, unit, chunk, bufs, send, recv):
        self.place, self.chunk = place, chunk
        self.diag, self.near, self.far, self.up, self.down = bufs
        self.send = lambda kind, zz: send.at[unit, kind, zz]
        self.recv = lambda kind, zz: recv.at[unit, kind, zz]

    def copy(self, src, dst, kind, zz, device):
        return remote(src, dst.at[zz], self.send(kind, zz), self.recv(kind, zz), device)

    def arrived(self, buf, kind, zz):
        self.copy(buf.at[zz], buf, kind, zz, self.place.sibling(1)).wait_recv()

    def start(self):
        pc = self.place

        @pl.loop(0, pc.length)
        def _(zz):
            near, far = pc.routes(zz)
            to = pc.at(pc.z, near)
            self.copy(self.chunk(zz * PLANE + pc.diag), self.diag, 0, zz, to).start()
            self.copy(self.chunk(zz * PLANE + near), self.near, 1, zz, to).start()

    def middle(self):
        pc = self.place

        @pl.loop(0, pc.length)
        def _(zz):
            near, far = pc.routes(zz)
            self.arrived(self.diag, 0, zz)
            total = self.diag[zz].astype(F32) + self.chunk(zz * PLANE + far)[...].astype(F32)
            self.diag[zz] = total.astype(BF16)
            self.copy(self.diag.at[zz], self.far, 2, zz, pc.at(pc.z, far)).start()

    def settle(self):
        pc = self.place

        @pl.loop(0, pc.length)
        def _(zz):
            self.arrived(self.near, 1, zz)
            self.arrived(self.far, 2, zz)
            total = self.near[zz].astype(F32) + self.far[zz].astype(F32)
            total += self.chunk(zz * PLANE + pc.p)[...].astype(F32)
            self.near[zz] = total.astype(BF16)

    def along(self, s):
        pc = self.place

        def pass_on(zz, buf, kind, more, onward):
            @pl.when(more)
            def _():
                self.arrived(buf, kind, zz)
                total = self.near[zz].astype(F32) + buf[zz].astype(F32)
                self.near[zz] = total.astype(BF16)

            self.copy(self.near.at[zz], buf, kind, zz, pc.at(onward, pc.p)).start()

        pl.when(pc.z + s < pc.length)(lambda: pass_on(pc.z + s, self.up, 3, pc.z > 0, pc.z + 1))
        pl.when(pc.z >= s)(
            lambda: pass_on(pc.z - s, self.down, 4, pc.z < pc.length - 1, pc.z - 1)
        )

    def finish(self, total):
        pc = self.place
        total[...] = self.near[pc.z].astype(F32)

        def more(buf, kind):
            self.arrived(buf, kind, pc.z)
            total[...] += buf[pc.z].astype(F32)

        pl.when(pc.z > 0)(lambda: more(self.up, 3))
        pl.when(pc.z < pc.length - 1)(lambda: more(self.down, 4))

    def drain(self):
        pc = self.place

        def sent(kind, zz):
            self.copy(self.near.at[zz], self.near, kind, zz, pc.sibling(1)).wait_send()

        @pl.loop(0, pc.length)
        def _(zz):
            sent(0, zz)
            sent(1, zz)
            sent(2, zz)
            pl.when(zz > pc.z)(lambda: sent(3, zz))
            pl.when(zz < pc.z)(lambda: sent(4, zz))


def scatter_kernel(n_dp, n_blk, *refs):
    grads, outs, rest = refs[:4], refs[4:8], refs[8:]
    bufs, totals, rest = rest[:20], rest[20:24], rest[24:]
    side_buf, send, recv, side, last = rest
    proj, fc, out, qkv = grads
    pc = Place(n_dp, n_blk)
    pc.greet()
    wide = out.shape[2] // n_blk

    def columns(core):
        return pl.ds(pl.multiple_of(core * wide, LANES), wide)

    chunks = [
        lambda slot: proj.at[slot],
        lambda slot: fc.at[slot],
        lambda slot: side_buf.at[0, slot],
        lambda slot: qkv.at[slot],
    ]
    units = [
        Scatter(pc, i, chunks[i], bufs[5 * i : 5 * i + 5], send, recv) for i in range(4)
    ]
    units[0].start()
    units[1].start()
    side_copies = []
    for k in range(1, n_blk):
        dev = pc.sibling(k)
        copy = remote(
            out.at[:, :, columns(dev[1])], side_buf.at[k], side.at[0, k], side.at[1, k], dev
        )
        copy.start()
        side_copies.append(copy)

    def side_sum():
        for copy in side_copies:
            copy.wait()

        @pl.loop(0, n_dp)
        def _(slot):
            total = out[slot, :, columns(pc.c)].astype(F32)
            for k in range(1, n_blk):
                total += side_buf[k, slot].astype(F32)
            side_buf[0, slot] = total.astype(BF16)

    pending = []

    def spread(i):
        units[i].finish(totals[i])
        total = totals[i]
        pieces = [(total, outs[i].at[pc.c])]
        for j, (src, dst) in enumerate(pieces):
            keep = pltpu.make_async_copy(src, dst, last.at[i, 0, 0])
            keep.start()
            pending.append(keep)
            for k in range(1, n_blk):
                copy = remote(src, dst, last.at[i, 0, k], last.at[i, 1, k], pc.sibling(k))
                copy.start()
                pending.append(copy)

    units[0].middle()
    side_sum()
    units[2].start()
    units[1].middle()
    units[3].start()
    units[0].settle()
    for s in range(pc.length - 1, 0, -1):
        units[0].along(s)
    units[2].middle()
    units[1].settle()
    for s in range(pc.length - 1, 0, -1):
        units[1].along(s)
    spread(0)
    units[3].middle()
    units[2].settle()
    for s in range(pc.length - 1, 0, -1):
        units[2].along(s)
    units[3].settle()
    for s in range(pc.length - 1, 0, -1):
        units[3].along(s)
    spread(1)
    spread(2)
    spread(3)
    for copy in pending:
        copy.wait()
    for unit in units:
        unit.drain()


def gather_weights(n_dp, n_blk, qkv, out, fc, proj, small):
    shards = (qkv, out, fc, proj, small)
    shapes = [
        jax.ShapeDtypeStruct((n_dp, a.shape[0], a.shape[1] * (n_blk if a is out else 1)), BF16)
        for a in shards
    ]
    length = n_dp // PLANE
    hbm = pl.BlockSpec(memory_space=pl.ANY)
    return pl.pallas_call(
        functools.partial(gather_kernel, n_dp, n_blk),
        out_shape=shapes,
        in_specs=[hbm] * 5,
        out_specs=[hbm] * 5,
        scratch_shapes=[
            pltpu.SemaphoreType.DMA((5, 5, length)),
            pltpu.SemaphoreType.DMA((5, n_dp)),
            pltpu.SemaphoreType.DMA((5,)),
            pltpu.SemaphoreType.DMA((2, n_blk)),
        ],
        compiler_params=pltpu.CompilerParams(
            collective_id=0, has_side_effects=True, vmem_limit_bytes=VMEM_BYTES
        ),
    )(*shards)


def scatter_grads(n_dp, n_blk, proj, fc, out, qkv):
    length = n_dp // PLANE
    grads = (proj, fc, out, qkv)
    sizes = [a.shape[1:] for a in grads]
    sizes[2] = (sizes[2][0], sizes[2][1] // n_blk)
    vmem = pl.BlockSpec(memory_space=pltpu.VMEM)
    scratch = [pltpu.VMEM((length,) + size, BF16) for size in sizes for _ in range(5)]
    scratch += [pltpu.VMEM(size, F32) for size in sizes]
    scratch += [
        pltpu.VMEM((n_blk, n_dp) + sizes[2], BF16),
        pltpu.SemaphoreType.DMA((4, 5, length)),
        pltpu.SemaphoreType.DMA((4, 5, length)),
        pltpu.SemaphoreType.DMA((2, n_blk)),
        pltpu.SemaphoreType.DMA((4, 2, n_blk)),
    ]
    return pl.pallas_call(
        functools.partial(scatter_kernel, n_dp, n_blk),
        out_shape=[jax.ShapeDtypeStruct((n_blk,) + size, F32) for size in sizes],
        in_specs=[vmem] * 4,
        out_specs=[pl.BlockSpec(memory_space=pl.ANY)] * 4,
        scratch_shapes=scratch,
        compiler_params=pltpu.CompilerParams(
            collective_id=1, has_side_effects=True, vmem_limit_bytes=VMEM_BYTES
        ),
    )(*grads)


def lane_split(value, lane, first, base):
    for i in range(3):
        term = value.astype(BF16)
        base = jnp.where(lane == first + i, term, base)
        value = value - term.astype(F32)
    return base


def causal_tail(scores, block, axis, masked):
    key_axis, query_axis = (0, 1) if axis == 0 else (1, 0)
    tail_shape = (block, block)
    keep = lax.broadcasted_iota(jnp.int32, tail_shape, key_axis) <= lax.broadcasted_iota(
        jnp.int32, tail_shape, query_axis
    )
    size = scores.shape[axis]
    if size == block:
        return jnp.where(keep, scores, masked)
    head = lax.slice_in_dim(scores, 0, size - block, axis=axis)
    tail = jnp.where(keep, lax.slice_in_dim(scores, size - block, size, axis=axis), masked)
    return jnp.concatenate([head, tail], axis=axis)


def causal_all(scores, offset, axis, masked):
    key_axis, query_axis = (0, 1) if axis == 0 else (1, 0)
    keep = (
        lax.broadcasted_iota(jnp.int32, scores.shape, key_axis)
        <= lax.broadcasted_iota(jnp.int32, scores.shape, query_axis) + offset
    )
    return jnp.where(keep, scores, masked)


def query_blocks(total, block, run):
    count = total // block
    if count <= 4:
        for b in range(count):
            run(
                b * block,
                (b + 1) * block,
                lambda scores, axis, masked: causal_tail(scores, block, axis, masked),
            )
    else:

        @pl.loop(0, count)
        def _(b):
            first = pl.multiple_of(b * block, block)
            run(first, total, lambda scores, axis, masked: causal_all(scores, first, axis, masked))


def attend_kernel(block, scale, q_ref, k_ref, v_ref, key_aug, query_aug, slope_ref, out_ref, qx_ref):
    total = q_ref.shape[0]
    half = LANES // 2
    lane = lax.broadcasted_iota(jnp.int32, (1, LANES), 1)

    def run(first, keys, mask):
        rows = pl.ds(first, block)
        result = None
        for hh in range(2):
            own = (lane < half) if hh == 0 else (lane >= half)
            base = half * (1 - hh)
            aug = query_aug[rows, :] + slope_ref[0, hh : hh + 1, :]
            query = jnp.where(own, q_ref[rows, :] * BF16(scale), aug)
            key = jnp.where(own, k_ref[0:keys, :], key_aug[0:keys, :])
            value = jnp.where(own, v_ref[0:keys, :], BF16(1))
            scores = mask(matmul_nt(query, key), 1, MASKED)
            top = jnp.max(scores, axis=1, keepdims=True)
            weights = jnp.exp(scores - top).astype(BF16)
            sums = matmul(weights, value)
            log_total = top + jnp.log(sums[:, base : base + 1])
            qx_ref[0, hh, rows, :] = lane_split(-log_total, lane, base + 8, query)
            part = sums / pltpu.roll(sums, half, 1)
            result = part if hh == 0 else jnp.where(own, part, result)
        out_ref[rows, :] = result.astype(BF16)

    query_blocks(total, block, run)


def attend_back_kernel(
    block, scale, qx_ref, k_ref, v_ref, key_aug, out_ref, grad_ref, dq_ref, dk_ref, dv_ref, dk_acc, dv_acc
):
    total = k_ref.shape[0]
    half = LANES // 2
    lane = lax.broadcasted_iota(jnp.int32, (1, LANES), 1)
    dk_acc[...] = jnp.zeros_like(dk_acc)
    dv_acc[...] = jnp.zeros_like(dv_acc)

    def run(first, keys, mask):
        rows = pl.ds(first, block)
        grad = grad_ref[rows, :]
        product = grad.astype(F32) * out_ref[rows, :].astype(F32)
        dq = None
        dk = None
        dv = None
        for hh in range(2):
            own = (lane < half) if hh == 0 else (lane >= half)
            base = half * (1 - hh)
            query = qx_ref[0, hh, rows, :]
            key = jnp.where(own, k_ref[0:keys, :], key_aug[0:keys, :])
            delta = jnp.sum(jnp.where(own, product, 0.0), axis=1, keepdims=True)
            grad_own = jnp.where(own, grad, BF16(0))
            grad_aug = lane_split(-delta, lane, base, grad_own)
            value = jnp.where(own, v_ref[0:keys, :], BF16(1))
            weights = mask(jnp.exp(matmul_nt(key, query)), 0, 0.0)
            change = (weights * matmul_nt(value, grad_aug)).astype(BF16)
            key_own = jnp.where(own, key, BF16(0))
            query_own = jnp.where(own, query, BF16(0))
            dv_part = matmul(weights.astype(BF16), grad_own)
            dk_part = matmul(change, query_own)
            dq_part = matmul_tn(change, key_own)
            dv = dv_part if hh == 0 else dv + dv_part
            dk = dk_part if hh == 0 else dk + dk_part
            dq = dq_part if hh == 0 else dq + dq_part
        dq_ref[rows, :] = (dq * scale).astype(BF16)
        dk_acc[0:keys, :] += dk
        dv_acc[0:keys, :] += dv

    query_blocks(total, block, run)
    dk_ref[...] = dk_acc[...].astype(BF16)
    dv_ref[...] = dv_acc[...].astype(BF16)


def gelu_pair(u):
    k = math.sqrt(2.0 / math.pi)
    square = u * u
    t = jnp.tanh(k * u * (1.0 + 0.044715 * square))
    plus = 0.5 * (1.0 + t)
    slope = plus + (0.5 * k) * u * (1.0 - t * t) * (1.0 + 3 * 0.044715 * square)
    return u * plus, slope


def whole(ref, cols):
    value = ref[:, :, cols]
    return value.reshape(value.shape[0] * value.shape[1], value.shape[2])


def forward_kernel(n_dp, n_blk, scale, *refs):
    (small, qkv, out, fc, proj, tokens, out_grad, key_own, query_own, slope_ref) = refs[:10]
    (w_qkv_o, w_out_o, w_fc_o, w_proj_o, vec_o, fcb_o, h1_o, mixed_o, heads_o, att_o, qx_o, mid_o, h2_o, hid_o, slope_o, dy_o, key_o, gp_o) = refs[10:28]
    (w_small, w_qkv, w_out, w_fc, w_proj, vec, fcb, x_all, h1, mixed, heads, att, qx, mid, h2, hid, gslope, dy, key_aug, query_aug, gp) = refs[28:49]
    send, recv, local, side, load, save_sem = refs[49:]
    pc = Place(n_dp, n_blk)
    sib = pc.sibling(1)
    width = tokens.shape[1]
    rows_own = tokens.shape[0]
    total = n_blk * rows_own
    wide = out.shape[1]
    tile = 256
    mine = pl.ds(pl.multiple_of(pc.c * rows_own, rows_own), rows_own)
    theirs = pl.ds(pl.multiple_of(sib[1] * rows_own, rows_own), rows_own)
    my_cols = pl.ds(pl.multiple_of(pc.c * wide, LANES), wide)
    pc.greet()
    parts = [
        (small, lambda slot: w_small.at[slot]),
        (qkv, lambda slot: w_qkv.at[slot]),
        (out, lambda slot: w_out.at[slot, :, my_cols]),
        (fc, lambda slot: w_fc.at[slot]),
        (proj, lambda slot: w_proj.at[slot]),
    ]
    u_small, u_qkv, u_out, u_fc, u_proj = [
        Gather(pc, i, own, chunk, send, recv, local) for i, (own, chunk) in enumerate(parts)
    ]
    saves = []

    def exchange(i, src, dst):
        copy = remote(src, dst, side.at[0, i], side.at[1, i], sib)
        copy.start()
        return copy

    def keep(i, src, dst):
        copy = pltpu.make_async_copy(src, dst, load.at[i])
        copy.start()
        return copy

    def save(i, src, dst):
        copy = pltpu.make_async_copy(src, dst, save_sem.at[i])
        copy.start()
        saves.append(copy)

    u_small.start()
    u_qkv.start()
    first = [
        exchange(0, tokens, x_all.at[mine]),
        keep(0, tokens, x_all.at[mine]),
        exchange(1, key_own, key_aug.at[mine]),
        keep(1, key_own, key_aug.at[mine]),
        exchange(2, query_own, query_aug.at[mine]),
        keep(2, query_own, query_aug.at[mine]),
    ]
    for s in range(1, pc.length):
        u_small.along(s)
        u_qkv.along(s)
    u_small.across()
    u_out.start()
    later = [exchange(3, out_grad, dy.at[mine]), keep(3, out_grad, dy.at[mine])]
    u_small.finish()
    for copy in first:
        copy.wait()
    per = n_dp // (width // LANES)
    for t in range(width // LANES):
        rows = w_small[t * per].astype(F32)
        for k in range(1, per):
            rows += w_small[t * per + k].astype(F32)
        vec[:, t * LANES : (t + 1) * LANES] = rows
    for t in range(n_dp):
        fcb[:, t * LANES : (t + 1) * LANES] = w_small[t, 8:9, :].astype(F32)
    save(0, vec, vec_o)
    save(1, fcb, fcb_o)

    @pl.loop(0, total // tile)
    def _(b):
        rows = pl.ds(pl.multiple_of(b * tile, tile), tile)
        h1[rows, :] = layer_norm(x_all[rows, :].astype(F32), vec[0:1, :], vec[1:2, :]).astype(BF16)

    save(2, h1, h1_o)
    for s in range(1, pc.length):
        u_out.along(s)
    u_fc.start()
    u_qkv.across()
    for s in range(1, pc.length):
        u_fc.along(s)
    u_out.across()
    u_qkv.finish()
    save(3, w_qkv, w_qkv_o)
    for third in range(3):
        for b in range(wide // tile):

            @pl.loop(0, total // 512)
            def _(m, third=third, b=b):
                rows = pl.ds(pl.multiple_of(m * 512, 512), 512)
                cols = pl.ds(third * wide + b * tile, tile)
                value = matmul(h1[rows, :], whole(w_qkv, cols))
                if third != 1:
                    at = pl.ds(pl.multiple_of(pc.c * wide, LANES) + b * tile, tile)
                    value += vec[pl.ds(2 + third // 2, 1), at]
                mixed[rows, cols] = value.astype(BF16)

    save(4, mixed, mixed_o)
    u_proj.start()
    for j in range(wide // LANES):
        cols = [pl.ds(i * wide + j * LANES, LANES) for i in range(3)]
        attend_kernel(
            tile,
            scale,
            mixed.at[:, cols[0]],
            mixed.at[:, cols[1]],
            mixed.at[:, cols[2]],
            key_aug,
            query_aug,
            slope_ref.at[pl.ds(j, 1)],
            heads.at[:, cols[0]],
            qx.at[pl.ds(j, 1)],
        )
        if j == 0:
            u_out.finish()
            piece = w_out.at[:, :, my_cols]
            share = exchange(4, piece, piece)
        if j + 1 < pc.length:
            u_proj.along(j + 1)
    save(5, heads, heads_o)
    save(6, qx, qx_o)
    swap = exchange(5, heads.at[theirs], att.at[:, my_cols])
    stay = keep(4, heads.at[mine], att.at[:, my_cols])
    share.wait()
    save(7, w_out, w_out_o)
    swap.wait()
    stay.wait()
    save(8, att, att_o)

    @pl.loop(0, width // tile)
    def _(b):
        cols = pl.ds(pl.multiple_of(b * tile, tile), tile)
        value = matmul(att[...], whole(w_out, cols))
        mid[:, cols] = x_all[mine, cols].astype(F32) + value + vec[4:5, cols]

    @pl.loop(0, rows_own // tile)
    def _(b):
        rows = pl.ds(pl.multiple_of(b * tile, tile), tile)
        into = pl.ds(pl.multiple_of(pc.c * rows_own + b * tile, tile), tile)
        h2[into, :] = layer_norm(mid[rows, :], vec[5:6, :], vec[6:7, :]).astype(BF16)

    both = exchange(6, h2.at[mine], h2.at[mine])
    save(9, mid, mid_o)
    u_fc.across()
    both.wait()
    save(10, h2, h2_o)
    u_fc.finish()
    save(11, w_fc, w_fc_o)

    def feed(b):
        cols = pl.ds(pl.multiple_of(b * tile, tile), tile)

        @pl.loop(0, total // 512)
        def _(m):
            rows = pl.ds(pl.multiple_of(m * 512, 512), 512)
            value = matmul(h2[rows, :], whole(w_fc, cols)) + fcb[:, cols]
            value, slope = gelu_pair(value)
            hid[rows, cols] = value.astype(BF16)
            gslope[rows, cols] = slope.astype(BF16)

    blocks = hid.shape[1] // tile
    pl.loop(0, blocks)(feed)
    save(12, hid, hid_o)
    save(13, gslope, slope_o)
    for copy in later:
        copy.wait()
    save(14, dy, dy_o)
    save(15, key_aug, key_o)
    u_proj.across()
    slots = tile // proj.shape[0]

    @pl.loop(0, blocks)
    def _(b):
        cols = pl.ds(pl.multiple_of(b * tile, tile), tile)
        for n in range(width // 512):
            value = matmul_tn(hid[:, cols], dy[:, n * 512 : (n + 1) * 512]).astype(BF16)
            gp[pl.ds(b * slots, slots), :, n * 512 : (n + 1) * 512] = value.reshape(slots, proj.shape[0], 512)

    save(16, gp, gp_o)
    u_proj.finish()
    save(17, w_proj, w_proj_o)
    for copy in saves:
        copy.wait()
    for unit in (u_small, u_qkv, u_out, u_fc, u_proj):
        unit.drain()


def forward(n_dp, n_blk, scale, qkv, out, fc, proj, small, tokens, out_grad, key_own, query_own, slope_aug):
    rows_own, width = tokens.shape
    total = n_blk * rows_own
    wide = out.shape[1]
    pairs = wide // LANES
    ff = n_dp * proj.shape[0]
    length = n_dp // PLANE
    shape = jax.ShapeDtypeStruct
    weights = [(n_dp,) + a.shape for a in (qkv, out, fc, proj)]
    weights[1] = (n_dp, out.shape[0], width)
    rest = [
        ((16, width), F32),
        ((1, ff), F32),
        ((total, width), BF16),
        ((total, 3 * wide), BF16),
        ((total, wide), BF16),
        ((rows_own, width), BF16),
        ((pairs, 2, total, LANES), BF16),
        ((rows_own, width), F32),
        ((total, width), BF16),
        ((total, ff), BF16),
        ((total, ff), BF16),
        ((total, width), BF16),
        ((total, LANES), BF16),
        (weights[3], BF16),
    ]
    outs = [(w, BF16) for w in weights] + rest
    scratch = [((n_dp,) + small.shape, BF16)] + outs[:6]
    scratch += [((total, width), BF16)] + outs[6:17] + [((total, LANES), BF16)] + outs[17:]
    hbm = pl.BlockSpec(memory_space=pl.ANY)
    vmem = pl.BlockSpec(memory_space=pltpu.VMEM)
    return pl.pallas_call(
        functools.partial(forward_kernel, n_dp, n_blk, scale),
        out_shape=[shape(*o) for o in outs],
        in_specs=[hbm] * 9 + [vmem],
        out_specs=[hbm] * len(outs),
        scratch_shapes=[pltpu.VMEM(*s) for s in scratch]
        + [
            pltpu.SemaphoreType.DMA((5, 5, length)),
            pltpu.SemaphoreType.DMA((5, n_dp)),
            pltpu.SemaphoreType.DMA((5,)),
            pltpu.SemaphoreType.DMA((2, 7)),
            pltpu.SemaphoreType.DMA((5,)),
            pltpu.SemaphoreType.DMA((18,)),
        ],
        compiler_params=pltpu.CompilerParams(
            collective_id=2, has_side_effects=True, vmem_limit_bytes=VMEM_BYTES
        ),
    )(small, qkv, out, fc, proj, tokens, out_grad, key_own, query_own, slope_aug)


def columns_spec(rows, first):
    return pl.BlockSpec((rows, LANES), lambda j: (0, first + j))


def attend(qkv, key_aug, query_aug, slope_aug, scale):
    total, wide = qkv.shape[0], qkv.shape[1] // 3
    pairs = wide // LANES
    block = math.gcd(total, 256)
    whole = pl.BlockSpec((total, LANES), lambda j: (0, 0))
    return pl.pallas_call(
        functools.partial(attend_kernel, block, scale),
        grid=(pairs,),
        out_shape=[
            jax.ShapeDtypeStruct((total, wide), BF16),
            jax.ShapeDtypeStruct((pairs, 2, total, LANES), BF16),
        ],
        in_specs=[
            columns_spec(total, 0),
            columns_spec(total, pairs),
            columns_spec(total, 2 * pairs),
            whole,
            whole,
            pl.BlockSpec((1, 2, LANES), lambda j: (j, 0, 0)),
        ],
        out_specs=[
            columns_spec(total, 0),
            pl.BlockSpec((1, 2, total, LANES), lambda j: (j, 0, 0, 0)),
        ],
        compiler_params=pltpu.CompilerParams(vmem_limit_bytes=VMEM_BYTES),
    )(qkv, qkv, qkv, key_aug, query_aug, slope_aug)


def attend_back(query_ext, qkv, key_aug, attended, grad, scale):
    total, wide = attended.shape
    pairs = wide // LANES
    block = math.gcd(total, 256)
    whole = pl.BlockSpec((total, LANES), lambda j: (0, 0))
    out = jax.ShapeDtypeStruct((total, wide), BF16)
    return pl.pallas_call(
        functools.partial(attend_back_kernel, block, scale),
        grid=(pairs,),
        out_shape=[out] * 3,
        in_specs=[
            pl.BlockSpec((1, 2, total, LANES), lambda j: (j, 0, 0, 0)),
            columns_spec(total, pairs),
            columns_spec(total, 2 * pairs),
            whole,
            columns_spec(total, 0),
            columns_spec(total, 0),
        ],
        out_specs=[columns_spec(total, 0)] * 3,
        scratch_shapes=[pltpu.VMEM((total, LANES), F32)] * 2,
        compiler_params=pltpu.CompilerParams(vmem_limit_bytes=VMEM_BYTES),
    )(query_ext, qkv, qkv, key_aug, attended, grad)


def attention_terms(positions, rows):
    high = (positions // 256) * 256
    low = positions - high
    first = rows == 0
    one = jnp.ones_like(positions)
    zero = jnp.zeros_like(positions)

    def table(columns):
        cols = jnp.stack([col.astype(F32) for col in columns], axis=1)
        cols = jnp.pad(cols, ((0, 0), (0, LANES // 2 - len(columns))))
        return jnp.concatenate([cols, cols], axis=1).astype(BF16)

    key_aug = table([high, high, high, low, low, low, first, ~first, one, one, one])
    other = jnp.where(first, 0.0, MASKED)
    query_aug = table([zero] * 6 + [other, jnp.where(first, MASKED, 0.0)])
    return key_aug, query_aug


def slope_terms(slopes, n_blk, c):
    heads = slopes.shape[0] // n_blk
    mine = lax.dynamic_slice_in_dim(slopes, c * heads, heads, 0)
    parts = []
    left = mine
    for _ in range(3):
        term = lax.reduce_precision(left, 8, 7)
        parts.append(term)
        left = left - term
    cols = jnp.stack(parts + parts, axis=1)
    cols = jnp.pad(cols, ((0, 0), (0, LANES // 2 - 6)))
    slope_aug = jnp.concatenate([cols, cols], axis=1).astype(BF16).reshape(heads // 2, 2, LANES)
    keep = (jnp.arange(LANES) // (LANES // 2))[None, None, :] == 1 - jnp.arange(2)[None, :, None]
    return jnp.where(keep, slope_aug, 0)


def body(
    n_dp,
    n_blk,
    tokens,
    positions,
    row_ids,
    alibi_slope,
    ln1_gain,
    ln1_bias,
    qkv_weight,
    query_bias,
    value_bias,
    out_weight,
    out_bias,
    ln2_gain,
    ln2_bias,
    fc_weight,
    fc_bias,
    proj_weight,
    proj_bias,
    out_grad,
):
    local, width = tokens.shape
    heads = alibi_slope.shape[0]
    hidden_all = fc_weight.shape[1]
    scale = 1.0 / math.sqrt(width // heads)
    c = lax.axis_index("blk")
    dp = lax.axis_index("dp")
    wide = width // n_blk
    shard = width // n_dp
    piece = hidden_all // (n_dp * n_blk)
    total = n_blk * local

    def swap(a):
        return lax.ppermute(a, "blk", [(0, 1), (1, 0)])

    def blk_gather(a):
        if n_blk != 2:
            return lax.all_gather(a, "blk", axis=0, tiled=True)
        other = swap(a)
        return jnp.where(
            c == 0, jnp.concatenate([a, other], 0), jnp.concatenate([other, a], 0)
        )

    def blk_sum(a):
        if n_blk != 2:
            return lax.psum_scatter(a.astype(BF16), "blk", scatter_dimension=0, tiled=True).astype(F32)
        own = lax.dynamic_slice_in_dim(a, c * local, local, 0)
        other = lax.dynamic_slice_in_dim(a, (1 - c) * local, local, 0)
        return own + swap(other.astype(BF16)).astype(F32)

    def to_tokens(a):
        if n_blk != 2:
            moved = lax.all_to_all(a.reshape(n_blk, local, wide), "blk", 0, 0)
            return jnp.transpose(moved, (1, 0, 2)).reshape(local, width)
        own = lax.dynamic_slice_in_dim(a, c * local, local, 0)
        other = swap(lax.dynamic_slice_in_dim(a, (1 - c) * local, local, 0))
        return jnp.where(
            c == 0, jnp.concatenate([own, other], 1), jnp.concatenate([other, own], 1)
        )

    def to_heads(a):
        if n_blk != 2:
            moved = lax.all_to_all(
                jnp.transpose(a.reshape(local, n_blk, wide), (1, 0, 2)), "blk", 0, 0
            )
            return moved.reshape(total, wide)
        own = lax.dynamic_slice_in_dim(a, c * wide, wide, 1)
        other = swap(lax.dynamic_slice_in_dim(a, (1 - c) * wide, wide, 1))
        return jnp.where(
            c == 0, jnp.concatenate([own, other], 0), jnp.concatenate([other, own], 0)
        )

    def mine(a, axis, size):
        return lax.dynamic_slice_in_dim(a, c * size, size, axis)

    qkv_own = jnp.concatenate(
        [mine(qkv_weight[:, i * width : (i + 1) * width], 1, wide) for i in range(3)], 1
    ).astype(BF16)
    out_own = mine(out_weight, 1, wide).astype(BF16)
    fc_own = mine(fc_weight.reshape(shard, n_dp, n_blk, piece), 2, 1).reshape(shard, n_dp * piece)
    proj_own = mine(proj_weight, 0, piece)
    vectors = [ln1_gain, ln1_bias, query_bias, value_bias, out_bias, ln2_gain, ln2_bias, proj_bias]
    vectors.append(mine(fc_bias, 0, piece))
    small = jnp.stack(
        [
            lax.dynamic_update_slice_in_dim(
                jnp.zeros((LANES,), F32), vec, lax.rem(dp * vec.shape[0], LANES), 0
            )
            for vec in vectors
        ]
    )
    small = jnp.pad(small, ((0, 16 - len(vectors)), (0, 0))).astype(BF16)
    inputs = tokens.astype(F32)
    grad_top = out_grad.astype(F32)
    slope_aug = slope_terms(alibi_slope, n_blk, c)
    shards = (qkv_own, out_own, fc_own.astype(BF16), proj_own.astype(BF16), small)
    if n_blk == 2 and piece == LANES:
        key_own, query_own = attention_terms(positions, row_ids)
        (
            full_qkv,
            full_out,
            full_fc,
            full_proj,
            vecs,
            _,
            normed,
            mixed,
            attended_heads,
            attended,
            query_ext,
            middle,
            every_two,
            hidden,
            gelu_slope,
            every_grad,
            key_aug,
            grad_proj_weight,
        ) = forward(n_dp, n_blk, scale, *shards, tokens, out_grad, key_own, query_own, slope_aug)
        weight_qkv = full_qkv.reshape(width, 3 * wide)
        weight_out = full_out.reshape(width, width)
        weight_fc = full_fc.reshape(width, n_dp * piece)
        weight_proj = full_proj.reshape(n_dp * piece, width)
        gain_one, bias_one, gain_two, bias_two, bias_proj = (vecs[i] for i in (0, 1, 5, 6, 7))
    else:
        full_qkv, full_out, full_fc, full_proj, full_small = gather_weights(
            n_dp, n_blk, *shards
        )
        weight_qkv = full_qkv.reshape(width, 3 * wide)
        weight_out = full_out.reshape(width, width)
        weight_fc = full_fc.reshape(width, n_dp * piece)
        weight_proj = full_proj.reshape(n_dp * piece, width)
        spread = full_small.astype(F32)

        def vector(i):
            size = vectors[i].shape[0]
            per = LANES // size
            rows = jnp.sum(spread[:, i].reshape(n_dp // per, per, LANES), axis=1)
            return rows.reshape(n_dp * size)

        gain_one, bias_one, bias_query, bias_value, bias_out, gain_two, bias_two, bias_proj, bias_fc = (
            vector(i) for i in range(len(vectors))
        )
        place = blk_gather(jnp.stack([positions, row_ids], axis=1))
        key_aug, query_aug = attention_terms(place[:, 0], place[:, 1])
        every_token = blk_gather(tokens).astype(F32)
        every_grad = blk_gather(out_grad)
        normed = layer_norm(every_token, gain_one, bias_one).astype(BF16)
        bias_qkv = jnp.concatenate(
            [mine(bias_query, 0, wide), jnp.zeros((wide,), F32), mine(bias_value, 0, wide)]
        )
        mixed = (matmul(normed, weight_qkv) + bias_qkv).astype(BF16)
        attended_heads, query_ext = attend(mixed, key_aug, query_aug, slope_aug, scale)
        attended = to_tokens(attended_heads)
        middle = inputs + matmul(attended, weight_out) + bias_out
        normed_two = layer_norm(middle, gain_two, bias_two).astype(BF16)
        every_two = blk_gather(normed_two)
        hidden_pre = matmul(every_two, weight_fc) + bias_fc
        hidden_vals, gelu_slope = gelu_pair(hidden_pre)
        hidden = hidden_vals.astype(BF16)
        grad_proj_weight = matmul_tn(hidden, every_grad).astype(BF16)
    layer_output = (middle + blk_sum(matmul(hidden, weight_proj)) + bias_proj).astype(BF16)
    grad_proj_bias = jnp.sum(grad_top, axis=0)
    grad_pre = (gelu_slope * matmul_nt(every_grad, weight_proj)).astype(BF16)
    grad_fc_weight = matmul_tn(every_two, grad_pre).astype(BF16)
    grad_fc_bias = jnp.sum(grad_pre.astype(F32), axis=0)
    grad_normed_two = blk_sum(matmul_nt(grad_pre, weight_fc))
    _, norm_two_back = jax.vjp(layer_norm, middle, gain_two, bias_two)
    grad_mid_norm, grad_gain_two, grad_bias_two = norm_two_back(grad_normed_two)
    grad_middle = grad_top + grad_mid_norm
    grad_branch = grad_middle.astype(BF16)
    grad_out_weight = matmul_tn(attended, grad_branch).astype(BF16)
    grad_out_bias = jnp.sum(grad_branch.astype(F32), axis=0)
    grad_heads = to_heads(matmul_nt(grad_branch, weight_out).astype(BF16))
    grad_mixed = jnp.concatenate(
        attend_back(query_ext, mixed, key_aug, attended_heads, grad_heads, scale), axis=1
    )
    grad_qkv_weight = matmul_tn(normed, grad_mixed).astype(BF16)
    sums = jnp.sum(grad_mixed.astype(F32), axis=0)
    grad_normed = blk_sum(matmul_nt(grad_mixed, weight_qkv))
    _, norm_one_back = jax.vjp(layer_norm, inputs, gain_one, bias_one)
    grad_in_norm, grad_gain_one, grad_bias_one = norm_one_back(grad_normed)
    input_grad = grad_middle + grad_in_norm

    proj_sum, fc_sum, out_sum, qkv_sum = scatter_grads(
        n_dp,
        n_blk,
        grad_proj_weight.reshape(n_dp, piece, width),
        grad_fc_weight.reshape(n_dp, shard, n_dp * piece),
        grad_out_weight.reshape(n_dp, shard, width),
        grad_qkv_weight.reshape(n_dp, shard, 3 * wide),
    )

    def spread_out(vec, size):
        parts = vec.reshape(-1, 1, size)
        return jnp.where((jnp.arange(n_blk) == c)[None, :, None], parts, 0.0).reshape(-1)

    small_grads = [
        grad_gain_one,
        grad_bias_one,
        spread_out(sums[:wide], wide),
        spread_out(sums[2 * wide :], wide),
        grad_out_bias,
        grad_gain_two,
        grad_bias_two,
        grad_proj_bias,
        spread_out(grad_fc_bias, piece),
    ]
    small_sum = lax.psum(jnp.concatenate(small_grads), ("dp", "blk"))
    finals = []
    at = 0
    for vec in small_grads:
        size = vec.shape[0]
        finals.append(lax.dynamic_slice_in_dim(small_sum, at + dp * (size // n_dp), size // n_dp, 0))
        at += size
    g_gain1, g_bias1, g_query, g_value, g_out, g_gain2, g_bias2, g_proj, g_fc = finals
    final_qkv = jnp.transpose(qkv_sum.reshape(n_blk, shard, 3, wide), (1, 2, 0, 3))
    final_fc = jnp.transpose(fc_sum.reshape(n_blk, shard, n_dp, piece), (1, 2, 0, 3))
    return (
        layer_output,
        input_grad,
        g_gain1,
        g_bias1,
        final_qkv.reshape(shard, 3 * width),
        g_query,
        g_value,
        jnp.transpose(out_sum, (1, 0, 2)).reshape(shard, width),
        g_out,
        g_gain2,
        g_bias2,
        final_fc.reshape(shard, hidden_all),
        g_fc,
        proj_sum.reshape(n_blk * piece, width),
        g_proj,
    )


def solution(mesh):
    both, rows, one = P(("dp", "blk"), None), P("dp", None), P("dp")
    tokens = P(("dp", "blk"))
    in_specs = (both, tokens, tokens, P(), one, one, rows, one, one, rows, one, one, one, rows, one, rows, one, both)
    out_specs = (both, both, one, one, rows, one, one, rows, one, one, one, rows, one, rows, one)
    return jax.shard_map(
        functools.partial(body, mesh.shape["dp"], mesh.shape["blk"]),
        mesh=mesh,
        in_specs=in_specs,
        out_specs=out_specs,
        check_vma=False,
    )
```

```python
import functools
import math

import jax
import jax.numpy as jnp
from jax import lax
from jax.experimental import pallas as pl
from jax.experimental.pallas import tpu as pltpu
from jax.sharding import PartitionSpec as P

EPSILON = 1e-05
MASKED = -1e30
BF16 = jnp.bfloat16
F32 = jnp.float32
MESH = pl.DeviceIdType.MESH
PLANE = 4
LANES = 128
VMEM_BYTES = 58 * 2**20
VMEM_BACK = 63 * 2**20


def matmul(left, right):
    return jnp.dot(left, right, preferred_element_type=F32)


def matmul_tn(left, right):
    return lax.dot_general(left, right, (((0,), (0,)), ((), ())), preferred_element_type=F32)


def matmul_nt(left, right):
    return lax.dot_general(left, right, (((1,), (1,)), ((), ())), preferred_element_type=F32)


def layer_norm(inputs, gain_vec, bias_vec):
    row_mean = jnp.mean(inputs, axis=-1, keepdims=True)
    centred = inputs - row_mean
    spread = jnp.mean(centred * centred, axis=-1, keepdims=True)
    return centred * lax.rsqrt(spread + EPSILON) * gain_vec + bias_vec


class Place:
    def __init__(self, n_dp, n_blk):
        self.n_dp, self.n_blk, self.length = n_dp, n_blk, n_dp // PLANE
        self.dp, self.c = lax.axis_index("dp"), lax.axis_index("blk")
        self.z, self.p = self.dp // PLANE, lax.rem(self.dp, PLANE)
        side, row = lax.rem(self.p, 2), self.p // 2
        self.flip_x, self.flip_y = self.p + 1 - 2 * side, self.p + 2 - 4 * row
        self.diag = PLANE - 1 - self.p

    def routes(self, zz):
        odd = lax.rem(zz, 2)
        return (
            self.flip_x * (1 - odd) + self.flip_y * odd,
            self.flip_x * odd + self.flip_y * (1 - odd),
        )

    def at(self, zz, pp):
        return (zz * PLANE + pp, self.c)

    def sibling(self, k):
        return (self.dp, lax.rem(self.c + k, self.n_blk))

    def greet(self):
        barrier = pltpu.get_barrier_semaphore()

        def hello(device):
            pl.semaphore_signal(barrier, inc=1, device_id=device, device_id_type=MESH)

        hello(self.at(self.z, self.flip_x))
        hello(self.at(self.z, self.flip_y))
        for k in range(1, self.n_blk):
            hello(self.sibling(k))
        pl.when(self.z > 0)(lambda: hello(self.at(self.z - 1, self.p)))
        pl.when(self.z < self.length - 1)(lambda: hello(self.at(self.z + 1, self.p)))
        ends = jnp.minimum(self.z, 1) + jnp.minimum(self.length - 1 - self.z, 1)
        pl.semaphore_wait(barrier, 1 + self.n_blk + ends)


def remote(src, dst, send_sem, recv_sem, device):
    return pltpu.make_async_remote_copy(
        src_ref=src,
        dst_ref=dst,
        send_sem=send_sem,
        recv_sem=recv_sem,
        device_id=device,
        device_id_type=MESH,
    )


class Gather:
    def __init__(self, place, unit, own, chunk, send, recv, local):
        self.place, self.own, self.chunk = place, own, chunk
        self.send = lambda kind, zz: send.at[unit, kind, zz]
        self.recv = lambda slot: recv.at[unit, slot]
        self.local = local.at[unit]

    def copy(self, src, slot, kind, zz, device):
        return remote(src, self.chunk(slot), self.send(kind, zz), self.recv(slot), device)

    def arrived(self, slot):
        piece = self.chunk(slot)
        remote(piece, piece, self.send(0, 0), self.recv(slot), self.place.sibling(1)).wait_recv()

    def start(self):
        pc = self.place
        keep = pltpu.make_async_copy(self.own, self.chunk(pc.dp), self.local)
        keep.start()

        def to(kind, device):
            self.copy(self.own, pc.dp, kind, pc.z, device).start()

        pl.when(pc.z < pc.length - 1)(lambda: to(3, pc.at(pc.z + 1, pc.p)))
        pl.when(pc.z > 0)(lambda: to(4, pc.at(pc.z - 1, pc.p)))
        to(0, pc.at(pc.z, pc.flip_x))
        to(1, pc.at(pc.z, pc.flip_y))

    def along(self, s):
        pc = self.place

        def pass_on(zz, more, onward):
            slot = zz * PLANE + pc.p
            self.arrived(slot)
            piece = self.chunk(slot)
            pl.when(more)(lambda: self.copy(piece, slot, 3, zz, pc.at(onward, pc.p)).start())
            self.copy(piece, slot, 0, zz, pc.at(pc.z, pc.flip_x)).start()
            self.copy(piece, slot, 1, zz, pc.at(pc.z, pc.flip_y)).start()

        pl.when(pc.z >= s)(lambda: pass_on(pc.z - s, pc.z < pc.length - 1, pc.z + 1))
        pl.when(pc.z + s < pc.length)(lambda: pass_on(pc.z + s, pc.z > 0, pc.z - 1))

    def across(self):
        pc = self.place

        @pl.loop(0, pc.length)
        def _(zz):
            near, far = pc.routes(zz)
            slot = zz * PLANE + near
            self.arrived(slot)
            self.copy(self.chunk(slot), slot, 2, zz, pc.at(pc.z, far)).start()

    def finish(self):
        pc = self.place
        pltpu.make_async_copy(self.own, self.chunk(pc.dp), self.local).wait()

        @pl.loop(0, pc.length)
        def _(zz):
            near, far = pc.routes(zz)
            self.arrived(zz * PLANE + far)
            self.arrived(zz * PLANE + pc.diag)

    def drain(self):
        pc = self.place
        piece = self.chunk(pc.dp)

        def sent(kind, zz):
            remote(piece, piece, self.send(kind, zz), self.recv(0), pc.sibling(1)).wait_send()

        @pl.loop(0, pc.length)
        def _(zz):
            sent(0, zz)
            sent(1, zz)
            sent(2, zz)
            pl.when((zz <= pc.z) & (pc.z < pc.length - 1))(lambda: sent(3, zz))
            pl.when((zz > pc.z) & (pc.z > 0))(lambda: sent(3, zz))

        pl.when(pc.z > 0)(lambda: sent(4, pc.z))


def gather_kernel(
    n_dp, n_blk, qkv, out, fc, proj, small, all_qkv, all_out, all_fc, all_proj, all_small, send, recv, local, side
):
    pc = Place(n_dp, n_blk)
    pc.greet()
    wide = out.shape[1]
    mine = pl.ds(pl.multiple_of(pc.c * wide, LANES), wide)
    parts = [
        (small, lambda slot: all_small.at[slot]),
        (qkv, lambda slot: all_qkv.at[slot]),
        (out, lambda slot: all_out.at[slot, :, mine]),
        (fc, lambda slot: all_fc.at[slot]),
        (proj, lambda slot: all_proj.at[slot]),
    ]
    units = [Gather(pc, i, own, chunk, send, recv, local) for i, (own, chunk) in enumerate(parts)]
    units[0].start()
    units[1].start()
    for i in range(5):
        for s in range(1, pc.length):
            units[i].along(s)
        if i + 2 < 5:
            units[i + 2].start()
        if i > 0:
            units[i - 1].across()
        if i > 1:
            units[i - 2].finish()
    units[4].across()
    side_copies = []
    piece = all_out.at[:, :, mine]
    for k in range(1, n_blk):
        copy = remote(piece, piece, side.at[0, k], side.at[1, k], pc.sibling(k))
        copy.start()
        side_copies.append(copy)
    units[3].finish()
    units[4].finish()
    for copy in side_copies:
        copy.wait()
    for unit in units:
        unit.drain()


class Scatter:
    def __init__(self, place, unit, chunk, bufs, send, recv):
        self.place, self.chunk = place, chunk
        self.diag, self.near, self.far, self.line = bufs
        self.kind = self.near.dtype
        self.send = lambda kind, zz: send.at[unit, kind, zz]
        self.recv = lambda kind, zz: recv.at[unit, kind, zz]

    def copy(self, src, dst, kind, zz, device):
        return remote(src, dst, self.send(kind, zz), self.recv(kind, zz), device)

    def arrived(self, piece, kind, zz):
        self.copy(piece, piece, kind, zz, self.place.sibling(1)).wait_recv()

    def start(self):
        pc = self.place

        @pl.loop(0, pc.length)
        def _(zz):
            to = pc.at(pc.z, pc.routes(zz)[0])
            self.copy(self.chunk(zz * PLANE + pc.diag), self.diag.at[zz], 0, zz, to).start()

        @pl.loop(0, pc.length)
        def _(zz):
            near = pc.routes(zz)[0]
            to = pc.at(pc.z, near)
            self.copy(self.chunk(zz * PLANE + near), self.near.at[zz], 1, zz, to).start()

    def middle(self, first, last):
        pc = self.place

        @pl.loop(first, last)
        def _(zz):
            far = pc.routes(zz)[1]
            self.arrived(self.diag.at[zz], 0, zz)
            total = self.diag[zz].astype(F32) + self.chunk(zz * PLANE + far)[...].astype(F32)
            self.diag[zz] = total.astype(self.kind)
            self.copy(self.diag.at[zz], self.far.at[zz], 2, zz, pc.at(pc.z, far)).start()

    def settle(self, first, last):
        pc = self.place

        @pl.loop(first, last)
        def _(zz):
            self.arrived(self.near.at[zz], 1, zz)
            self.arrived(self.far.at[zz], 2, zz)
            total = self.near[zz].astype(F32) + self.far[zz].astype(F32)
            total += self.chunk(zz * PLANE + pc.p)[...].astype(F32)
            self.near[zz] = total.astype(self.kind)

    def along(self, s):
        pc = self.place

        def pass_on(zz, at, kind, more, onward):
            @pl.when(more)
            def _():
                self.arrived(self.line.at[zz], kind, zz)
                total = self.near[zz].astype(F32) + self.line[zz].astype(F32)
                self.near[zz] = total.astype(self.kind)

            to = pc.at(onward, pc.p)
            self.copy(self.near.at[zz], self.line.at[at], kind, zz, to).start()

        def up():
            pass_on(pc.z + s, pc.z + s, 3, pc.z > 0, pc.z + 1)

        def down():
            at = pc.length if s == 1 else pc.z - s
            pass_on(pc.z - s, at, 4, pc.z < pc.length - 1, pc.z - 1)

        pl.when(pc.z + s < pc.length)(up)
        pl.when(pc.z >= s)(down)

    def finish(self, total):
        pc = self.place
        total[...] = self.near[pc.z].astype(F32)

        def more(at, kind):
            self.arrived(self.line.at[at], kind, pc.z)
            total[...] += self.line[at].astype(F32)

        pl.when(pc.z > 0)(lambda: more(pc.z, 3))
        pl.when(pc.z < pc.length - 1)(lambda: more(pc.length, 4))

    def drain(self):
        pc = self.place

        def sent(kind, zz):
            piece = self.near.at[zz]
            self.copy(piece, piece, kind, zz, pc.sibling(1)).wait_send()

        @pl.loop(0, pc.length)
        def _(zz):
            sent(0, zz)
            sent(1, zz)
            sent(2, zz)
            pl.when(zz > pc.z)(lambda: sent(3, zz))
            pl.when(zz < pc.z)(lambda: sent(4, zz))


def scatter_kernel(n_dp, n_blk, *refs):
    grads, outs, rest = refs[:4], refs[4:8], refs[8:]
    bufs, totals, rest = rest[:16], rest[16:20], rest[20:]
    side_buf, send, recv, side, last = rest
    proj, fc, out, qkv = grads
    pc = Place(n_dp, n_blk)
    pc.greet()
    wide = out.shape[2] // n_blk

    def columns(core):
        return pl.ds(pl.multiple_of(core * wide, LANES), wide)

    chunks = [
        lambda slot: proj.at[slot],
        lambda slot: fc.at[slot],
        lambda slot: side_buf.at[0, slot],
        lambda slot: qkv.at[slot],
    ]
    units = [
        Scatter(pc, i, chunks[i], bufs[4 * i : 4 * i + 4], send, recv) for i in range(4)
    ]
    units[0].start()
    units[1].start()
    side_copies = []
    for k in range(1, n_blk):
        dev = pc.sibling(k)
        copy = remote(
            out.at[:, :, columns(dev[1])], side_buf.at[k], side.at[0, k], side.at[1, k], dev
        )
        copy.start()
        side_copies.append(copy)

    def side_sum():
        for copy in side_copies:
            copy.wait()

        @pl.loop(0, n_dp)
        def _(slot):
            total = out[slot, :, columns(pc.c)].astype(F32)
            for k in range(1, n_blk):
                total += side_buf[k, slot].astype(F32)
            side_buf[0, slot] = total.astype(BF16)

    pending = []

    def spread(i):
        units[i].finish(totals[i])
        total = totals[i]
        pieces = [(total, outs[i].at[pc.c])]
        for j, (src, dst) in enumerate(pieces):
            keep = pltpu.make_async_copy(src, dst, last.at[i, 0, 0])
            keep.start()
            pending.append(keep)
            for k in range(1, n_blk):
                copy = remote(src, dst, last.at[i, 0, k], last.at[i, 1, k], pc.sibling(k))
                copy.start()
                pending.append(copy)

    units[0].middle(0, pc.length)
    side_sum()
    units[2].start()
    units[1].middle(0, pc.length)
    units[3].start()
    units[0].settle(0, pc.length)
    for s in range(pc.length - 1, 0, -1):
        units[0].along(s)
    units[2].middle(0, pc.length)
    units[1].settle(0, pc.length)
    for s in range(pc.length - 1, 0, -1):
        units[1].along(s)
    spread(0)
    units[3].middle(0, pc.length)
    units[2].settle(0, pc.length)
    for s in range(pc.length - 1, 0, -1):
        units[2].along(s)
    units[3].settle(0, pc.length)
    for s in range(pc.length - 1, 0, -1):
        units[3].along(s)
    spread(1)
    spread(2)
    spread(3)
    for copy in pending:
        copy.wait()
    for unit in units:
        unit.drain()


def gather_weights(n_dp, n_blk, qkv, out, fc, proj, small):
    shards = (qkv, out, fc, proj, small)
    shapes = [
        jax.ShapeDtypeStruct((n_dp, a.shape[0], a.shape[1] * (n_blk if a is out else 1)), BF16)
        for a in shards
    ]
    length = n_dp // PLANE
    hbm = pl.BlockSpec(memory_space=pl.ANY)
    return pl.pallas_call(
        functools.partial(gather_kernel, n_dp, n_blk),
        out_shape=shapes,
        in_specs=[hbm] * 5,
        out_specs=[hbm] * 5,
        scratch_shapes=[
            pltpu.SemaphoreType.DMA((5, 5, length)),
            pltpu.SemaphoreType.DMA((5, n_dp)),
            pltpu.SemaphoreType.DMA((5,)),
            pltpu.SemaphoreType.DMA((2, n_blk)),
        ],
        compiler_params=pltpu.CompilerParams(
            collective_id=0, has_side_effects=True, vmem_limit_bytes=VMEM_BYTES
        ),
    )(*shards)


def scatter_grads(n_dp, n_blk, proj, fc, out, qkv):
    length = n_dp // PLANE
    grads = (proj, fc, out, qkv)
    sizes = [a.shape[1:] for a in grads]
    sizes[2] = (sizes[2][0], sizes[2][1] // n_blk)
    vmem = pl.BlockSpec(memory_space=pltpu.VMEM)
    scratch = []
    for size in sizes:
        scratch += [pltpu.VMEM((length,) + size, BF16)] * 3 + [pltpu.VMEM((length + 1,) + size, BF16)]
    scratch += [pltpu.VMEM(size, F32) for size in sizes]
    scratch += [
        pltpu.VMEM((n_blk, n_dp) + sizes[2], BF16),
        pltpu.SemaphoreType.DMA((4, 5, length)),
        pltpu.SemaphoreType.DMA((4, 5, length)),
        pltpu.SemaphoreType.DMA((2, n_blk)),
        pltpu.SemaphoreType.DMA((4, 2, n_blk)),
    ]
    return pl.pallas_call(
        functools.partial(scatter_kernel, n_dp, n_blk),
        out_shape=[jax.ShapeDtypeStruct((n_blk,) + size, F32) for size in sizes],
        in_specs=[vmem] * 4,
        out_specs=[pl.BlockSpec(memory_space=pl.ANY)] * 4,
        scratch_shapes=scratch,
        compiler_params=pltpu.CompilerParams(
            collective_id=1, has_side_effects=True, vmem_limit_bytes=VMEM_BYTES
        ),
    )(*grads)


def lane_split(value, lane, first, base):
    for i in range(3):
        term = value.astype(BF16)
        base = jnp.where(lane == first + i, term, base)
        value = value - term.astype(F32)
    return base


def causal_tail(scores, block, axis, masked):
    key_axis, query_axis = (0, 1) if axis == 0 else (1, 0)
    tail_shape = (block, block)
    keep = lax.broadcasted_iota(jnp.int32, tail_shape, key_axis) <= lax.broadcasted_iota(
        jnp.int32, tail_shape, query_axis
    )
    size = scores.shape[axis]
    if size == block:
        return jnp.where(keep, scores, masked)
    head = lax.slice_in_dim(scores, 0, size - block, axis=axis)
    tail = jnp.where(keep, lax.slice_in_dim(scores, size - block, size, axis=axis), masked)
    return jnp.concatenate([head, tail], axis=axis)


def causal_all(scores, offset, axis, masked):
    key_axis, query_axis = (0, 1) if axis == 0 else (1, 0)
    keep = (
        lax.broadcasted_iota(jnp.int32, scores.shape, key_axis)
        <= lax.broadcasted_iota(jnp.int32, scores.shape, query_axis) + offset
    )
    return jnp.where(keep, scores, masked)


def query_blocks(total, block, run):
    count = total // block
    if count <= 4:
        for b in range(count):
            run(
                b * block,
                (b + 1) * block,
                lambda scores, axis, masked: causal_tail(scores, block, axis, masked),
            )
    else:

        @pl.loop(0, count)
        def _(b):
            first = pl.multiple_of(b * block, block)
            run(first, total, lambda scores, axis, masked: causal_all(scores, first, axis, masked))


def attend_kernel(block, scale, q_ref, k_ref, v_ref, key_aug, query_aug, slope_ref, out_ref, qx_ref):
    total = q_ref.shape[0]
    half = LANES // 2
    lane = lax.broadcasted_iota(jnp.int32, (1, LANES), 1)

    def run(first, keys, mask):
        rows = pl.ds(first, block)
        result = None
        for hh in range(2):
            own = (lane < half) if hh == 0 else (lane >= half)
            base = half * (1 - hh)
            aug = query_aug[rows, :] + slope_ref[0, hh : hh + 1, :]
            query = jnp.where(own, q_ref[rows, :] * BF16(scale), aug)
            key = jnp.where(own, k_ref[0:keys, :], key_aug[0:keys, :])
            value = jnp.where(own, v_ref[0:keys, :], BF16(1))
            scores = mask(matmul_nt(query, key), 1, MASKED)
            top = jnp.max(scores, axis=1, keepdims=True)
            weights = jnp.exp(scores - top).astype(BF16)
            sums = matmul(weights, value)
            log_total = top + jnp.log(sums[:, base : base + 1])
            qx_ref[0, hh, rows, :] = lane_split(-log_total, lane, base + 8, query)
            part = sums / pltpu.roll(sums, half, 1)
            result = part if hh == 0 else jnp.where(own, part, result)
        out_ref[rows, :] = result.astype(BF16)

    query_blocks(total, block, run)


def attend_back_kernel(
    block, scale, qx_ref, k_ref, v_ref, key_aug, out_ref, grad_ref, dq_ref, dk_ref, dv_ref, dk_acc, dv_acc
):
    total = k_ref.shape[0]
    half = LANES // 2
    lane = lax.broadcasted_iota(jnp.int32, (1, LANES), 1)
    dk_acc[...] = jnp.zeros_like(dk_acc)
    dv_acc[...] = jnp.zeros_like(dv_acc)

    def run(first, keys, mask):
        rows = pl.ds(first, block)
        grad = grad_ref[rows, :]
        product = grad.astype(F32) * out_ref[rows, :].astype(F32)
        dq = None
        dk = None
        dv = None
        for hh in range(2):
            own = (lane < half) if hh == 0 else (lane >= half)
            base = half * (1 - hh)
            query = qx_ref[0, hh, rows, :]
            key = jnp.where(own, k_ref[0:keys, :], key_aug[0:keys, :])
            delta = jnp.sum(jnp.where(own, product, 0.0), axis=1, keepdims=True)
            grad_own = jnp.where(own, grad, BF16(0))
            grad_aug = lane_split(-delta, lane, base, grad_own)
            value = jnp.where(own, v_ref[0:keys, :], BF16(1))
            weights = mask(jnp.exp(matmul_nt(key, query)), 0, 0.0)
            change = (weights * matmul_nt(value, grad_aug)).astype(BF16)
            key_own = jnp.where(own, key, BF16(0))
            query_own = jnp.where(own, query, BF16(0))
            dv_part = matmul(weights.astype(BF16), grad_own)
            dk_part = matmul(change, query_own)
            dq_part = matmul_tn(change, key_own)
            dv = dv_part if hh == 0 else dv + dv_part
            dk = dk_part if hh == 0 else dk + dk_part
            dq = dq_part if hh == 0 else dq + dq_part
        dq_ref[rows, :] = (dq * scale).astype(BF16)
        dk_acc[0:keys, :] += dk
        dv_acc[0:keys, :] += dv

    query_blocks(total, block, run)
    dk_ref[...] = dk_acc[...].astype(BF16)
    dv_ref[...] = dv_acc[...].astype(BF16)


def gelu_pair(u):
    k = math.sqrt(2.0 / math.pi)
    square = u * u
    t = jnp.tanh(k * u * (1.0 + 0.044715 * square))
    plus = 0.5 * (1.0 + t)
    slope = plus + (0.5 * k) * u * (1.0 - t * t) * (1.0 + 3 * 0.044715 * square)
    return u * plus, slope


def whole(ref, cols):
    value = ref[:, :, cols]
    return value.reshape(value.shape[0] * value.shape[1], value.shape[2])


def forward_kernel(n_dp, n_blk, scale, *refs):
    (small, qkv, out, fc, proj, tokens, out_grad, key_own, query_own, slope_ref) = refs[:10]
    (w_qkv_o, w_out_o, w_fc_o, w_proj_o, vec_o, fcb_o, h1_o, mixed_o, heads_o, att_o, qx_o, mid_o, h2_o, hid_o, slope_o, dy_o, key_o, gp_o) = refs[10:28]
    (w_small, w_qkv, w_out, w_fc, w_proj, vec, fcb, x_all, h1, mixed, heads, att, qx, mid, h2, hid, gslope, dy, key_aug, query_aug, gp) = refs[28:49]
    send, recv, local, side, load, save_sem = refs[49:]
    pc = Place(n_dp, n_blk)
    sib = pc.sibling(1)
    width = tokens.shape[1]
    rows_own = tokens.shape[0]
    total = n_blk * rows_own
    wide = out.shape[1]
    tile = 256
    mine = pl.ds(pl.multiple_of(pc.c * rows_own, rows_own), rows_own)
    theirs = pl.ds(pl.multiple_of(sib[1] * rows_own, rows_own), rows_own)
    my_cols = pl.ds(pl.multiple_of(pc.c * wide, LANES), wide)
    pc.greet()
    parts = [
        (small, lambda slot: w_small.at[slot]),
        (qkv, lambda slot: w_qkv.at[slot]),
        (out, lambda slot: w_out.at[slot, :, my_cols]),
        (fc, lambda slot: w_fc.at[slot]),
        (proj, lambda slot: w_proj.at[slot]),
    ]
    u_small, u_qkv, u_out, u_fc, u_proj = [
        Gather(pc, i, own, chunk, send, recv, local) for i, (own, chunk) in enumerate(parts)
    ]
    saves = []

    def exchange(i, src, dst):
        copy = remote(src, dst, side.at[0, i], side.at[1, i], sib)
        copy.start()
        return copy

    def keep(i, src, dst):
        copy = pltpu.make_async_copy(src, dst, load.at[i])
        copy.start()
        return copy

    def save(i, src, dst):
        copy = pltpu.make_async_copy(src, dst, save_sem.at[i])
        copy.start()
        saves.append(copy)

    u_small.start()
    u_qkv.start()
    first = [
        exchange(0, tokens, x_all.at[mine]),
        keep(0, tokens, x_all.at[mine]),
        exchange(1, key_own, key_aug.at[mine]),
        keep(1, key_own, key_aug.at[mine]),
        exchange(2, query_own, query_aug.at[mine]),
        keep(2, query_own, query_aug.at[mine]),
    ]
    for s in range(1, pc.length):
        u_small.along(s)
        u_qkv.along(s)
    u_small.across()
    u_out.start()
    later = [exchange(3, out_grad, dy.at[mine]), keep(3, out_grad, dy.at[mine])]
    u_small.finish()
    for copy in first:
        copy.wait()
    per = n_dp // (width // LANES)
    for t in range(width // LANES):
        rows = w_small[t * per].astype(F32)
        for k in range(1, per):
            rows += w_small[t * per + k].astype(F32)
        vec[:, t * LANES : (t + 1) * LANES] = rows
    for t in range(n_dp):
        fcb[:, t * LANES : (t + 1) * LANES] = w_small[t, 8:9, :].astype(F32)
    save(0, vec, vec_o)
    save(1, fcb, fcb_o)

    @pl.loop(0, total // tile)
    def _(b):
        rows = pl.ds(pl.multiple_of(b * tile, tile), tile)
        h1[rows, :] = layer_norm(x_all[rows, :].astype(F32), vec[0:1, :], vec[1:2, :]).astype(BF16)

    save(2, h1, h1_o)
    for s in range(1, pc.length):
        u_out.along(s)
    u_fc.start()
    u_qkv.across()
    for s in range(1, pc.length):
        u_fc.along(s)
    u_out.across()
    u_qkv.finish()
    save(3, w_qkv, w_qkv_o)
    for third in range(3):
        for b in range(wide // tile):

            @pl.loop(0, total // 512)
            def _(m, third=third, b=b):
                rows = pl.ds(pl.multiple_of(m * 512, 512), 512)
                cols = pl.ds(third * wide + b * tile, tile)
                value = matmul(h1[rows, :], whole(w_qkv, cols))
                if third != 1:
                    at = pl.ds(pl.multiple_of(pc.c * wide, LANES) + b * tile, tile)
                    value += vec[pl.ds(2 + third // 2, 1), at]
                mixed[rows, cols] = value.astype(BF16)

    save(4, mixed, mixed_o)
    u_proj.start()
    for j in range(wide // LANES):
        cols = [pl.ds(i * wide + j * LANES, LANES) for i in range(3)]
        attend_kernel(
            tile,
            scale,
            mixed.at[:, cols[0]],
            mixed.at[:, cols[1]],
            mixed.at[:, cols[2]],
            key_aug,
            query_aug,
            slope_ref.at[pl.ds(j, 1)],
            heads.at[:, cols[0]],
            qx.at[pl.ds(j, 1)],
        )
        if j == 0:
            u_out.finish()
            piece = w_out.at[:, :, my_cols]
            share = exchange(4, piece, piece)
        if j + 1 < pc.length:
            u_proj.along(j + 1)
    save(5, heads, heads_o)
    save(6, qx, qx_o)
    swap = exchange(5, heads.at[theirs], att.at[:, my_cols])
    stay = keep(4, heads.at[mine], att.at[:, my_cols])
    share.wait()
    save(7, w_out, w_out_o)
    swap.wait()
    stay.wait()
    save(8, att, att_o)

    @pl.loop(0, width // tile)
    def _(b):
        cols = pl.ds(pl.multiple_of(b * tile, tile), tile)
        value = matmul(att[...], whole(w_out, cols))
        mid[:, cols] = x_all[mine, cols].astype(F32) + value + vec[4:5, cols]

    @pl.loop(0, rows_own // tile)
    def _(b):
        rows = pl.ds(pl.multiple_of(b * tile, tile), tile)
        into = pl.ds(pl.multiple_of(pc.c * rows_own + b * tile, tile), tile)
        h2[into, :] = layer_norm(mid[rows, :], vec[5:6, :], vec[6:7, :]).astype(BF16)

    both = exchange(6, h2.at[mine], h2.at[mine])
    save(9, mid, mid_o)
    u_fc.across()
    both.wait()
    save(10, h2, h2_o)
    u_fc.finish()
    save(11, w_fc, w_fc_o)

    def feed(b):
        cols = pl.ds(pl.multiple_of(b * tile, tile), tile)

        @pl.loop(0, total // 512)
        def _(m):
            rows = pl.ds(pl.multiple_of(m * 512, 512), 512)
            value = matmul(h2[rows, :], whole(w_fc, cols)) + fcb[:, cols]
            value, slope = gelu_pair(value)
            hid[rows, cols] = value.astype(BF16)
            gslope[rows, cols] = slope.astype(BF16)

    blocks = hid.shape[1] // tile
    pl.loop(0, blocks)(feed)
    save(12, hid, hid_o)
    save(13, gslope, slope_o)
    for copy in later:
        copy.wait()
    save(14, dy, dy_o)
    save(15, key_aug, key_o)
    u_proj.across()
    slots = tile // proj.shape[0]

    @pl.loop(0, blocks)
    def _(b):
        cols = pl.ds(pl.multiple_of(b * tile, tile), tile)
        for n in range(width // 512):
            value = matmul_tn(hid[:, cols], dy[:, n * 512 : (n + 1) * 512]).astype(BF16)
            gp[pl.ds(b * slots, slots), :, n * 512 : (n + 1) * 512] = value.reshape(slots, proj.shape[0], 512)

    save(16, gp, gp_o)
    u_proj.finish()
    save(17, w_proj, w_proj_o)
    for copy in saves:
        copy.wait()
    for unit in (u_small, u_qkv, u_out, u_fc, u_proj):
        unit.drain()


def forward(n_dp, n_blk, scale, qkv, out, fc, proj, small, tokens, out_grad, key_own, query_own, slope_aug):
    rows_own, width = tokens.shape
    total = n_blk * rows_own
    wide = out.shape[1]
    pairs = wide // LANES
    ff = n_dp * proj.shape[0]
    length = n_dp // PLANE
    shape = jax.ShapeDtypeStruct
    weights = [(n_dp,) + a.shape for a in (qkv, out, fc, proj)]
    weights[1] = (n_dp, out.shape[0], width)
    rest = [
        ((16, width), F32),
        ((1, ff), F32),
        ((total, width), BF16),
        ((total, 3 * wide), BF16),
        ((total, wide), BF16),
        ((rows_own, width), BF16),
        ((pairs, 2, total, LANES), BF16),
        ((rows_own, width), F32),
        ((total, width), BF16),
        ((total, ff), BF16),
        ((total, ff), BF16),
        ((total, width), BF16),
        ((total, LANES), BF16),
        (weights[3], BF16),
    ]
    outs = [(w, BF16) for w in weights] + rest
    scratch = [((n_dp,) + small.shape, BF16)] + outs[:6]
    scratch += [((total, width), BF16)] + outs[6:17] + [((total, LANES), BF16)] + outs[17:]
    hbm = pl.BlockSpec(memory_space=pl.ANY)
    vmem = pl.BlockSpec(memory_space=pltpu.VMEM)
    return pl.pallas_call(
        functools.partial(forward_kernel, n_dp, n_blk, scale),
        out_shape=[shape(*o) for o in outs],
        in_specs=[hbm] * 9 + [vmem],
        out_specs=[hbm] * len(outs),
        scratch_shapes=[pltpu.VMEM(*s) for s in scratch]
        + [
            pltpu.SemaphoreType.DMA((5, 5, length)),
            pltpu.SemaphoreType.DMA((5, n_dp)),
            pltpu.SemaphoreType.DMA((5,)),
            pltpu.SemaphoreType.DMA((2, 7)),
            pltpu.SemaphoreType.DMA((5,)),
            pltpu.SemaphoreType.DMA((18,)),
        ],
        compiler_params=pltpu.CompilerParams(
            collective_id=2, has_side_effects=True, vmem_limit_bytes=VMEM_BYTES
        ),
    )(small, qkv, out, fc, proj, tokens, out_grad, key_own, query_own, slope_aug)


def normed_rows(rows):
    centred = rows - jnp.mean(rows, axis=-1, keepdims=True)
    inverse = lax.rsqrt(jnp.mean(centred * centred, axis=-1, keepdims=True) + EPSILON)
    return centred * inverse, inverse


def norm_back(rows, gain_vec, grad):
    unit, inverse = normed_rows(rows)
    m = grad * gain_vec
    shift = jnp.mean(m, axis=-1, keepdims=True)
    stretch = jnp.mean(m * unit, axis=-1, keepdims=True)
    return (m - shift - unit * stretch) * inverse, grad * unit


def column_sum(value):
    return jnp.sum(value, axis=0, keepdims=True)


def backward_kernel(n_dp, n_blk, scale, *refs):
    (w_qkv_h, w_out_h, w_fc_h, w_proj_h, vec, h1_h, mixed_h, heads_h, att_h, qx_h, mid_h, h2_h, hid_h, slope_h, dy_h, key_h, gp_h, tokens_h) = refs[:18]
    (layer_o, input_o, proj_o, fc_o, qkv_o, out_o, small_o) = refs[18:25]
    (P2, S, Y, F, H, A, M, T, O, Q, E, K, GP, side0, side1, R1, R2, R3, DH, SB, PF, acc_k, acc_v, VG, fcg, SG, small_in) = refs[25:52]
    bufs, rest = refs[52:72], refs[72:]
    totals, rest = rest[:5], rest[5:]
    send, recv, xsem, load, last = rest
    pc = Place(n_dp, n_blk)
    sib = pc.sibling(1)
    rows_own, width = tokens_h.shape
    total = n_blk * rows_own
    wide = width // n_blk
    ff = A.shape[1]
    shard = width // n_dp
    piece = ff // n_dp
    tile = 256
    mine = pl.ds(pl.multiple_of(pc.c * rows_own, rows_own), rows_own)
    theirs = pl.ds(pl.multiple_of(sib[1] * rows_own, rows_own), rows_own)
    my_cols = pl.ds(pl.multiple_of(pc.c * wide, LANES), wide)
    their_cols = pl.ds(pl.multiple_of(sib[1] * wide, LANES), wide)

    def fetch(i, src, dst):
        copy = pltpu.make_async_copy(src, dst, load.at[i])
        copy.start()
        return copy

    def exchange(i, src, dst):
        copy = remote(src, dst, xsem.at[0, i], xsem.at[1, i], sib)
        copy.start()
        return copy

    def span(i, size=tile):
        return pl.ds(pl.multiple_of(i * size, size), size)

    get_gp = fetch(0, gp_h, GP)
    get_hid = fetch(1, hid_h, A)
    get_proj = fetch(2, w_proj_h, P2)
    get_dy = fetch(3, dy_h, Y)
    get_slope = fetch(4, slope_h, S)
    get_h2 = fetch(5, h2_h, H)
    get_mid = fetch(6, mid_h, M)
    get_fc = fetch(7, w_fc_h, F)
    get_att = fetch(8, att_h, T)
    get_out = fetch(9, w_out_h, O)
    get_qx = fetch(10, qx_h, Q)
    get_heads = fetch(11, heads_h, E)
    get_key = fetch(12, key_h, K)
    pc.greet()
    chunks = [
        lambda slot: GP.at[slot],
        lambda slot: A.at[span(slot, shard)],
        lambda slot: F.at[span(slot, shard), 0 : 3 * wide],
        lambda slot: side0.at[span(slot, shard)],
        lambda slot: SG.at[slot],
    ]
    u_proj, u_fc, u_qkv, u_out, u_small = [
        Scatter(pc, i, chunks[i], bufs[4 * i : 4 * i + 4], send, recv) for i in range(5)
    ]
    length = pc.length
    pending = []

    def give(i, src, dst):
        keep = pltpu.make_async_copy(src, dst, last.at[0, i])
        copy = remote(src, dst, last.at[1, i], last.at[2, i], sib)
        keep.start()
        copy.start()
        return keep, copy

    VG[...] = jnp.zeros_like(VG)
    get_gp.wait()
    u_proj.start()
    get_hid.wait()
    get_proj.wait()

    @pl.loop(0, width // tile)
    def _(b):
        SB[:, span(b)] = matmul(A[theirs, :], P2[:, span(b)]).astype(BF16)

    swap_out = exchange(0, SB, R1)

    @pl.loop(0, width // tile)
    def _(b):
        PF[:, span(b)] = matmul(A[mine, :], P2[:, span(b)])

    u_proj.middle(0, 2)
    get_dy.wait()
    get_slope.wait()

    def hidden_grads(b):
        cols = span(b)
        sums = None
        for m in range(total // 512):
            rows = pl.ds(m * 512, 512)
            value = S[rows, cols].astype(F32) * matmul_nt(Y[rows, :], P2[cols, :])
            value = value.astype(BF16)
            S[rows, cols] = value
            part = column_sum(value.astype(F32))
            sums = part if sums is None else sums + part
        fcg[:, cols] = sums

    blocks = ff // tile
    pl.loop(0, blocks // 2)(hidden_grads)
    u_proj.middle(2, length)
    pl.loop(blocks // 2, blocks)(hidden_grads)
    get_h2.wait()

    @pl.loop(0, width // tile)
    def _(b):
        for n in range(ff // 1024):
            cols = pl.ds(n * 1024, 1024)
            A[span(b), cols] = matmul_tn(H[:, span(b)], S[:, cols]).astype(BF16)

    u_fc.start()
    get_qkv = [
        fetch(13, w_qkv_h.at[:, 0 : 2 * wide], P2.at[0:width]),
        fetch(14, w_qkv_h.at[:, 2 * wide :], P2.at[width : 2 * width, 0:wide]),
    ]
    get_mid.wait()
    swap_out.wait()

    @pl.loop(0, rows_own // LANES)
    def _(b):
        rows = span(b, LANES)
        value = M[rows, :] + PF[rows, :] + R1[rows, :].astype(F32) + vec[7:8, :]
        R1[rows, :] = value.astype(BF16)

    put_layer = pltpu.make_async_copy(R1, layer_o, load.at[15])
    put_layer.start()
    get_fc.wait()

    @pl.loop(0, width // tile)
    def _(b):
        SB[:, span(b)] = matmul_nt(S[theirs, :], F[span(b), :]).astype(BF16)

    swap_two = exchange(1, SB, R2)
    u_proj.settle(0, 2)

    @pl.loop(0, width // tile)
    def _(b):
        PF[:, span(b)] = matmul_nt(S[mine, :], F[span(b), :])

    swap_two.wait()
    get_h1 = fetch(16, h1_h, S.at[:, 0:width])
    get_kv = fetch(17, mixed_h.at[:, wide:], S.at[:, width : 2 * width])

    @pl.loop(0, rows_own // LANES)
    def _(b):
        rows = span(b, LANES)
        from_mine = pl.ds(pl.multiple_of(pc.c * rows_own + b * LANES, LANES), LANES)
        into = pl.ds(pl.multiple_of(sib[1] * rows_own + b * LANES, LANES), LANES)
        grad = PF[rows, :] + R2[rows, :].astype(F32)
        top = Y[from_mine, :].astype(F32)
        back, terms = norm_back(M[rows, :], vec[5:6, :], grad)
        value = top + back
        M[rows, :] = value
        branch = value.astype(BF16)
        Y[into, :] = branch
        VG[4:5, :] += column_sum(branch.astype(F32))
        VG[5:6, :] += column_sum(terms)
        VG[6:7, :] += column_sum(grad)
        VG[7:8, :] += column_sum(top)

    get_out.wait()

    @pl.loop(0, width // tile)
    def _(b):
        Y[mine, span(b)] = matmul_nt(Y[theirs, :], O[span(b), :]).astype(BF16)

    swap_heads = exchange(2, Y.at[mine, their_cols], DH.at[mine])
    stay_heads = fetch(18, Y.at[mine, my_cols], DH.at[mine])
    u_proj.settle(2, length)
    u_proj.along(length - 1)
    get_att.wait()

    @pl.loop(0, width // tile)
    def _(b):
        O[span(b), :] = matmul_tn(T[:, span(b)], Y[theirs, :]).astype(BF16)

    swap_side = exchange(3, O.at[:, their_cols], side1)
    get_tokens = fetch(19, tokens_h, T)
    get_qx.wait()
    get_heads.wait()
    get_key.wait()
    get_kv.wait()
    stay_heads.wait()
    swap_heads.wait()
    pairs = wide // LANES
    for j in range(pairs):
        cols = pl.ds(j * LANES, LANES)
        attend_back_kernel(
            tile,
            scale,
            Q.at[pl.ds(j, 1)],
            S.at[:, pl.ds(width + j * LANES, LANES)],
            S.at[:, pl.ds(width + wide + j * LANES, LANES)],
            K,
            E.at[:, cols],
            DH.at[:, cols],
            H.at[:, cols],
            H.at[:, pl.ds(wide + j * LANES, LANES)],
            P2.at[width : 2 * width, pl.ds(wide + j * LANES, LANES)],
            acc_k,
            acc_v,
        )
        if j == 0:
            for s in range(length - 2, 0, -1):
                u_proj.along(s)
            u_fc.middle(0, 2)
            swap_side.wait()

            @pl.loop(0, n_dp)
            def _(slot):
                rows = span(slot, shard)
                value = O[rows, my_cols].astype(F32) + side1[rows, :].astype(F32)
                side0[rows, :] = value.astype(BF16)

        if j == 1:
            u_fc.middle(2, length)
            u_proj.finish(totals[0])
            pending += give(0, totals[0], proj_o.at[pl.ds(pl.multiple_of(pc.c * piece, piece), piece)])
    get_h1.wait()

    @pl.loop(0, width // tile)
    def _(b):
        F[span(b), 0 : 2 * wide] = matmul_tn(S[:, span(b)], H[...]).astype(BF16)
        value = matmul_tn(S[:, span(b)], P2[width : 2 * width, wide : 2 * wide])
        F[span(b), 2 * wide : 3 * wide] = value.astype(BF16)

    u_qkv.start()
    u_out.start()
    VG[2:3, my_cols] = column_sum(H[:, 0:wide].astype(F32))
    VG[3:4, my_cols] = column_sum(P2[width : 2 * width, wide : 2 * wide].astype(F32))
    u_fc.settle(0, 2)
    for copy in get_qkv:
        copy.wait()

    def input_part(first, b):
        rows = pl.ds(pl.multiple_of(first, rows_own), rows_own)
        below = pl.ds(pl.multiple_of(width + first, rows_own), rows_own)
        after = pl.ds(pl.multiple_of(width + b * tile, tile), tile)
        part = matmul_nt(P2[below, wide : 2 * wide], P2[after, 0:wide])
        return part + matmul_nt(H[rows, :], P2[span(b), :])

    @pl.loop(0, width // tile)
    def _(b):
        SB[:, span(b)] = input_part(sib[1] * rows_own, b).astype(BF16)

    swap_one = exchange(4, SB, R3)
    u_fc.settle(2, length)
    u_fc.along(length - 1)

    @pl.loop(0, width // tile)
    def _(b):
        PF[:, span(b)] = input_part(pc.c * rows_own, b)

    get_tokens.wait()
    swap_one.wait()

    @pl.loop(0, rows_own // LANES)
    def _(b):
        rows = span(b, LANES)
        grad = PF[rows, :] + R3[rows, :].astype(F32)
        back, terms = norm_back(T[rows, :].astype(F32), vec[0:1, :], grad)
        M[rows, :] += back
        VG[0:1, :] += column_sum(terms)
        VG[1:2, :] += column_sum(grad)

    put_input = pltpu.make_async_copy(M, input_o, load.at[20])
    put_input.start()
    per = n_dp // (width // LANES)
    for slot in range(n_dp):
        t = slot // per
        SG[slot, 0:8, :] = VG[0:8, t * LANES : (t + 1) * LANES]
        SG[slot, 8:16, :] = jnp.broadcast_to(fcg[:, slot * LANES : (slot + 1) * LANES], (8, LANES))
    u_small.start()
    for s in range(length - 2, 0, -1):
        u_fc.along(s)
    u_qkv.middle(0, 2)
    u_small.middle(0, length)
    u_fc.finish(totals[1])

    @pl.loop(0, n_dp)
    def _(j):
        dst = fc_o.at[:, pl.ds(pl.multiple_of((j * n_blk + pc.c) * piece, piece), piece)]
        give(1 + j, totals[1].at[:, span(j, piece)], dst)

    u_qkv.middle(2, length)
    u_small.settle(0, length)
    for s in range(length - 1, 0, -1):
        u_small.along(s)
    u_small.finish(totals[4])
    swap_small = exchange(5, totals[4], small_in)
    u_out.middle(0, length)
    u_qkv.settle(0, length)
    u_qkv.along(length - 1)
    u_out.settle(0, length)
    for s in range(length - 2, 0, -1):
        u_qkv.along(s)
        u_out.along(s + 1)
    u_out.along(1)
    u_qkv.finish(totals[2])
    for j in range(3):
        at = pl.ds(pl.multiple_of(pc.c * wide, LANES) + j * width, wide)
        pending += give(1 + n_dp + j, totals[2].at[:, j * wide : (j + 1) * wide], qkv_o.at[:, at])
    u_out.finish(totals[3])
    pending += give(4 + n_dp, totals[3], out_o.at[:, my_cols])
    swap_small.wait()
    low = jnp.where(pc.c == 0, totals[4][...], small_in[...])
    high = jnp.where(pc.c == 0, small_in[...], totals[4][...])
    small_o[0:8, :] = low[0:8] + high[0:8]
    small_o[8:16, :] = low[8:16]
    small_o[16:24, :] = high[8:16]

    @pl.loop(0, n_dp)
    def _(j):
        dst = fc_o.at[:, pl.ds(pl.multiple_of((j * n_blk + pc.c) * piece, piece), piece)]
        src = totals[1].at[:, span(j, piece)]
        pltpu.make_async_copy(src, dst, last.at[0, 1 + j]).wait()
        remote(src, dst, last.at[1, 1 + j], last.at[2, 1 + j], sib).wait()

    for copy in pending:
        copy.wait()
    put_layer.wait()
    put_input.wait()
    for unit in (u_proj, u_fc, u_qkv, u_out, u_small):
        unit.drain()


def backward(n_dp, n_blk, scale, saved, tokens):
    rows_own, width = tokens.shape
    total = n_blk * rows_own
    wide = width // n_blk
    w_proj = saved[3]
    ff = w_proj.shape[0]
    piece, shard, length = ff // n_dp, width // n_dp, n_dp // PLANE
    square, long, own = ((total, width), BF16), ((total, ff), BF16), ((rows_own, width), BF16)
    own_f32 = ((rows_own, width), F32)
    sizes = [
        ((piece, width), BF16),
        ((shard, ff), BF16),
        ((shard, 3 * wide), BF16),
        ((shard, wide), BF16),
        ((16, LANES), F32),
    ]
    scratch = [((ff, width), BF16), long, square, long, square, long, own_f32, own]
    scratch += [((width, width), BF16), (saved[9].shape, BF16), ((total, wide), BF16)]
    scratch += [((total, LANES), BF16), ((n_dp, piece, width), BF16)]
    scratch += [((width, wide), BF16)] * 2 + [own] * 3 + [((total, wide), BF16), own, own_f32]
    scratch += [((total, LANES), F32)] * 2 + [((8, width), F32), ((1, ff), F32)]
    scratch += [((n_dp, 16, LANES), F32), ((16, LANES), F32)]
    for size, kind in sizes:
        scratch += [((length,) + size, kind)] * 3 + [((length + 1,) + size, kind)]
    scratch += [(size, F32) for size, _ in sizes]
    outs = [own, own_f32, ((n_blk * piece, width), F32), ((shard, n_blk * ff), F32)]
    outs += [((shard, 3 * width), F32), ((shard, width), F32), ((24, LANES), F32)]
    hbm = pl.BlockSpec(memory_space=pl.ANY)
    vmem = pl.BlockSpec(memory_space=pltpu.VMEM)
    return pl.pallas_call(
        functools.partial(backward_kernel, n_dp, n_blk, scale),
        out_shape=[jax.ShapeDtypeStruct(*o) for o in outs],
        in_specs=[vmem if i == 4 else hbm for i in range(18)],
        out_specs=[hbm] * 6 + [vmem],
        scratch_shapes=[pltpu.VMEM(*s) for s in scratch]
        + [
            pltpu.SemaphoreType.DMA((5, 5, length)),
            pltpu.SemaphoreType.DMA((5, 5, length)),
            pltpu.SemaphoreType.DMA((2, 6)),
            pltpu.SemaphoreType.DMA((21,)),
            pltpu.SemaphoreType.DMA((3, 5 + n_dp)),
        ],
        compiler_params=pltpu.CompilerParams(
            collective_id=3, has_side_effects=True, vmem_limit_bytes=VMEM_BACK
        ),
    )(*saved, tokens)


def columns_spec(rows, first):
    return pl.BlockSpec((rows, LANES), lambda j: (0, first + j))


def attend(qkv, key_aug, query_aug, slope_aug, scale):
    total, wide = qkv.shape[0], qkv.shape[1] // 3
    pairs = wide // LANES
    block = math.gcd(total, 256)
    whole = pl.BlockSpec((total, LANES), lambda j: (0, 0))
    return pl.pallas_call(
        functools.partial(attend_kernel, block, scale),
        grid=(pairs,),
        out_shape=[
            jax.ShapeDtypeStruct((total, wide), BF16),
            jax.ShapeDtypeStruct((pairs, 2, total, LANES), BF16),
        ],
        in_specs=[
            columns_spec(total, 0),
            columns_spec(total, pairs),
            columns_spec(total, 2 * pairs),
            whole,
            whole,
            pl.BlockSpec((1, 2, LANES), lambda j: (j, 0, 0)),
        ],
        out_specs=[
            columns_spec(total, 0),
            pl.BlockSpec((1, 2, total, LANES), lambda j: (j, 0, 0, 0)),
        ],
        compiler_params=pltpu.CompilerParams(vmem_limit_bytes=VMEM_BYTES),
    )(qkv, qkv, qkv, key_aug, query_aug, slope_aug)


def attend_back(query_ext, qkv, key_aug, attended, grad, scale):
    total, wide = attended.shape
    pairs = wide // LANES
    block = math.gcd(total, 256)
    whole = pl.BlockSpec((total, LANES), lambda j: (0, 0))
    out = jax.ShapeDtypeStruct((total, wide), BF16)
    return pl.pallas_call(
        functools.partial(attend_back_kernel, block, scale),
        grid=(pairs,),
        out_shape=[out] * 3,
        in_specs=[
            pl.BlockSpec((1, 2, total, LANES), lambda j: (j, 0, 0, 0)),
            columns_spec(total, pairs),
            columns_spec(total, 2 * pairs),
            whole,
            columns_spec(total, 0),
            columns_spec(total, 0),
        ],
        out_specs=[columns_spec(total, 0)] * 3,
        scratch_shapes=[pltpu.VMEM((total, LANES), F32)] * 2,
        compiler_params=pltpu.CompilerParams(vmem_limit_bytes=VMEM_BYTES),
    )(query_ext, qkv, qkv, key_aug, attended, grad)


def attention_terms(positions, rows):
    high = (positions // 256) * 256
    low = positions - high
    first = rows == 0
    one = jnp.ones_like(positions)
    zero = jnp.zeros_like(positions)

    def table(columns):
        cols = jnp.stack([col.astype(F32) for col in columns], axis=1)
        cols = jnp.pad(cols, ((0, 0), (0, LANES // 2 - len(columns))))
        return jnp.concatenate([cols, cols], axis=1).astype(BF16)

    key_aug = table([high, high, high, low, low, low, first, ~first, one, one, one])
    other = jnp.where(first, 0.0, MASKED)
    query_aug = table([zero] * 6 + [other, jnp.where(first, MASKED, 0.0)])
    return key_aug, query_aug


def slope_terms(slopes, n_blk, c):
    heads = slopes.shape[0] // n_blk
    mine = lax.dynamic_slice_in_dim(slopes, c * heads, heads, 0)
    parts = []
    left = mine
    for _ in range(3):
        term = lax.reduce_precision(left, 8, 7)
        parts.append(term)
        left = left - term
    cols = jnp.stack(parts + parts, axis=1)
    cols = jnp.pad(cols, ((0, 0), (0, LANES // 2 - 6)))
    slope_aug = jnp.concatenate([cols, cols], axis=1).astype(BF16).reshape(heads // 2, 2, LANES)
    keep = (jnp.arange(LANES) // (LANES // 2))[None, None, :] == 1 - jnp.arange(2)[None, :, None]
    return jnp.where(keep, slope_aug, 0)


def body(
    n_dp,
    n_blk,
    tokens,
    positions,
    row_ids,
    alibi_slope,
    ln1_gain,
    ln1_bias,
    qkv_weight,
    query_bias,
    value_bias,
    out_weight,
    out_bias,
    ln2_gain,
    ln2_bias,
    fc_weight,
    fc_bias,
    proj_weight,
    proj_bias,
    out_grad,
):
    local, width = tokens.shape
    heads = alibi_slope.shape[0]
    hidden_all = fc_weight.shape[1]
    scale = 1.0 / math.sqrt(width // heads)
    c = lax.axis_index("blk")
    dp = lax.axis_index("dp")
    wide = width // n_blk
    shard = width // n_dp
    piece = hidden_all // (n_dp * n_blk)
    total = n_blk * local

    def swap(a):
        return lax.ppermute(a, "blk", [(0, 1), (1, 0)])

    def blk_gather(a):
        if n_blk != 2:
            return lax.all_gather(a, "blk", axis=0, tiled=True)
        other = swap(a)
        return jnp.where(
            c == 0, jnp.concatenate([a, other], 0), jnp.concatenate([other, a], 0)
        )

    def blk_sum(a):
        if n_blk != 2:
            return lax.psum_scatter(a.astype(BF16), "blk", scatter_dimension=0, tiled=True).astype(F32)
        own = lax.dynamic_slice_in_dim(a, c * local, local, 0)
        other = lax.dynamic_slice_in_dim(a, (1 - c) * local, local, 0)
        return own + swap(other.astype(BF16)).astype(F32)

    def to_tokens(a):
        if n_blk != 2:
            moved = lax.all_to_all(a.reshape(n_blk, local, wide), "blk", 0, 0)
            return jnp.transpose(moved, (1, 0, 2)).reshape(local, width)
        own = lax.dynamic_slice_in_dim(a, c * local, local, 0)
        other = swap(lax.dynamic_slice_in_dim(a, (1 - c) * local, local, 0))
        return jnp.where(
            c == 0, jnp.concatenate([own, other], 1), jnp.concatenate([other, own], 1)
        )

    def to_heads(a):
        if n_blk != 2:
            moved = lax.all_to_all(
                jnp.transpose(a.reshape(local, n_blk, wide), (1, 0, 2)), "blk", 0, 0
            )
            return moved.reshape(total, wide)
        own = lax.dynamic_slice_in_dim(a, c * wide, wide, 1)
        other = swap(lax.dynamic_slice_in_dim(a, (1 - c) * wide, wide, 1))
        return jnp.where(
            c == 0, jnp.concatenate([own, other], 0), jnp.concatenate([other, own], 0)
        )

    def mine(a, axis, size):
        return lax.dynamic_slice_in_dim(a, c * size, size, axis)

    qkv_own = jnp.concatenate(
        [mine(qkv_weight[:, i * width : (i + 1) * width], 1, wide) for i in range(3)], 1
    ).astype(BF16)
    out_own = mine(out_weight, 1, wide).astype(BF16)
    fc_own = mine(fc_weight.reshape(shard, n_dp, n_blk, piece), 2, 1).reshape(shard, n_dp * piece)
    proj_own = mine(proj_weight, 0, piece)
    vectors = [ln1_gain, ln1_bias, query_bias, value_bias, out_bias, ln2_gain, ln2_bias, proj_bias]
    vectors.append(mine(fc_bias, 0, piece))
    small = jnp.stack(
        [
            lax.dynamic_update_slice_in_dim(
                jnp.zeros((LANES,), F32), vec, lax.rem(dp * vec.shape[0], LANES), 0
            )
            for vec in vectors
        ]
    )
    small = jnp.pad(small, ((0, 16 - len(vectors)), (0, 0))).astype(BF16)
    inputs = tokens.astype(F32)
    grad_top = out_grad.astype(F32)
    slope_aug = slope_terms(alibi_slope, n_blk, c)
    shards = (qkv_own, out_own, fc_own.astype(BF16), proj_own.astype(BF16), small)
    if n_blk == 2 and piece == LANES:
        key_own, query_own = attention_terms(positions, row_ids)
        saved = forward(n_dp, n_blk, scale, *shards, tokens, out_grad, key_own, query_own, slope_aug)
        saved = [a.reshape(-1, a.shape[-1]) for a in saved[:4]] + [saved[4], *saved[6:]]
        layer_output, input_grad, proj_sum, fc_sum, qkv_sum, out_sum, smalls = backward(
            n_dp, n_blk, scale, saved, tokens
        )
        at = lax.rem(dp * shard, LANES)
        part = lax.dynamic_slice_in_dim(smalls[0:8], at, shard, 1)
        g_fc = smalls[8:24:8].reshape(n_blk * piece)
        return (
            layer_output,
            input_grad,
            part[0],
            part[1],
            qkv_sum,
            part[2],
            part[3],
            out_sum,
            part[4],
            part[5],
            part[6],
            fc_sum,
            g_fc,
            proj_sum,
            part[7],
        )

    full_qkv, full_out, full_fc, full_proj, full_small = gather_weights(
        n_dp, n_blk, *shards
    )
    weight_qkv = full_qkv.reshape(width, 3 * wide)
    weight_out = full_out.reshape(width, width)
    weight_fc = full_fc.reshape(width, n_dp * piece)
    weight_proj = full_proj.reshape(n_dp * piece, width)
    spread = full_small.astype(F32)

    def vector(i):
        size = vectors[i].shape[0]
        per = LANES // size
        rows = jnp.sum(spread[:, i].reshape(n_dp // per, per, LANES), axis=1)
        return rows.reshape(n_dp * size)

    gain_one, bias_one, bias_query, bias_value, bias_out, gain_two, bias_two, bias_proj, bias_fc = (
        vector(i) for i in range(len(vectors))
    )
    place = blk_gather(jnp.stack([positions, row_ids], axis=1))
    key_aug, query_aug = attention_terms(place[:, 0], place[:, 1])
    every_token = blk_gather(tokens).astype(F32)
    every_grad = blk_gather(out_grad)
    normed = layer_norm(every_token, gain_one, bias_one).astype(BF16)
    bias_qkv = jnp.concatenate(
        [mine(bias_query, 0, wide), jnp.zeros((wide,), F32), mine(bias_value, 0, wide)]
    )
    mixed = (matmul(normed, weight_qkv) + bias_qkv).astype(BF16)
    attended_heads, query_ext = attend(mixed, key_aug, query_aug, slope_aug, scale)
    attended = to_tokens(attended_heads)
    middle = inputs + matmul(attended, weight_out) + bias_out
    normed_two = layer_norm(middle, gain_two, bias_two).astype(BF16)
    every_two = blk_gather(normed_two)
    hidden_pre = matmul(every_two, weight_fc) + bias_fc
    hidden_vals, gelu_slope = gelu_pair(hidden_pre)
    hidden = hidden_vals.astype(BF16)
    grad_proj_weight = matmul_tn(hidden, every_grad).astype(BF16)
    layer_output = (middle + blk_sum(matmul(hidden, weight_proj)) + bias_proj).astype(BF16)
    grad_proj_bias = jnp.sum(grad_top, axis=0)
    grad_pre = (gelu_slope * matmul_nt(every_grad, weight_proj)).astype(BF16)
    grad_fc_weight = matmul_tn(every_two, grad_pre).astype(BF16)
    grad_fc_bias = jnp.sum(grad_pre.astype(F32), axis=0)
    grad_normed_two = blk_sum(matmul_nt(grad_pre, weight_fc))
    _, norm_two_back = jax.vjp(layer_norm, middle, gain_two, bias_two)
    grad_mid_norm, grad_gain_two, grad_bias_two = norm_two_back(grad_normed_two)
    grad_middle = grad_top + grad_mid_norm
    grad_branch = grad_middle.astype(BF16)
    grad_out_weight = matmul_tn(attended, grad_branch).astype(BF16)
    grad_out_bias = jnp.sum(grad_branch.astype(F32), axis=0)
    grad_heads = to_heads(matmul_nt(grad_branch, weight_out).astype(BF16))
    grad_mixed = jnp.concatenate(
        attend_back(query_ext, mixed, key_aug, attended_heads, grad_heads, scale), axis=1
    )
    grad_qkv_weight = matmul_tn(normed, grad_mixed).astype(BF16)
    sums = jnp.sum(grad_mixed.astype(F32), axis=0)
    grad_normed = blk_sum(matmul_nt(grad_mixed, weight_qkv))
    _, norm_one_back = jax.vjp(layer_norm, inputs, gain_one, bias_one)
    grad_in_norm, grad_gain_one, grad_bias_one = norm_one_back(grad_normed)
    input_grad = grad_middle + grad_in_norm

    proj_sum, fc_sum, out_sum, qkv_sum = scatter_grads(
        n_dp,
        n_blk,
        grad_proj_weight.reshape(n_dp, piece, width),
        grad_fc_weight.reshape(n_dp, shard, n_dp * piece),
        grad_out_weight.reshape(n_dp, shard, width),
        grad_qkv_weight.reshape(n_dp, shard, 3 * wide),
    )

    def spread_out(vec, size):
        parts = vec.reshape(-1, 1, size)
        return jnp.where((jnp.arange(n_blk) == c)[None, :, None], parts, 0.0).reshape(-1)

    small_grads = [
        grad_gain_one,
        grad_bias_one,
        spread_out(sums[:wide], wide),
        spread_out(sums[2 * wide :], wide),
        grad_out_bias,
        grad_gain_two,
        grad_bias_two,
        grad_proj_bias,
        spread_out(grad_fc_bias, piece),
    ]
    small_sum = lax.psum(jnp.concatenate(small_grads), ("dp", "blk"))
    finals = []
    at = 0
    for vec in small_grads:
        size = vec.shape[0]
        finals.append(lax.dynamic_slice_in_dim(small_sum, at + dp * (size // n_dp), size // n_dp, 0))
        at += size
    g_gain1, g_bias1, g_query, g_value, g_out, g_gain2, g_bias2, g_proj, g_fc = finals
    final_qkv = jnp.transpose(qkv_sum.reshape(n_blk, shard, 3, wide), (1, 2, 0, 3))
    final_fc = jnp.transpose(fc_sum.reshape(n_blk, shard, n_dp, piece), (1, 2, 0, 3))
    return (
        layer_output,
        input_grad,
        g_gain1,
        g_bias1,
        final_qkv.reshape(shard, 3 * width),
        g_query,
        g_value,
        jnp.transpose(out_sum, (1, 0, 2)).reshape(shard, width),
        g_out,
        g_gain2,
        g_bias2,
        final_fc.reshape(shard, hidden_all),
        g_fc,
        proj_sum.reshape(n_blk * piece, width),
        g_proj,
    )


def solution(mesh):
    both, rows, one = P(("dp", "blk"), None), P("dp", None), P("dp")
    tokens = P(("dp", "blk"))
    in_specs = (both, tokens, tokens, P(), one, one, rows, one, one, rows, one, one, one, rows, one, rows, one, both)
    out_specs = (both, both, one, one, rows, one, one, rows, one, one, one, rows, one, rows, one)
    return jax.shard_map(
        functools.partial(body, mesh.shape["dp"], mesh.shape["blk"]),
        mesh=mesh,
        in_specs=in_specs,
        out_specs=out_specs,
        check_vma=False,
    )
```

```python
import functools
import math

import jax
import jax.numpy as jnp
from jax import lax
from jax.experimental import pallas as pl
from jax.experimental.pallas import tpu as pltpu
from jax.sharding import PartitionSpec as P

EPSILON = 1e-05
MASKED = -1e30
BF16 = jnp.bfloat16
F32 = jnp.float32
MESH = pl.DeviceIdType.MESH
PLANE = 4
LANES = 128
VMEM_BYTES = 58 * 2**20
VMEM_BACK = 63 * 2**20


def matmul(left, right):
    return jnp.dot(left, right, preferred_element_type=F32)


def matmul_tn(left, right):
    return lax.dot_general(left, right, (((0,), (0,)), ((), ())), preferred_element_type=F32)


def matmul_nt(left, right):
    return lax.dot_general(left, right, (((1,), (1,)), ((), ())), preferred_element_type=F32)


def layer_norm(inputs, gain_vec, bias_vec):
    row_mean = jnp.mean(inputs, axis=-1, keepdims=True)
    centred = inputs - row_mean
    spread = jnp.mean(centred * centred, axis=-1, keepdims=True)
    return centred * lax.rsqrt(spread + EPSILON) * gain_vec + bias_vec


class Place:
    def __init__(self, n_dp, n_blk):
        self.n_dp, self.n_blk, self.length = n_dp, n_blk, n_dp // PLANE
        self.dp, self.c = lax.axis_index("dp"), lax.axis_index("blk")
        self.z, self.p = self.dp // PLANE, lax.rem(self.dp, PLANE)
        side, row = lax.rem(self.p, 2), self.p // 2
        self.flip_x, self.flip_y = self.p + 1 - 2 * side, self.p + 2 - 4 * row
        self.diag = PLANE - 1 - self.p

    def routes(self, zz):
        odd = lax.rem(zz, 2)
        return (
            self.flip_x * (1 - odd) + self.flip_y * odd,
            self.flip_x * odd + self.flip_y * (1 - odd),
        )

    def at(self, zz, pp):
        return (zz * PLANE + pp, self.c)

    def sibling(self, k):
        return (self.dp, lax.rem(self.c + k, self.n_blk))

    def apart(self, s, run):
        if s == 0:
            run(self.z)
            return

        @pl.loop(0, 2)
        def _(k):
            zz = self.z + s * (1 - 2 * k)
            pl.when((zz >= 0) & (zz < self.length))(lambda: run(zz))

    def up_down(self, run_up, run_down):
        pl.when(self.z < self.length - 1)(run_up)
        pl.when(self.z > 0)(run_down)

    def greet(self):
        barrier = pltpu.get_barrier_semaphore()

        def hello(device):
            pl.semaphore_signal(barrier, inc=1, device_id=device, device_id_type=MESH)

        hello(self.at(self.z, self.flip_x))
        hello(self.at(self.z, self.flip_y))
        for k in range(1, self.n_blk):
            hello(self.sibling(k))
        self.up_down(
            lambda: hello(self.at(self.z + 1, self.p)), lambda: hello(self.at(self.z - 1, self.p))
        )
        ends = jnp.minimum(self.z, 1) + jnp.minimum(self.length - 1 - self.z, 1)
        pl.semaphore_wait(barrier, 1 + self.n_blk + ends)


def remote(src, dst, send_sem, recv_sem, device):
    return pltpu.make_async_remote_copy(
        src_ref=src,
        dst_ref=dst,
        send_sem=send_sem,
        recv_sem=recv_sem,
        device_id=device,
        device_id_type=MESH,
    )


class Gather:
    def __init__(self, place, unit, chunk, send, recv):
        self.place, self.chunk = place, chunk
        self.send = lambda kind, zz: send.at[unit, kind, zz]
        self.recv = lambda slot: recv.at[unit, slot]

    def copy(self, slot, kind, zz, device):
        piece = self.chunk(slot)
        return remote(piece, piece, self.send(kind, zz), self.recv(slot), device)

    def arrived(self, slot):
        self.copy(slot, 0, 0, self.place.sibling(1)).wait_recv()

    def line(self):
        pc = self.place
        pc.up_down(
            lambda: self.copy(pc.dp, 3, pc.z, pc.at(pc.z + 1, pc.p)).start(),
            lambda: self.copy(pc.dp, 4, pc.z, pc.at(pc.z - 1, pc.p)).start(),
        )

    def along(self, s):
        pc = self.place

        def pass_on(zz):
            slot = zz * PLANE + pc.p
            self.arrived(slot)
            below = jnp.where(zz < pc.z, 1, 0)
            onward = pc.z + 2 * below - 1
            more = (onward >= 0) & (onward < pc.length)
            pl.when(more)(lambda: self.copy(slot, 3, zz, pc.at(onward, pc.p)).start())

        pc.apart(s, pass_on)

    def ring(self, s):
        pc = self.place

        def both(zz):
            slot = zz * PLANE + pc.p
            self.copy(slot, 0, zz, pc.at(pc.z, pc.flip_x)).start()
            self.copy(slot, 1, zz, pc.at(pc.z, pc.flip_y)).start()

        pc.apart(s, both)

    def across(self, s):
        pc = self.place

        def turn(zz):
            near, far = pc.routes(zz)
            slot = zz * PLANE + near
            self.arrived(slot)
            self.copy(slot, 2, zz, pc.at(pc.z, far)).start()

        pc.apart(s, turn)

    def finish(self):
        pc = self.place

        @pl.loop(0, pc.length)
        def _(zz):
            self.arrived(zz * PLANE + pc.routes(zz)[1])
            self.arrived(zz * PLANE + pc.diag)

    def drain(self):
        pc = self.place

        def sent(kind, zz):
            self.copy(pc.dp, kind, zz, pc.sibling(1)).wait_send()

        @pl.loop(0, pc.length)
        def _(zz):
            sent(0, zz)
            sent(1, zz)
            sent(2, zz)
            pl.when((zz <= pc.z) & (pc.z < pc.length - 1))(lambda: sent(3, zz))
            pl.when((zz > pc.z) & (pc.z > 0))(lambda: sent(3, zz))

        pl.when(pc.z > 0)(lambda: sent(4, pc.z))


class RingGather:
    def __init__(self, place, unit, chunk, part, send, recv):
        self.place, self.chunk, self.part = place, chunk, part
        self.lift = lambda pp, zz: send.at[unit, pp, zz]
        self.side = lambda k: send.at[unit + 1, 0, k]
        self.recv = lambda slot: recv.at[unit, slot]
        self.other = recv.at[unit + 1, 0]

    def copy(self, piece, sem, recv, device):
        return remote(piece, piece, sem, recv, device)

    def arrived(self, slot):
        self.copy(self.chunk(slot), self.side(0), self.recv(slot), self.place.sibling(1)).wait_recv()

    def start(self):
        pc = self.place
        piece, recv = self.chunk(pc.dp), self.recv(pc.dp)
        self.copy(piece, self.side(0), recv, pc.at(pc.z, pc.flip_x)).start()
        self.copy(piece, self.side(1), recv, pc.at(pc.z, pc.flip_y)).start()

    def across(self):
        pc = self.place
        base = pc.z * PLANE
        self.arrived(base + pc.flip_x)
        half = self.part(base + pc.flip_x, 0)
        self.copy(half, self.side(2), self.recv(base + pc.flip_x), pc.at(pc.z, pc.flip_y)).start()
        self.arrived(base + pc.flip_y)
        half = self.part(base + pc.flip_y, 1)
        self.copy(half, self.side(3), self.other, pc.at(pc.z, pc.flip_x)).start()

    def rise(self):
        pc = self.place
        slot = pc.z * PLANE + pc.diag
        for i, recv in enumerate((self.recv(slot), self.other)):
            self.copy(self.part(slot, i), self.side(0), recv, pc.sibling(1)).wait_recv()

        @pl.loop(0, PLANE)
        def _(pp):
            at = pc.z * PLANE + pp
            piece = self.chunk(at)

            def to(sem, zz):
                self.copy(piece, sem, self.recv(at), pc.at(zz, pc.p)).start()

            pc.up_down(
                lambda: to(self.lift(pp, pc.z), pc.z + 1), lambda: to(self.lift(4, pp), pc.z - 1)
            )

    def along(self, s):
        pc = self.place

        def pass_on(zz):
            below = jnp.where(zz < pc.z, 1, 0)
            onward = pc.z + 2 * below - 1

            @pl.loop(0, PLANE)
            def _(pp):
                slot = zz * PLANE + pp
                self.arrived(slot)
                copy = self.copy(
                    self.chunk(slot), self.lift(pp, zz), self.recv(slot), pc.at(onward, pc.p)
                )
                pl.when((onward >= 0) & (onward < pc.length))(copy.start)

        pc.apart(s, pass_on)

    def drain(self):
        pc = self.place
        piece = self.chunk(pc.dp)

        def sent(sem, view=piece):
            self.copy(view, sem, self.recv(pc.dp), pc.sibling(1)).wait_send()

        sent(self.side(0))
        sent(self.side(1))
        sent(self.side(2), self.part(pc.dp, 0))
        sent(self.side(3), self.part(pc.dp, 1))

        @pl.loop(0, PLANE)
        def _(pp):
            @pl.loop(0, pc.length)
            def _(zz):
                pl.when((zz <= pc.z) & (pc.z < pc.length - 1))(lambda: sent(self.lift(pp, zz)))
                pl.when((zz > pc.z) & (pc.z > 0))(lambda: sent(self.lift(pp, zz)))

            pl.when(pc.z > 0)(lambda: sent(self.lift(4, pp)))


def gather_kernel(
    n_dp, n_blk, qkv, out, fc, proj, small, all_qkv, all_out, all_fc, all_proj, all_small, send, recv, local, side
):
    pc = Place(n_dp, n_blk)
    wide = out.shape[1]
    mine = pl.ds(pl.multiple_of(pc.c * wide, LANES), wide)
    parts = [
        (small, lambda slot: all_small.at[slot]),
        (qkv, lambda slot: all_qkv.at[slot]),
        (out, lambda slot: all_out.at[slot, :, mine]),
        (fc, lambda slot: all_fc.at[slot]),
        (proj, lambda slot: all_proj.at[slot]),
    ]
    for i, (own, chunk) in enumerate(parts):
        pltpu.make_async_copy(own, chunk(pc.dp), local.at[i]).start()
    pc.greet()
    for i, (own, chunk) in enumerate(parts):
        pltpu.make_async_copy(own, chunk(pc.dp), local.at[i]).wait()
    units = [Gather(pc, i, chunk, send, recv) for i, (_, chunk) in enumerate(parts)]
    steps = range(pc.length)
    for i, unit in enumerate(units):
        unit.line()
        for s in steps:
            if s:
                unit.along(s)
            unit.ring(s)
        if i > 0:
            for s in steps:
                units[i - 1].across(s)
            units[i - 1].finish()
    for s in steps:
        units[4].across(s)
    side_copies = []
    piece = all_out.at[:, :, mine]
    for k in range(1, n_blk):
        copy = remote(piece, piece, side.at[0, k], side.at[1, k], pc.sibling(k))
        copy.start()
        side_copies.append(copy)
    units[4].finish()
    for copy in side_copies:
        copy.wait()
    for unit in units:
        unit.drain()


class Scatter:
    def __init__(self, place, unit, chunk, bufs, send, recv):
        self.place, self.chunk = place, chunk
        self.diag, self.near, self.far, self.line = bufs
        self.kind = self.near.dtype
        self.send = lambda kind, zz: send.at[unit, kind, zz]
        self.recv = lambda kind, zz: recv.at[unit, kind, zz]

    def copy(self, src, dst, kind, zz, device):
        return remote(src, dst, self.send(kind, zz), self.recv(kind, zz), device)

    def arrived(self, piece, kind, zz):
        self.copy(piece, piece, kind, zz, self.place.sibling(1)).wait_recv()

    def start(self):
        pc = self.place

        def first(zz):
            to = pc.at(pc.z, pc.routes(zz)[0])
            self.copy(self.chunk(zz * PLANE + pc.diag), self.diag.at[zz], 0, zz, to).start()

        def second(zz):
            near = pc.routes(zz)[0]
            to = pc.at(pc.z, near)
            self.copy(self.chunk(zz * PLANE + near), self.near.at[zz], 1, zz, to).start()

        for s in range(pc.length - 1, -1, -1):
            pc.apart(s, first)
        for s in range(pc.length - 1, -1, -1):
            pc.apart(s, second)

    def middle(self, s):
        pc = self.place

        def turn(zz):
            far = pc.routes(zz)[1]
            self.arrived(self.diag.at[zz], 0, zz)
            total = self.diag[zz].astype(F32) + self.chunk(zz * PLANE + far)[...].astype(F32)
            self.diag[zz] = total.astype(self.kind)
            self.copy(self.diag.at[zz], self.far.at[zz], 2, zz, pc.at(pc.z, far)).start()

        pc.apart(s, turn)

    def settle(self, s):
        pc = self.place

        def add(zz):
            self.arrived(self.near.at[zz], 1, zz)
            self.arrived(self.far.at[zz], 2, zz)
            total = self.near[zz].astype(F32) + self.far[zz].astype(F32)
            total += self.chunk(zz * PLANE + pc.p)[...].astype(F32)
            self.near[zz] = total.astype(self.kind)

        pc.apart(s, add)

    def along(self, s):
        pc = self.place

        def pass_on(zz):
            above = jnp.where(zz > pc.z, 1, 0)
            onward = pc.z + 2 * above - 1
            before = pc.z - 2 * above + 1

            def more():
                self.arrived(self.line.at[zz], 4 - above, zz)
                total = self.near[zz].astype(F32) + self.line[zz].astype(F32)
                self.near[zz] = total.astype(self.kind)

            if s < pc.length - 1:
                pl.when((before >= 0) & (before < pc.length))(more)
            at = zz if s > 1 else zz * above + pc.length * (1 - above)
            to = pc.at(onward, pc.p)
            self.copy(self.near.at[zz], self.line.at[at], 4 - above, zz, to).start()

        pc.apart(s, pass_on)

    def finish(self, total):
        pc = self.place
        total[...] = self.near[pc.z].astype(F32)

        def more(at, kind):
            self.arrived(self.line.at[at], kind, pc.z)
            total[...] += self.line[at].astype(F32)

        pl.when(pc.z > 0)(lambda: more(pc.z, 3))
        pl.when(pc.z < pc.length - 1)(lambda: more(pc.length, 4))

    def drain(self):
        pc = self.place

        def sent(kind, zz):
            piece = self.near.at[zz]
            self.copy(piece, piece, kind, zz, pc.sibling(1)).wait_send()

        @pl.loop(0, pc.length)
        def _(zz):
            sent(0, zz)
            sent(1, zz)
            sent(2, zz)
            pl.when(zz > pc.z)(lambda: sent(3, zz))
            pl.when(zz < pc.z)(lambda: sent(4, zz))


class LineScatter:
    def __init__(self, place, unit, chunk, bufs, send, recv):
        self.place, self.chunk = place, chunk
        self.line, self.half, self.ring = bufs
        self.lift = lambda pp, zz: send.at[unit, pp, zz]
        self.drop = lambda kind, zz: recv.at[unit, kind, zz]
        self.side = lambda k: (send.at[unit + 1, 0, k], recv.at[unit + 1, 0, k])
        self.middle_row = self.half.shape[1]

    def arrived(self, piece, sem):
        remote(piece, piece, self.lift(0, 0), sem, self.place.sibling(1)).wait_recv()

    def along(self, s):
        pc = self.place

        def pass_on(zz):
            above = jnp.where(zz > pc.z, 1, 0)
            onward = pc.z + 2 * above - 1
            before = pc.z - 2 * above + 1
            at = zz if s > 1 else zz * above + pc.length * (1 - above)

            @pl.loop(0, PLANE)
            def _(pp):
                last = pp * (1 - above) + zz * above if s == 1 else zz
                kind = pp if s > 1 else pp * above + PLANE * (1 - above)
                sem = self.drop(kind, last)
                dst, to = self.line.at[pp, at], pc.at(onward, pc.p)
                own = self.chunk(zz * PLANE + pp)

                def plain():
                    remote(own, dst, self.lift(pp, zz), sem, to).start()

                def more():
                    piece = self.line.at[pp, zz]
                    self.arrived(piece, self.drop(pp, zz))
                    piece[...] = (piece[...].astype(F32) + own[...].astype(F32)).astype(BF16)
                    remote(piece, dst, self.lift(pp, zz), sem, to).start()

                inside = (before >= 0) & (before < pc.length)
                if s == pc.length - 1:
                    plain()
                else:
                    pl.when(inside)(more)
                    pl.when(jnp.logical_not(inside))(plain)

        pc.apart(s, pass_on)

    def settle(self):
        pc = self.place

        @pl.loop(0, PLANE)
        def _(pp):
            own = self.chunk(pc.z * PLANE + pp)
            piece, over = self.line.at[pp, pc.z], self.line.at[pp, pc.length]

            def below():
                self.arrived(piece, self.drop(pp, pc.z))
                piece[...] = (piece[...].astype(F32) + own[...].astype(F32)).astype(BF16)

            def bottom():
                piece[...] = own[...]

            def above():
                self.arrived(over, self.drop(PLANE, pp))
                piece[...] = (piece[...].astype(F32) + over[...].astype(F32)).astype(BF16)

            pl.when(pc.z > 0)(below)
            pl.when(pc.z == 0)(bottom)
            pl.when(pc.z < pc.length - 1)(above)

        for i, to in enumerate((pc.flip_x, pc.flip_y)):
            rows = pl.ds(i * self.middle_row, self.middle_row)
            piece = self.line.at[pc.diag, pc.z, rows]
            remote(piece, self.half.at[i], *self.side(i), pc.at(pc.z, to)).start()

    def turn(self):
        pc = self.place
        for i, (dest, to) in enumerate(((pc.flip_y, pc.flip_y), (pc.flip_x, pc.flip_x))):
            rows = pl.ds(i * self.middle_row, self.middle_row)
            self.arrived(self.half.at[i], self.side(i)[1])
            value = self.line[dest, pc.z, rows].astype(F32) + self.half[i].astype(F32)
            self.line[dest, pc.z, rows] = value.astype(BF16)
            piece = self.line.at[dest, pc.z]
            remote(piece, self.ring.at[1 - i], *self.side(3 - i), pc.at(pc.z, to)).start()

    def finish(self, total):
        pc = self.place
        value = self.line[pc.p, pc.z].astype(F32)
        for i in range(2):
            self.arrived(self.ring.at[i], self.side(2 + i)[1])
            value += self.ring[i].astype(F32)
        total[...] = value

    def drain(self):
        pc = self.place

        def sent(piece, sem):
            remote(piece, piece, sem, self.drop(0, 0), pc.sibling(1)).wait_send()

        for i in range(2):
            sent(self.half.at[i], self.side(i)[0])
            sent(self.ring.at[i], self.side(2 + i)[0])

        @pl.loop(0, PLANE)
        def _(pp):
            @pl.loop(0, pc.length)
            def _(zz):
                piece = self.line.at[pp, zz]
                pl.when(zz > pc.z)(lambda: sent(piece, self.lift(pp, zz)))
                pl.when(zz < pc.z)(lambda: sent(piece, self.lift(pp, zz)))


def scatter_kernel(n_dp, n_blk, *refs):
    grads, outs, rest = refs[:4], refs[4:8], refs[8:]
    bufs, totals, rest = rest[:16], rest[16:20], rest[20:]
    side_buf, send, recv, side, last = rest
    proj, fc, out, qkv = grads
    pc = Place(n_dp, n_blk)
    pc.greet()
    wide = out.shape[2] // n_blk

    def columns(core):
        return pl.ds(pl.multiple_of(core * wide, LANES), wide)

    chunks = [
        lambda slot: proj.at[slot],
        lambda slot: fc.at[slot],
        lambda slot: side_buf.at[0, slot],
        lambda slot: qkv.at[slot],
    ]
    units = [
        Scatter(pc, i, chunks[i], bufs[4 * i : 4 * i + 4], send, recv) for i in range(4)
    ]
    units[0].start()
    units[1].start()
    side_copies = []
    for k in range(1, n_blk):
        dev = pc.sibling(k)
        copy = remote(
            out.at[:, :, columns(dev[1])], side_buf.at[k], side.at[0, k], side.at[1, k], dev
        )
        copy.start()
        side_copies.append(copy)

    def side_sum():
        for copy in side_copies:
            copy.wait()

        @pl.loop(0, n_dp)
        def _(slot):
            total = out[slot, :, columns(pc.c)].astype(F32)
            for k in range(1, n_blk):
                total += side_buf[k, slot].astype(F32)
            side_buf[0, slot] = total.astype(BF16)

    pending = []

    def spread(i):
        units[i].finish(totals[i])
        total = totals[i]
        pieces = [(total, outs[i].at[pc.c])]
        for j, (src, dst) in enumerate(pieces):
            keep = pltpu.make_async_copy(src, dst, last.at[i, 0, 0])
            keep.start()
            pending.append(keep)
            for k in range(1, n_blk):
                copy = remote(src, dst, last.at[i, 0, k], last.at[i, 1, k], pc.sibling(k))
                copy.start()
                pending.append(copy)

    steps = range(pc.length - 1, -1, -1)

    def middle(i):
        for s in steps:
            units[i].middle(s)

    def settle(i):
        for s in steps:
            units[i].settle(s)
            if s:
                units[i].along(s)

    middle(0)
    side_sum()
    units[2].start()
    middle(1)
    units[3].start()
    settle(0)
    middle(2)
    settle(1)
    spread(0)
    middle(3)
    settle(2)
    settle(3)
    spread(1)
    spread(2)
    spread(3)
    for copy in pending:
        copy.wait()
    for unit in units:
        unit.drain()


def gather_weights(n_dp, n_blk, qkv, out, fc, proj, small):
    shards = (qkv, out, fc, proj, small)
    shapes = [
        jax.ShapeDtypeStruct((n_dp, a.shape[0], a.shape[1] * (n_blk if a is out else 1)), BF16)
        for a in shards
    ]
    length = n_dp // PLANE
    hbm = pl.BlockSpec(memory_space=pl.ANY)
    return pl.pallas_call(
        functools.partial(gather_kernel, n_dp, n_blk),
        out_shape=shapes,
        in_specs=[hbm] * 5,
        out_specs=[hbm] * 5,
        scratch_shapes=[
            pltpu.SemaphoreType.DMA((5, 5, length)),
            pltpu.SemaphoreType.DMA((5, n_dp)),
            pltpu.SemaphoreType.DMA((5,)),
            pltpu.SemaphoreType.DMA((2, n_blk)),
        ],
        compiler_params=pltpu.CompilerParams(
            collective_id=0, has_side_effects=True, vmem_limit_bytes=VMEM_BYTES
        ),
    )(*shards)


def scatter_grads(n_dp, n_blk, proj, fc, out, qkv):
    length = n_dp // PLANE
    grads = (proj, fc, out, qkv)
    sizes = [a.shape[1:] for a in grads]
    sizes[2] = (sizes[2][0], sizes[2][1] // n_blk)
    vmem = pl.BlockSpec(memory_space=pltpu.VMEM)
    scratch = []
    for size in sizes:
        scratch += [pltpu.VMEM((length,) + size, BF16)] * 3 + [pltpu.VMEM((length + 1,) + size, BF16)]
    scratch += [pltpu.VMEM(size, F32) for size in sizes]
    scratch += [
        pltpu.VMEM((n_blk, n_dp) + sizes[2], BF16),
        pltpu.SemaphoreType.DMA((4, 5, length)),
        pltpu.SemaphoreType.DMA((4, 5, length)),
        pltpu.SemaphoreType.DMA((2, n_blk)),
        pltpu.SemaphoreType.DMA((4, 2, n_blk)),
    ]
    return pl.pallas_call(
        functools.partial(scatter_kernel, n_dp, n_blk),
        out_shape=[jax.ShapeDtypeStruct((n_blk,) + size, F32) for size in sizes],
        in_specs=[vmem] * 4,
        out_specs=[pl.BlockSpec(memory_space=pl.ANY)] * 4,
        scratch_shapes=scratch,
        compiler_params=pltpu.CompilerParams(
            collective_id=1, has_side_effects=True, vmem_limit_bytes=VMEM_BYTES
        ),
    )(*grads)


def lane_split(value, lane, first, base):
    for i in range(3):
        term = value.astype(BF16)
        base = jnp.where(lane == first + i, term, base)
        value = value - term.astype(F32)
    return base


def causal_tail(scores, block, axis, masked):
    key_axis, query_axis = (0, 1) if axis == 0 else (1, 0)
    tail_shape = (block, block)
    keep = lax.broadcasted_iota(jnp.int32, tail_shape, key_axis) <= lax.broadcasted_iota(
        jnp.int32, tail_shape, query_axis
    )
    size = scores.shape[axis]
    if size == block:
        return jnp.where(keep, scores, masked)
    head = lax.slice_in_dim(scores, 0, size - block, axis=axis)
    tail = jnp.where(keep, lax.slice_in_dim(scores, size - block, size, axis=axis), masked)
    return jnp.concatenate([head, tail], axis=axis)


def causal_all(scores, offset, axis, masked):
    key_axis, query_axis = (0, 1) if axis == 0 else (1, 0)
    keep = (
        lax.broadcasted_iota(jnp.int32, scores.shape, key_axis)
        <= lax.broadcasted_iota(jnp.int32, scores.shape, query_axis) + offset
    )
    return jnp.where(keep, scores, masked)


def query_blocks(total, block, run):
    count = total // block
    if count <= 4:
        for b in range(count):
            run(
                b * block,
                (b + 1) * block,
                lambda scores, axis, masked: causal_tail(scores, block, axis, masked),
            )
    else:

        @pl.loop(0, count)
        def _(b):
            first = pl.multiple_of(b * block, block)
            run(first, total, lambda scores, axis, masked: causal_all(scores, first, axis, masked))


def attend_kernel(block, scale, q_ref, k_ref, v_ref, key_aug, query_aug, slopes, out_ref, qx_ref):
    total = q_ref.shape[0]
    half = LANES // 2
    lane = lax.broadcasted_iota(jnp.int32, (1, LANES), 1)
    slope_rows = []
    for hh in range(2):
        base = half * (1 - hh)
        slope = jnp.full((1, LANES), slopes[hh], F32)
        row = lane_split(slope, lane, base, jnp.zeros((1, LANES), BF16))
        slope_rows.append(lane_split(slope, lane, base + 3, row))

    def run(first, keys, mask):
        rows = pl.ds(first, block)
        result = None
        for hh in range(2):
            own = (lane < half) if hh == 0 else (lane >= half)
            base = half * (1 - hh)
            aug = query_aug[rows, :] + slope_rows[hh]
            query = jnp.where(own, q_ref[rows, :] * BF16(scale), aug)
            key = jnp.where(own, k_ref[0:keys, :], key_aug[0:keys, :])
            value = jnp.where(own, v_ref[0:keys, :], BF16(1))
            scores = mask(matmul_nt(query, key), 1, MASKED)
            top = jnp.max(scores, axis=1, keepdims=True)
            weights = jnp.exp(scores - top).astype(BF16)
            sums = matmul(weights, value)
            log_total = top + jnp.log(sums[:, base : base + 1])
            qx_ref[0, hh, rows, :] = lane_split(-log_total, lane, base + 8, query)
            part = sums / pltpu.roll(sums, half, 1)
            result = part if hh == 0 else jnp.where(own, part, result)
        out_ref[rows, :] = result.astype(BF16)

    query_blocks(total, block, run)


def attend_back_kernel(
    block, scale, qx_ref, k_ref, v_ref, key_aug, out_ref, grad_ref, dq_ref, dk_ref, dv_ref, dk_acc, dv_acc
):
    total = k_ref.shape[0]
    half = LANES // 2
    lane = lax.broadcasted_iota(jnp.int32, (1, LANES), 1)
    dk_acc[...] = jnp.zeros_like(dk_acc)
    dv_acc[...] = jnp.zeros_like(dv_acc)

    def run(first, keys, mask):
        rows = pl.ds(first, block)
        grad = grad_ref[rows, :]
        product = grad.astype(F32) * out_ref[rows, :].astype(F32)
        dq = None
        dk = None
        dv = None
        for hh in range(2):
            own = (lane < half) if hh == 0 else (lane >= half)
            base = half * (1 - hh)
            query = qx_ref[0, hh, rows, :]
            key = jnp.where(own, k_ref[0:keys, :], key_aug[0:keys, :])
            delta = jnp.sum(jnp.where(own, product, 0.0), axis=1, keepdims=True)
            grad_own = jnp.where(own, grad, BF16(0))
            grad_aug = lane_split(-delta, lane, base, grad_own)
            value = jnp.where(own, v_ref[0:keys, :], BF16(1))
            weights = mask(jnp.exp(matmul_nt(key, query)), 0, 0.0)
            change = (weights * matmul_nt(value, grad_aug)).astype(BF16)
            key_own = jnp.where(own, key, BF16(0))
            query_own = jnp.where(own, query, BF16(0))
            dv_part = matmul(weights.astype(BF16), grad_own)
            dk_part = matmul(change, query_own)
            dq_part = matmul_tn(change, key_own)
            dv = dv_part if hh == 0 else dv + dv_part
            dk = dk_part if hh == 0 else dk + dk_part
            dq = dq_part if hh == 0 else dq + dq_part
        dq_ref[rows, :] = (dq * scale).astype(BF16)
        dk_acc[0:keys, :] += dk
        dv_acc[0:keys, :] += dv

    query_blocks(total, block, run)
    dk_ref[...] = dk_acc[...].astype(BF16)
    dv_ref[...] = dv_acc[...].astype(BF16)


def gelu_pair(u):
    k = math.sqrt(2.0 / math.pi)
    square = u * u
    t = jnp.tanh(k * u * (1.0 + 0.044715 * square))
    plus = 0.5 * (1.0 + t)
    slope = plus + (0.5 * k) * u * (1.0 - t * t) * (1.0 + 3 * 0.044715 * square)
    return u * plus, slope


def whole(ref, cols):
    value = ref[:, :, cols]
    return value.reshape(value.shape[0] * value.shape[1], value.shape[2])


def token_tables(pos_ref, row_ref, key_ref, query_ref, first):
    lane = lax.rem(lax.broadcasted_iota(jnp.int32, (1, LANES), 1), LANES // 2)
    for b in range(pos_ref.shape[0]):

        def column(ref):
            row = ref[b : b + 1, :].astype(F32)
            return jnp.transpose(jnp.broadcast_to(row, (LANES, LANES)))

        place, other = column(pos_ref), column(row_ref)
        high = jnp.floor(place * (1.0 / 256)) * 256
        key = jnp.where(lane < 3, high, place - high)
        key = jnp.where(lane == 6, 1.0 - other, key)
        key = jnp.where(lane == 7, other, key)
        key = jnp.where(lane < 8, key, jnp.where(lane < 11, 1.0, 0.0))
        query = jnp.where(lane == 6, other * MASKED, 0.0)
        query = jnp.where(lane == 7, (1.0 - other) * MASKED, query)
        rows = pl.ds(pl.multiple_of(first + b * LANES, LANES), LANES)
        key_ref[rows, :] = key.astype(BF16)
        query_ref[rows, :] = query.astype(BF16)


def forward_kernel(n_dp, n_blk, scale, *refs):
    (qkv, out, fc, proj, tokens, out_grad, pos, rows_id, slopes, fc_bias) = refs[:10]
    vectors, refs = refs[10:18], refs[18:]
    (w_qkv_o, w_out_o, w_fc_o, w_proj_o, vec_o, h1_o, mixed_o, heads_o, att_o, qx_o, mid_o, h2_o, hid_o, slope_o, dy_o, key_o, gp_o) = refs[:17]
    (w_qkv, w_out, w_fc, w_proj, vec, h1, mixed, heads, att, qx, mid, h2, hid, gslope, dy, key_aug, gp) = refs[17:34]
    (w_small, fcb, x_all, query_aug, f_qkv, f_out, f_fc, f_proj) = refs[34:42]
    send, recv, side, load, save_sem = refs[42:]
    pc = Place(n_dp, n_blk)
    sib = pc.sibling(1)
    rows_own, width = tokens.shape
    total = n_blk * rows_own
    wide = width // n_blk
    piece = f_proj.shape[0]
    tile = 256
    mine = pl.ds(pl.multiple_of(pc.c * rows_own, rows_own), rows_own)
    theirs = pl.ds(pl.multiple_of(sib[1] * rows_own, rows_own), rows_own)
    my_start = pl.multiple_of(pc.c * wide, LANES)
    my_cols = pl.ds(my_start, wide)
    saves = []

    def exchange(i, src, dst):
        copy = remote(src, dst, side.at[0, i], side.at[1, i], sib)
        copy.start()
        return copy

    def keep(i, src, dst):
        copy = pltpu.make_async_copy(src, dst, load.at[i])
        copy.start()
        return copy

    def save(i, src, dst):
        copy = pltpu.make_async_copy(src, dst, save_sem.at[i])
        copy.start()
        saves.append(copy)

    get_qkv = [
        keep(i, qkv.at[:, pl.ds(my_start + i * width, wide)], f_qkv.at[:, i * wide : (i + 1) * wide])
        for i in range(3)
    ]
    get_out = keep(3, out.at[:, my_cols], f_out)
    get_proj = keep(4, proj.at[pl.ds(pl.multiple_of(pc.c * piece, piece), piece)], f_proj)

    def fc_part(j):
        src = fc.at[:, pl.ds(pl.multiple_of((j * n_blk + pc.c) * piece, piece), piece)]
        dst = f_fc.at[:, pl.ds(pl.multiple_of(j * piece, piece), piece)]
        return pltpu.make_async_copy(src, dst, load.at[8 + j])

    pl.loop(0, n_dp)(lambda j: fc_part(j).start())
    get_x = keep(5, tokens, x_all.at[mine])
    pc.greet()
    first = [exchange(0, tokens, x_all.at[mine])]
    lane = lax.broadcasted_iota(jnp.int32, (1, LANES), 1)
    shard = width // n_dp
    own_part = lane // shard == lax.rem(pc.dp, LANES // shard)
    lines = []
    for ref in vectors:
        lines.append(jnp.where(own_part, jnp.concatenate([ref[...]] * (LANES // shard), axis=1), 0.0))
    lines.append(fc_bias[:, pl.ds(pl.multiple_of(pc.c * piece, piece), piece)])
    lines.append(jnp.zeros((16 - len(lines), LANES), F32))
    w_small[pc.dp] = jnp.concatenate(lines, axis=0).astype(BF16)
    cut = piece // 2
    quarter = cut // 2
    chunks = [
        lambda slot: w_small.at[slot],
        lambda slot: w_qkv.at[slot],
        lambda slot: w_out.at[slot, :, my_cols],
        lambda slot: w_fc.at[slot],
        lambda slot: w_proj.at[slot, cut:piece],
    ]
    u_small, u_qkv, u_out, u_fc, u_proj = [
        Gather(pc, i, chunk, send, recv) for i, chunk in enumerate(chunks)
    ]
    u_ring = RingGather(
        pc,
        5,
        lambda slot: w_proj.at[slot, 0:cut],
        lambda slot, i: w_proj.at[slot, i * quarter : (i + 1) * quarter],
        send,
        recv,
    )
    steps = range(1, pc.length)
    u_small.line()
    u_small.ring(0)
    for copy in get_qkv:
        copy.wait()
    w_qkv[pc.dp] = f_qkv[...].astype(BF16)
    u_qkv.line()
    u_qkv.ring(0)
    get_out.wait()
    w_out[pc.dp, :, my_cols] = f_out[...].astype(BF16)
    get_proj.wait()
    w_proj[pc.dp] = f_proj[...].astype(BF16)
    token_tables(pos, rows_id, key_aug, query_aug, pc.c * rows_own)
    first.append(exchange(1, key_aug.at[mine], key_aug.at[mine]))
    first.append(exchange(2, query_aug.at[mine], query_aug.at[mine]))
    u_small.along(1)
    u_small.ring(1)
    u_qkv.along(1)
    u_qkv.ring(1)
    for s in steps[1:]:
        u_small.along(s)
        u_small.ring(s)
    for s in range(pc.length):
        u_small.across(s)
    pl.loop(0, n_dp)(lambda j: fc_part(j).wait())
    w_fc[pc.dp] = f_fc[...].astype(BF16)
    later = [exchange(3, out_grad, dy.at[mine]), keep(6, out_grad, dy.at[mine])]
    u_small.finish()
    u_qkv.along(2)
    u_qkv.ring(2)
    u_out.line()
    get_x.wait()
    for copy in first:
        copy.wait()
    per = n_dp // (width // LANES)
    for t in range(width // LANES):
        rows = w_small[t * per].astype(F32)
        for k in range(1, per):
            rows += w_small[t * per + k].astype(F32)
        vec[:, t * LANES : (t + 1) * LANES] = rows
    for t in range(n_dp):
        fcb[:, t * LANES : (t + 1) * LANES] = w_small[t, 8:9, :].astype(F32)
    save(0, vec, vec_o)

    def first_norm(b):
        rows = pl.ds(pl.multiple_of(b * LANES, LANES), LANES)
        h1[rows, :] = layer_norm(x_all[rows, :].astype(F32), vec[0:1, :], vec[1:2, :]).astype(BF16)

    norm_blocks = total // LANES
    pl.loop(0, norm_blocks // 2)(first_norm)
    for s in steps[2:]:
        u_qkv.along(s)
        u_qkv.ring(s)
    u_fc.line()
    u_out.ring(0)
    pl.loop(norm_blocks // 2, norm_blocks)(first_norm)
    save(2, h1, h1_o)
    for s in range(pc.length):
        u_qkv.across(s)
    u_ring.start()
    for s in steps:
        u_out.along(s)
        u_out.ring(s)
    u_fc.along(1)
    u_qkv.finish()
    save(3, w_qkv, w_qkv_o)
    for third in range(3):
        for b in range(wide // tile):

            @pl.loop(0, total // 512)
            def _(m, third=third, b=b):
                rows = pl.ds(pl.multiple_of(m * 512, 512), 512)
                cols = pl.ds(third * wide + b * tile, tile)
                value = matmul(h1[rows, :], whole(w_qkv, cols))
                if third != 1:
                    at = pl.ds(my_start + b * tile, tile)
                    value += vec[pl.ds(2 + third // 2, 1), at]
                mixed[rows, cols] = value.astype(BF16)

        if third == 0:
            u_fc.along(2)
            for s in range(pc.length):
                u_out.across(s)
            u_ring.across()
    save(4, mixed, mixed_o)
    for s in steps[2:]:
        u_fc.along(s)
    for s in range(pc.length):
        u_fc.ring(s)
    u_proj.line()
    pairs = wide // LANES
    for j in range(pairs):
        cols = [pl.ds(i * wide + j * LANES, LANES) for i in range(3)]
        attend_kernel(
            tile,
            scale,
            mixed.at[:, cols[0]],
            mixed.at[:, cols[1]],
            mixed.at[:, cols[2]],
            key_aug,
            query_aug,
            [slopes[pc.c * 2 * pairs + 2 * j + hh] for hh in range(2)],
            heads.at[:, cols[0]],
            qx.at[pl.ds(j, 1)],
        )
        if j == 0:
            u_ring.rise()
        if j < pc.length - 1:
            u_proj.along(j + 1)
        if j == 1:
            u_fc.across(0)
        if j == 2:
            u_ring.along(1)
            u_fc.across(1)
            u_out.finish()
            part = w_out.at[:, :, my_cols]
            share = exchange(4, part, part)
    swap = exchange(5, heads.at[theirs], att.at[:, my_cols])
    stay = keep(7, heads.at[mine], att.at[:, my_cols])
    save(5, heads, heads_o)
    save(6, qx, qx_o)
    share.wait()
    save(7, w_out, w_out_o)
    swap.wait()
    stay.wait()
    save(8, att, att_o)

    @pl.loop(0, width // tile)
    def _(b):
        cols = pl.ds(pl.multiple_of(b * tile, tile), tile)
        value = matmul(att[...], whole(w_out, cols))
        mid[:, cols] = x_all[mine, cols].astype(F32) + value + vec[4:5, cols]

    u_fc.across(2)

    @pl.loop(0, rows_own // LANES)
    def _(b):
        rows = pl.ds(pl.multiple_of(b * LANES, LANES), LANES)
        into = pl.ds(pl.multiple_of(pc.c * rows_own + b * LANES, LANES), LANES)
        h2[into, :] = layer_norm(mid[rows, :], vec[5:6, :], vec[6:7, :]).astype(BF16)

    both = exchange(6, h2.at[mine], h2.at[mine])
    save(9, mid, mid_o)
    u_ring.along(2)
    for s in range(3, pc.length):
        u_fc.across(s)
    for s in range(pc.length):
        u_proj.ring(s)
    both.wait()
    save(10, h2, h2_o)
    u_fc.finish()
    save(11, w_fc, w_fc_o)

    def feed(b):
        cols = pl.ds(pl.multiple_of(b * tile, tile), tile)

        @pl.loop(0, total // 512)
        def _(m):
            rows = pl.ds(pl.multiple_of(m * 512, 512), 512)
            value = matmul(h2[rows, :], whole(w_fc, cols)) + fcb[:, cols]
            value, slope = gelu_pair(value)
            hid[rows, cols] = value.astype(BF16)
            gslope[rows, cols] = slope.astype(BF16)

    blocks = hid.shape[1] // tile
    pl.loop(0, blocks // 4)(feed)
    for s in range(3, pc.length):
        u_ring.along(s)
    u_proj.across(0)
    pl.loop(blocks // 4, blocks // 2)(feed)
    u_proj.across(1)
    pl.loop(blocks // 2, blocks)(feed)
    for s in range(2, pc.length):
        u_proj.across(s)
    save(12, hid, hid_o)
    save(13, gslope, slope_o)
    for copy in later:
        copy.wait()
    save(14, dy, dy_o)
    save(15, key_aug, key_o)
    slots = tile // piece

    @pl.loop(0, blocks)
    def _(b):
        cols = pl.ds(pl.multiple_of(b * tile, tile), tile)
        for n in range(width // 512):
            value = matmul_tn(hid[:, cols], dy[:, n * 512 : (n + 1) * 512]).astype(BF16)
            gp[pl.ds(b * slots, slots), :, n * 512 : (n + 1) * 512] = value.reshape(slots, piece, 512)

    save(16, gp, gp_o)
    u_proj.finish()
    save(1, w_proj, w_proj_o)
    for copy in saves:
        copy.wait()
    for unit in (u_small, u_qkv, u_out, u_fc, u_proj, u_ring):
        unit.drain()


def forward(n_dp, n_blk, scale, qkv, out, fc, proj, tokens, out_grad, positions, row_ids, slopes, fc_bias, vectors):
    rows_own, width = tokens.shape
    total = n_blk * rows_own
    wide = width // n_blk
    pairs = wide // LANES
    piece = proj.shape[0] // n_blk
    ff = n_dp * piece
    shard, length = qkv.shape[0], n_dp // PLANE
    weights = [(shard, 3 * wide), (shard, width), (shard, ff), (piece, width)]
    outs = [((n_dp,) + w, BF16) for w in weights] + [
        ((16, width), F32),
        ((total, width), BF16),
        ((total, 3 * wide), BF16),
        ((total, wide), BF16),
        ((rows_own, width), BF16),
        ((pairs, 2, total, LANES), BF16),
        ((rows_own, width), F32),
        ((total, width), BF16),
        ((total, ff), BF16),
        ((total, ff), BF16),
        ((total, width), BF16),
        ((total, LANES), BF16),
        ((n_dp, piece, width), BF16),
    ]
    scratch = outs + [
        ((n_dp, 16, LANES), BF16),
        ((1, ff), F32),
        ((total, width), BF16),
        ((total, LANES), BF16),
        ((shard, 3 * wide), F32),
        ((shard, wide), F32),
        ((shard, ff), F32),
        ((piece, width), F32),
    ]
    hbm = pl.BlockSpec(memory_space=pl.ANY)
    vmem = pl.BlockSpec(memory_space=pltpu.VMEM)
    smem = pl.BlockSpec(memory_space=pltpu.SMEM)
    grid = (rows_own // LANES, LANES)
    small = [a.reshape(1, -1) for a in (fc_bias, *vectors)]
    return pl.pallas_call(
        functools.partial(forward_kernel, n_dp, n_blk, scale),
        out_shape=[jax.ShapeDtypeStruct(*o) for o in outs],
        in_specs=[hbm] * 6 + [vmem] * 2 + [smem] + [vmem] * len(small),
        out_specs=[hbm] * len(outs),
        scratch_shapes=[pltpu.VMEM(*s) for s in scratch]
        + [
            pltpu.SemaphoreType.DMA((7, 5, length)),
            pltpu.SemaphoreType.DMA((7, n_dp)),
            pltpu.SemaphoreType.DMA((2, 7)),
            pltpu.SemaphoreType.DMA((8 + n_dp,)),
            pltpu.SemaphoreType.DMA((17,)),
        ],
        compiler_params=pltpu.CompilerParams(
            collective_id=2, has_side_effects=True, vmem_limit_bytes=VMEM_BYTES
        ),
    )(qkv, out, fc, proj, tokens, out_grad, positions.reshape(grid), row_ids.reshape(grid), slopes, *small)


def normed_rows(rows):
    centred = rows - jnp.mean(rows, axis=-1, keepdims=True)
    inverse = lax.rsqrt(jnp.mean(centred * centred, axis=-1, keepdims=True) + EPSILON)
    return centred * inverse, inverse


def norm_back(rows, gain_vec, grad):
    unit, inverse = normed_rows(rows)
    m = grad * gain_vec
    shift = jnp.mean(m, axis=-1, keepdims=True)
    stretch = jnp.mean(m * unit, axis=-1, keepdims=True)
    return (m - shift - unit * stretch) * inverse, grad * unit


def column_sum(value):
    return jnp.sum(value, axis=0, keepdims=True)


def backward_kernel(n_dp, n_blk, scale, *refs):
    (w_qkv_h, w_out_h, w_fc_h, w_proj_h, vec, h1_h, mixed_h, heads_h, att_h, qx_h, mid_h, h2_h, hid_h, slope_h, dy_h, key_h, gp_h, tokens_h) = refs[:18]
    (layer_o, input_o, proj_o, fc_o, qkv_o, out_o, small_o) = refs[18:25]
    (P2, S, Y, F, H, A, M, T, O, Q, E, K, GP, side0, side1, R1, R2, R3, DH, SB, PF, acc_k, acc_v, VG, fcg, SG, small_in) = refs[25:52]
    bufs, rest = refs[52:72], refs[72:]
    ring_bufs, rest = rest[:3], rest[3:]
    totals, rest = rest[:6], rest[6:]
    send, recv, xsem, load, last = rest
    pc = Place(n_dp, n_blk)
    sib = pc.sibling(1)
    rows_own, width = tokens_h.shape
    total = n_blk * rows_own
    wide = width // n_blk
    ff = A.shape[1]
    shard = width // n_dp
    piece = ff // n_dp
    tile = 256
    mine = pl.ds(pl.multiple_of(pc.c * rows_own, rows_own), rows_own)
    theirs = pl.ds(pl.multiple_of(sib[1] * rows_own, rows_own), rows_own)
    my_cols = pl.ds(pl.multiple_of(pc.c * wide, LANES), wide)
    their_cols = pl.ds(pl.multiple_of(sib[1] * wide, LANES), wide)

    def fetch(i, src, dst):
        copy = pltpu.make_async_copy(src, dst, load.at[i])
        copy.start()
        return copy

    def exchange(i, src, dst):
        copy = remote(src, dst, xsem.at[0, i], xsem.at[1, i], sib)
        copy.start()
        return copy

    def span(i, size=tile):
        return pl.ds(pl.multiple_of(i * size, size), size)

    get_gp = fetch(0, gp_h, GP)
    get_proj = fetch(2, w_proj_h, P2)
    get_dy = fetch(3, dy_h, Y)
    get_slope = fetch(4, slope_h, S)
    get_h2 = fetch(5, h2_h, H)
    get_mid = fetch(6, mid_h, M)
    get_fc = fetch(7, w_fc_h, F)
    get_att = fetch(8, att_h, T)
    get_out = fetch(9, w_out_h, O)
    get_qx = fetch(10, qx_h, Q)
    get_heads = fetch(11, heads_h, E)
    get_key = fetch(12, key_h, K)
    pc.greet()
    cut = piece // 2
    chunks = [
        lambda slot: GP.at[pl.ds(pl.multiple_of(slot * piece + cut, cut), cut)],
        lambda slot: A.at[span(slot, shard)],
        lambda slot: F.at[span(slot, shard), 0 : 3 * wide],
        lambda slot: side0.at[span(slot, shard)],
        lambda slot: SG.at[slot],
    ]
    u_proj, u_fc, u_qkv, u_out, u_small = [
        Scatter(pc, i, chunks[i], bufs[4 * i : 4 * i + 4], send, recv) for i in range(5)
    ]
    u_line = LineScatter(
        pc, 5, lambda slot: GP.at[pl.ds(pl.multiple_of(slot * piece, cut), cut)], ring_bufs, send, recv
    )
    length = pc.length
    far_first = range(length - 1, -1, -1)
    pending = []

    def give(i, src, dst):
        keep = pltpu.make_async_copy(src, dst, last.at[0, i])
        copy = remote(src, dst, last.at[1, i], last.at[2, i], sib)
        keep.start()
        copy.start()
        return keep, copy

    VG[...] = jnp.zeros_like(VG)
    get_gp.wait()
    u_line.along(length - 1)
    u_proj.start()
    get_proj.wait()
    get_dy.wait()
    get_slope.wait()

    def hidden_grads(b):
        cols = span(b)
        sums = None
        for m in range(total // 512):
            rows = pl.ds(m * 512, 512)
            value = S[rows, cols].astype(F32) * matmul_nt(Y[rows, :], P2[cols, :])
            value = value.astype(BF16)
            S[rows, cols] = value
            part = column_sum(value.astype(F32))
            sums = part if sums is None else sums + part
        fcg[:, cols] = sums

    blocks = ff // tile
    pl.loop(0, blocks // 2)(hidden_grads)
    for s in far_first[:2]:
        u_proj.middle(s)
    pl.loop(blocks // 2, blocks)(hidden_grads)
    for s in far_first[2:]:
        u_proj.middle(s)
    get_h2.wait()

    @pl.loop(0, width // tile)
    def _(b):
        for n in range(ff // 1024):
            cols = pl.ds(n * 1024, 1024)
            A[span(b), cols] = matmul_tn(H[:, span(b)], S[:, cols]).astype(BF16)

    u_fc.start()
    u_line.along(length - 2)
    get_qkv = [
        fetch(13, w_qkv_h.at[:, 0 : 2 * wide], P2.at[0:width]),
        fetch(14, w_qkv_h.at[:, 2 * wide :], P2.at[width : 2 * width, 0:wide]),
    ]
    get_mid.wait()
    get_fc.wait()

    @pl.loop(0, width // tile)
    def _(b):
        SB[:, span(b)] = matmul_nt(S[theirs, :], F[span(b), :]).astype(BF16)

    swap_two = exchange(1, SB, R2)
    for s in far_first[:2]:
        u_proj.settle(s)
        u_proj.along(s)

    @pl.loop(0, width // tile)
    def _(b):
        PF[:, span(b)] = matmul_nt(S[mine, :], F[span(b), :])

    for s in far_first[2:]:
        u_proj.settle(s)
    swap_two.wait()
    get_h1 = fetch(16, h1_h, S.at[:, 0:width])
    get_kv = fetch(17, mixed_h.at[:, wide:], S.at[:, width : 2 * width])

    @pl.loop(0, rows_own // LANES)
    def _(b):
        rows = span(b, LANES)
        from_mine = pl.ds(pl.multiple_of(pc.c * rows_own + b * LANES, LANES), LANES)
        into = pl.ds(pl.multiple_of(sib[1] * rows_own + b * LANES, LANES), LANES)
        grad = PF[rows, :] + R2[rows, :].astype(F32)
        top = Y[from_mine, :].astype(F32)
        back, terms = norm_back(M[rows, :], vec[5:6, :], grad)
        value = top + back
        M[rows, :] = value
        branch = value.astype(BF16)
        Y[into, :] = branch
        VG[4:5, :] += column_sum(branch.astype(F32))
        VG[5:6, :] += column_sum(terms)
        VG[6:7, :] += column_sum(grad)
        VG[7:8, :] += column_sum(top)

    get_out.wait()

    @pl.loop(0, width // tile)
    def _(b):
        Y[mine, span(b)] = matmul_nt(Y[theirs, :], O[span(b), :]).astype(BF16)

    swap_heads = exchange(2, Y.at[mine, their_cols], DH.at[mine])
    stay_heads = fetch(18, Y.at[mine, my_cols], DH.at[mine])
    for s in range(length - 3, 0, -1):
        u_line.along(s)
    get_att.wait()

    @pl.loop(0, width // tile)
    def _(b):
        O[span(b), :] = matmul_tn(T[:, span(b)], Y[theirs, :]).astype(BF16)

    swap_side = exchange(3, O.at[:, their_cols], side1)
    get_tokens = fetch(19, tokens_h, T)
    get_qx.wait()
    get_heads.wait()
    get_key.wait()
    get_kv.wait()
    stay_heads.wait()
    swap_heads.wait()
    pairs = wide // LANES
    for j in range(pairs):
        cols = pl.ds(j * LANES, LANES)
        attend_back_kernel(
            tile,
            scale,
            Q.at[pl.ds(j, 1)],
            S.at[:, pl.ds(width + j * LANES, LANES)],
            S.at[:, pl.ds(width + wide + j * LANES, LANES)],
            K,
            E.at[:, cols],
            DH.at[:, cols],
            H.at[:, cols],
            H.at[:, pl.ds(wide + j * LANES, LANES)],
            P2.at[width : 2 * width, pl.ds(wide + j * LANES, LANES)],
            acc_k,
            acc_v,
        )
        if j == 0:
            for s in range(length - 3, 0, -1):
                u_proj.along(s)
            swap_side.wait()

            @pl.loop(0, n_dp)
            def _(slot):
                rows = span(slot, shard)
                value = O[rows, my_cols].astype(F32) + side1[rows, :].astype(F32)
                side0[rows, :] = value.astype(BF16)

            u_out.start()
            for s in far_first[:2]:
                u_fc.middle(s)
            u_line.settle()
        if j == 1:
            for s in far_first[2:]:
                u_fc.middle(s)
            u_line.turn()
            u_proj.finish(totals[0])
            at = pl.multiple_of(pc.c * piece + cut, cut)
            pending += give(0, totals[0], proj_o.at[pl.ds(at, cut)])
        if j == 2:
            for s in far_first[:1]:
                u_fc.settle(s)
                u_fc.along(s)
    get_h1.wait()

    @pl.loop(0, width // tile)
    def _(b):
        F[span(b), 0 : 2 * wide] = matmul_tn(S[:, span(b)], H[...]).astype(BF16)
        value = matmul_tn(S[:, span(b)], P2[width : 2 * width, wide : 2 * wide])
        F[span(b), 2 * wide : 3 * wide] = value.astype(BF16)

    u_qkv.start()
    VG[2:3, my_cols] = column_sum(H[:, 0:wide].astype(F32))
    VG[3:4, my_cols] = column_sum(P2[width : 2 * width, wide : 2 * wide].astype(F32))
    get_hid = fetch(1, hid_h, S)
    for s in far_first[1:3]:
        u_fc.settle(s)
        u_fc.along(s)
    for copy in get_qkv:
        copy.wait()

    def input_part(first, b):
        rows = pl.ds(pl.multiple_of(first, rows_own), rows_own)
        below = pl.ds(pl.multiple_of(width + first, rows_own), rows_own)
        after = pl.ds(pl.multiple_of(width + b * tile, tile), tile)
        part = matmul_nt(P2[below, wide : 2 * wide], P2[after, 0:wide])
        return part + matmul_nt(H[rows, :], P2[span(b), :])

    @pl.loop(0, width // tile)
    def _(b):
        SB[:, span(b)] = input_part(sib[1] * rows_own, b).astype(BF16)

    swap_one = exchange(4, SB, R3)
    for s in far_first[3:]:
        u_fc.settle(s)
        if s:
            u_fc.along(s)
    for s in far_first:
        u_out.middle(s)

    @pl.loop(0, width // tile)
    def _(b):
        PF[:, span(b)] = input_part(pc.c * rows_own, b)

    get_tokens.wait()
    swap_one.wait()

    @pl.loop(0, rows_own // LANES)
    def _(b):
        rows = span(b, LANES)
        grad = PF[rows, :] + R3[rows, :].astype(F32)
        back, terms = norm_back(T[rows, :].astype(F32), vec[0:1, :], grad)
        M[rows, :] += back
        VG[0:1, :] += column_sum(terms)
        VG[1:2, :] += column_sum(grad)

    get_mid_again = fetch(21, mid_h, PF)
    put_input = pltpu.make_async_copy(M, input_o, load.at[20])
    put_input.start()
    per = n_dp // (width // LANES)
    for slot in range(n_dp):
        t = slot // per
        SG[slot, 0:8, :] = VG[0:8, t * LANES : (t + 1) * LANES]
        SG[slot, 8:16, :] = jnp.broadcast_to(fcg[:, slot * LANES : (slot + 1) * LANES], (8, LANES))
    u_small.start()
    u_line.finish(totals[5])
    pending += give(5 + n_dp, totals[5], proj_o.at[pl.ds(pl.multiple_of(pc.c * piece, cut), cut)])
    u_proj.drain()
    u_line.drain()
    get_proj = fetch(2, w_proj_h, GP)
    for s in far_first[:2]:
        u_qkv.middle(s)
    for s in far_first:
        u_small.middle(s)
    u_fc.finish(totals[1])

    @pl.loop(0, n_dp)
    def _(j):
        dst = fc_o.at[:, pl.ds(pl.multiple_of((j * n_blk + pc.c) * piece, piece), piece)]
        give(1 + j, totals[1].at[:, span(j, piece)], dst)

    get_hid.wait()
    get_proj.wait()

    def layer_part(rows, b):
        return matmul(S[rows, :], GP[:, span(b)])

    @pl.loop(0, width // tile)
    def _(b):
        SB[:, span(b)] = layer_part(theirs, b).astype(BF16)

    swap_out = exchange(0, SB, R1)
    for s in far_first[2:]:
        u_qkv.middle(s)
    for s in far_first:
        u_small.settle(s)
        if s:
            u_small.along(s)

    get_mid_again.wait()

    @pl.loop(0, width // tile)
    def _(b):
        PF[:, span(b)] += layer_part(mine, b)

    u_small.finish(totals[4])
    swap_small = exchange(5, totals[4], small_in)
    for s in far_first:
        u_out.settle(s)
        if s:
            u_out.along(s)
    swap_out.wait()

    @pl.loop(0, rows_own // LANES)
    def _(b):
        rows = span(b, LANES)
        value = PF[rows, :] + R1[rows, :].astype(F32) + vec[7:8, :]
        R1[rows, :] = value.astype(BF16)

    put_layer = pltpu.make_async_copy(R1, layer_o, load.at[15])
    put_layer.start()
    u_out.finish(totals[3])
    pending += give(4 + n_dp, totals[3], out_o.at[:, my_cols])
    for s in far_first:
        u_qkv.settle(s)
        if s:
            u_qkv.along(s)
    u_qkv.finish(totals[2])
    for j in range(3):
        at = pl.ds(pl.multiple_of(pc.c * wide, LANES) + j * width, wide)
        pending += give(1 + n_dp + j, totals[2].at[:, j * wide : (j + 1) * wide], qkv_o.at[:, at])
    swap_small.wait()
    low = jnp.where(pc.c == 0, totals[4][...], small_in[...])
    high = jnp.where(pc.c == 0, small_in[...], totals[4][...])
    small_o[0:8, :] = low[0:8] + high[0:8]
    small_o[8:16, :] = low[8:16]
    small_o[16:24, :] = high[8:16]

    @pl.loop(0, n_dp)
    def _(j):
        dst = fc_o.at[:, pl.ds(pl.multiple_of((j * n_blk + pc.c) * piece, piece), piece)]
        src = totals[1].at[:, span(j, piece)]
        pltpu.make_async_copy(src, dst, last.at[0, 1 + j]).wait()
        remote(src, dst, last.at[1, 1 + j], last.at[2, 1 + j], sib).wait()

    for copy in pending:
        copy.wait()
    put_layer.wait()
    put_input.wait()
    for unit in (u_fc, u_qkv, u_out, u_small):
        unit.drain()


def backward(n_dp, n_blk, scale, saved, tokens):
    rows_own, width = tokens.shape
    total = n_blk * rows_own
    wide = width // n_blk
    w_proj = saved[3]
    ff = w_proj.shape[0]
    piece, shard, length = ff // n_dp, width // n_dp, n_dp // PLANE
    square, long, own = ((total, width), BF16), ((total, ff), BF16), ((rows_own, width), BF16)
    own_f32 = ((rows_own, width), F32)
    sizes = [
        ((piece // 2, width), BF16),
        ((shard, ff), BF16),
        ((shard, 3 * wide), BF16),
        ((shard, wide), BF16),
        ((16, LANES), F32),
    ]
    scratch = [((ff, width), BF16), long, square, long, square, long, own_f32, own]
    scratch += [((width, width), BF16), (saved[9].shape, BF16), ((total, wide), BF16)]
    scratch += [((total, LANES), BF16), ((ff, width), BF16)]
    scratch += [((width, wide), BF16)] * 2 + [own] * 3 + [((total, wide), BF16), own, own_f32]
    scratch += [((total, LANES), F32)] * 2 + [((8, width), F32), ((1, ff), F32)]
    scratch += [((n_dp, 16, LANES), F32), ((16, LANES), F32)]
    for size, kind in sizes:
        scratch += [((length,) + size, kind)] * 3 + [((length + 1,) + size, kind)]
    half, quarter = (piece // 2, width), (piece // 4, width)
    scratch += [((PLANE, length + 1) + half, BF16), ((2,) + quarter, BF16), ((2,) + half, BF16)]
    scratch += [(size, F32) for size, _ in sizes] + [(half, F32)]
    outs = [own, own_f32, ((n_blk * piece, width), F32), ((shard, n_blk * ff), F32)]
    outs += [((shard, 3 * width), F32), ((shard, width), F32), ((24, LANES), F32)]
    hbm = pl.BlockSpec(memory_space=pl.ANY)
    vmem = pl.BlockSpec(memory_space=pltpu.VMEM)
    return pl.pallas_call(
        functools.partial(backward_kernel, n_dp, n_blk, scale),
        out_shape=[jax.ShapeDtypeStruct(*o) for o in outs],
        in_specs=[vmem if i == 4 else hbm for i in range(18)],
        out_specs=[hbm] * 6 + [vmem],
        scratch_shapes=[pltpu.VMEM(*s) for s in scratch]
        + [
            pltpu.SemaphoreType.DMA((7, 5, length)),
            pltpu.SemaphoreType.DMA((7, 5, length)),
            pltpu.SemaphoreType.DMA((2, 6)),
            pltpu.SemaphoreType.DMA((22,)),
            pltpu.SemaphoreType.DMA((3, 6 + n_dp)),
        ],
        compiler_params=pltpu.CompilerParams(
            collective_id=3, has_side_effects=True, vmem_limit_bytes=VMEM_BACK
        ),
    )(*saved, tokens)


def columns_spec(rows, first):
    return pl.BlockSpec((rows, LANES), lambda j: (0, first + j))


def attend_step(block, scale, q_ref, k_ref, v_ref, key_aug, query_aug, slopes, out_ref, qx_ref):
    j = pl.program_id(0)
    pair = [slopes[2 * j + hh] for hh in range(2)]
    attend_kernel(block, scale, q_ref, k_ref, v_ref, key_aug, query_aug, pair, out_ref, qx_ref)


def attend(qkv, key_aug, query_aug, slopes, scale):
    total, wide = qkv.shape[0], qkv.shape[1] // 3
    pairs = wide // LANES
    block = math.gcd(total, 256)
    whole = pl.BlockSpec((total, LANES), lambda j: (0, 0))
    return pl.pallas_call(
        functools.partial(attend_step, block, scale),
        grid=(pairs,),
        out_shape=[
            jax.ShapeDtypeStruct((total, wide), BF16),
            jax.ShapeDtypeStruct((pairs, 2, total, LANES), BF16),
        ],
        in_specs=[
            columns_spec(total, 0),
            columns_spec(total, pairs),
            columns_spec(total, 2 * pairs),
            whole,
            whole,
            pl.BlockSpec(memory_space=pltpu.SMEM),
        ],
        out_specs=[
            columns_spec(total, 0),
            pl.BlockSpec((1, 2, total, LANES), lambda j: (j, 0, 0, 0)),
        ],
        compiler_params=pltpu.CompilerParams(vmem_limit_bytes=VMEM_BYTES),
    )(qkv, qkv, qkv, key_aug, query_aug, slopes)


def attend_back(query_ext, qkv, key_aug, attended, grad, scale):
    total, wide = attended.shape
    pairs = wide // LANES
    block = math.gcd(total, 256)
    whole = pl.BlockSpec((total, LANES), lambda j: (0, 0))
    out = jax.ShapeDtypeStruct((total, wide), BF16)
    return pl.pallas_call(
        functools.partial(attend_back_kernel, block, scale),
        grid=(pairs,),
        out_shape=[out] * 3,
        in_specs=[
            pl.BlockSpec((1, 2, total, LANES), lambda j: (j, 0, 0, 0)),
            columns_spec(total, pairs),
            columns_spec(total, 2 * pairs),
            whole,
            columns_spec(total, 0),
            columns_spec(total, 0),
        ],
        out_specs=[columns_spec(total, 0)] * 3,
        scratch_shapes=[pltpu.VMEM((total, LANES), F32)] * 2,
        compiler_params=pltpu.CompilerParams(vmem_limit_bytes=VMEM_BYTES),
    )(query_ext, qkv, qkv, key_aug, attended, grad)


def attention_terms(positions, rows):
    high = (positions // 256) * 256
    low = positions - high
    first = rows == 0
    one = jnp.ones_like(positions)
    zero = jnp.zeros_like(positions)

    def table(columns):
        cols = jnp.stack([col.astype(F32) for col in columns], axis=1)
        cols = jnp.pad(cols, ((0, 0), (0, LANES // 2 - len(columns))))
        return jnp.concatenate([cols, cols], axis=1).astype(BF16)

    key_aug = table([high, high, high, low, low, low, first, ~first, one, one, one])
    other = jnp.where(first, 0.0, MASKED)
    query_aug = table([zero] * 6 + [other, jnp.where(first, MASKED, 0.0)])
    return key_aug, query_aug


def body(
    n_dp,
    n_blk,
    tokens,
    positions,
    row_ids,
    alibi_slope,
    ln1_gain,
    ln1_bias,
    qkv_weight,
    query_bias,
    value_bias,
    out_weight,
    out_bias,
    ln2_gain,
    ln2_bias,
    fc_weight,
    fc_bias,
    proj_weight,
    proj_bias,
    out_grad,
):
    local, width = tokens.shape
    heads = alibi_slope.shape[0]
    hidden_all = fc_weight.shape[1]
    scale = 1.0 / math.sqrt(width // heads)
    c = lax.axis_index("blk")
    dp = lax.axis_index("dp")
    wide = width // n_blk
    shard = width // n_dp
    piece = hidden_all // (n_dp * n_blk)
    total = n_blk * local

    def swap(a):
        return lax.ppermute(a, "blk", [(0, 1), (1, 0)])

    def blk_gather(a):
        if n_blk != 2:
            return lax.all_gather(a, "blk", axis=0, tiled=True)
        other = swap(a)
        return jnp.where(
            c == 0, jnp.concatenate([a, other], 0), jnp.concatenate([other, a], 0)
        )

    def blk_sum(a):
        if n_blk != 2:
            return lax.psum_scatter(a.astype(BF16), "blk", scatter_dimension=0, tiled=True).astype(F32)
        own = lax.dynamic_slice_in_dim(a, c * local, local, 0)
        other = lax.dynamic_slice_in_dim(a, (1 - c) * local, local, 0)
        return own + swap(other.astype(BF16)).astype(F32)

    def to_tokens(a):
        if n_blk != 2:
            moved = lax.all_to_all(a.reshape(n_blk, local, wide), "blk", 0, 0)
            return jnp.transpose(moved, (1, 0, 2)).reshape(local, width)
        own = lax.dynamic_slice_in_dim(a, c * local, local, 0)
        other = swap(lax.dynamic_slice_in_dim(a, (1 - c) * local, local, 0))
        return jnp.where(
            c == 0, jnp.concatenate([own, other], 1), jnp.concatenate([other, own], 1)
        )

    def to_heads(a):
        if n_blk != 2:
            moved = lax.all_to_all(
                jnp.transpose(a.reshape(local, n_blk, wide), (1, 0, 2)), "blk", 0, 0
            )
            return moved.reshape(total, wide)
        own = lax.dynamic_slice_in_dim(a, c * wide, wide, 1)
        other = swap(lax.dynamic_slice_in_dim(a, (1 - c) * wide, wide, 1))
        return jnp.where(
            c == 0, jnp.concatenate([own, other], 0), jnp.concatenate([other, own], 0)
        )

    def mine(a, axis, size):
        return lax.dynamic_slice_in_dim(a, c * size, size, axis)

    vectors = [ln1_gain, ln1_bias, query_bias, value_bias, out_bias, ln2_gain, ln2_bias, proj_bias]
    if n_blk == 2 and piece == LANES:
        weights = (qkv_weight, out_weight, fc_weight, proj_weight)
        saved = forward(
            n_dp, n_blk, scale, *weights, tokens, out_grad, positions, row_ids, alibi_slope, fc_bias, vectors
        )
        saved = [a if i == 9 else a.reshape(-1, a.shape[-1]) for i, a in enumerate(saved)]
        outs = backward(n_dp, n_blk, scale, saved, tokens)
        layer_output, input_grad, proj_sum, fc_sum, qkv_sum, out_sum, smalls = outs
        at = lax.rem(dp * shard, LANES)
        part = lax.dynamic_slice_in_dim(smalls[0:8], at, shard, 1)
        g_fc = smalls[8:24:8].reshape(n_blk * piece)
        return (
            layer_output,
            input_grad,
            part[0],
            part[1],
            qkv_sum,
            part[2],
            part[3],
            out_sum,
            part[4],
            part[5],
            part[6],
            fc_sum,
            g_fc,
            proj_sum,
            part[7],
        )

    qkv_own = jnp.concatenate(
        [mine(qkv_weight[:, i * width : (i + 1) * width], 1, wide) for i in range(3)], 1
    ).astype(BF16)
    out_own = mine(out_weight, 1, wide).astype(BF16)
    fc_own = mine(fc_weight.reshape(shard, n_dp, n_blk, piece), 2, 1).reshape(shard, n_dp * piece)
    proj_own = mine(proj_weight, 0, piece)
    vectors.append(mine(fc_bias, 0, piece))
    small = jnp.stack(
        [
            lax.dynamic_update_slice_in_dim(
                jnp.zeros((LANES,), F32), vec, lax.rem(dp * vec.shape[0], LANES), 0
            )
            for vec in vectors
        ]
    )
    small = jnp.pad(small, ((0, 16 - len(vectors)), (0, 0))).astype(BF16)
    inputs = tokens.astype(F32)
    grad_top = out_grad.astype(F32)
    shards = (qkv_own, out_own, fc_own.astype(BF16), proj_own.astype(BF16), small)
    full_qkv, full_out, full_fc, full_proj, full_small = gather_weights(
        n_dp, n_blk, *shards
    )
    weight_qkv = full_qkv.reshape(width, 3 * wide)
    weight_out = full_out.reshape(width, width)
    weight_fc = full_fc.reshape(width, n_dp * piece)
    weight_proj = full_proj.reshape(n_dp * piece, width)
    spread = full_small.astype(F32)

    def vector(i):
        size = vectors[i].shape[0]
        per = LANES // size
        rows = jnp.sum(spread[:, i].reshape(n_dp // per, per, LANES), axis=1)
        return rows.reshape(n_dp * size)

    gain_one, bias_one, bias_query, bias_value, bias_out, gain_two, bias_two, bias_proj, bias_fc = (
        vector(i) for i in range(len(vectors))
    )
    place = blk_gather(jnp.stack([positions, row_ids], axis=1))
    key_aug, query_aug = attention_terms(place[:, 0], place[:, 1])
    every_token = blk_gather(tokens).astype(F32)
    every_grad = blk_gather(out_grad)
    normed = layer_norm(every_token, gain_one, bias_one).astype(BF16)
    bias_qkv = jnp.concatenate(
        [mine(bias_query, 0, wide), jnp.zeros((wide,), F32), mine(bias_value, 0, wide)]
    )
    mixed = (matmul(normed, weight_qkv) + bias_qkv).astype(BF16)
    slopes = mine(alibi_slope, 0, heads // n_blk)
    attended_heads, query_ext = attend(mixed, key_aug, query_aug, slopes, scale)
    attended = to_tokens(attended_heads)
    middle = inputs + matmul(attended, weight_out) + bias_out
    normed_two = layer_norm(middle, gain_two, bias_two).astype(BF16)
    every_two = blk_gather(normed_two)
    hidden_pre = matmul(every_two, weight_fc) + bias_fc
    hidden_vals, gelu_slope = gelu_pair(hidden_pre)
    hidden = hidden_vals.astype(BF16)
    grad_proj_weight = matmul_tn(hidden, every_grad).astype(BF16)
    layer_output = (middle + blk_sum(matmul(hidden, weight_proj)) + bias_proj).astype(BF16)
    grad_proj_bias = jnp.sum(grad_top, axis=0)
    grad_pre = (gelu_slope * matmul_nt(every_grad, weight_proj)).astype(BF16)
    grad_fc_weight = matmul_tn(every_two, grad_pre).astype(BF16)
    grad_fc_bias = jnp.sum(grad_pre.astype(F32), axis=0)
    grad_normed_two = blk_sum(matmul_nt(grad_pre, weight_fc))
    _, norm_two_back = jax.vjp(layer_norm, middle, gain_two, bias_two)
    grad_mid_norm, grad_gain_two, grad_bias_two = norm_two_back(grad_normed_two)
    grad_middle = grad_top + grad_mid_norm
    grad_branch = grad_middle.astype(BF16)
    grad_out_weight = matmul_tn(attended, grad_branch).astype(BF16)
    grad_out_bias = jnp.sum(grad_branch.astype(F32), axis=0)
    grad_heads = to_heads(matmul_nt(grad_branch, weight_out).astype(BF16))
    grad_mixed = jnp.concatenate(
        attend_back(query_ext, mixed, key_aug, attended_heads, grad_heads, scale), axis=1
    )
    grad_qkv_weight = matmul_tn(normed, grad_mixed).astype(BF16)
    sums = jnp.sum(grad_mixed.astype(F32), axis=0)
    grad_normed = blk_sum(matmul_nt(grad_mixed, weight_qkv))
    _, norm_one_back = jax.vjp(layer_norm, inputs, gain_one, bias_one)
    grad_in_norm, grad_gain_one, grad_bias_one = norm_one_back(grad_normed)
    input_grad = grad_middle + grad_in_norm

    proj_sum, fc_sum, out_sum, qkv_sum = scatter_grads(
        n_dp,
        n_blk,
        grad_proj_weight.reshape(n_dp, piece, width),
        grad_fc_weight.reshape(n_dp, shard, n_dp * piece),
        grad_out_weight.reshape(n_dp, shard, width),
        grad_qkv_weight.reshape(n_dp, shard, 3 * wide),
    )

    def spread_out(vec, size):
        parts = vec.reshape(-1, 1, size)
        return jnp.where((jnp.arange(n_blk) == c)[None, :, None], parts, 0.0).reshape(-1)

    small_grads = [
        grad_gain_one,
        grad_bias_one,
        spread_out(sums[:wide], wide),
        spread_out(sums[2 * wide :], wide),
        grad_out_bias,
        grad_gain_two,
        grad_bias_two,
        grad_proj_bias,
        spread_out(grad_fc_bias, piece),
    ]
    small_sum = lax.psum(jnp.concatenate(small_grads), ("dp", "blk"))
    finals = []
    at = 0
    for vec in small_grads:
        size = vec.shape[0]
        finals.append(lax.dynamic_slice_in_dim(small_sum, at + dp * (size // n_dp), size // n_dp, 0))
        at += size
    g_gain1, g_bias1, g_query, g_value, g_out, g_gain2, g_bias2, g_proj, g_fc = finals
    final_qkv = jnp.transpose(qkv_sum.reshape(n_blk, shard, 3, wide), (1, 2, 0, 3))
    final_fc = jnp.transpose(fc_sum.reshape(n_blk, shard, n_dp, piece), (1, 2, 0, 3))
    return (
        layer_output,
        input_grad,
        g_gain1,
        g_bias1,
        final_qkv.reshape(shard, 3 * width),
        g_query,
        g_value,
        jnp.transpose(out_sum, (1, 0, 2)).reshape(shard, width),
        g_out,
        g_gain2,
        g_bias2,
        final_fc.reshape(shard, hidden_all),
        g_fc,
        proj_sum.reshape(n_blk * piece, width),
        g_proj,
    )


def solution(mesh):
    both, rows, one = P(("dp", "blk"), None), P("dp", None), P("dp")
    tokens = P(("dp", "blk"))
    in_specs = (both, tokens, tokens, P(), one, one, rows, one, one, rows, one, one, one, rows, one, rows, one, both)
    out_specs = (both, both, one, one, rows, one, one, rows, one, one, one, rows, one, rows, one)
    return jax.shard_map(
        functools.partial(body, mesh.shape["dp"], mesh.shape["blk"]),
        mesh=mesh,
        in_specs=in_specs,
        out_specs=out_specs,
        check_vma=False,
    )
```

```python
import functools
import math

import jax
import jax.numpy as jnp
from jax import lax
from jax.experimental import pallas as pl
from jax.experimental.pallas import tpu as pltpu
from jax.sharding import PartitionSpec as P

EPSILON = 1e-05
MASKED = -1e30
BF16 = jnp.bfloat16
F32 = jnp.float32
MESH = pl.DeviceIdType.MESH
PLANE = 4
LANES = 128
VMEM_BYTES = 58 * 2**20
VMEM_BACK = 63 * 2**20


def matmul(left, right):
    return jnp.dot(left, right, preferred_element_type=F32)


def matmul_tn(left, right):
    return lax.dot_general(left, right, (((0,), (0,)), ((), ())), preferred_element_type=F32)


def matmul_nt(left, right):
    return lax.dot_general(left, right, (((1,), (1,)), ((), ())), preferred_element_type=F32)


def layer_norm(inputs, gain_vec, bias_vec):
    row_mean = jnp.mean(inputs, axis=-1, keepdims=True)
    centred = inputs - row_mean
    spread = jnp.mean(centred * centred, axis=-1, keepdims=True)
    return centred * lax.rsqrt(spread + EPSILON) * gain_vec + bias_vec


class Place:
    def __init__(self, n_dp, n_blk):
        self.n_dp, self.n_blk, self.length = n_dp, n_blk, n_dp // PLANE
        self.dp, self.c = lax.axis_index("dp"), lax.axis_index("blk")
        self.z, self.p = self.dp // PLANE, lax.rem(self.dp, PLANE)
        side, row = lax.rem(self.p, 2), self.p // 2
        self.flip_x, self.flip_y = self.p + 1 - 2 * side, self.p + 2 - 4 * row
        self.diag = PLANE - 1 - self.p

    def routes(self, zz):
        odd = lax.rem(zz, 2)
        return (
            self.flip_x * (1 - odd) + self.flip_y * odd,
            self.flip_x * odd + self.flip_y * (1 - odd),
        )

    def at(self, zz, pp):
        return (zz * PLANE + pp, self.c)

    def sibling(self, k):
        return (self.dp, lax.rem(self.c + k, self.n_blk))

    def apart(self, s, run):
        if s == 0:
            run(self.z)
            return

        @pl.loop(0, 2)
        def _(k):
            zz = self.z + s * (1 - 2 * k)
            pl.when((zz >= 0) & (zz < self.length))(lambda: run(zz))

    def up_down(self, run_up, run_down):
        pl.when(self.z < self.length - 1)(run_up)
        pl.when(self.z > 0)(run_down)

    def greet(self):
        barrier = pltpu.get_barrier_semaphore()

        def hello(device):
            pl.semaphore_signal(barrier, inc=1, device_id=device, device_id_type=MESH)

        hello(self.at(self.z, self.flip_x))
        hello(self.at(self.z, self.flip_y))
        hello(self.at(self.z, self.diag))
        for k in range(1, self.n_blk):
            hello(self.sibling(k))

        @pl.loop(1, self.length)
        def _(k):
            hello(self.at(lax.rem(self.z + k, self.length), self.p))

        pl.semaphore_wait(barrier, self.n_blk + self.length + 1)


def remote(src, dst, send_sem, recv_sem, device):
    return pltpu.make_async_remote_copy(
        src_ref=src,
        dst_ref=dst,
        send_sem=send_sem,
        recv_sem=recv_sem,
        device_id=device,
        device_id_type=MESH,
    )


class Gather:
    def __init__(self, place, unit, chunk, send, recv):
        self.place, self.chunk = place, chunk
        self.send = lambda kind, zz: send.at[unit, kind, zz]
        self.recv = lambda slot: recv.at[unit, slot]

    def copy(self, slot, kind, zz, device):
        piece = self.chunk(slot)
        return remote(piece, piece, self.send(kind, zz), self.recv(slot), device)

    def arrived(self, slot):
        self.copy(slot, 0, 0, self.place.sibling(1)).wait_recv()

    def line(self):
        pc = self.place
        pc.up_down(
            lambda: self.copy(pc.dp, 3, pc.z, pc.at(pc.z + 1, pc.p)).start(),
            lambda: self.copy(pc.dp, 4, pc.z, pc.at(pc.z - 1, pc.p)).start(),
        )

    def along(self, s):
        pc = self.place

        def pass_on(zz):
            slot = zz * PLANE + pc.p
            self.arrived(slot)
            below = jnp.where(zz < pc.z, 1, 0)
            onward = pc.z + 2 * below - 1
            more = (onward >= 0) & (onward < pc.length)
            pl.when(more)(lambda: self.copy(slot, 3, zz, pc.at(onward, pc.p)).start())

        pc.apart(s, pass_on)

    def ring(self, s):
        pc = self.place

        def both(zz):
            slot = zz * PLANE + pc.p
            self.copy(slot, 0, zz, pc.at(pc.z, pc.flip_x)).start()
            self.copy(slot, 1, zz, pc.at(pc.z, pc.flip_y)).start()

        pc.apart(s, both)

    def across(self, s):
        pc = self.place

        def turn(zz):
            near, far = pc.routes(zz)
            slot = zz * PLANE + near
            self.arrived(slot)
            self.copy(slot, 2, zz, pc.at(pc.z, far)).start()

        pc.apart(s, turn)

    def finish(self):
        pc = self.place

        @pl.loop(0, pc.length)
        def _(zz):
            self.arrived(zz * PLANE + pc.routes(zz)[1])
            self.arrived(zz * PLANE + pc.diag)

    def drain(self):
        pc = self.place

        def sent(kind, zz):
            self.copy(pc.dp, kind, zz, pc.sibling(1)).wait_send()

        @pl.loop(0, pc.length)
        def _(zz):
            sent(0, zz)
            sent(1, zz)
            sent(2, zz)
            pl.when((zz <= pc.z) & (pc.z < pc.length - 1))(lambda: sent(3, zz))
            pl.when((zz > pc.z) & (pc.z > 0))(lambda: sent(3, zz))

        pl.when(pc.z > 0)(lambda: sent(4, pc.z))


class RingGather:
    def __init__(self, place, unit, chunk, part, send, recv):
        self.place, self.chunk, self.part = place, chunk, part
        self.lift = lambda pp, zz: send.at[unit, pp, zz]
        self.side = lambda k: send.at[unit + 1, 0, k]
        self.recv = lambda slot: recv.at[unit, slot]
        self.other = recv.at[unit + 1, 0]

    def copy(self, piece, sem, recv, device):
        return remote(piece, piece, sem, recv, device)

    def arrived(self, slot):
        self.copy(self.chunk(slot), self.side(0), self.recv(slot), self.place.sibling(1)).wait_recv()

    def start(self):
        pc = self.place
        piece, recv = self.chunk(pc.dp), self.recv(pc.dp)
        self.copy(piece, self.side(0), recv, pc.at(pc.z, pc.flip_x)).start()
        self.copy(piece, self.side(1), recv, pc.at(pc.z, pc.flip_y)).start()

    def across(self):
        pc = self.place
        base = pc.z * PLANE
        self.arrived(base + pc.flip_x)
        half = self.part(base + pc.flip_x, 0)
        self.copy(half, self.side(2), self.recv(base + pc.flip_x), pc.at(pc.z, pc.flip_y)).start()
        self.arrived(base + pc.flip_y)
        half = self.part(base + pc.flip_y, 1)
        self.copy(half, self.side(3), self.other, pc.at(pc.z, pc.flip_x)).start()

    def rise(self):
        pc = self.place
        slot = pc.z * PLANE + pc.diag
        for i, recv in enumerate((self.recv(slot), self.other)):
            self.copy(self.part(slot, i), self.side(0), recv, pc.sibling(1)).wait_recv()

        @pl.loop(0, PLANE)
        def _(pp):
            at = pc.z * PLANE + pp
            piece = self.chunk(at)

            def to(sem, zz):
                self.copy(piece, sem, self.recv(at), pc.at(zz, pc.p)).start()

            pc.up_down(
                lambda: to(self.lift(pp, pc.z), pc.z + 1), lambda: to(self.lift(4, pp), pc.z - 1)
            )

    def along(self, s):
        pc = self.place

        def pass_on(zz):
            below = jnp.where(zz < pc.z, 1, 0)
            onward = pc.z + 2 * below - 1

            @pl.loop(0, PLANE)
            def _(pp):
                slot = zz * PLANE + pp
                self.arrived(slot)
                copy = self.copy(
                    self.chunk(slot), self.lift(pp, zz), self.recv(slot), pc.at(onward, pc.p)
                )
                pl.when((onward >= 0) & (onward < pc.length))(copy.start)

        pc.apart(s, pass_on)

    def drain(self):
        pc = self.place
        piece = self.chunk(pc.dp)

        def sent(sem, view=piece):
            self.copy(view, sem, self.recv(pc.dp), pc.sibling(1)).wait_send()

        sent(self.side(0))
        sent(self.side(1))
        sent(self.side(2), self.part(pc.dp, 0))
        sent(self.side(3), self.part(pc.dp, 1))

        @pl.loop(0, PLANE)
        def _(pp):
            @pl.loop(0, pc.length)
            def _(zz):
                pl.when((zz <= pc.z) & (pc.z < pc.length - 1))(lambda: sent(self.lift(pp, zz)))
                pl.when((zz > pc.z) & (pc.z > 0))(lambda: sent(self.lift(pp, zz)))

            pl.when(pc.z > 0)(lambda: sent(self.lift(4, pp)))


def gather_kernel(
    n_dp, n_blk, qkv, out, fc, proj, small, all_qkv, all_out, all_fc, all_proj, all_small, send, recv, local, side
):
    pc = Place(n_dp, n_blk)
    wide = out.shape[1]
    mine = pl.ds(pl.multiple_of(pc.c * wide, LANES), wide)
    parts = [
        (small, lambda slot: all_small.at[slot]),
        (qkv, lambda slot: all_qkv.at[slot]),
        (out, lambda slot: all_out.at[slot, :, mine]),
        (fc, lambda slot: all_fc.at[slot]),
        (proj, lambda slot: all_proj.at[slot]),
    ]
    for i, (own, chunk) in enumerate(parts):
        pltpu.make_async_copy(own, chunk(pc.dp), local.at[i]).start()
    pc.greet()
    for i, (own, chunk) in enumerate(parts):
        pltpu.make_async_copy(own, chunk(pc.dp), local.at[i]).wait()
    units = [Gather(pc, i, chunk, send, recv) for i, (_, chunk) in enumerate(parts)]
    steps = range(pc.length)
    for i, unit in enumerate(units):
        unit.line()
        for s in steps:
            if s:
                unit.along(s)
            unit.ring(s)
        if i > 0:
            for s in steps:
                units[i - 1].across(s)
            units[i - 1].finish()
    for s in steps:
        units[4].across(s)
    side_copies = []
    piece = all_out.at[:, :, mine]
    for k in range(1, n_blk):
        copy = remote(piece, piece, side.at[0, k], side.at[1, k], pc.sibling(k))
        copy.start()
        side_copies.append(copy)
    units[4].finish()
    for copy in side_copies:
        copy.wait()
    for unit in units:
        unit.drain()


class Scatter:
    def __init__(self, place, unit, chunk, bufs, send, recv, source=None):
        self.place, self.chunk, self.source = place, chunk, source or chunk
        self.diag, self.near, self.far, self.line = bufs
        self.kind = self.near.dtype
        self.send = lambda kind, zz: send.at[unit, kind, zz]
        self.recv = lambda kind, zz: recv.at[unit, kind, zz]

    def copy(self, src, dst, kind, zz, device):
        return remote(src, dst, self.send(kind, zz), self.recv(kind, zz), device)

    def arrived(self, piece, kind, zz):
        self.copy(piece, piece, kind, zz, self.place.sibling(1)).wait_recv()

    def start(self, near=True):
        pc = self.place

        def first(zz):
            to = pc.at(pc.z, pc.routes(zz)[0])
            self.copy(self.source(zz * PLANE + pc.diag), self.diag.at[zz], 0, zz, to).start()

        for s in range(pc.length - 1, -1, -1):
            pc.apart(s, first)
        if near:
            for s in range(pc.length - 1, -1, -1):
                pc.apart(s, self.send_near)

    def send_near(self, zz):
        pc = self.place
        near = pc.routes(zz)[0]
        piece = self.source(zz * PLANE + near)
        self.copy(piece, self.near.at[zz], 1, zz, pc.at(pc.z, near)).start()

    def middle(self, s, near=False):
        pc = self.place

        def turn(zz):
            far = pc.routes(zz)[1]
            self.arrived(self.diag.at[zz], 0, zz)
            total = self.diag[zz].astype(F32) + self.chunk(zz * PLANE + far)[...].astype(F32)
            self.diag[zz] = total.astype(self.kind)
            self.copy(self.diag.at[zz], self.far.at[zz], 2, zz, pc.at(pc.z, far)).start()
            if near:
                self.send_near(zz)

        pc.apart(s, turn)

    def settle(self, s):
        pc = self.place

        def add(zz):
            self.arrived(self.near.at[zz], 1, zz)
            self.arrived(self.far.at[zz], 2, zz)
            total = self.near[zz].astype(F32) + self.far[zz].astype(F32)
            total += self.chunk(zz * PLANE + pc.p)[...].astype(F32)
            self.near[zz] = total.astype(self.kind)

        pc.apart(s, add)

    def along(self, s):
        pc = self.place

        def send_on(zz):
            to = pc.at(zz, pc.p)
            sems = self.send(3, zz), self.recv(3, pc.z)
            remote(self.near.at[zz], self.line.at[pc.z], *sems, to).start()

        pc.apart(s, send_on)

    def finish(self, total):
        pc = self.place
        total[...] = self.near[pc.z].astype(F32)

        @pl.loop(1, pc.length)
        def _(k):
            zz = lax.rem(pc.z + k, pc.length)
            self.arrived(self.line.at[zz], 3, zz)
            total[...] += self.line[zz].astype(F32)

    def drain(self):
        pc = self.place

        def sent(kind, zz):
            piece = self.near.at[zz]
            self.copy(piece, piece, kind, zz, pc.sibling(1)).wait_send()

        @pl.loop(0, pc.length)
        def _(zz):
            sent(0, zz)
            sent(1, zz)
            sent(2, zz)
            pl.when(zz != pc.z)(lambda: sent(3, zz))


class LineScatter:
    def __init__(self, place, unit, chunk, bufs, send, recv, source=None):
        self.place, self.chunk, self.source = place, chunk, source or chunk
        self.line, self.half, self.ring = bufs
        self.lift = lambda pp, zz: send.at[unit, pp, zz]
        self.drop = lambda kind, zz: recv.at[unit, kind, zz]
        self.side = lambda k: (send.at[unit + 1, 0, k], recv.at[unit + 1, 0, k])
        self.middle_row = self.half.shape[1]

    def arrived(self, piece, sem):
        remote(piece, piece, self.lift(0, 0), sem, self.place.sibling(1)).wait_recv()

    def along(self, s):
        pc = self.place

        def pass_on(zz):
            above = jnp.where(zz > pc.z, 1, 0)
            onward = pc.z + 2 * above - 1
            before = pc.z - 2 * above + 1
            at = zz if s > 1 else zz * above + pc.length * (1 - above)

            @pl.loop(0, PLANE)
            def _(pp):
                last = pp * (1 - above) + zz * above if s == 1 else zz
                kind = pp if s > 1 else pp * above + PLANE * (1 - above)
                sem = self.drop(kind, last)
                dst, to = self.line.at[pp, at], pc.at(onward, pc.p)
                own = self.chunk(zz * PLANE + pp)

                def plain():
                    first = self.source(zz * PLANE + pp)
                    remote(first, dst, self.lift(pp, zz), sem, to).start()

                def more():
                    piece = self.line.at[pp, zz]
                    self.arrived(piece, self.drop(pp, zz))
                    piece[...] = (piece[...].astype(F32) + own[...].astype(F32)).astype(BF16)
                    remote(piece, dst, self.lift(pp, zz), sem, to).start()

                inside = (before >= 0) & (before < pc.length)
                if s == pc.length - 1:
                    plain()
                else:
                    pl.when(inside)(more)
                    pl.when(jnp.logical_not(inside))(plain)

        pc.apart(s, pass_on)

    def settle(self):
        pc = self.place

        @pl.loop(0, PLANE)
        def _(pp):
            own = self.chunk(pc.z * PLANE + pp)
            piece, over = self.line.at[pp, pc.z], self.line.at[pp, pc.length]

            def below():
                self.arrived(piece, self.drop(pp, pc.z))
                piece[...] = (piece[...].astype(F32) + own[...].astype(F32)).astype(BF16)

            def bottom():
                piece[...] = own[...]

            def above():
                self.arrived(over, self.drop(PLANE, pp))
                piece[...] = (piece[...].astype(F32) + over[...].astype(F32)).astype(BF16)

            pl.when(pc.z > 0)(below)
            pl.when(pc.z == 0)(bottom)
            pl.when(pc.z < pc.length - 1)(above)

        for i, to in enumerate((pc.flip_x, pc.flip_y)):
            rows = pl.ds(i * self.middle_row, self.middle_row)
            piece = self.line.at[pc.diag, pc.z, rows]
            remote(piece, self.half.at[i], *self.side(i), pc.at(pc.z, to)).start()

    def turn(self):
        pc = self.place
        for i, (dest, to) in enumerate(((pc.flip_y, pc.flip_y), (pc.flip_x, pc.flip_x))):
            rows = pl.ds(i * self.middle_row, self.middle_row)
            self.arrived(self.half.at[i], self.side(i)[1])
            value = self.line[dest, pc.z, rows].astype(F32) + self.half[i].astype(F32)
            self.line[dest, pc.z, rows] = value.astype(BF16)
            piece = self.line.at[dest, pc.z]
            remote(piece, self.ring.at[1 - i], *self.side(3 - i), pc.at(pc.z, to)).start()

    def finish(self, total):
        pc = self.place
        value = self.line[pc.p, pc.z].astype(F32)
        for i in range(2):
            self.arrived(self.ring.at[i], self.side(2 + i)[1])
            value += self.ring[i].astype(F32)
        total[...] = value

    def drain(self):
        pc = self.place

        def sent(piece, sem):
            remote(piece, piece, sem, self.drop(0, 0), pc.sibling(1)).wait_send()

        for i in range(2):
            sent(self.half.at[i], self.side(i)[0])
            sent(self.ring.at[i], self.side(2 + i)[0])

        @pl.loop(0, PLANE)
        def _(pp):
            @pl.loop(0, pc.length)
            def _(zz):
                piece = self.line.at[pp, zz]
                pl.when(zz > pc.z)(lambda: sent(piece, self.lift(pp, zz)))
                pl.when(zz < pc.z)(lambda: sent(piece, self.lift(pp, zz)))


class SmallSum:
    def __init__(self, place, unit, chunks, bufs, send, recv):
        self.place, self.chunks = place, chunks
        self.ring, self.sums, self.line = bufs
        self.sems = lambda kind, k: (send.at[unit, kind, k], recv.at[unit, kind, k])

    def flat(self):
        pc = self.place
        dests = ((1, pc.flip_x), (2, pc.flip_y), (3, pc.diag))
        return [
            remote(self.chunks.at[to], self.ring.at[k - 1], *self.sems(0, k), pc.at(pc.z, to))
            for k, to in dests
        ]

    def start(self):
        for copy in self.flat():
            copy.start()

    def middle(self):
        pc = self.place
        for copy in self.flat():
            copy.wait()
        self.sums[...] = self.chunks[pc.p] + self.ring[0] + self.ring[1] + self.ring[2]

        @pl.loop(1, pc.length)
        def _(k):
            zz = lax.rem(pc.z + k, pc.length)
            send, recv = self.sems(1, zz)[0], self.sems(1, pc.z)[1]
            remote(self.sums.at[zz], self.line.at[pc.z], send, recv, pc.at(zz, pc.p)).start()

    def finish(self, total):
        pc = self.place
        total[...] = self.sums[pc.z]

        @pl.loop(1, pc.length)
        def _(k):
            zz = lax.rem(pc.z + k, pc.length)
            piece = self.line.at[zz]
            remote(piece, piece, *self.sems(1, zz), pc.sibling(1)).wait()
            total[...] += self.line[zz]


def scatter_kernel(n_dp, n_blk, *refs):
    grads, outs, rest = refs[:4], refs[4:8], refs[8:]
    bufs, totals, rest = rest[:16], rest[16:20], rest[20:]
    side_buf, send, recv, side, last = rest
    proj, fc, out, qkv = grads
    pc = Place(n_dp, n_blk)
    pc.greet()
    wide = out.shape[2] // n_blk

    def columns(core):
        return pl.ds(pl.multiple_of(core * wide, LANES), wide)

    chunks = [
        lambda slot: proj.at[slot],
        lambda slot: fc.at[slot],
        lambda slot: side_buf.at[0, slot],
        lambda slot: qkv.at[slot],
    ]
    units = [
        Scatter(pc, i, chunks[i], bufs[4 * i : 4 * i + 4], send, recv) for i in range(4)
    ]
    units[0].start()
    units[1].start()
    side_copies = []
    for k in range(1, n_blk):
        dev = pc.sibling(k)
        copy = remote(
            out.at[:, :, columns(dev[1])], side_buf.at[k], side.at[0, k], side.at[1, k], dev
        )
        copy.start()
        side_copies.append(copy)

    def side_sum():
        for copy in side_copies:
            copy.wait()

        @pl.loop(0, n_dp)
        def _(slot):
            total = out[slot, :, columns(pc.c)].astype(F32)
            for k in range(1, n_blk):
                total += side_buf[k, slot].astype(F32)
            side_buf[0, slot] = total.astype(BF16)

    pending = []

    def spread(i):
        units[i].finish(totals[i])
        total = totals[i]
        pieces = [(total, outs[i].at[pc.c])]
        for j, (src, dst) in enumerate(pieces):
            keep = pltpu.make_async_copy(src, dst, last.at[i, 0, 0])
            keep.start()
            pending.append(keep)
            for k in range(1, n_blk):
                copy = remote(src, dst, last.at[i, 0, k], last.at[i, 1, k], pc.sibling(k))
                copy.start()
                pending.append(copy)

    steps = range(pc.length - 1, -1, -1)

    def middle(i):
        for s in steps:
            units[i].middle(s)

    def settle(i):
        for s in steps:
            units[i].settle(s)
            if s:
                units[i].along(s)

    middle(0)
    side_sum()
    units[2].start()
    middle(1)
    units[3].start()
    settle(0)
    middle(2)
    settle(1)
    spread(0)
    middle(3)
    settle(2)
    settle(3)
    spread(1)
    spread(2)
    spread(3)
    for copy in pending:
        copy.wait()
    for unit in units:
        unit.drain()


def gather_weights(n_dp, n_blk, qkv, out, fc, proj, small):
    shards = (qkv, out, fc, proj, small)
    shapes = [
        jax.ShapeDtypeStruct((n_dp, a.shape[0], a.shape[1] * (n_blk if a is out else 1)), BF16)
        for a in shards
    ]
    length = n_dp // PLANE
    hbm = pl.BlockSpec(memory_space=pl.ANY)
    return pl.pallas_call(
        functools.partial(gather_kernel, n_dp, n_blk),
        out_shape=shapes,
        in_specs=[hbm] * 5,
        out_specs=[hbm] * 5,
        scratch_shapes=[
            pltpu.SemaphoreType.DMA((5, 5, length)),
            pltpu.SemaphoreType.DMA((5, n_dp)),
            pltpu.SemaphoreType.DMA((5,)),
            pltpu.SemaphoreType.DMA((2, n_blk)),
        ],
        compiler_params=pltpu.CompilerParams(
            collective_id=0, has_side_effects=True, vmem_limit_bytes=VMEM_BYTES
        ),
    )(*shards)


def scatter_grads(n_dp, n_blk, proj, fc, out, qkv):
    length = n_dp // PLANE
    grads = (proj, fc, out, qkv)
    sizes = [a.shape[1:] for a in grads]
    sizes[2] = (sizes[2][0], sizes[2][1] // n_blk)
    vmem = pl.BlockSpec(memory_space=pltpu.VMEM)
    scratch = []
    for size in sizes:
        scratch += [pltpu.VMEM((length,) + size, BF16)] * 4
    scratch += [pltpu.VMEM(size, F32) for size in sizes]
    scratch += [
        pltpu.VMEM((n_blk, n_dp) + sizes[2], BF16),
        pltpu.SemaphoreType.DMA((4, 5, length)),
        pltpu.SemaphoreType.DMA((4, 5, length)),
        pltpu.SemaphoreType.DMA((2, n_blk)),
        pltpu.SemaphoreType.DMA((4, 2, n_blk)),
    ]
    return pl.pallas_call(
        functools.partial(scatter_kernel, n_dp, n_blk),
        out_shape=[jax.ShapeDtypeStruct((n_blk,) + size, F32) for size in sizes],
        in_specs=[vmem] * 4,
        out_specs=[pl.BlockSpec(memory_space=pl.ANY)] * 4,
        scratch_shapes=scratch,
        compiler_params=pltpu.CompilerParams(
            collective_id=1, has_side_effects=True, vmem_limit_bytes=VMEM_BYTES
        ),
    )(*grads)


def lane_split(value, lane, first, base):
    for i in range(3):
        term = value.astype(BF16)
        base = jnp.where(lane == first + i, term, base)
        value = value - term.astype(F32)
    return base


def causal_tail(scores, block, axis, masked):
    key_axis, query_axis = (0, 1) if axis == 0 else (1, 0)
    tail_shape = (block, block)
    keep = lax.broadcasted_iota(jnp.int32, tail_shape, key_axis) <= lax.broadcasted_iota(
        jnp.int32, tail_shape, query_axis
    )
    size = scores.shape[axis]
    if size == block:
        return jnp.where(keep, scores, masked)
    head = lax.slice_in_dim(scores, 0, size - block, axis=axis)
    tail = jnp.where(keep, lax.slice_in_dim(scores, size - block, size, axis=axis), masked)
    return jnp.concatenate([head, tail], axis=axis)


def causal_all(scores, offset, axis, masked):
    key_axis, query_axis = (0, 1) if axis == 0 else (1, 0)
    keep = (
        lax.broadcasted_iota(jnp.int32, scores.shape, key_axis)
        <= lax.broadcasted_iota(jnp.int32, scores.shape, query_axis) + offset
    )
    return jnp.where(keep, scores, masked)


def query_blocks(total, block, run):
    count = total // block
    if count <= 4:
        for b in range(count):
            run(
                b * block,
                (b + 1) * block,
                lambda scores, axis, masked: causal_tail(scores, block, axis, masked),
            )
    else:

        @pl.loop(0, count)
        def _(b):
            first = pl.multiple_of(b * block, block)
            run(first, total, lambda scores, axis, masked: causal_all(scores, first, axis, masked))


def attend_kernel(block, scale, q_ref, k_ref, v_ref, key_aug, query_aug, slopes, out_ref, qx_ref):
    total = q_ref.shape[0]
    half = LANES // 2
    lane = lax.broadcasted_iota(jnp.int32, (1, LANES), 1)
    slope_rows = []
    for hh in range(2):
        base = half * (1 - hh)
        slope = jnp.full((1, LANES), slopes[hh], F32)
        row = lane_split(slope, lane, base, jnp.zeros((1, LANES), BF16))
        slope_rows.append(lane_split(slope, lane, base + 3, row))

    def run(first, keys, mask):
        rows = pl.ds(first, block)
        result = None
        for hh in range(2):
            own = (lane < half) if hh == 0 else (lane >= half)
            base = half * (1 - hh)
            aug = query_aug[rows, :] + slope_rows[hh]
            query = jnp.where(own, q_ref[rows, :] * BF16(scale), aug)
            key = jnp.where(own, k_ref[0:keys, :], key_aug[0:keys, :])
            value = jnp.where(own, v_ref[0:keys, :], BF16(1))
            scores = mask(matmul_nt(query, key), 1, MASKED)
            top = jnp.max(scores, axis=1, keepdims=True)
            weights = jnp.exp(scores - top).astype(BF16)
            sums = matmul(weights, value)
            log_total = top + jnp.log(sums[:, base : base + 1])
            qx_ref[0, hh, rows, :] = lane_split(-log_total, lane, base + 8, query)
            part = sums / pltpu.roll(sums, half, 1)
            result = part if hh == 0 else jnp.where(own, part, result)
        out_ref[rows, :] = result.astype(BF16)

    query_blocks(total, block, run)


def attend_back_kernel(
    block, scale, qx_ref, k_ref, v_ref, key_aug, out_ref, grad_ref, dq_ref, dk_ref, dv_ref, dk_acc, dv_acc
):
    total = k_ref.shape[0]
    half = LANES // 2
    lane = lax.broadcasted_iota(jnp.int32, (1, LANES), 1)
    dk_acc[...] = jnp.zeros_like(dk_acc)
    dv_acc[...] = jnp.zeros_like(dv_acc)

    def run(first, keys, mask):
        rows = pl.ds(first, block)
        grad = grad_ref[rows, :]
        product = grad.astype(F32) * out_ref[rows, :].astype(F32)
        dq = None
        dk = None
        dv = None
        for hh in range(2):
            own = (lane < half) if hh == 0 else (lane >= half)
            base = half * (1 - hh)
            query = qx_ref[0, hh, rows, :]
            key = jnp.where(own, k_ref[0:keys, :], key_aug[0:keys, :])
            delta = jnp.sum(jnp.where(own, product, 0.0), axis=1, keepdims=True)
            grad_own = jnp.where(own, grad, BF16(0))
            grad_aug = lane_split(-delta, lane, base, grad_own)
            value = jnp.where(own, v_ref[0:keys, :], BF16(1))
            weights = mask(jnp.exp(matmul_nt(key, query)), 0, 0.0)
            change = (weights * matmul_nt(value, grad_aug)).astype(BF16)
            key_own = jnp.where(own, key, BF16(0))
            query_own = jnp.where(own, query, BF16(0))
            dv_part = matmul(weights.astype(BF16), grad_own)
            dk_part = matmul(change, query_own)
            dq_part = matmul_tn(change, key_own)
            dv = dv_part if hh == 0 else dv + dv_part
            dk = dk_part if hh == 0 else dk + dk_part
            dq = dq_part if hh == 0 else dq + dq_part
        dq_ref[rows, :] = (dq * scale).astype(BF16)
        dk_acc[0:keys, :] += dk
        dv_acc[0:keys, :] += dv

    query_blocks(total, block, run)
    dk_ref[...] = dk_acc[...].astype(BF16)
    dv_ref[...] = dv_acc[...].astype(BF16)


def gelu_pair(u):
    k = math.sqrt(2.0 / math.pi)
    square = u * u
    t = jnp.tanh(k * u * (1.0 + 0.044715 * square))
    plus = 0.5 * (1.0 + t)
    slope = plus + (0.5 * k) * u * (1.0 - t * t) * (1.0 + 3 * 0.044715 * square)
    return u * plus, slope


def whole(ref, cols):
    value = ref[:, :, cols]
    return value.reshape(value.shape[0] * value.shape[1], value.shape[2])


def token_tables(pos_ref, row_ref, key_ref, query_ref, first):
    lane = lax.rem(lax.broadcasted_iota(jnp.int32, (1, LANES), 1), LANES // 2)
    for b in range(pos_ref.shape[0]):

        def column(ref):
            row = ref[b : b + 1, :].astype(F32)
            return jnp.transpose(jnp.broadcast_to(row, (LANES, LANES)))

        place, other = column(pos_ref), column(row_ref)
        high = jnp.floor(place * (1.0 / 256)) * 256
        key = jnp.where(lane < 3, high, place - high)
        key = jnp.where(lane == 6, 1.0 - other, key)
        key = jnp.where(lane == 7, other, key)
        key = jnp.where(lane < 8, key, jnp.where(lane < 11, 1.0, 0.0))
        query = jnp.where(lane == 6, other * MASKED, 0.0)
        query = jnp.where(lane == 7, (1.0 - other) * MASKED, query)
        rows = pl.ds(pl.multiple_of(first + b * LANES, LANES), LANES)
        key_ref[rows, :] = key.astype(BF16)
        query_ref[rows, :] = query.astype(BF16)


def forward_kernel(n_dp, n_blk, scale, *refs):
    (qkv, out, fc, proj, tokens, out_grad, pos, rows_id, slopes, fc_bias) = refs[:10]
    vectors, refs = refs[10:18], refs[18:]
    (w_qkv_o, w_out_o, w_fc_o, w_proj_o, vec_o, h1_o, mixed_o, heads_o, att_o, qx_o, mid_o, h2_o, hid_o, slope_o, dy_o, key_o, gp_o) = refs[:17]
    (w_qkv, w_out, w_fc, w_proj, vec, h1, mixed, heads, att, qx, mid, h2, hid, gslope, dy, key_aug, gp) = refs[17:34]
    (w_small, fcb, x_all, query_aug, f_qkv, f_out, f_fc, f_proj) = refs[34:42]
    send, recv, side, load, save_sem = refs[42:]
    pc = Place(n_dp, n_blk)
    sib = pc.sibling(1)
    rows_own, width = tokens.shape
    total = n_blk * rows_own
    wide = width // n_blk
    piece = f_proj.shape[0]
    tile = 256
    mine = pl.ds(pl.multiple_of(pc.c * rows_own, rows_own), rows_own)
    theirs = pl.ds(pl.multiple_of(sib[1] * rows_own, rows_own), rows_own)
    my_start = pl.multiple_of(pc.c * wide, LANES)
    my_cols = pl.ds(my_start, wide)
    saves = []

    def exchange(i, src, dst):
        copy = remote(src, dst, side.at[0, i], side.at[1, i], sib)
        copy.start()
        return copy

    def keep(i, src, dst):
        copy = pltpu.make_async_copy(src, dst, load.at[i])
        copy.start()
        return copy

    def save(i, src, dst):
        copy = pltpu.make_async_copy(src, dst, save_sem.at[i])
        copy.start()
        saves.append(copy)

    get_qkv = [
        keep(i, qkv.at[:, pl.ds(my_start + i * width, wide)], f_qkv.at[:, i * wide : (i + 1) * wide])
        for i in range(3)
    ]
    get_out = keep(3, out.at[:, my_cols], f_out)
    get_proj = keep(4, proj.at[pl.ds(pl.multiple_of(pc.c * piece, piece), piece)], f_proj)

    def fc_part(j):
        src = fc.at[:, pl.ds(pl.multiple_of((j * n_blk + pc.c) * piece, piece), piece)]
        dst = f_fc.at[:, pl.ds(pl.multiple_of(j * piece, piece), piece)]
        return pltpu.make_async_copy(src, dst, load.at[8 + j])

    pl.loop(0, n_dp)(lambda j: fc_part(j).start())
    get_x = keep(5, tokens, x_all.at[mine])
    pc.greet()
    first = [exchange(0, tokens, x_all.at[mine])]
    lane = lax.broadcasted_iota(jnp.int32, (1, LANES), 1)
    shard = width // n_dp
    own_part = lane // shard == lax.rem(pc.dp, LANES // shard)
    lines = []
    for ref in vectors:
        lines.append(jnp.where(own_part, jnp.concatenate([ref[...]] * (LANES // shard), axis=1), 0.0))
    lines.append(fc_bias[:, pl.ds(pl.multiple_of(pc.c * piece, piece), piece)])
    lines.append(jnp.zeros((16 - len(lines), LANES), F32))
    w_small[pc.dp] = jnp.concatenate(lines, axis=0).astype(BF16)
    cut = piece // 2
    quarter = cut // 2
    chunks = [
        lambda slot: w_small.at[slot],
        lambda slot: w_qkv.at[slot],
        lambda slot: w_out.at[slot, :, my_cols],
        lambda slot: w_fc.at[slot],
        lambda slot: w_proj.at[slot, cut:piece],
    ]
    u_small, u_qkv, u_out, u_fc, u_proj = [
        Gather(pc, i, chunk, send, recv) for i, chunk in enumerate(chunks)
    ]
    u_ring = RingGather(
        pc,
        5,
        lambda slot: w_proj.at[slot, 0:cut],
        lambda slot, i: w_proj.at[slot, i * quarter : (i + 1) * quarter],
        send,
        recv,
    )
    steps = range(1, pc.length)
    u_small.line()
    u_small.ring(0)
    for copy in get_qkv:
        copy.wait()
    w_qkv[pc.dp] = f_qkv[...].astype(BF16)
    u_qkv.line()
    u_qkv.ring(0)
    get_out.wait()
    w_out[pc.dp, :, my_cols] = f_out[...].astype(BF16)
    get_proj.wait()
    w_proj[pc.dp] = f_proj[...].astype(BF16)
    token_tables(pos, rows_id, key_aug, query_aug, pc.c * rows_own)
    first.append(exchange(1, key_aug.at[mine], key_aug.at[mine]))
    first.append(exchange(2, query_aug.at[mine], query_aug.at[mine]))
    u_small.along(1)
    u_small.ring(1)
    u_qkv.along(1)
    u_qkv.ring(1)
    for s in steps[1:]:
        u_small.along(s)
        u_small.ring(s)
    for s in range(pc.length):
        u_small.across(s)
    pl.loop(0, n_dp)(lambda j: fc_part(j).wait())
    w_fc[pc.dp] = f_fc[...].astype(BF16)
    later = [exchange(3, out_grad, dy.at[mine]), keep(6, out_grad, dy.at[mine])]
    u_small.finish()
    u_qkv.along(2)
    u_qkv.ring(2)
    u_out.line()
    get_x.wait()
    for copy in first:
        copy.wait()
    per = n_dp // (width // LANES)
    for t in range(width // LANES):
        rows = w_small[t * per].astype(F32)
        for k in range(1, per):
            rows += w_small[t * per + k].astype(F32)
        vec[:, t * LANES : (t + 1) * LANES] = rows
    for t in range(n_dp):
        fcb[:, t * LANES : (t + 1) * LANES] = w_small[t, 8:9, :].astype(F32)
    save(0, vec, vec_o)

    def first_norm(b):
        rows = pl.ds(pl.multiple_of(b * LANES, LANES), LANES)
        h1[rows, :] = layer_norm(x_all[rows, :].astype(F32), vec[0:1, :], vec[1:2, :]).astype(BF16)

    norm_blocks = total // LANES
    pl.loop(0, norm_blocks // 2)(first_norm)
    for s in steps[2:]:
        u_qkv.along(s)
        u_qkv.ring(s)
    u_fc.line()
    u_out.ring(0)
    pl.loop(norm_blocks // 2, norm_blocks)(first_norm)
    save(2, h1, h1_o)
    for s in range(pc.length):
        u_qkv.across(s)
    u_ring.start()
    for s in steps:
        u_out.along(s)
        u_out.ring(s)
    u_fc.along(1)
    u_qkv.finish()
    save(3, w_qkv, w_qkv_o)
    for third in range(3):
        for b in range(wide // tile):

            @pl.loop(0, total // 512)
            def _(m, third=third, b=b):
                rows = pl.ds(pl.multiple_of(m * 512, 512), 512)
                cols = pl.ds(third * wide + b * tile, tile)
                value = matmul(h1[rows, :], whole(w_qkv, cols))
                if third != 1:
                    at = pl.ds(my_start + b * tile, tile)
                    value += vec[pl.ds(2 + third // 2, 1), at]
                mixed[rows, cols] = value.astype(BF16)

        if third == 0:
            u_fc.along(2)
            for s in range(pc.length):
                u_out.across(s)
            u_ring.across()
    save(4, mixed, mixed_o)
    for s in steps[2:]:
        u_fc.along(s)
    for s in range(pc.length):
        u_fc.ring(s)
    u_proj.line()
    pairs = wide // LANES
    for j in range(pairs):
        cols = [pl.ds(i * wide + j * LANES, LANES) for i in range(3)]
        attend_kernel(
            tile,
            scale,
            mixed.at[:, cols[0]],
            mixed.at[:, cols[1]],
            mixed.at[:, cols[2]],
            key_aug,
            query_aug,
            [slopes[pc.c * 2 * pairs + 2 * j + hh] for hh in range(2)],
            heads.at[:, cols[0]],
            qx.at[pl.ds(j, 1)],
        )
        if j == 0:
            u_ring.rise()
        if j < pc.length - 1:
            u_proj.along(j + 1)
        if j == 1:
            u_fc.across(0)
        if j == 2:
            u_ring.along(1)
            u_fc.across(1)
            u_out.finish()
            part = w_out.at[:, :, my_cols]
            share = exchange(4, part, part)
    swap = exchange(5, heads.at[theirs], att.at[:, my_cols])
    stay = keep(7, heads.at[mine], att.at[:, my_cols])
    save(5, heads, heads_o)
    save(6, qx, qx_o)
    share.wait()
    save(7, w_out, w_out_o)
    swap.wait()
    stay.wait()
    save(8, att, att_o)

    @pl.loop(0, width // tile)
    def _(b):
        cols = pl.ds(pl.multiple_of(b * tile, tile), tile)
        value = matmul(att[...], whole(w_out, cols))
        mid[:, cols] = x_all[mine, cols].astype(F32) + value + vec[4:5, cols]

    u_fc.across(2)

    @pl.loop(0, rows_own // LANES)
    def _(b):
        rows = pl.ds(pl.multiple_of(b * LANES, LANES), LANES)
        into = pl.ds(pl.multiple_of(pc.c * rows_own + b * LANES, LANES), LANES)
        h2[into, :] = layer_norm(mid[rows, :], vec[5:6, :], vec[6:7, :]).astype(BF16)

    both = exchange(6, h2.at[mine], h2.at[mine])
    save(9, mid, mid_o)
    u_ring.along(2)
    for s in range(3, pc.length):
        u_fc.across(s)
    for s in range(pc.length):
        u_proj.ring(s)
    both.wait()
    save(10, h2, h2_o)
    u_fc.finish()
    save(11, w_fc, w_fc_o)

    def feed(b):
        cols = pl.ds(pl.multiple_of(b * tile, tile), tile)

        @pl.loop(0, total // 512)
        def _(m):
            rows = pl.ds(pl.multiple_of(m * 512, 512), 512)
            value = matmul(h2[rows, :], whole(w_fc, cols)) + fcb[:, cols]
            value, slope = gelu_pair(value)
            hid[rows, cols] = value.astype(BF16)
            gslope[rows, cols] = slope.astype(BF16)

    blocks = hid.shape[1] // tile
    pl.loop(0, blocks // 4)(feed)
    for s in range(3, pc.length):
        u_ring.along(s)
    u_proj.across(0)
    pl.loop(blocks // 4, blocks // 2)(feed)
    u_proj.across(1)
    pl.loop(blocks // 2, blocks)(feed)
    for s in range(2, pc.length):
        u_proj.across(s)
    save(12, hid, hid_o)
    save(13, gslope, slope_o)
    for copy in later:
        copy.wait()
    save(14, dy, dy_o)
    save(15, key_aug, key_o)
    slots = tile // piece

    @pl.loop(0, blocks)
    def _(b):
        cols = pl.ds(pl.multiple_of(b * tile, tile), tile)
        for n in range(width // 512):
            value = matmul_tn(hid[:, cols], dy[:, n * 512 : (n + 1) * 512]).astype(BF16)
            gp[pl.ds(b * slots, slots), :, n * 512 : (n + 1) * 512] = value.reshape(slots, piece, 512)

    save(16, gp, gp_o)
    u_proj.finish()
    save(1, w_proj, w_proj_o)
    for copy in saves:
        copy.wait()
    for unit in (u_small, u_qkv, u_out, u_fc, u_proj, u_ring):
        unit.drain()


def forward(n_dp, n_blk, scale, qkv, out, fc, proj, tokens, out_grad, positions, row_ids, slopes, fc_bias, vectors):
    rows_own, width = tokens.shape
    total = n_blk * rows_own
    wide = width // n_blk
    pairs = wide // LANES
    piece = proj.shape[0] // n_blk
    ff = n_dp * piece
    shard, length = qkv.shape[0], n_dp // PLANE
    weights = [(shard, 3 * wide), (shard, width), (shard, ff), (piece, width)]
    outs = [((n_dp,) + w, BF16) for w in weights] + [
        ((16, width), F32),
        ((total, width), BF16),
        ((total, 3 * wide), BF16),
        ((total, wide), BF16),
        ((rows_own, width), BF16),
        ((pairs, 2, total, LANES), BF16),
        ((rows_own, width), F32),
        ((total, width), BF16),
        ((total, ff), BF16),
        ((total, ff), BF16),
        ((total, width), BF16),
        ((total, LANES), BF16),
        ((n_dp, piece, width), BF16),
    ]
    scratch = outs + [
        ((n_dp, 16, LANES), BF16),
        ((1, ff), F32),
        ((total, width), BF16),
        ((total, LANES), BF16),
        ((shard, 3 * wide), F32),
        ((shard, wide), F32),
        ((shard, ff), F32),
        ((piece, width), F32),
    ]
    hbm = pl.BlockSpec(memory_space=pl.ANY)
    vmem = pl.BlockSpec(memory_space=pltpu.VMEM)
    smem = pl.BlockSpec(memory_space=pltpu.SMEM)
    grid = (rows_own // LANES, LANES)
    small = [a.reshape(1, -1) for a in (fc_bias, *vectors)]
    return pl.pallas_call(
        functools.partial(forward_kernel, n_dp, n_blk, scale),
        out_shape=[jax.ShapeDtypeStruct(*o) for o in outs],
        in_specs=[hbm] * 6 + [vmem] * 2 + [smem] + [vmem] * len(small),
        out_specs=[hbm] * len(outs),
        scratch_shapes=[pltpu.VMEM(*s) for s in scratch]
        + [
            pltpu.SemaphoreType.DMA((7, 5, length)),
            pltpu.SemaphoreType.DMA((7, n_dp)),
            pltpu.SemaphoreType.DMA((2, 7)),
            pltpu.SemaphoreType.DMA((8 + n_dp,)),
            pltpu.SemaphoreType.DMA((17,)),
        ],
        compiler_params=pltpu.CompilerParams(
            collective_id=2, has_side_effects=True, vmem_limit_bytes=VMEM_BYTES
        ),
    )(qkv, out, fc, proj, tokens, out_grad, positions.reshape(grid), row_ids.reshape(grid), slopes, *small)


def normed_rows(rows):
    centred = rows - jnp.mean(rows, axis=-1, keepdims=True)
    inverse = lax.rsqrt(jnp.mean(centred * centred, axis=-1, keepdims=True) + EPSILON)
    return centred * inverse, inverse


def norm_back(rows, gain_vec, grad):
    unit, inverse = normed_rows(rows)
    m = grad * gain_vec
    shift = jnp.mean(m, axis=-1, keepdims=True)
    stretch = jnp.mean(m * unit, axis=-1, keepdims=True)
    return (m - shift - unit * stretch) * inverse, grad * unit


def column_sum(value):
    return jnp.sum(value, axis=0, keepdims=True)


def backward_kernel(n_dp, n_blk, scale, *refs):
    (w_qkv_h, w_out_h, w_fc_h, w_proj_h, vec, h1_h, mixed_h, heads_h, att_h, qx_h, mid_h, h2_h, hid_h, slope_h, dy_h, key_h, gp_h, tokens_h) = refs[:18]
    (layer_o, input_o, proj_o, fc_o, qkv_o, out_o, small_o) = refs[18:25]
    (P2, S, Y, F, H, A, M, T, O, Q, E, K, GP, side0, side1, R1, R2, R3, DH, SB, PF, acc_k, acc_v, VG, fcg, SG, small_in) = refs[25:52]
    bufs, small_bufs, rest = refs[52:68], refs[68:71], refs[71:]
    ring_bufs, rest = rest[:3], rest[3:]
    totals, rest = rest[:6], rest[6:]
    send, recv, xsem, load, last = rest
    pc = Place(n_dp, n_blk)
    sib = pc.sibling(1)
    rows_own, width = tokens_h.shape
    total = n_blk * rows_own
    wide = width // n_blk
    ff = A.shape[1]
    shard = width // n_dp
    piece = ff // n_dp
    tile = 256
    mine = pl.ds(pl.multiple_of(pc.c * rows_own, rows_own), rows_own)
    theirs = pl.ds(pl.multiple_of(sib[1] * rows_own, rows_own), rows_own)
    my_cols = pl.ds(pl.multiple_of(pc.c * wide, LANES), wide)
    their_cols = pl.ds(pl.multiple_of(sib[1] * wide, LANES), wide)

    def fetch(i, src, dst):
        copy = pltpu.make_async_copy(src, dst, load.at[i])
        copy.start()
        return copy

    def exchange(i, src, dst):
        copy = remote(src, dst, xsem.at[0, i], xsem.at[1, i], sib)
        copy.start()
        return copy

    def span(i, size=tile):
        return pl.ds(pl.multiple_of(i * size, size), size)

    get_proj = fetch(2, w_proj_h, P2)
    get_dy = fetch(3, dy_h, Y)
    get_slope = fetch(4, slope_h, S)
    get_gp = fetch(0, gp_h, GP)
    get_h2 = fetch(5, h2_h, H)
    get_mid = fetch(6, mid_h, M)
    get_fc = fetch(7, w_fc_h, F)
    get_att = fetch(8, att_h, T)
    get_out = fetch(9, w_out_h, O)
    get_qx = fetch(10, qx_h, Q)
    get_heads = fetch(11, heads_h, E)
    get_key = fetch(12, key_h, K)
    pc.greet()
    cut = piece // 2
    chunks = [
        lambda slot: GP.at[pl.ds(pl.multiple_of(slot * piece + cut, cut), cut)],
        lambda slot: A.at[span(slot, shard)],
        lambda slot: F.at[span(slot, shard), 0 : 3 * wide],
        lambda slot: side0.at[span(slot, shard)],
    ]

    def from_proj(ref, first):
        return lambda slot: ref.at[pl.ds(pl.multiple_of(slot * piece + first, cut), cut)]

    u_proj, u_fc, u_qkv, u_out = [
        Scatter(
            pc, i, chunks[i], bufs[4 * i : 4 * i + 4], send, recv, None if i else from_proj(gp_h, cut)
        )
        for i in range(4)
    ]
    u_small = SmallSum(pc, 4, SG, small_bufs, send, recv)
    u_line = LineScatter(pc, 5, from_proj(GP, 0), ring_bufs, send, recv, from_proj(gp_h, 0))
    length = pc.length
    far_first = range(length - 1, -1, -1)
    pending = []

    def give(i, src, dst):
        keep = pltpu.make_async_copy(src, dst, last.at[0, i])
        copy = remote(src, dst, last.at[1, i], last.at[2, i], sib)
        keep.start()
        copy.start()
        return keep, copy

    VG[...] = jnp.zeros_like(VG)
    u_line.along(length - 1)
    u_proj.start()
    get_proj.wait()
    get_dy.wait()
    get_slope.wait()

    def hidden_grads(b):
        cols = span(b)
        sums = None
        for m in range(total // 512):
            rows = pl.ds(m * 512, 512)
            value = S[rows, cols].astype(F32) * matmul_nt(Y[rows, :], P2[cols, :])
            value = value.astype(BF16)
            S[rows, cols] = value
            part = column_sum(value.astype(F32))
            sums = part if sums is None else sums + part
        fcg[:, cols] = sums

    blocks = ff // tile
    pl.loop(0, blocks // 2)(hidden_grads)
    get_gp.wait()
    for s in far_first[:2]:
        u_proj.middle(s)
    pl.loop(blocks // 2, blocks)(hidden_grads)
    for s in far_first[2:]:
        u_proj.middle(s)
    get_h2.wait()

    @pl.loop(0, width // tile)
    def _(b):
        for n in range(ff // 1024):
            cols = pl.ds(n * 1024, 1024)
            A[span(b), cols] = matmul_tn(H[:, span(b)], S[:, cols]).astype(BF16)

    u_fc.start()
    u_line.along(length - 2)
    get_qkv = [
        fetch(13, w_qkv_h.at[:, 0 : 2 * wide], P2.at[0:width]),
        fetch(14, w_qkv_h.at[:, 2 * wide :], P2.at[width : 2 * width, 0:wide]),
    ]
    get_mid.wait()
    get_fc.wait()

    @pl.loop(0, width // tile)
    def _(b):
        SB[:, span(b)] = matmul_nt(S[theirs, :], F[span(b), :]).astype(BF16)

    swap_two = exchange(1, SB, R2)
    for s in far_first[:2]:
        u_proj.settle(s)

    @pl.loop(0, width // tile)
    def _(b):
        PF[:, span(b)] = matmul_nt(S[mine, :], F[span(b), :])

    for s in far_first[2:]:
        u_proj.settle(s)
    swap_two.wait()
    get_h1 = fetch(16, h1_h, S.at[:, 0:width])
    get_kv = fetch(17, mixed_h.at[:, wide:], S.at[:, width : 2 * width])

    @pl.loop(0, rows_own // LANES)
    def _(b):
        rows = span(b, LANES)
        from_mine = pl.ds(pl.multiple_of(pc.c * rows_own + b * LANES, LANES), LANES)
        into = pl.ds(pl.multiple_of(sib[1] * rows_own + b * LANES, LANES), LANES)
        grad = PF[rows, :] + R2[rows, :].astype(F32)
        top = Y[from_mine, :].astype(F32)
        back, terms = norm_back(M[rows, :], vec[5:6, :], grad)
        value = top + back
        M[rows, :] = value
        branch = value.astype(BF16)
        Y[into, :] = branch
        VG[4:5, :] += column_sum(branch.astype(F32))
        VG[5:6, :] += column_sum(terms)
        VG[6:7, :] += column_sum(grad)
        VG[7:8, :] += column_sum(top)

    get_out.wait()

    @pl.loop(0, width // tile)
    def _(b):
        Y[mine, span(b)] = matmul_nt(Y[theirs, :], O[span(b), :]).astype(BF16)

    swap_heads = exchange(2, Y.at[mine, their_cols], DH.at[mine])
    stay_heads = fetch(18, Y.at[mine, my_cols], DH.at[mine])
    for s in range(length - 3, 0, -1):
        u_line.along(s)
    get_att.wait()

    @pl.loop(0, width // tile)
    def _(b):
        O[span(b), :] = matmul_tn(T[:, span(b)], Y[theirs, :]).astype(BF16)

    swap_side = exchange(3, O.at[:, their_cols], side1)
    get_tokens = fetch(19, tokens_h, T)
    get_qx.wait()
    get_heads.wait()
    get_key.wait()
    get_kv.wait()
    stay_heads.wait()
    swap_heads.wait()
    pairs = wide // LANES
    for j in range(pairs):
        cols = pl.ds(j * LANES, LANES)
        attend_back_kernel(
            tile,
            scale,
            Q.at[pl.ds(j, 1)],
            S.at[:, pl.ds(width + j * LANES, LANES)],
            S.at[:, pl.ds(width + wide + j * LANES, LANES)],
            K,
            E.at[:, cols],
            DH.at[:, cols],
            H.at[:, cols],
            H.at[:, pl.ds(wide + j * LANES, LANES)],
            P2.at[width : 2 * width, pl.ds(wide + j * LANES, LANES)],
            acc_k,
            acc_v,
        )
        if j == 0:
            swap_side.wait()

            @pl.loop(0, n_dp)
            def _(slot):
                rows = span(slot, shard)
                value = O[rows, my_cols].astype(F32) + side1[rows, :].astype(F32)
                side0[rows, :] = value.astype(BF16)

            u_out.start()
            for s in far_first[:2]:
                u_fc.middle(s)
        if j == 1:
            for s in far_first[2:]:
                u_fc.middle(s)
            for s in far_first[:-1]:
                u_proj.along(s)
        if j == 2:
            for s in far_first[:1]:
                u_fc.settle(s)
                u_fc.along(s)
            for s in far_first[:2]:
                u_out.middle(s)
        if j == 3:
            u_line.settle()
            for s in far_first[1:2]:
                u_fc.settle(s)
                u_fc.along(s)
            for s in far_first[2:]:
                u_out.middle(s)
    get_h1.wait()

    @pl.loop(0, width // tile)
    def _(b):
        F[span(b), 0 : 2 * wide] = matmul_tn(S[:, span(b)], H[...]).astype(BF16)
        value = matmul_tn(S[:, span(b)], P2[width : 2 * width, wide : 2 * wide])
        F[span(b), 2 * wide : 3 * wide] = value.astype(BF16)

    u_qkv.start(near=False)
    VG[2:3, my_cols] = column_sum(H[:, 0:wide].astype(F32))
    VG[3:4, my_cols] = column_sum(P2[width : 2 * width, wide : 2 * wide].astype(F32))
    get_hid = fetch(1, hid_h, S)
    for copy in get_qkv:
        copy.wait()

    def input_part(first, b):
        rows = pl.ds(pl.multiple_of(first, rows_own), rows_own)
        below = pl.ds(pl.multiple_of(width + first, rows_own), rows_own)
        after = pl.ds(pl.multiple_of(width + b * tile, tile), tile)
        part = matmul_nt(P2[below, wide : 2 * wide], P2[after, 0:wide])
        return part + matmul_nt(H[rows, :], P2[span(b), :])

    @pl.loop(0, width // tile)
    def _(b):
        SB[:, span(b)] = input_part(sib[1] * rows_own, b).astype(BF16)

    swap_one = exchange(4, SB, R3)
    for s in far_first[2:]:
        u_fc.settle(s)
        if s:
            u_fc.along(s)

    @pl.loop(0, width // tile)
    def _(b):
        PF[:, span(b)] = input_part(pc.c * rows_own, b)

    get_tokens.wait()
    swap_one.wait()

    def last_norm(b):
        rows = span(b, LANES)
        grad = PF[rows, :] + R3[rows, :].astype(F32)
        back, terms = norm_back(T[rows, :].astype(F32), vec[0:1, :], grad)
        M[rows, :] += back
        VG[0:1, :] += column_sum(terms)
        VG[1:2, :] += column_sum(grad)

    norm_blocks = rows_own // LANES
    for s in far_first[:2]:
        u_qkv.middle(s, near=True)
    pl.loop(0, norm_blocks // 2)(last_norm)
    u_line.turn()
    for s in far_first[2:]:
        u_qkv.middle(s, near=True)
    pl.loop(norm_blocks // 2, norm_blocks)(last_norm)
    get_mid_again = fetch(21, mid_h, PF)
    put_input = pltpu.make_async_copy(M, input_o, load.at[20])
    put_input.start()
    per = n_dp // (width // LANES)
    for slot in range(n_dp):
        t = slot // per
        at = slot % PLANE, slot // PLANE
        SG[*at, 0:8, :] = VG[0:8, t * LANES : (t + 1) * LANES]
        SG[*at, 8:16, :] = jnp.broadcast_to(fcg[:, slot * LANES : (slot + 1) * LANES], (8, LANES))
    u_small.start()
    u_proj.finish(totals[0])
    at = pl.multiple_of(pc.c * piece + cut, cut)
    pending += give(0, totals[0], proj_o.at[pl.ds(at, cut)])
    u_proj.drain()
    u_line.finish(totals[5])
    pending += give(5 + n_dp, totals[5], proj_o.at[pl.ds(pl.multiple_of(pc.c * piece, cut), cut)])
    u_line.drain()
    get_proj = fetch(2, w_proj_h, GP)
    u_fc.finish(totals[1])

    @pl.loop(0, n_dp)
    def _(j):
        dst = fc_o.at[:, pl.ds(pl.multiple_of((j * n_blk + pc.c) * piece, piece), piece)]
        give(1 + j, totals[1].at[:, span(j, piece)], dst)

    get_hid.wait()
    get_proj.wait()

    def layer_part(rows, b):
        return matmul(S[rows, :], GP[:, span(b)])

    @pl.loop(0, width // tile)
    def _(b):
        SB[:, span(b)] = layer_part(theirs, b).astype(BF16)

    swap_out = exchange(0, SB, R1)
    for s in far_first:
        u_out.settle(s)
        if s:
            u_out.along(s)
    get_mid_again.wait()

    @pl.loop(0, width // tile)
    def _(b):
        PF[:, span(b)] += layer_part(mine, b)

    for s in far_first[:2]:
        u_qkv.settle(s)
        u_qkv.along(s)
    u_small.middle()
    swap_out.wait()

    @pl.loop(0, rows_own // LANES)
    def _(b):
        rows = span(b, LANES)
        value = PF[rows, :] + R1[rows, :].astype(F32) + vec[7:8, :]
        R1[rows, :] = value.astype(BF16)

    put_layer = pltpu.make_async_copy(R1, layer_o, load.at[15])
    put_layer.start()
    u_out.finish(totals[3])
    pending += give(4 + n_dp, totals[3], out_o.at[:, my_cols])
    for s in far_first[2:]:
        u_qkv.settle(s)
        if s:
            u_qkv.along(s)
    u_small.finish(totals[4])
    swap_small = exchange(5, totals[4], small_in)
    u_qkv.finish(totals[2])
    for j in range(3):
        at = pl.ds(pl.multiple_of(pc.c * wide, LANES) + j * width, wide)
        pending += give(1 + n_dp + j, totals[2].at[:, j * wide : (j + 1) * wide], qkv_o.at[:, at])
    swap_small.wait()
    low = jnp.where(pc.c == 0, totals[4][...], small_in[...])
    high = jnp.where(pc.c == 0, small_in[...], totals[4][...])
    small_o[0:8, :] = low[0:8] + high[0:8]
    small_o[8:16, :] = low[8:16]
    small_o[16:24, :] = high[8:16]

    @pl.loop(0, n_dp)
    def _(j):
        dst = fc_o.at[:, pl.ds(pl.multiple_of((j * n_blk + pc.c) * piece, piece), piece)]
        src = totals[1].at[:, span(j, piece)]
        pltpu.make_async_copy(src, dst, last.at[0, 1 + j]).wait()
        remote(src, dst, last.at[1, 1 + j], last.at[2, 1 + j], sib).wait()

    for copy in pending:
        copy.wait()
    put_layer.wait()
    put_input.wait()
    for unit in (u_fc, u_qkv, u_out):
        unit.drain()


def backward(n_dp, n_blk, scale, saved, tokens):
    rows_own, width = tokens.shape
    total = n_blk * rows_own
    wide = width // n_blk
    w_proj = saved[3]
    ff = w_proj.shape[0]
    piece, shard, length = ff // n_dp, width // n_dp, n_dp // PLANE
    square, long, own = ((total, width), BF16), ((total, ff), BF16), ((rows_own, width), BF16)
    own_f32 = ((rows_own, width), F32)
    sizes = [
        ((piece // 2, width), BF16),
        ((shard, ff), BF16),
        ((shard, 3 * wide), BF16),
        ((shard, wide), BF16),
        ((16, LANES), F32),
    ]
    scratch = [((ff, width), BF16), long, square, long, square, long, own_f32, own]
    scratch += [((width, width), BF16), (saved[9].shape, BF16), ((total, wide), BF16)]
    scratch += [((total, LANES), BF16), ((ff, width), BF16)]
    scratch += [((width, wide), BF16)] * 2 + [own] * 3 + [((total, wide), BF16), own, own_f32]
    scratch += [((total, LANES), F32)] * 2 + [((8, width), F32), ((1, ff), F32)]
    scratch += [((PLANE, length, 16, LANES), F32), ((16, LANES), F32)]
    for size, kind in sizes[:4]:
        scratch += [((length,) + size, kind)] * 4
    one = ((length, 16, LANES), F32)
    scratch += [((PLANE - 1,) + one[0], F32), one, one]
    half, quarter = (piece // 2, width), (piece // 4, width)
    scratch += [((PLANE, length + 1) + half, BF16), ((2,) + quarter, BF16), ((2,) + half, BF16)]
    scratch += [(size, F32) for size, _ in sizes] + [(half, F32)]
    outs = [own, own_f32, ((n_blk * piece, width), F32), ((shard, n_blk * ff), F32)]
    outs += [((shard, 3 * width), F32), ((shard, width), F32), ((24, LANES), F32)]
    hbm = pl.BlockSpec(memory_space=pl.ANY)
    vmem = pl.BlockSpec(memory_space=pltpu.VMEM)
    return pl.pallas_call(
        functools.partial(backward_kernel, n_dp, n_blk, scale),
        out_shape=[jax.ShapeDtypeStruct(*o) for o in outs],
        in_specs=[vmem if i == 4 else hbm for i in range(18)],
        out_specs=[hbm] * 6 + [vmem],
        scratch_shapes=[pltpu.VMEM(*s) for s in scratch]
        + [
            pltpu.SemaphoreType.DMA((7, 5, length)),
            pltpu.SemaphoreType.DMA((7, 5, length)),
            pltpu.SemaphoreType.DMA((2, 6)),
            pltpu.SemaphoreType.DMA((22,)),
            pltpu.SemaphoreType.DMA((3, 6 + n_dp)),
        ],
        compiler_params=pltpu.CompilerParams(
            collective_id=3, has_side_effects=True, vmem_limit_bytes=VMEM_BACK
        ),
    )(*saved, tokens)


def columns_spec(rows, first):
    return pl.BlockSpec((rows, LANES), lambda j: (0, first + j))


def attend_step(block, scale, q_ref, k_ref, v_ref, key_aug, query_aug, slopes, out_ref, qx_ref):
    j = pl.program_id(0)
    pair = [slopes[2 * j + hh] for hh in range(2)]
    attend_kernel(block, scale, q_ref, k_ref, v_ref, key_aug, query_aug, pair, out_ref, qx_ref)


def attend(qkv, key_aug, query_aug, slopes, scale):
    total, wide = qkv.shape[0], qkv.shape[1] // 3
    pairs = wide // LANES
    block = math.gcd(total, 256)
    whole = pl.BlockSpec((total, LANES), lambda j: (0, 0))
    return pl.pallas_call(
        functools.partial(attend_step, block, scale),
        grid=(pairs,),
        out_shape=[
            jax.ShapeDtypeStruct((total, wide), BF16),
            jax.ShapeDtypeStruct((pairs, 2, total, LANES), BF16),
        ],
        in_specs=[
            columns_spec(total, 0),
            columns_spec(total, pairs),
            columns_spec(total, 2 * pairs),
            whole,
            whole,
            pl.BlockSpec(memory_space=pltpu.SMEM),
        ],
        out_specs=[
            columns_spec(total, 0),
            pl.BlockSpec((1, 2, total, LANES), lambda j: (j, 0, 0, 0)),
        ],
        compiler_params=pltpu.CompilerParams(vmem_limit_bytes=VMEM_BYTES),
    )(qkv, qkv, qkv, key_aug, query_aug, slopes)


def attend_back(query_ext, qkv, key_aug, attended, grad, scale):
    total, wide = attended.shape
    pairs = wide // LANES
    block = math.gcd(total, 256)
    whole = pl.BlockSpec((total, LANES), lambda j: (0, 0))
    out = jax.ShapeDtypeStruct((total, wide), BF16)
    return pl.pallas_call(
        functools.partial(attend_back_kernel, block, scale),
        grid=(pairs,),
        out_shape=[out] * 3,
        in_specs=[
            pl.BlockSpec((1, 2, total, LANES), lambda j: (j, 0, 0, 0)),
            columns_spec(total, pairs),
            columns_spec(total, 2 * pairs),
            whole,
            columns_spec(total, 0),
            columns_spec(total, 0),
        ],
        out_specs=[columns_spec(total, 0)] * 3,
        scratch_shapes=[pltpu.VMEM((total, LANES), F32)] * 2,
        compiler_params=pltpu.CompilerParams(vmem_limit_bytes=VMEM_BYTES),
    )(query_ext, qkv, qkv, key_aug, attended, grad)


def attention_terms(positions, rows):
    high = (positions // 256) * 256
    low = positions - high
    first = rows == 0
    one = jnp.ones_like(positions)
    zero = jnp.zeros_like(positions)

    def table(columns):
        cols = jnp.stack([col.astype(F32) for col in columns], axis=1)
        cols = jnp.pad(cols, ((0, 0), (0, LANES // 2 - len(columns))))
        return jnp.concatenate([cols, cols], axis=1).astype(BF16)

    key_aug = table([high, high, high, low, low, low, first, ~first, one, one, one])
    other = jnp.where(first, 0.0, MASKED)
    query_aug = table([zero] * 6 + [other, jnp.where(first, MASKED, 0.0)])
    return key_aug, query_aug


def body(
    n_dp,
    n_blk,
    tokens,
    positions,
    row_ids,
    alibi_slope,
    ln1_gain,
    ln1_bias,
    qkv_weight,
    query_bias,
    value_bias,
    out_weight,
    out_bias,
    ln2_gain,
    ln2_bias,
    fc_weight,
    fc_bias,
    proj_weight,
    proj_bias,
    out_grad,
):
    local, width = tokens.shape
    heads = alibi_slope.shape[0]
    hidden_all = fc_weight.shape[1]
    scale = 1.0 / math.sqrt(width // heads)
    c = lax.axis_index("blk")
    dp = lax.axis_index("dp")
    wide = width // n_blk
    shard = width // n_dp
    piece = hidden_all // (n_dp * n_blk)
    total = n_blk * local

    def swap(a):
        return lax.ppermute(a, "blk", [(0, 1), (1, 0)])

    def blk_gather(a):
        if n_blk != 2:
            return lax.all_gather(a, "blk", axis=0, tiled=True)
        other = swap(a)
        return jnp.where(
            c == 0, jnp.concatenate([a, other], 0), jnp.concatenate([other, a], 0)
        )

    def blk_sum(a):
        if n_blk != 2:
            return lax.psum_scatter(a.astype(BF16), "blk", scatter_dimension=0, tiled=True).astype(F32)
        own = lax.dynamic_slice_in_dim(a, c * local, local, 0)
        other = lax.dynamic_slice_in_dim(a, (1 - c) * local, local, 0)
        return own + swap(other.astype(BF16)).astype(F32)

    def to_tokens(a):
        if n_blk != 2:
            moved = lax.all_to_all(a.reshape(n_blk, local, wide), "blk", 0, 0)
            return jnp.transpose(moved, (1, 0, 2)).reshape(local, width)
        own = lax.dynamic_slice_in_dim(a, c * local, local, 0)
        other = swap(lax.dynamic_slice_in_dim(a, (1 - c) * local, local, 0))
        return jnp.where(
            c == 0, jnp.concatenate([own, other], 1), jnp.concatenate([other, own], 1)
        )

    def to_heads(a):
        if n_blk != 2:
            moved = lax.all_to_all(
                jnp.transpose(a.reshape(local, n_blk, wide), (1, 0, 2)), "blk", 0, 0
            )
            return moved.reshape(total, wide)
        own = lax.dynamic_slice_in_dim(a, c * wide, wide, 1)
        other = swap(lax.dynamic_slice_in_dim(a, (1 - c) * wide, wide, 1))
        return jnp.where(
            c == 0, jnp.concatenate([own, other], 0), jnp.concatenate([other, own], 0)
        )

    def mine(a, axis, size):
        return lax.dynamic_slice_in_dim(a, c * size, size, axis)

    vectors = [ln1_gain, ln1_bias, query_bias, value_bias, out_bias, ln2_gain, ln2_bias, proj_bias]
    if n_blk == 2 and piece == LANES:
        weights = (qkv_weight, out_weight, fc_weight, proj_weight)
        saved = forward(
            n_dp, n_blk, scale, *weights, tokens, out_grad, positions, row_ids, alibi_slope, fc_bias, vectors
        )
        saved = [a if i == 9 else a.reshape(-1, a.shape[-1]) for i, a in enumerate(saved)]
        outs = backward(n_dp, n_blk, scale, saved, tokens)
        layer_output, input_grad, proj_sum, fc_sum, qkv_sum, out_sum, smalls = outs
        at = lax.rem(dp * shard, LANES)
        part = lax.dynamic_slice_in_dim(smalls[0:8], at, shard, 1)
        g_fc = smalls[8:24:8].reshape(n_blk * piece)
        return (
            layer_output,
            input_grad,
            part[0],
            part[1],
            qkv_sum,
            part[2],
            part[3],
            out_sum,
            part[4],
            part[5],
            part[6],
            fc_sum,
            g_fc,
            proj_sum,
            part[7],
        )

    qkv_own = jnp.concatenate(
        [mine(qkv_weight[:, i * width : (i + 1) * width], 1, wide) for i in range(3)], 1
    ).astype(BF16)
    out_own = mine(out_weight, 1, wide).astype(BF16)
    fc_own = mine(fc_weight.reshape(shard, n_dp, n_blk, piece), 2, 1).reshape(shard, n_dp * piece)
    proj_own = mine(proj_weight, 0, piece)
    vectors.append(mine(fc_bias, 0, piece))
    small = jnp.stack(
        [
            lax.dynamic_update_slice_in_dim(
                jnp.zeros((LANES,), F32), vec, lax.rem(dp * vec.shape[0], LANES), 0
            )
            for vec in vectors
        ]
    )
    small = jnp.pad(small, ((0, 16 - len(vectors)), (0, 0))).astype(BF16)
    inputs = tokens.astype(F32)
    grad_top = out_grad.astype(F32)
    shards = (qkv_own, out_own, fc_own.astype(BF16), proj_own.astype(BF16), small)
    full_qkv, full_out, full_fc, full_proj, full_small = gather_weights(
        n_dp, n_blk, *shards
    )
    weight_qkv = full_qkv.reshape(width, 3 * wide)
    weight_out = full_out.reshape(width, width)
    weight_fc = full_fc.reshape(width, n_dp * piece)
    weight_proj = full_proj.reshape(n_dp * piece, width)
    spread = full_small.astype(F32)

    def vector(i):
        size = vectors[i].shape[0]
        per = LANES // size
        rows = jnp.sum(spread[:, i].reshape(n_dp // per, per, LANES), axis=1)
        return rows.reshape(n_dp * size)

    gain_one, bias_one, bias_query, bias_value, bias_out, gain_two, bias_two, bias_proj, bias_fc = (
        vector(i) for i in range(len(vectors))
    )
    place = blk_gather(jnp.stack([positions, row_ids], axis=1))
    key_aug, query_aug = attention_terms(place[:, 0], place[:, 1])
    every_token = blk_gather(tokens).astype(F32)
    every_grad = blk_gather(out_grad)
    normed = layer_norm(every_token, gain_one, bias_one).astype(BF16)
    bias_qkv = jnp.concatenate(
        [mine(bias_query, 0, wide), jnp.zeros((wide,), F32), mine(bias_value, 0, wide)]
    )
    mixed = (matmul(normed, weight_qkv) + bias_qkv).astype(BF16)
    slopes = mine(alibi_slope, 0, heads // n_blk)
    attended_heads, query_ext = attend(mixed, key_aug, query_aug, slopes, scale)
    attended = to_tokens(attended_heads)
    middle = inputs + matmul(attended, weight_out) + bias_out
    normed_two = layer_norm(middle, gain_two, bias_two).astype(BF16)
    every_two = blk_gather(normed_two)
    hidden_pre = matmul(every_two, weight_fc) + bias_fc
    hidden_vals, gelu_slope = gelu_pair(hidden_pre)
    hidden = hidden_vals.astype(BF16)
    grad_proj_weight = matmul_tn(hidden, every_grad).astype(BF16)
    layer_output = (middle + blk_sum(matmul(hidden, weight_proj)) + bias_proj).astype(BF16)
    grad_proj_bias = jnp.sum(grad_top, axis=0)
    grad_pre = (gelu_slope * matmul_nt(every_grad, weight_proj)).astype(BF16)
    grad_fc_weight = matmul_tn(every_two, grad_pre).astype(BF16)
    grad_fc_bias = jnp.sum(grad_pre.astype(F32), axis=0)
    grad_normed_two = blk_sum(matmul_nt(grad_pre, weight_fc))
    _, norm_two_back = jax.vjp(layer_norm, middle, gain_two, bias_two)
    grad_mid_norm, grad_gain_two, grad_bias_two = norm_two_back(grad_normed_two)
    grad_middle = grad_top + grad_mid_norm
    grad_branch = grad_middle.astype(BF16)
    grad_out_weight = matmul_tn(attended, grad_branch).astype(BF16)
    grad_out_bias = jnp.sum(grad_branch.astype(F32), axis=0)
    grad_heads = to_heads(matmul_nt(grad_branch, weight_out).astype(BF16))
    grad_mixed = jnp.concatenate(
        attend_back(query_ext, mixed, key_aug, attended_heads, grad_heads, scale), axis=1
    )
    grad_qkv_weight = matmul_tn(normed, grad_mixed).astype(BF16)
    sums = jnp.sum(grad_mixed.astype(F32), axis=0)
    grad_normed = blk_sum(matmul_nt(grad_mixed, weight_qkv))
    _, norm_one_back = jax.vjp(layer_norm, inputs, gain_one, bias_one)
    grad_in_norm, grad_gain_one, grad_bias_one = norm_one_back(grad_normed)
    input_grad = grad_middle + grad_in_norm

    proj_sum, fc_sum, out_sum, qkv_sum = scatter_grads(
        n_dp,
        n_blk,
        grad_proj_weight.reshape(n_dp, piece, width),
        grad_fc_weight.reshape(n_dp, shard, n_dp * piece),
        grad_out_weight.reshape(n_dp, shard, width),
        grad_qkv_weight.reshape(n_dp, shard, 3 * wide),
    )

    def spread_out(vec, size):
        parts = vec.reshape(-1, 1, size)
        return jnp.where((jnp.arange(n_blk) == c)[None, :, None], parts, 0.0).reshape(-1)

    small_grads = [
        grad_gain_one,
        grad_bias_one,
        spread_out(sums[:wide], wide),
        spread_out(sums[2 * wide :], wide),
        grad_out_bias,
        grad_gain_two,
        grad_bias_two,
        grad_proj_bias,
        spread_out(grad_fc_bias, piece),
    ]
    small_sum = lax.psum(jnp.concatenate(small_grads), ("dp", "blk"))
    finals = []
    at = 0
    for vec in small_grads:
        size = vec.shape[0]
        finals.append(lax.dynamic_slice_in_dim(small_sum, at + dp * (size // n_dp), size // n_dp, 0))
        at += size
    g_gain1, g_bias1, g_query, g_value, g_out, g_gain2, g_bias2, g_proj, g_fc = finals
    final_qkv = jnp.transpose(qkv_sum.reshape(n_blk, shard, 3, wide), (1, 2, 0, 3))
    final_fc = jnp.transpose(fc_sum.reshape(n_blk, shard, n_dp, piece), (1, 2, 0, 3))
    return (
        layer_output,
        input_grad,
        g_gain1,
        g_bias1,
        final_qkv.reshape(shard, 3 * width),
        g_query,
        g_value,
        jnp.transpose(out_sum, (1, 0, 2)).reshape(shard, width),
        g_out,
        g_gain2,
        g_bias2,
        final_fc.reshape(shard, hidden_all),
        g_fc,
        proj_sum.reshape(n_blk * piece, width),
        g_proj,
    )


def solution(mesh):
    both, rows, one = P(("dp", "blk"), None), P("dp", None), P("dp")
    tokens = P(("dp", "blk"))
    in_specs = (both, tokens, tokens, P(), one, one, rows, one, one, rows, one, one, one, rows, one, rows, one, both)
    out_specs = (both, both, one, one, rows, one, one, rows, one, one, one, rows, one, rows, one)
    return jax.shard_map(
        functools.partial(body, mesh.shape["dp"], mesh.shape["blk"]),
        mesh=mesh,
        in_specs=in_specs,
        out_specs=out_specs,
        check_vma=False,
    )
```

```python
import functools
import math

import jax
import jax.numpy as jnp
from jax import lax
from jax.experimental import pallas as pl
from jax.experimental.pallas import tpu as pltpu
from jax.sharding import PartitionSpec as P

EPSILON = 1e-05
MASKED = -1e30
BF16 = jnp.bfloat16
F32 = jnp.float32
MESH = pl.DeviceIdType.MESH
PLANE = 4
LANES = 128
VMEM_BYTES = 58 * 2**20
VMEM_BACK = 63 * 2**20


def matmul(left, right):
    return jnp.dot(left, right, preferred_element_type=F32)


def matmul_tn(left, right):
    return lax.dot_general(left, right, (((0,), (0,)), ((), ())), preferred_element_type=F32)


def matmul_nt(left, right):
    return lax.dot_general(left, right, (((1,), (1,)), ((), ())), preferred_element_type=F32)


def layer_norm(inputs, gain_vec, bias_vec):
    row_mean = jnp.mean(inputs, axis=-1, keepdims=True)
    centred = inputs - row_mean
    spread = jnp.mean(centred * centred, axis=-1, keepdims=True)
    return centred * lax.rsqrt(spread + EPSILON) * gain_vec + bias_vec


class Place:
    def __init__(self, n_dp, n_blk):
        self.n_dp, self.n_blk, self.length = n_dp, n_blk, n_dp // PLANE
        self.dp, self.c = lax.axis_index("dp"), lax.axis_index("blk")
        self.z, self.p = self.dp // PLANE, lax.rem(self.dp, PLANE)
        side, row = lax.rem(self.p, 2), self.p // 2
        self.flip_x, self.flip_y = self.p + 1 - 2 * side, self.p + 2 - 4 * row
        self.diag = PLANE - 1 - self.p

    def routes(self, zz):
        odd = lax.rem(zz, 2)
        return (
            self.flip_x * (1 - odd) + self.flip_y * odd,
            self.flip_x * odd + self.flip_y * (1 - odd),
        )

    def at(self, zz, pp):
        return (zz * PLANE + pp, self.c)

    def sibling(self, k):
        return (self.dp, lax.rem(self.c + k, self.n_blk))

    def apart(self, s, run):
        if s == 0:
            run(self.z)
            return

        @pl.loop(0, 2)
        def _(k):
            zz = self.z + s * (1 - 2 * k)
            pl.when((zz >= 0) & (zz < self.length))(lambda: run(zz))

    def up_down(self, run_up, run_down):
        pl.when(self.z < self.length - 1)(run_up)
        pl.when(self.z > 0)(run_down)

    def greet(self):
        barrier = pltpu.get_barrier_semaphore()

        def hello(device):
            pl.semaphore_signal(barrier, inc=1, device_id=device, device_id_type=MESH)

        hello(self.at(self.z, self.flip_x))
        hello(self.at(self.z, self.flip_y))
        hello(self.at(self.z, self.diag))
        for k in range(1, self.n_blk):
            hello(self.sibling(k))

        @pl.loop(1, self.length)
        def _(k):
            hello(self.at(lax.rem(self.z + k, self.length), self.p))

        pl.semaphore_wait(barrier, self.n_blk + self.length + 1)


def remote(src, dst, send_sem, recv_sem, device):
    return pltpu.make_async_remote_copy(
        src_ref=src,
        dst_ref=dst,
        send_sem=send_sem,
        recv_sem=recv_sem,
        device_id=device,
        device_id_type=MESH,
    )


class Gather:
    def __init__(self, place, unit, chunk, send, recv):
        self.place, self.chunk = place, chunk
        self.send = lambda kind, zz: send.at[unit, kind, zz]
        self.recv = lambda slot: recv.at[unit, slot]

    def copy(self, slot, kind, zz, device):
        piece = self.chunk(slot)
        return remote(piece, piece, self.send(kind, zz), self.recv(slot), device)

    def arrived(self, slot):
        self.copy(slot, 0, 0, self.place.sibling(1)).wait_recv()

    def line(self):
        pc = self.place
        pc.up_down(
            lambda: self.copy(pc.dp, 3, pc.z, pc.at(pc.z + 1, pc.p)).start(),
            lambda: self.copy(pc.dp, 4, pc.z, pc.at(pc.z - 1, pc.p)).start(),
        )

    def along(self, s):
        pc = self.place

        def pass_on(zz):
            slot = zz * PLANE + pc.p
            self.arrived(slot)
            below = jnp.where(zz < pc.z, 1, 0)
            onward = pc.z + 2 * below - 1
            more = (onward >= 0) & (onward < pc.length)
            pl.when(more)(lambda: self.copy(slot, 3, zz, pc.at(onward, pc.p)).start())

        pc.apart(s, pass_on)

    def ring(self, s):
        pc = self.place

        def both(zz):
            slot = zz * PLANE + pc.p
            self.copy(slot, 0, zz, pc.at(pc.z, pc.flip_x)).start()
            self.copy(slot, 1, zz, pc.at(pc.z, pc.flip_y)).start()

        pc.apart(s, both)

    def across(self, s):
        pc = self.place

        def turn(zz):
            near, far = pc.routes(zz)
            slot = zz * PLANE + near
            self.arrived(slot)
            self.copy(slot, 2, zz, pc.at(pc.z, far)).start()

        pc.apart(s, turn)

    def finish(self):
        pc = self.place

        @pl.loop(0, pc.length)
        def _(zz):
            self.arrived(zz * PLANE + pc.routes(zz)[1])
            self.arrived(zz * PLANE + pc.diag)

    def drain(self):
        pc = self.place

        def sent(kind, zz):
            self.copy(pc.dp, kind, zz, pc.sibling(1)).wait_send()

        @pl.loop(0, pc.length)
        def _(zz):
            sent(0, zz)
            sent(1, zz)
            sent(2, zz)
            pl.when((zz <= pc.z) & (pc.z < pc.length - 1))(lambda: sent(3, zz))
            pl.when((zz > pc.z) & (pc.z > 0))(lambda: sent(3, zz))

        pl.when(pc.z > 0)(lambda: sent(4, pc.z))


class RingGather:
    def __init__(self, place, unit, chunk, part, send, recv):
        self.place, self.chunk, self.part = place, chunk, part
        self.lift = lambda pp, zz: send.at[unit, pp, zz]
        self.side = lambda k: send.at[unit + 1, 0, k]
        self.recv = lambda slot: recv.at[unit, slot]
        self.other = recv.at[unit + 1, 0]

    def copy(self, piece, sem, recv, device):
        return remote(piece, piece, sem, recv, device)

    def arrived(self, slot):
        self.copy(self.chunk(slot), self.side(0), self.recv(slot), self.place.sibling(1)).wait_recv()

    def start(self):
        pc = self.place
        piece, recv = self.chunk(pc.dp), self.recv(pc.dp)
        self.copy(piece, self.side(0), recv, pc.at(pc.z, pc.flip_x)).start()
        self.copy(piece, self.side(1), recv, pc.at(pc.z, pc.flip_y)).start()

    def across(self):
        pc = self.place
        base = pc.z * PLANE
        self.arrived(base + pc.flip_x)
        half = self.part(base + pc.flip_x, 0)
        self.copy(half, self.side(2), self.recv(base + pc.flip_x), pc.at(pc.z, pc.flip_y)).start()
        self.arrived(base + pc.flip_y)
        half = self.part(base + pc.flip_y, 1)
        self.copy(half, self.side(3), self.other, pc.at(pc.z, pc.flip_x)).start()

    def rise(self):
        pc = self.place
        slot = pc.z * PLANE + pc.diag
        for i, recv in enumerate((self.recv(slot), self.other)):
            self.copy(self.part(slot, i), self.side(0), recv, pc.sibling(1)).wait_recv()

        @pl.loop(0, PLANE)
        def _(pp):
            at = pc.z * PLANE + pp
            piece = self.chunk(at)

            def to(sem, zz):
                self.copy(piece, sem, self.recv(at), pc.at(zz, pc.p)).start()

            pc.up_down(
                lambda: to(self.lift(pp, pc.z), pc.z + 1), lambda: to(self.lift(4, pp), pc.z - 1)
            )

    def along(self, s):
        pc = self.place

        def pass_on(zz):
            below = jnp.where(zz < pc.z, 1, 0)
            onward = pc.z + 2 * below - 1

            @pl.loop(0, PLANE)
            def _(pp):
                slot = zz * PLANE + pp
                self.arrived(slot)
                copy = self.copy(
                    self.chunk(slot), self.lift(pp, zz), self.recv(slot), pc.at(onward, pc.p)
                )
                pl.when((onward >= 0) & (onward < pc.length))(copy.start)

        pc.apart(s, pass_on)

    def drain(self):
        pc = self.place
        piece = self.chunk(pc.dp)

        def sent(sem, view=piece):
            self.copy(view, sem, self.recv(pc.dp), pc.sibling(1)).wait_send()

        sent(self.side(0))
        sent(self.side(1))
        sent(self.side(2), self.part(pc.dp, 0))
        sent(self.side(3), self.part(pc.dp, 1))

        @pl.loop(0, PLANE)
        def _(pp):
            @pl.loop(0, pc.length)
            def _(zz):
                pl.when((zz <= pc.z) & (pc.z < pc.length - 1))(lambda: sent(self.lift(pp, zz)))
                pl.when((zz > pc.z) & (pc.z > 0))(lambda: sent(self.lift(pp, zz)))

            pl.when(pc.z > 0)(lambda: sent(self.lift(4, pp)))


def gather_kernel(
    n_dp, n_blk, qkv, out, fc, proj, small, all_qkv, all_out, all_fc, all_proj, all_small, send, recv, local, side
):
    pc = Place(n_dp, n_blk)
    wide = out.shape[1]
    mine = pl.ds(pl.multiple_of(pc.c * wide, LANES), wide)
    parts = [
        (small, lambda slot: all_small.at[slot]),
        (qkv, lambda slot: all_qkv.at[slot]),
        (out, lambda slot: all_out.at[slot, :, mine]),
        (fc, lambda slot: all_fc.at[slot]),
        (proj, lambda slot: all_proj.at[slot]),
    ]
    for i, (own, chunk) in enumerate(parts):
        pltpu.make_async_copy(own, chunk(pc.dp), local.at[i]).start()
    pc.greet()
    for i, (own, chunk) in enumerate(parts):
        pltpu.make_async_copy(own, chunk(pc.dp), local.at[i]).wait()
    units = [Gather(pc, i, chunk, send, recv) for i, (_, chunk) in enumerate(parts)]
    steps = range(pc.length)
    for i, unit in enumerate(units):
        unit.line()
        for s in steps:
            if s:
                unit.along(s)
            unit.ring(s)
        if i > 0:
            for s in steps:
                units[i - 1].across(s)
            units[i - 1].finish()
    for s in steps:
        units[4].across(s)
    side_copies = []
    piece = all_out.at[:, :, mine]
    for k in range(1, n_blk):
        copy = remote(piece, piece, side.at[0, k], side.at[1, k], pc.sibling(k))
        copy.start()
        side_copies.append(copy)
    units[4].finish()
    for copy in side_copies:
        copy.wait()
    for unit in units:
        unit.drain()


class Scatter:
    def __init__(self, place, unit, chunk, bufs, send, recv, source=None):
        self.place, self.chunk, self.source = place, chunk, source or chunk
        self.diag, self.near, self.far, self.line = bufs
        self.kind = self.near.dtype
        self.send = lambda kind, zz: send.at[unit, kind, zz]
        self.recv = lambda kind, zz: recv.at[unit, kind, zz]

    def copy(self, src, dst, kind, zz, device):
        return remote(src, dst, self.send(kind, zz), self.recv(kind, zz), device)

    def arrived(self, piece, kind, zz):
        self.copy(piece, piece, kind, zz, self.place.sibling(1)).wait_recv()

    def start(self, near=True):
        pc = self.place
        steps = range(pc.length - 1, -1, -1)

        def first(zz):
            to = pc.at(pc.z, pc.routes(zz)[0])
            self.copy(self.source(zz * PLANE + pc.diag), self.diag.at[zz], 0, zz, to).start()

        for s in steps:
            pc.apart(s, first)
        if near:
            for s in steps:
                pc.apart(s, self.send_near)

    def send_near(self, zz):
        pc = self.place
        near = pc.routes(zz)[0]
        piece = self.source(zz * PLANE + near)
        self.copy(piece, self.near.at[zz], 1, zz, pc.at(pc.z, near)).start()

    def middle(self, s, near=False):
        pc = self.place

        def turn(zz):
            far = pc.routes(zz)[1]
            self.arrived(self.diag.at[zz], 0, zz)
            total = self.diag[zz].astype(F32) + self.chunk(zz * PLANE + far)[...].astype(F32)
            self.diag[zz] = total.astype(self.kind)
            self.copy(self.diag.at[zz], self.far.at[zz], 2, zz, pc.at(pc.z, far)).start()
            if near:
                self.send_near(zz)

        pc.apart(s, turn)

    def settle(self, s):
        pc = self.place

        def add(zz):
            self.arrived(self.near.at[zz], 1, zz)
            self.arrived(self.far.at[zz], 2, zz)
            total = self.near[zz].astype(F32) + self.far[zz].astype(F32)
            total += self.chunk(zz * PLANE + pc.p)[...].astype(F32)
            self.near[zz] = total.astype(self.kind)

        pc.apart(s, add)

    def along(self, s):
        pc = self.place

        def send_on(zz):
            to = pc.at(zz, pc.p)
            sems = self.send(3, zz), self.recv(3, pc.z)
            remote(self.near.at[zz], self.line.at[pc.z], *sems, to).start()

        pc.apart(s, send_on)

    def finish(self, total):
        pc = self.place
        total[...] = self.near[pc.z].astype(F32)

        @pl.loop(1, pc.length)
        def _(k):
            zz = lax.rem(pc.z + k, pc.length)
            self.arrived(self.line.at[zz], 3, zz)
            total[...] += self.line[zz].astype(F32)

    def drain(self):
        pc = self.place

        def sent(kind, zz):
            piece = self.near.at[zz]
            self.copy(piece, piece, kind, zz, pc.sibling(1)).wait_send()

        @pl.loop(0, pc.length)
        def _(zz):
            sent(0, zz)
            sent(1, zz)
            sent(2, zz)
            pl.when(zz != pc.z)(lambda: sent(3, zz))


class LineScatter:
    def __init__(self, place, unit, chunk, bufs, send, recv, source=None):
        self.place, self.chunk, self.source = place, chunk, source or chunk
        self.line, self.half, self.ring = bufs
        self.lift = lambda pp, zz: send.at[unit, pp, zz]
        self.drop = lambda kind, zz: recv.at[unit, kind, zz]
        self.side = lambda k: (send.at[unit + 1, 0, k], recv.at[unit + 1, 0, k])
        self.middle_row = self.half.shape[1]

    def arrived(self, piece, sem):
        remote(piece, piece, self.lift(0, 0), sem, self.place.sibling(1)).wait_recv()

    def along(self, s):
        pc = self.place

        def pass_on(zz):
            above = jnp.where(zz > pc.z, 1, 0)
            onward = pc.z + 2 * above - 1
            before = pc.z - 2 * above + 1
            at = zz if s > 1 else zz * above + pc.length * (1 - above)

            @pl.loop(0, PLANE)
            def _(pp):
                last = pp * (1 - above) + zz * above if s == 1 else zz
                kind = pp if s > 1 else pp * above + PLANE * (1 - above)
                sem = self.drop(kind, last)
                dst, to = self.line.at[pp, at], pc.at(onward, pc.p)
                own = self.chunk(zz * PLANE + pp)

                def plain():
                    first = self.source(zz * PLANE + pp)
                    remote(first, dst, self.lift(pp, zz), sem, to).start()

                def more():
                    piece = self.line.at[pp, zz]
                    self.arrived(piece, self.drop(pp, zz))
                    piece[...] = (piece[...].astype(F32) + own[...].astype(F32)).astype(BF16)
                    remote(piece, dst, self.lift(pp, zz), sem, to).start()

                inside = (before >= 0) & (before < pc.length)
                if s == pc.length - 1:
                    plain()
                else:
                    pl.when(inside)(more)
                    pl.when(jnp.logical_not(inside))(plain)

        pc.apart(s, pass_on)

    def settle(self):
        pc = self.place

        @pl.loop(0, PLANE)
        def _(pp):
            own = self.chunk(pc.z * PLANE + pp)
            piece, over = self.line.at[pp, pc.z], self.line.at[pp, pc.length]

            def below():
                self.arrived(piece, self.drop(pp, pc.z))
                piece[...] = (piece[...].astype(F32) + own[...].astype(F32)).astype(BF16)

            def bottom():
                piece[...] = own[...]

            def above():
                self.arrived(over, self.drop(PLANE, pp))
                piece[...] = (piece[...].astype(F32) + over[...].astype(F32)).astype(BF16)

            pl.when(pc.z > 0)(below)
            pl.when(pc.z == 0)(bottom)
            pl.when(pc.z < pc.length - 1)(above)

        for i, to in enumerate((pc.flip_x, pc.flip_y)):
            rows = pl.ds(i * self.middle_row, self.middle_row)
            piece = self.line.at[pc.diag, pc.z, rows]
            remote(piece, self.half.at[i], *self.side(i), pc.at(pc.z, to)).start()

    def turn(self):
        pc = self.place
        for i, (dest, to) in enumerate(((pc.flip_y, pc.flip_y), (pc.flip_x, pc.flip_x))):
            rows = pl.ds(i * self.middle_row, self.middle_row)
            self.arrived(self.half.at[i], self.side(i)[1])
            value = self.line[dest, pc.z, rows].astype(F32) + self.half[i].astype(F32)
            self.line[dest, pc.z, rows] = value.astype(BF16)
            piece = self.line.at[dest, pc.z]
            remote(piece, self.ring.at[1 - i], *self.side(3 - i), pc.at(pc.z, to)).start()

    def finish(self, total):
        pc = self.place
        value = self.line[pc.p, pc.z].astype(F32)
        for i in range(2):
            self.arrived(self.ring.at[i], self.side(2 + i)[1])
            value += self.ring[i].astype(F32)
        total[...] = value

    def drain(self):
        pc = self.place

        def sent(piece, sem):
            remote(piece, piece, sem, self.drop(0, 0), pc.sibling(1)).wait_send()

        for i in range(2):
            sent(self.half.at[i], self.side(i)[0])
            sent(self.ring.at[i], self.side(2 + i)[0])

        @pl.loop(0, PLANE)
        def _(pp):
            @pl.loop(0, pc.length)
            def _(zz):
                piece = self.line.at[pp, zz]
                pl.when(zz > pc.z)(lambda: sent(piece, self.lift(pp, zz)))
                pl.when(zz < pc.z)(lambda: sent(piece, self.lift(pp, zz)))


class SmallSum:
    def __init__(self, place, unit, chunks, bufs, send, recv):
        self.place, self.chunks = place, chunks
        self.ring, self.sums, self.line = bufs
        self.sems = lambda kind, k: (send.at[unit, kind, k], recv.at[unit, kind, k])

    def flat(self):
        pc = self.place
        dests = ((1, pc.flip_x), (2, pc.flip_y), (3, pc.diag))
        return [
            remote(self.chunks.at[to], self.ring.at[k - 1], *self.sems(0, k), pc.at(pc.z, to))
            for k, to in dests
        ]

    def start(self):
        for copy in self.flat():
            copy.start()

    def middle(self):
        pc = self.place
        for copy in self.flat():
            copy.wait()
        self.sums[...] = self.chunks[pc.p] + self.ring[0] + self.ring[1] + self.ring[2]

        @pl.loop(1, pc.length)
        def _(k):
            zz = lax.rem(pc.z + k, pc.length)
            send, recv = self.sems(1, zz)[0], self.sems(1, pc.z)[1]
            remote(self.sums.at[zz], self.line.at[pc.z], send, recv, pc.at(zz, pc.p)).start()

    def finish(self, total):
        pc = self.place
        total[...] = self.sums[pc.z]

        @pl.loop(1, pc.length)
        def _(k):
            zz = lax.rem(pc.z + k, pc.length)
            piece = self.line.at[zz]
            remote(piece, piece, *self.sems(1, zz), pc.sibling(1)).wait()
            total[...] += self.line[zz]


def scatter_kernel(n_dp, n_blk, *refs):
    grads, outs, rest = refs[:4], refs[4:8], refs[8:]
    bufs, totals, rest = rest[:16], rest[16:20], rest[20:]
    side_buf, send, recv, side, last = rest
    proj, fc, out, qkv = grads
    pc = Place(n_dp, n_blk)
    pc.greet()
    wide = out.shape[2] // n_blk

    def columns(core):
        return pl.ds(pl.multiple_of(core * wide, LANES), wide)

    chunks = [
        lambda slot: proj.at[slot],
        lambda slot: fc.at[slot],
        lambda slot: side_buf.at[0, slot],
        lambda slot: qkv.at[slot],
    ]
    units = [
        Scatter(pc, i, chunks[i], bufs[4 * i : 4 * i + 4], send, recv) for i in range(4)
    ]
    units[0].start()
    units[1].start()
    side_copies = []
    for k in range(1, n_blk):
        dev = pc.sibling(k)
        copy = remote(
            out.at[:, :, columns(dev[1])], side_buf.at[k], side.at[0, k], side.at[1, k], dev
        )
        copy.start()
        side_copies.append(copy)

    def side_sum():
        for copy in side_copies:
            copy.wait()

        @pl.loop(0, n_dp)
        def _(slot):
            total = out[slot, :, columns(pc.c)].astype(F32)
            for k in range(1, n_blk):
                total += side_buf[k, slot].astype(F32)
            side_buf[0, slot] = total.astype(BF16)

    pending = []

    def spread(i):
        units[i].finish(totals[i])
        total = totals[i]
        pieces = [(total, outs[i].at[pc.c])]
        for j, (src, dst) in enumerate(pieces):
            keep = pltpu.make_async_copy(src, dst, last.at[i, 0, 0])
            keep.start()
            pending.append(keep)
            for k in range(1, n_blk):
                copy = remote(src, dst, last.at[i, 0, k], last.at[i, 1, k], pc.sibling(k))
                copy.start()
                pending.append(copy)

    steps = range(pc.length - 1, -1, -1)

    def middle(i):
        for s in steps:
            units[i].middle(s)

    def settle(i):
        for s in steps:
            units[i].settle(s)
            if s:
                units[i].along(s)

    middle(0)
    side_sum()
    units[2].start()
    middle(1)
    units[3].start()
    settle(0)
    middle(2)
    settle(1)
    spread(0)
    middle(3)
    settle(2)
    settle(3)
    spread(1)
    spread(2)
    spread(3)
    for copy in pending:
        copy.wait()
    for unit in units:
        unit.drain()


def gather_weights(n_dp, n_blk, qkv, out, fc, proj, small):
    shards = (qkv, out, fc, proj, small)
    shapes = [
        jax.ShapeDtypeStruct((n_dp, a.shape[0], a.shape[1] * (n_blk if a is out else 1)), BF16)
        for a in shards
    ]
    length = n_dp // PLANE
    hbm = pl.BlockSpec(memory_space=pl.ANY)
    return pl.pallas_call(
        functools.partial(gather_kernel, n_dp, n_blk),
        out_shape=shapes,
        in_specs=[hbm] * 5,
        out_specs=[hbm] * 5,
        scratch_shapes=[
            pltpu.SemaphoreType.DMA((5, 5, length)),
            pltpu.SemaphoreType.DMA((5, n_dp)),
            pltpu.SemaphoreType.DMA((5,)),
            pltpu.SemaphoreType.DMA((2, n_blk)),
        ],
        compiler_params=pltpu.CompilerParams(
            collective_id=0, has_side_effects=True, vmem_limit_bytes=VMEM_BYTES
        ),
    )(*shards)


def scatter_grads(n_dp, n_blk, proj, fc, out, qkv):
    length = n_dp // PLANE
    grads = (proj, fc, out, qkv)
    sizes = [a.shape[1:] for a in grads]
    sizes[2] = (sizes[2][0], sizes[2][1] // n_blk)
    vmem = pl.BlockSpec(memory_space=pltpu.VMEM)
    scratch = []
    for size in sizes:
        scratch += [pltpu.VMEM((length,) + size, BF16)] * 4
    scratch += [pltpu.VMEM(size, F32) for size in sizes]
    scratch += [
        pltpu.VMEM((n_blk, n_dp) + sizes[2], BF16),
        pltpu.SemaphoreType.DMA((4, 5, length)),
        pltpu.SemaphoreType.DMA((4, 5, length)),
        pltpu.SemaphoreType.DMA((2, n_blk)),
        pltpu.SemaphoreType.DMA((4, 2, n_blk)),
    ]
    return pl.pallas_call(
        functools.partial(scatter_kernel, n_dp, n_blk),
        out_shape=[jax.ShapeDtypeStruct((n_blk,) + size, F32) for size in sizes],
        in_specs=[vmem] * 4,
        out_specs=[pl.BlockSpec(memory_space=pl.ANY)] * 4,
        scratch_shapes=scratch,
        compiler_params=pltpu.CompilerParams(
            collective_id=1, has_side_effects=True, vmem_limit_bytes=VMEM_BYTES
        ),
    )(*grads)


def lane_split(value, lane, first, base):
    for i in range(3):
        term = value.astype(BF16)
        base = jnp.where(lane == first + i, term, base)
        value = value - term.astype(F32)
    return base


def causal_tail(scores, block, axis, masked):
    key_axis, query_axis = (0, 1) if axis == 0 else (1, 0)
    tail_shape = (block, block)
    keep = lax.broadcasted_iota(jnp.int32, tail_shape, key_axis) <= lax.broadcasted_iota(
        jnp.int32, tail_shape, query_axis
    )
    size = scores.shape[axis]
    if size == block:
        return jnp.where(keep, scores, masked)
    head = lax.slice_in_dim(scores, 0, size - block, axis=axis)
    tail = jnp.where(keep, lax.slice_in_dim(scores, size - block, size, axis=axis), masked)
    return jnp.concatenate([head, tail], axis=axis)


def causal_all(scores, offset, axis, masked):
    key_axis, query_axis = (0, 1) if axis == 0 else (1, 0)
    keep = (
        lax.broadcasted_iota(jnp.int32, scores.shape, key_axis)
        <= lax.broadcasted_iota(jnp.int32, scores.shape, query_axis) + offset
    )
    return jnp.where(keep, scores, masked)


def query_blocks(total, block, run):
    count = total // block
    if count <= 4:
        for b in range(count):
            run(
                b * block,
                (b + 1) * block,
                lambda scores, axis, masked: causal_tail(scores, block, axis, masked),
            )
    else:

        @pl.loop(0, count)
        def _(b):
            first = pl.multiple_of(b * block, block)
            run(first, total, lambda scores, axis, masked: causal_all(scores, first, axis, masked))


def attend_kernel(block, scale, q_ref, k_ref, v_ref, key_aug, query_aug, slopes, out_ref, qx_ref):
    total = q_ref.shape[0]
    half = LANES // 2
    lane = lax.broadcasted_iota(jnp.int32, (1, LANES), 1)
    slope_rows = []
    for hh in range(2):
        base = half * (1 - hh)
        slope = jnp.full((1, LANES), slopes[hh], F32)
        row = lane_split(slope, lane, base, jnp.zeros((1, LANES), BF16))
        slope_rows.append(lane_split(slope, lane, base + 3, row))

    def run(first, keys, mask):
        rows = pl.ds(first, block)
        result = None
        for hh in range(2):
            own = (lane < half) if hh == 0 else (lane >= half)
            base = half * (1 - hh)
            aug = query_aug[rows, :] + slope_rows[hh]
            query = jnp.where(own, q_ref[rows, :] * BF16(scale), aug)
            key = jnp.where(own, k_ref[0:keys, :], key_aug[0:keys, :])
            value = jnp.where(own, v_ref[0:keys, :], BF16(1))
            scores = mask(matmul_nt(query, key), 1, MASKED)
            top = jnp.max(scores, axis=1, keepdims=True)
            weights = jnp.exp(scores - top).astype(BF16)
            sums = matmul(weights, value)
            log_total = top + jnp.log(sums[:, base : base + 1])
            qx_ref[0, hh, rows, :] = lane_split(-log_total, lane, base + 8, query)
            part = sums / pltpu.roll(sums, half, 1)
            result = part if hh == 0 else jnp.where(own, part, result)
        out_ref[rows, :] = result.astype(BF16)

    query_blocks(total, block, run)


def attend_back_kernel(
    block, scale, qx_ref, k_ref, v_ref, key_aug, out_ref, grad_ref, dq_ref, dk_ref, dv_ref, dk_acc, dv_acc
):
    total = k_ref.shape[0]
    half = LANES // 2
    lane = lax.broadcasted_iota(jnp.int32, (1, LANES), 1)
    dk_acc[...] = jnp.zeros_like(dk_acc)
    dv_acc[...] = jnp.zeros_like(dv_acc)

    def run(first, keys, mask):
        rows = pl.ds(first, block)
        grad = grad_ref[rows, :]
        product = grad.astype(F32) * out_ref[rows, :].astype(F32)
        dq = None
        dk = None
        dv = None
        for hh in range(2):
            own = (lane < half) if hh == 0 else (lane >= half)
            base = half * (1 - hh)
            query = qx_ref[0, hh, rows, :]
            key = jnp.where(own, k_ref[0:keys, :], key_aug[0:keys, :])
            delta = jnp.sum(jnp.where(own, product, 0.0), axis=1, keepdims=True)
            grad_own = jnp.where(own, grad, BF16(0))
            grad_aug = lane_split(-delta, lane, base, grad_own)
            value = jnp.where(own, v_ref[0:keys, :], BF16(1))
            weights = mask(jnp.exp(matmul_nt(key, query)), 0, 0.0)
            change = (weights * matmul_nt(value, grad_aug)).astype(BF16)
            key_own = jnp.where(own, key, BF16(0))
            query_own = jnp.where(own, query, BF16(0))
            dv_part = matmul(weights.astype(BF16), grad_own)
            dk_part = matmul(change, query_own)
            dq_part = matmul_tn(change, key_own)
            dv = dv_part if hh == 0 else dv + dv_part
            dk = dk_part if hh == 0 else dk + dk_part
            dq = dq_part if hh == 0 else dq + dq_part
        dq_ref[rows, :] = (dq * scale).astype(BF16)
        dk_acc[0:keys, :] += dk
        dv_acc[0:keys, :] += dv

    query_blocks(total, block, run)
    dk_ref[...] = dk_acc[...].astype(BF16)
    dv_ref[...] = dv_acc[...].astype(BF16)


def gelu_pair(u):
    k = math.sqrt(2.0 / math.pi)
    square = u * u
    t = jnp.tanh(k * u * (1.0 + 0.044715 * square))
    plus = 0.5 * (1.0 + t)
    slope = plus + (0.5 * k) * u * (1.0 - t * t) * (1.0 + 3 * 0.044715 * square)
    return u * plus, slope


def whole(ref, cols):
    value = ref[:, :, cols]
    return value.reshape(value.shape[0] * value.shape[1], value.shape[2])


def token_tables(pos_ref, row_ref, key_ref, query_ref, first):
    lane = lax.rem(lax.broadcasted_iota(jnp.int32, (1, LANES), 1), LANES // 2)
    for b in range(pos_ref.shape[0]):

        def column(ref):
            row = ref[b : b + 1, :].astype(F32)
            return jnp.transpose(jnp.broadcast_to(row, (LANES, LANES)))

        place, other = column(pos_ref), column(row_ref)
        high = jnp.floor(place * (1.0 / 256)) * 256
        key = jnp.where(lane < 3, high, place - high)
        key = jnp.where(lane == 6, 1.0 - other, key)
        key = jnp.where(lane == 7, other, key)
        key = jnp.where(lane < 8, key, jnp.where(lane < 11, 1.0, 0.0))
        query = jnp.where(lane == 6, other * MASKED, 0.0)
        query = jnp.where(lane == 7, (1.0 - other) * MASKED, query)
        rows = pl.ds(pl.multiple_of(first + b * LANES, LANES), LANES)
        key_ref[rows, :] = key.astype(BF16)
        query_ref[rows, :] = query.astype(BF16)


def forward_kernel(n_dp, n_blk, scale, *refs):
    (qkv, out, fc, proj, tokens, out_grad, pos, rows_id, slopes, fc_bias) = refs[:10]
    vectors, refs = refs[10:18], refs[18:]
    (w_qkv_o, w_out_o, w_fc_o, w_proj_o, vec_o, h1_o, mixed_o, heads_o, att_o, qx_o, mid_o, h2_o, hid_o, slope_o, dy_o, key_o, gp_o) = refs[:17]
    (w_qkv, w_out, w_fc, w_proj, vec, h1, mixed, heads, att, qx, mid, h2, hid, gslope, dy, key_aug, gp) = refs[17:34]
    (w_small, fcb, x_all, query_aug, f_qkv, f_out, f_fc, f_proj) = refs[34:42]
    send, recv, side, load, save_sem = refs[42:]
    pc = Place(n_dp, n_blk)
    sib = pc.sibling(1)
    rows_own, width = tokens.shape
    total = n_blk * rows_own
    wide = width // n_blk
    piece = f_proj.shape[0]
    tile = 256
    mine = pl.ds(pl.multiple_of(pc.c * rows_own, rows_own), rows_own)
    theirs = pl.ds(pl.multiple_of(sib[1] * rows_own, rows_own), rows_own)
    my_start = pl.multiple_of(pc.c * wide, LANES)
    my_cols = pl.ds(my_start, wide)
    saves = []

    def exchange(i, src, dst):
        copy = remote(src, dst, side.at[0, i], side.at[1, i], sib)
        copy.start()
        return copy

    def keep(i, src, dst):
        copy = pltpu.make_async_copy(src, dst, load.at[i])
        copy.start()
        return copy

    def save(i, src, dst):
        copy = pltpu.make_async_copy(src, dst, save_sem.at[i])
        copy.start()
        saves.append(copy)

    get_qkv = [
        keep(i, qkv.at[:, pl.ds(my_start + i * width, wide)], f_qkv.at[:, i * wide : (i + 1) * wide])
        for i in range(3)
    ]
    get_out = keep(3, out.at[:, my_cols], f_out)
    get_proj = keep(4, proj.at[pl.ds(pl.multiple_of(pc.c * piece, piece), piece)], f_proj)

    def fc_part(j):
        src = fc.at[:, pl.ds(pl.multiple_of((j * n_blk + pc.c) * piece, piece), piece)]
        dst = f_fc.at[:, pl.ds(pl.multiple_of(j * piece, piece), piece)]
        return pltpu.make_async_copy(src, dst, load.at[8 + j])

    pl.loop(0, n_dp)(lambda j: fc_part(j).start())
    get_x = keep(5, tokens, x_all.at[mine])
    pc.greet()
    first = [exchange(0, tokens, x_all.at[mine])]
    lane = lax.broadcasted_iota(jnp.int32, (1, LANES), 1)
    shard = width // n_dp
    own_part = lane // shard == lax.rem(pc.dp, LANES // shard)
    lines = []
    for ref in vectors:
        lines.append(jnp.where(own_part, jnp.concatenate([ref[...]] * (LANES // shard), axis=1), 0.0))
    lines.append(fc_bias[:, pl.ds(pl.multiple_of(pc.c * piece, piece), piece)])
    lines.append(jnp.zeros((16 - len(lines), LANES), F32))
    w_small[pc.dp] = jnp.concatenate(lines, axis=0).astype(BF16)
    cut = piece // 2
    quarter = cut // 2
    chunks = [
        lambda slot: w_small.at[slot],
        lambda slot: w_qkv.at[slot],
        lambda slot: w_out.at[slot, :, my_cols],
        lambda slot: w_fc.at[slot],
        lambda slot: w_proj.at[slot, cut:piece],
    ]
    u_small, u_qkv, u_out, u_fc, u_proj = [
        Gather(pc, i, chunk, send, recv) for i, chunk in enumerate(chunks)
    ]
    u_ring = RingGather(
        pc,
        5,
        lambda slot: w_proj.at[slot, 0:cut],
        lambda slot, i: w_proj.at[slot, i * quarter : (i + 1) * quarter],
        send,
        recv,
    )
    steps = range(1, pc.length)
    u_small.line()
    u_small.ring(0)
    for copy in get_qkv:
        copy.wait()
    w_qkv[pc.dp] = f_qkv[...].astype(BF16)
    u_qkv.line()
    u_qkv.ring(0)
    get_out.wait()
    w_out[pc.dp, :, my_cols] = f_out[...].astype(BF16)
    get_proj.wait()
    w_proj[pc.dp] = f_proj[...].astype(BF16)
    token_tables(pos, rows_id, key_aug, query_aug, pc.c * rows_own)
    first.append(exchange(1, key_aug.at[mine], key_aug.at[mine]))
    first.append(exchange(2, query_aug.at[mine], query_aug.at[mine]))
    u_small.along(1)
    u_small.ring(1)
    u_qkv.along(1)
    u_qkv.ring(1)
    for s in steps[1:]:
        u_small.along(s)
        u_small.ring(s)
    for s in range(pc.length):
        u_small.across(s)
    pl.loop(0, n_dp)(lambda j: fc_part(j).wait())
    w_fc[pc.dp] = f_fc[...].astype(BF16)
    later = [exchange(3, out_grad, dy.at[mine]), keep(6, out_grad, dy.at[mine])]
    u_small.finish()
    u_qkv.along(2)
    u_qkv.ring(2)
    u_out.line()
    get_x.wait()
    for copy in first:
        copy.wait()
    per = n_dp // (width // LANES)
    for t in range(width // LANES):
        rows = w_small[t * per].astype(F32)
        for k in range(1, per):
            rows += w_small[t * per + k].astype(F32)
        vec[:, t * LANES : (t + 1) * LANES] = rows
    for t in range(n_dp):
        fcb[:, t * LANES : (t + 1) * LANES] = w_small[t, 8:9, :].astype(F32)
    save(0, vec, vec_o)

    def first_norm(b):
        rows = pl.ds(pl.multiple_of(b * LANES, LANES), LANES)
        h1[rows, :] = layer_norm(x_all[rows, :].astype(F32), vec[0:1, :], vec[1:2, :]).astype(BF16)

    norm_blocks = total // LANES
    pl.loop(0, norm_blocks // 2)(first_norm)
    for s in steps[2:]:
        u_qkv.along(s)
        u_qkv.ring(s)
    u_fc.line()
    u_out.ring(0)
    pl.loop(norm_blocks // 2, norm_blocks)(first_norm)
    save(2, h1, h1_o)
    for s in range(pc.length):
        u_qkv.across(s)
    u_ring.start()
    for s in steps:
        u_out.along(s)
        u_out.ring(s)
    u_fc.along(1)
    u_qkv.finish()
    save(3, w_qkv, w_qkv_o)
    for third in range(3):
        for b in range(wide // tile):

            @pl.loop(0, total // 512)
            def _(m, third=third, b=b):
                rows = pl.ds(pl.multiple_of(m * 512, 512), 512)
                cols = pl.ds(third * wide + b * tile, tile)
                value = matmul(h1[rows, :], whole(w_qkv, cols))
                if third != 1:
                    at = pl.ds(my_start + b * tile, tile)
                    value += vec[pl.ds(2 + third // 2, 1), at]
                mixed[rows, cols] = value.astype(BF16)

        if third == 0:
            u_fc.along(2)
            for s in range(pc.length):
                u_out.across(s)
            u_ring.across()
    save(4, mixed, mixed_o)
    for s in steps[2:]:
        u_fc.along(s)
    for s in range(pc.length):
        u_fc.ring(s)
    u_proj.line()
    pairs = wide // LANES
    for j in range(pairs):
        cols = [pl.ds(i * wide + j * LANES, LANES) for i in range(3)]
        attend_kernel(
            tile,
            scale,
            mixed.at[:, cols[0]],
            mixed.at[:, cols[1]],
            mixed.at[:, cols[2]],
            key_aug,
            query_aug,
            [slopes[pc.c * 2 * pairs + 2 * j + hh] for hh in range(2)],
            heads.at[:, cols[0]],
            qx.at[pl.ds(j, 1)],
        )
        if j == 0:
            u_ring.rise()
        if j < pc.length - 1:
            u_proj.along(j + 1)
        if j == 1:
            u_fc.across(0)
        if j == 2:
            u_ring.along(1)
            u_fc.across(1)
            u_out.finish()
            part = w_out.at[:, :, my_cols]
            share = exchange(4, part, part)
    swap = exchange(5, heads.at[theirs], att.at[:, my_cols])
    stay = keep(7, heads.at[mine], att.at[:, my_cols])
    save(5, heads, heads_o)
    save(6, qx, qx_o)
    share.wait()
    save(7, w_out, w_out_o)
    swap.wait()
    stay.wait()
    save(8, att, att_o)

    @pl.loop(0, width // tile)
    def _(b):
        cols = pl.ds(pl.multiple_of(b * tile, tile), tile)
        value = matmul(att[...], whole(w_out, cols))
        mid[:, cols] = x_all[mine, cols].astype(F32) + value + vec[4:5, cols]

    u_fc.across(2)

    @pl.loop(0, rows_own // LANES)
    def _(b):
        rows = pl.ds(pl.multiple_of(b * LANES, LANES), LANES)
        into = pl.ds(pl.multiple_of(pc.c * rows_own + b * LANES, LANES), LANES)
        h2[into, :] = layer_norm(mid[rows, :], vec[5:6, :], vec[6:7, :]).astype(BF16)

    both = exchange(6, h2.at[mine], h2.at[mine])
    save(9, mid, mid_o)
    u_ring.along(2)
    for s in range(3, pc.length):
        u_fc.across(s)
    for s in range(pc.length):
        u_proj.ring(s)
    both.wait()
    save(10, h2, h2_o)
    u_fc.finish()
    save(11, w_fc, w_fc_o)

    def feed(b):
        cols = pl.ds(pl.multiple_of(b * tile, tile), tile)

        @pl.loop(0, total // 512)
        def _(m):
            rows = pl.ds(pl.multiple_of(m * 512, 512), 512)
            value = matmul(h2[rows, :], whole(w_fc, cols)) + fcb[:, cols]
            value, slope = gelu_pair(value)
            hid[rows, cols] = value.astype(BF16)
            gslope[rows, cols] = slope.astype(BF16)

    blocks = hid.shape[1] // tile
    pl.loop(0, blocks // 4)(feed)
    for s in range(3, pc.length):
        u_ring.along(s)
    u_proj.across(0)
    pl.loop(blocks // 4, blocks // 2)(feed)
    u_proj.across(1)
    pl.loop(blocks // 2, blocks)(feed)
    for s in range(2, pc.length):
        u_proj.across(s)
    save(12, hid, hid_o)
    save(13, gslope, slope_o)
    for copy in later:
        copy.wait()
    save(14, dy, dy_o)
    save(15, key_aug, key_o)
    slots = tile // piece

    @pl.loop(0, blocks)
    def _(b):
        cols = pl.ds(pl.multiple_of(b * tile, tile), tile)
        for n in range(width // 512):
            value = matmul_tn(hid[:, cols], dy[:, n * 512 : (n + 1) * 512]).astype(BF16)
            gp[pl.ds(b * slots, slots), :, n * 512 : (n + 1) * 512] = value.reshape(slots, piece, 512)

    save(16, gp, gp_o)
    u_proj.finish()
    save(1, w_proj, w_proj_o)
    for copy in saves:
        copy.wait()
    for unit in (u_small, u_qkv, u_out, u_fc, u_proj, u_ring):
        unit.drain()


def forward(n_dp, n_blk, scale, qkv, out, fc, proj, tokens, out_grad, positions, row_ids, slopes, fc_bias, vectors):
    rows_own, width = tokens.shape
    total = n_blk * rows_own
    wide = width // n_blk
    pairs = wide // LANES
    piece = proj.shape[0] // n_blk
    ff = n_dp * piece
    shard, length = qkv.shape[0], n_dp // PLANE
    weights = [(shard, 3 * wide), (shard, width), (shard, ff), (piece, width)]
    outs = [((n_dp,) + w, BF16) for w in weights] + [
        ((16, width), F32),
        ((total, width), BF16),
        ((total, 3 * wide), BF16),
        ((total, wide), BF16),
        ((rows_own, width), BF16),
        ((pairs, 2, total, LANES), BF16),
        ((rows_own, width), F32),
        ((total, width), BF16),
        ((total, ff), BF16),
        ((total, ff), BF16),
        ((total, width), BF16),
        ((total, LANES), BF16),
        ((n_dp, piece, width), BF16),
    ]
    scratch = outs + [
        ((n_dp, 16, LANES), BF16),
        ((1, ff), F32),
        ((total, width), BF16),
        ((total, LANES), BF16),
        ((shard, 3 * wide), F32),
        ((shard, wide), F32),
        ((shard, ff), F32),
        ((piece, width), F32),
    ]
    hbm = pl.BlockSpec(memory_space=pl.ANY)
    vmem = pl.BlockSpec(memory_space=pltpu.VMEM)
    smem = pl.BlockSpec(memory_space=pltpu.SMEM)
    grid = (rows_own // LANES, LANES)
    small = [a.reshape(1, -1) for a in (fc_bias, *vectors)]
    return pl.pallas_call(
        functools.partial(forward_kernel, n_dp, n_blk, scale),
        out_shape=[jax.ShapeDtypeStruct(*o) for o in outs],
        in_specs=[hbm] * 6 + [vmem] * 2 + [smem] + [vmem] * len(small),
        out_specs=[hbm] * len(outs),
        scratch_shapes=[pltpu.VMEM(*s) for s in scratch]
        + [
            pltpu.SemaphoreType.DMA((7, 5, length)),
            pltpu.SemaphoreType.DMA((7, n_dp)),
            pltpu.SemaphoreType.DMA((2, 7)),
            pltpu.SemaphoreType.DMA((8 + n_dp,)),
            pltpu.SemaphoreType.DMA((17,)),
        ],
        compiler_params=pltpu.CompilerParams(
            collective_id=2, has_side_effects=True, vmem_limit_bytes=VMEM_BYTES
        ),
    )(qkv, out, fc, proj, tokens, out_grad, positions.reshape(grid), row_ids.reshape(grid), slopes, *small)


def normed_rows(rows):
    centred = rows - jnp.mean(rows, axis=-1, keepdims=True)
    inverse = lax.rsqrt(jnp.mean(centred * centred, axis=-1, keepdims=True) + EPSILON)
    return centred * inverse, inverse


def norm_back(rows, gain_vec, grad):
    unit, inverse = normed_rows(rows)
    m = grad * gain_vec
    shift = jnp.mean(m, axis=-1, keepdims=True)
    stretch = jnp.mean(m * unit, axis=-1, keepdims=True)
    return (m - shift - unit * stretch) * inverse, grad * unit


def column_sum(value):
    return jnp.sum(value, axis=0, keepdims=True)


def backward_kernel(n_dp, n_blk, scale, *refs):
    (w_qkv_h, w_out_h, w_fc_h, w_proj_h, vec, h1_h, mixed_h, heads_h, att_h, qx_h, mid_h, h2_h, hid_h, slope_h, dy_h, key_h, gp_h, tokens_h) = refs[:18]
    (layer_o, input_o, proj_o, fc_o, qkv_o, out_o, small_o) = refs[18:25]
    (P2, S, Y, F, H, A, M, T, O, Q, E, K, GP, side0, side1, R1, R2, R3, DH, SB, PF, acc_k, acc_v, VG, fcg, SG, small_in) = refs[25:52]
    bufs, small_bufs, rest = refs[52:68], refs[68:71], refs[71:]
    ring_bufs, rest = rest[:3], rest[3:]
    totals, rest = rest[:6], rest[6:]
    send, recv, xsem, load, last = rest
    pc = Place(n_dp, n_blk)
    sib = pc.sibling(1)
    rows_own, width = tokens_h.shape
    total = n_blk * rows_own
    wide = width // n_blk
    ff = A.shape[1]
    shard = width // n_dp
    piece = ff // n_dp
    tile = 256
    mine = pl.ds(pl.multiple_of(pc.c * rows_own, rows_own), rows_own)
    theirs = pl.ds(pl.multiple_of(sib[1] * rows_own, rows_own), rows_own)
    my_cols = pl.ds(pl.multiple_of(pc.c * wide, LANES), wide)
    their_cols = pl.ds(pl.multiple_of(sib[1] * wide, LANES), wide)

    def fetch(i, src, dst):
        copy = pltpu.make_async_copy(src, dst, load.at[i])
        copy.start()
        return copy

    def exchange(i, src, dst):
        copy = remote(src, dst, xsem.at[0, i], xsem.at[1, i], sib)
        copy.start()
        return copy

    def span(i, size=tile):
        return pl.ds(pl.multiple_of(i * size, size), size)

    get_proj = fetch(2, w_proj_h, P2)
    get_dy = fetch(3, dy_h, Y)
    get_slope = fetch(4, slope_h, S)
    get_gp = fetch(0, gp_h, GP)
    get_h2 = fetch(5, h2_h, H)
    get_mid = fetch(6, mid_h, M)
    get_fc = fetch(7, w_fc_h, F)
    get_att = fetch(8, att_h, T)
    get_out = fetch(9, w_out_h, O)
    get_qx = fetch(10, qx_h, Q)
    get_heads = fetch(11, heads_h, E)
    get_key = fetch(12, key_h, K)
    pc.greet()
    cut = piece // 2
    chunks = [
        lambda slot: GP.at[pl.ds(pl.multiple_of(slot * piece + cut, cut), cut)],
        lambda slot: A.at[span(slot, shard)],
        lambda slot: F.at[span(slot, shard), 0 : 3 * wide],
        lambda slot: side0.at[span(slot, shard)],
    ]

    def from_proj(ref, first):
        return lambda slot: ref.at[pl.ds(pl.multiple_of(slot * piece + first, cut), cut)]

    u_proj, u_fc, u_qkv, u_out = [
        Scatter(
            pc, i, chunks[i], bufs[4 * i : 4 * i + 4], send, recv, None if i else from_proj(gp_h, cut)
        )
        for i in range(4)
    ]
    u_small = SmallSum(pc, 4, SG, small_bufs, send, recv)
    u_line = LineScatter(pc, 5, from_proj(GP, 0), ring_bufs, send, recv, from_proj(gp_h, 0))
    length = pc.length
    far_first = range(length - 1, -1, -1)
    pending = []

    def give(i, src, dst):
        keep = pltpu.make_async_copy(src, dst, last.at[0, i])
        copy = remote(src, dst, last.at[1, i], last.at[2, i], sib)
        keep.start()
        copy.start()
        return keep, copy

    VG[...] = jnp.zeros_like(VG)
    u_line.along(length - 1)
    u_proj.start()
    get_proj.wait()
    get_dy.wait()
    get_slope.wait()

    def hidden_grads(b):
        cols = span(b)
        sums = None
        for m in range(total // 512):
            rows = pl.ds(m * 512, 512)
            value = S[rows, cols].astype(F32) * matmul_nt(Y[rows, :], P2[cols, :])
            value = value.astype(BF16)
            S[rows, cols] = value
            part = column_sum(value.astype(F32))
            sums = part if sums is None else sums + part
        fcg[:, cols] = sums

    blocks = ff // tile
    pl.loop(0, blocks // 2)(hidden_grads)
    get_gp.wait()
    for s in far_first[:2]:
        u_proj.middle(s)
    pl.loop(blocks // 2, blocks)(hidden_grads)
    for s in far_first[2:]:
        u_proj.middle(s)
    get_h2.wait()

    @pl.loop(0, width // tile)
    def _(b):
        for n in range(ff // 1024):
            cols = pl.ds(n * 1024, 1024)
            A[span(b), cols] = matmul_tn(H[:, span(b)], S[:, cols]).astype(BF16)

    u_fc.start()
    u_line.along(length - 2)
    get_qkv = [
        fetch(13, w_qkv_h.at[:, 0 : 2 * wide], P2.at[0:width]),
        fetch(14, w_qkv_h.at[:, 2 * wide :], P2.at[width : 2 * width, 0:wide]),
    ]
    get_mid.wait()
    get_fc.wait()

    @pl.loop(0, width // tile)
    def _(b):
        SB[:, span(b)] = matmul_nt(S[theirs, :], F[span(b), :]).astype(BF16)

    swap_two = exchange(1, SB, R2)
    for s in far_first[:2]:
        u_proj.settle(s)

    @pl.loop(0, width // tile)
    def _(b):
        PF[:, span(b)] = matmul_nt(S[mine, :], F[span(b), :])

    for s in far_first[2:]:
        u_proj.settle(s)
    swap_two.wait()
    get_h1 = fetch(16, h1_h, S.at[:, 0:width])
    get_kv = fetch(17, mixed_h.at[:, wide:], S.at[:, width : 2 * width])

    @pl.loop(0, rows_own // LANES)
    def _(b):
        rows = span(b, LANES)
        from_mine = pl.ds(pl.multiple_of(pc.c * rows_own + b * LANES, LANES), LANES)
        into = pl.ds(pl.multiple_of(sib[1] * rows_own + b * LANES, LANES), LANES)
        grad = PF[rows, :] + R2[rows, :].astype(F32)
        top = Y[from_mine, :].astype(F32)
        back, terms = norm_back(M[rows, :], vec[5:6, :], grad)
        value = top + back
        M[rows, :] = value
        branch = value.astype(BF16)
        Y[into, :] = branch
        VG[4:5, :] += column_sum(branch.astype(F32))
        VG[5:6, :] += column_sum(terms)
        VG[6:7, :] += column_sum(grad)
        VG[7:8, :] += column_sum(top)

    get_out.wait()

    @pl.loop(0, width // tile)
    def _(b):
        Y[mine, span(b)] = matmul_nt(Y[theirs, :], O[span(b), :]).astype(BF16)

    swap_heads = exchange(2, Y.at[mine, their_cols], DH.at[mine])
    stay_heads = fetch(18, Y.at[mine, my_cols], DH.at[mine])
    for s in range(length - 3, 0, -1):
        u_line.along(s)
    get_att.wait()

    @pl.loop(0, width // tile)
    def _(b):
        O[span(b), :] = matmul_tn(T[:, span(b)], Y[theirs, :]).astype(BF16)

    swap_side = exchange(3, O.at[:, their_cols], side1)
    get_tokens = fetch(19, tokens_h, T)
    get_qx.wait()
    get_heads.wait()
    get_key.wait()
    get_kv.wait()
    stay_heads.wait()
    swap_heads.wait()
    pairs = wide // LANES
    for j in range(pairs):
        cols = pl.ds(j * LANES, LANES)
        attend_back_kernel(
            tile,
            scale,
            Q.at[pl.ds(j, 1)],
            S.at[:, pl.ds(width + j * LANES, LANES)],
            S.at[:, pl.ds(width + wide + j * LANES, LANES)],
            K,
            E.at[:, cols],
            DH.at[:, cols],
            H.at[:, cols],
            H.at[:, pl.ds(wide + j * LANES, LANES)],
            P2.at[width : 2 * width, pl.ds(wide + j * LANES, LANES)],
            acc_k,
            acc_v,
        )
        if j == 0:
            swap_side.wait()

            @pl.loop(0, n_dp)
            def _(slot):
                rows = span(slot, shard)
                value = O[rows, my_cols].astype(F32) + side1[rows, :].astype(F32)
                side0[rows, :] = value.astype(BF16)

            u_out.start()
            for s in far_first[:2]:
                u_fc.middle(s)
        if j == 1:
            for s in far_first[2:]:
                u_fc.middle(s)
            for s in far_first[:-1]:
                u_proj.along(s)
        if j == 2:
            for s in far_first[:1]:
                u_fc.settle(s)
                u_fc.along(s)
            for s in far_first[:2]:
                u_out.middle(s)
        if j == 3:
            u_line.settle()
            for s in far_first[1:2]:
                u_fc.settle(s)
                u_fc.along(s)
            for s in far_first[2:]:
                u_out.middle(s)
    get_h1.wait()

    @pl.loop(0, width // tile)
    def _(b):
        F[span(b), 0 : 2 * wide] = matmul_tn(S[:, span(b)], H[...]).astype(BF16)
        value = matmul_tn(S[:, span(b)], P2[width : 2 * width, wide : 2 * wide])
        F[span(b), 2 * wide : 3 * wide] = value.astype(BF16)

    u_qkv.start(near=False)
    VG[2:3, my_cols] = column_sum(H[:, 0:wide].astype(F32))
    VG[3:4, my_cols] = column_sum(P2[width : 2 * width, wide : 2 * wide].astype(F32))
    get_hid = fetch(1, hid_h, S)
    for copy in get_qkv:
        copy.wait()

    def input_part(first, b):
        rows = pl.ds(pl.multiple_of(first, rows_own), rows_own)
        below = pl.ds(pl.multiple_of(width + first, rows_own), rows_own)
        after = pl.ds(pl.multiple_of(width + b * tile, tile), tile)
        part = matmul_nt(P2[below, wide : 2 * wide], P2[after, 0:wide])
        return part + matmul_nt(H[rows, :], P2[span(b), :])

    @pl.loop(0, width // tile)
    def _(b):
        SB[:, span(b)] = input_part(sib[1] * rows_own, b).astype(BF16)

    swap_one = exchange(4, SB, R3)
    for s in far_first[2:]:
        u_fc.settle(s)
        if s:
            u_fc.along(s)

    @pl.loop(0, width // tile)
    def _(b):
        PF[:, span(b)] = input_part(pc.c * rows_own, b)

    get_proj = fetch(2, w_proj_h, P2)
    get_tokens.wait()
    swap_one.wait()

    def last_norm(b):
        rows = span(b, LANES)
        grad = PF[rows, :] + R3[rows, :].astype(F32)
        back, terms = norm_back(T[rows, :].astype(F32), vec[0:1, :], grad)
        M[rows, :] += back
        VG[0:1, :] += column_sum(terms)
        VG[1:2, :] += column_sum(grad)

    norm_blocks = rows_own // LANES
    for s in far_first[:2]:
        u_qkv.middle(s, near=True)
    pl.loop(0, norm_blocks // 2)(last_norm)
    u_line.turn()
    for s in far_first[2:]:
        u_qkv.middle(s, near=True)
    pl.loop(norm_blocks // 2, norm_blocks)(last_norm)
    get_mid_again = fetch(21, mid_h, PF)
    put_input = pltpu.make_async_copy(M, input_o, load.at[20])
    put_input.start()
    per = n_dp // (width // LANES)
    for slot in range(n_dp):
        t = slot // per
        at = slot % PLANE, slot // PLANE
        SG[*at, 0:8, :] = VG[0:8, t * LANES : (t + 1) * LANES]
        SG[*at, 8:16, :] = jnp.broadcast_to(fcg[:, slot * LANES : (slot + 1) * LANES], (8, LANES))
    u_small.start()
    get_hid.wait()
    get_proj.wait()

    def layer_part(rows, b):
        return matmul(S[rows, :], P2[:, span(b)])

    @pl.loop(0, width // tile)
    def _(b):
        SB[:, span(b)] = layer_part(theirs, b).astype(BF16)

    swap_out = exchange(0, SB, R1)
    for s in far_first:
        u_out.settle(s)
        if s:
            u_out.along(s)
    get_mid_again.wait()

    @pl.loop(0, width // tile)
    def _(b):
        PF[:, span(b)] += layer_part(mine, b)

    for s in far_first[:2]:
        u_qkv.settle(s)
        u_qkv.along(s)
    u_small.middle()
    swap_out.wait()

    @pl.loop(0, rows_own // LANES)
    def _(b):
        rows = span(b, LANES)
        value = PF[rows, :] + R1[rows, :].astype(F32) + vec[7:8, :]
        R1[rows, :] = value.astype(BF16)

    put_layer = pltpu.make_async_copy(R1, layer_o, load.at[15])
    put_layer.start()
    u_fc.finish(totals[1])

    @pl.loop(0, n_dp)
    def _(j):
        dst = fc_o.at[:, pl.ds(pl.multiple_of((j * n_blk + pc.c) * piece, piece), piece)]
        give(1 + j, totals[1].at[:, span(j, piece)], dst)

    u_proj.finish(totals[0])
    at = pl.multiple_of(pc.c * piece + cut, cut)
    pending += give(0, totals[0], proj_o.at[pl.ds(at, cut)])
    u_line.finish(totals[5])
    pending += give(5 + n_dp, totals[5], proj_o.at[pl.ds(pl.multiple_of(pc.c * piece, cut), cut)])
    u_out.finish(totals[3])
    pending += give(4 + n_dp, totals[3], out_o.at[:, my_cols])
    for s in far_first[2:]:
        u_qkv.settle(s)
        if s:
            u_qkv.along(s)
    u_small.finish(totals[4])
    swap_small = exchange(5, totals[4], small_in)
    u_qkv.finish(totals[2])
    for j in range(3):
        at = pl.ds(pl.multiple_of(pc.c * wide, LANES) + j * width, wide)
        pending += give(1 + n_dp + j, totals[2].at[:, j * wide : (j + 1) * wide], qkv_o.at[:, at])
    swap_small.wait()
    low = jnp.where(pc.c == 0, totals[4][...], small_in[...])
    high = jnp.where(pc.c == 0, small_in[...], totals[4][...])
    small_o[0:8, :] = low[0:8] + high[0:8]
    small_o[8:16, :] = low[8:16]
    small_o[16:24, :] = high[8:16]

    @pl.loop(0, n_dp)
    def _(j):
        dst = fc_o.at[:, pl.ds(pl.multiple_of((j * n_blk + pc.c) * piece, piece), piece)]
        src = totals[1].at[:, span(j, piece)]
        pltpu.make_async_copy(src, dst, last.at[0, 1 + j]).wait()
        remote(src, dst, last.at[1, 1 + j], last.at[2, 1 + j], sib).wait()

    for copy in pending:
        copy.wait()
    put_layer.wait()
    put_input.wait()
    for unit in (u_proj, u_line, u_fc, u_qkv, u_out):
        unit.drain()


def backward(n_dp, n_blk, scale, saved, tokens):
    rows_own, width = tokens.shape
    total = n_blk * rows_own
    wide = width // n_blk
    w_proj = saved[3]
    ff = w_proj.shape[0]
    piece, shard, length = ff // n_dp, width // n_dp, n_dp // PLANE
    square, long, own = ((total, width), BF16), ((total, ff), BF16), ((rows_own, width), BF16)
    own_f32 = ((rows_own, width), F32)
    sizes = [
        ((piece // 2, width), BF16),
        ((shard, ff), BF16),
        ((shard, 3 * wide), BF16),
        ((shard, wide), BF16),
        ((16, LANES), F32),
    ]
    scratch = [((ff, width), BF16), long, square, long, square, long, own_f32, own]
    scratch += [((width, width), BF16), (saved[9].shape, BF16), ((total, wide), BF16)]
    scratch += [((total, LANES), BF16), ((ff, width), BF16)]
    scratch += [((width, wide), BF16)] * 2 + [own] * 3 + [((total, wide), BF16), own, own_f32]
    scratch += [((total, LANES), F32)] * 2 + [((8, width), F32), ((1, ff), F32)]
    scratch += [((PLANE, length, 16, LANES), F32), ((16, LANES), F32)]
    for size, kind in sizes[:4]:
        scratch += [((length,) + size, kind)] * 4
    one = ((length, 16, LANES), F32)
    scratch += [((PLANE - 1,) + one[0], F32), one, one]
    half, quarter = (piece // 2, width), (piece // 4, width)
    scratch += [((PLANE, length + 1) + half, BF16), ((2,) + quarter, BF16), ((2,) + half, BF16)]
    scratch += [(size, F32) for size, _ in sizes] + [(half, F32)]
    outs = [own, own_f32, ((n_blk * piece, width), F32), ((shard, n_blk * ff), F32)]
    outs += [((shard, 3 * width), F32), ((shard, width), F32), ((24, LANES), F32)]
    hbm = pl.BlockSpec(memory_space=pl.ANY)
    vmem = pl.BlockSpec(memory_space=pltpu.VMEM)
    return pl.pallas_call(
        functools.partial(backward_kernel, n_dp, n_blk, scale),
        out_shape=[jax.ShapeDtypeStruct(*o) for o in outs],
        in_specs=[vmem if i == 4 else hbm for i in range(18)],
        out_specs=[hbm] * 6 + [vmem],
        scratch_shapes=[pltpu.VMEM(*s) for s in scratch]
        + [
            pltpu.SemaphoreType.DMA((7, 5, length)),
            pltpu.SemaphoreType.DMA((7, 5, length)),
            pltpu.SemaphoreType.DMA((2, 6)),
            pltpu.SemaphoreType.DMA((22,)),
            pltpu.SemaphoreType.DMA((3, 6 + n_dp)),
        ],
        compiler_params=pltpu.CompilerParams(
            collective_id=3, has_side_effects=True, vmem_limit_bytes=VMEM_BACK
        ),
    )(*saved, tokens)


def results_kernel(n_dp, piece, layer, inputs, proj, fc, qkv, out, small, *refs):
    big, vectors, fc_bias = refs[:6], refs[6:14], refs[14]
    hold, fetched, stored = refs[15:21], refs[21], refs[22]
    sources = (layer, inputs, proj, fc, qkv, out)
    loads = [pltpu.make_async_copy(s, h, fetched.at[i]) for i, (s, h) in enumerate(zip(sources, hold))]
    stores = [pltpu.make_async_copy(h, d, stored.at[i]) for i, (h, d) in enumerate(zip(hold, big))]
    for load in loads:
        load.start()
    shard = vectors[0].shape[1]
    per = LANES // shard
    turn = lax.rem(lax.axis_index("dp"), per)
    rows = small[0:8, 0:shard]
    for k in range(1, per):
        rows = jnp.where(turn == k, small[0:8, k * shard : (k + 1) * shard], rows)
    for i, vector in enumerate(vectors):
        vector[...] = rows[i : i + 1]
    for k in range(2):
        fc_bias[:, k * piece : (k + 1) * piece] = small[8 + 8 * k : 9 + 8 * k, :]
    for load, store in zip(loads, stores):
        load.wait()
        store.start()
    for store in stores:
        store.wait()


def results(n_dp, piece, outs):
    big, small = outs[:6], outs[6]
    shapes = [jax.ShapeDtypeStruct(a.shape, a.dtype) for a in big]
    shard = big[5].shape[0]
    sizes = [shard] * 8 + [2 * piece]
    shapes += [jax.ShapeDtypeStruct((1, size), F32) for size in sizes]
    hbm = pl.BlockSpec(memory_space=pl.ANY)
    vmem = pl.BlockSpec(memory_space=pltpu.VMEM)
    got = pl.pallas_call(
        functools.partial(results_kernel, n_dp, piece),
        out_shape=shapes,
        in_specs=[hbm] * 6 + [vmem],
        out_specs=[hbm] * 6 + [vmem] * 9,
        scratch_shapes=[pltpu.VMEM(a.shape, a.dtype) for a in big]
        + [pltpu.SemaphoreType.DMA((6,)), pltpu.SemaphoreType.DMA((6,))],
        compiler_params=pltpu.CompilerParams(vmem_limit_bytes=VMEM_BYTES),
    )(*outs)
    return got[:6], [a.reshape(-1) for a in got[6:]]


def columns_spec(rows, first):
    return pl.BlockSpec((rows, LANES), lambda j: (0, first + j))


def attend_step(block, scale, q_ref, k_ref, v_ref, key_aug, query_aug, slopes, out_ref, qx_ref):
    j = pl.program_id(0)
    pair = [slopes[2 * j + hh] for hh in range(2)]
    attend_kernel(block, scale, q_ref, k_ref, v_ref, key_aug, query_aug, pair, out_ref, qx_ref)


def attend(qkv, key_aug, query_aug, slopes, scale):
    total, wide = qkv.shape[0], qkv.shape[1] // 3
    pairs = wide // LANES
    block = math.gcd(total, 256)
    whole = pl.BlockSpec((total, LANES), lambda j: (0, 0))
    return pl.pallas_call(
        functools.partial(attend_step, block, scale),
        grid=(pairs,),
        out_shape=[
            jax.ShapeDtypeStruct((total, wide), BF16),
            jax.ShapeDtypeStruct((pairs, 2, total, LANES), BF16),
        ],
        in_specs=[
            columns_spec(total, 0),
            columns_spec(total, pairs),
            columns_spec(total, 2 * pairs),
            whole,
            whole,
            pl.BlockSpec(memory_space=pltpu.SMEM),
        ],
        out_specs=[
            columns_spec(total, 0),
            pl.BlockSpec((1, 2, total, LANES), lambda j: (j, 0, 0, 0)),
        ],
        compiler_params=pltpu.CompilerParams(vmem_limit_bytes=VMEM_BYTES),
    )(qkv, qkv, qkv, key_aug, query_aug, slopes)


def attend_back(query_ext, qkv, key_aug, attended, grad, scale):
    total, wide = attended.shape
    pairs = wide // LANES
    block = math.gcd(total, 256)
    whole = pl.BlockSpec((total, LANES), lambda j: (0, 0))
    out = jax.ShapeDtypeStruct((total, wide), BF16)
    return pl.pallas_call(
        functools.partial(attend_back_kernel, block, scale),
        grid=(pairs,),
        out_shape=[out] * 3,
        in_specs=[
            pl.BlockSpec((1, 2, total, LANES), lambda j: (j, 0, 0, 0)),
            columns_spec(total, pairs),
            columns_spec(total, 2 * pairs),
            whole,
            columns_spec(total, 0),
            columns_spec(total, 0),
        ],
        out_specs=[columns_spec(total, 0)] * 3,
        scratch_shapes=[pltpu.VMEM((total, LANES), F32)] * 2,
        compiler_params=pltpu.CompilerParams(vmem_limit_bytes=VMEM_BYTES),
    )(query_ext, qkv, qkv, key_aug, attended, grad)


def attention_terms(positions, rows):
    high = (positions // 256) * 256
    low = positions - high
    first = rows == 0
    one = jnp.ones_like(positions)
    zero = jnp.zeros_like(positions)

    def table(columns):
        cols = jnp.stack([col.astype(F32) for col in columns], axis=1)
        cols = jnp.pad(cols, ((0, 0), (0, LANES // 2 - len(columns))))
        return jnp.concatenate([cols, cols], axis=1).astype(BF16)

    key_aug = table([high, high, high, low, low, low, first, ~first, one, one, one])
    other = jnp.where(first, 0.0, MASKED)
    query_aug = table([zero] * 6 + [other, jnp.where(first, MASKED, 0.0)])
    return key_aug, query_aug


def body(
    n_dp,
    n_blk,
    tokens,
    positions,
    row_ids,
    alibi_slope,
    ln1_gain,
    ln1_bias,
    qkv_weight,
    query_bias,
    value_bias,
    out_weight,
    out_bias,
    ln2_gain,
    ln2_bias,
    fc_weight,
    fc_bias,
    proj_weight,
    proj_bias,
    out_grad,
):
    local, width = tokens.shape
    heads = alibi_slope.shape[0]
    hidden_all = fc_weight.shape[1]
    scale = 1.0 / math.sqrt(width // heads)
    c = lax.axis_index("blk")
    dp = lax.axis_index("dp")
    wide = width // n_blk
    shard = width // n_dp
    piece = hidden_all // (n_dp * n_blk)
    total = n_blk * local

    def swap(a):
        return lax.ppermute(a, "blk", [(0, 1), (1, 0)])

    def blk_gather(a):
        if n_blk != 2:
            return lax.all_gather(a, "blk", axis=0, tiled=True)
        other = swap(a)
        return jnp.where(
            c == 0, jnp.concatenate([a, other], 0), jnp.concatenate([other, a], 0)
        )

    def blk_sum(a):
        if n_blk != 2:
            return lax.psum_scatter(a.astype(BF16), "blk", scatter_dimension=0, tiled=True).astype(F32)
        own = lax.dynamic_slice_in_dim(a, c * local, local, 0)
        other = lax.dynamic_slice_in_dim(a, (1 - c) * local, local, 0)
        return own + swap(other.astype(BF16)).astype(F32)

    def to_tokens(a):
        if n_blk != 2:
            moved = lax.all_to_all(a.reshape(n_blk, local, wide), "blk", 0, 0)
            return jnp.transpose(moved, (1, 0, 2)).reshape(local, width)
        own = lax.dynamic_slice_in_dim(a, c * local, local, 0)
        other = swap(lax.dynamic_slice_in_dim(a, (1 - c) * local, local, 0))
        return jnp.where(
            c == 0, jnp.concatenate([own, other], 1), jnp.concatenate([other, own], 1)
        )

    def to_heads(a):
        if n_blk != 2:
            moved = lax.all_to_all(
                jnp.transpose(a.reshape(local, n_blk, wide), (1, 0, 2)), "blk", 0, 0
            )
            return moved.reshape(total, wide)
        own = lax.dynamic_slice_in_dim(a, c * wide, wide, 1)
        other = swap(lax.dynamic_slice_in_dim(a, (1 - c) * wide, wide, 1))
        return jnp.where(
            c == 0, jnp.concatenate([own, other], 0), jnp.concatenate([other, own], 0)
        )

    def mine(a, axis, size):
        return lax.dynamic_slice_in_dim(a, c * size, size, axis)

    vectors = [ln1_gain, ln1_bias, query_bias, value_bias, out_bias, ln2_gain, ln2_bias, proj_bias]
    if n_blk == 2 and piece == LANES:
        weights = (qkv_weight, out_weight, fc_weight, proj_weight)
        saved = forward(
            n_dp, n_blk, scale, *weights, tokens, out_grad, positions, row_ids, alibi_slope, fc_bias, vectors
        )
        saved = [a if i == 9 else a.reshape(-1, a.shape[-1]) for i, a in enumerate(saved)]
        outs = backward(n_dp, n_blk, scale, saved, tokens)
        big, vectors = results(n_dp, piece, outs)
        layer_output, input_grad, proj_sum, fc_sum, qkv_sum, out_sum = big
        return (
            layer_output,
            input_grad,
            vectors[0],
            vectors[1],
            qkv_sum,
            vectors[2],
            vectors[3],
            out_sum,
            vectors[4],
            vectors[5],
            vectors[6],
            fc_sum,
            vectors[8],
            proj_sum,
            vectors[7],
        )

    qkv_own = jnp.concatenate(
        [mine(qkv_weight[:, i * width : (i + 1) * width], 1, wide) for i in range(3)], 1
    ).astype(BF16)
    out_own = mine(out_weight, 1, wide).astype(BF16)
    fc_own = mine(fc_weight.reshape(shard, n_dp, n_blk, piece), 2, 1).reshape(shard, n_dp * piece)
    proj_own = mine(proj_weight, 0, piece)
    vectors.append(mine(fc_bias, 0, piece))
    small = jnp.stack(
        [
            lax.dynamic_update_slice_in_dim(
                jnp.zeros((LANES,), F32), vec, lax.rem(dp * vec.shape[0], LANES), 0
            )
            for vec in vectors
        ]
    )
    small = jnp.pad(small, ((0, 16 - len(vectors)), (0, 0))).astype(BF16)
    inputs = tokens.astype(F32)
    grad_top = out_grad.astype(F32)
    shards = (qkv_own, out_own, fc_own.astype(BF16), proj_own.astype(BF16), small)
    full_qkv, full_out, full_fc, full_proj, full_small = gather_weights(
        n_dp, n_blk, *shards
    )
    weight_qkv = full_qkv.reshape(width, 3 * wide)
    weight_out = full_out.reshape(width, width)
    weight_fc = full_fc.reshape(width, n_dp * piece)
    weight_proj = full_proj.reshape(n_dp * piece, width)
    spread = full_small.astype(F32)

    def vector(i):
        size = vectors[i].shape[0]
        per = LANES // size
        rows = jnp.sum(spread[:, i].reshape(n_dp // per, per, LANES), axis=1)
        return rows.reshape(n_dp * size)

    gain_one, bias_one, bias_query, bias_value, bias_out, gain_two, bias_two, bias_proj, bias_fc = (
        vector(i) for i in range(len(vectors))
    )
    place = blk_gather(jnp.stack([positions, row_ids], axis=1))
    key_aug, query_aug = attention_terms(place[:, 0], place[:, 1])
    every_token = blk_gather(tokens).astype(F32)
    every_grad = blk_gather(out_grad)
    normed = layer_norm(every_token, gain_one, bias_one).astype(BF16)
    bias_qkv = jnp.concatenate(
        [mine(bias_query, 0, wide), jnp.zeros((wide,), F32), mine(bias_value, 0, wide)]
    )
    mixed = (matmul(normed, weight_qkv) + bias_qkv).astype(BF16)
    slopes = mine(alibi_slope, 0, heads // n_blk)
    attended_heads, query_ext = attend(mixed, key_aug, query_aug, slopes, scale)
    attended = to_tokens(attended_heads)
    middle = inputs + matmul(attended, weight_out) + bias_out
    normed_two = layer_norm(middle, gain_two, bias_two).astype(BF16)
    every_two = blk_gather(normed_two)
    hidden_pre = matmul(every_two, weight_fc) + bias_fc
    hidden_vals, gelu_slope = gelu_pair(hidden_pre)
    hidden = hidden_vals.astype(BF16)
    grad_proj_weight = matmul_tn(hidden, every_grad).astype(BF16)
    layer_output = (middle + blk_sum(matmul(hidden, weight_proj)) + bias_proj).astype(BF16)
    grad_proj_bias = jnp.sum(grad_top, axis=0)
    grad_pre = (gelu_slope * matmul_nt(every_grad, weight_proj)).astype(BF16)
    grad_fc_weight = matmul_tn(every_two, grad_pre).astype(BF16)
    grad_fc_bias = jnp.sum(grad_pre.astype(F32), axis=0)
    grad_normed_two = blk_sum(matmul_nt(grad_pre, weight_fc))
    _, norm_two_back = jax.vjp(layer_norm, middle, gain_two, bias_two)
    grad_mid_norm, grad_gain_two, grad_bias_two = norm_two_back(grad_normed_two)
    grad_middle = grad_top + grad_mid_norm
    grad_branch = grad_middle.astype(BF16)
    grad_out_weight = matmul_tn(attended, grad_branch).astype(BF16)
    grad_out_bias = jnp.sum(grad_branch.astype(F32), axis=0)
    grad_heads = to_heads(matmul_nt(grad_branch, weight_out).astype(BF16))
    grad_mixed = jnp.concatenate(
        attend_back(query_ext, mixed, key_aug, attended_heads, grad_heads, scale), axis=1
    )
    grad_qkv_weight = matmul_tn(normed, grad_mixed).astype(BF16)
    sums = jnp.sum(grad_mixed.astype(F32), axis=0)
    grad_normed = blk_sum(matmul_nt(grad_mixed, weight_qkv))
    _, norm_one_back = jax.vjp(layer_norm, inputs, gain_one, bias_one)
    grad_in_norm, grad_gain_one, grad_bias_one = norm_one_back(grad_normed)
    input_grad = grad_middle + grad_in_norm

    proj_sum, fc_sum, out_sum, qkv_sum = scatter_grads(
        n_dp,
        n_blk,
        grad_proj_weight.reshape(n_dp, piece, width),
        grad_fc_weight.reshape(n_dp, shard, n_dp * piece),
        grad_out_weight.reshape(n_dp, shard, width),
        grad_qkv_weight.reshape(n_dp, shard, 3 * wide),
    )

    def spread_out(vec, size):
        parts = vec.reshape(-1, 1, size)
        return jnp.where((jnp.arange(n_blk) == c)[None, :, None], parts, 0.0).reshape(-1)

    small_grads = [
        grad_gain_one,
        grad_bias_one,
        spread_out(sums[:wide], wide),
        spread_out(sums[2 * wide :], wide),
        grad_out_bias,
        grad_gain_two,
        grad_bias_two,
        grad_proj_bias,
        spread_out(grad_fc_bias, piece),
    ]
    small_sum = lax.psum(jnp.concatenate(small_grads), ("dp", "blk"))
    finals = []
    at = 0
    for vec in small_grads:
        size = vec.shape[0]
        finals.append(lax.dynamic_slice_in_dim(small_sum, at + dp * (size // n_dp), size // n_dp, 0))
        at += size
    g_gain1, g_bias1, g_query, g_value, g_out, g_gain2, g_bias2, g_proj, g_fc = finals
    final_qkv = jnp.transpose(qkv_sum.reshape(n_blk, shard, 3, wide), (1, 2, 0, 3))
    final_fc = jnp.transpose(fc_sum.reshape(n_blk, shard, n_dp, piece), (1, 2, 0, 3))
    return (
        layer_output,
        input_grad,
        g_gain1,
        g_bias1,
        final_qkv.reshape(shard, 3 * width),
        g_query,
        g_value,
        jnp.transpose(out_sum, (1, 0, 2)).reshape(shard, width),
        g_out,
        g_gain2,
        g_bias2,
        final_fc.reshape(shard, hidden_all),
        g_fc,
        proj_sum.reshape(n_blk * piece, width),
        g_proj,
    )


def solution(mesh):
    both, rows, one = P(("dp", "blk"), None), P("dp", None), P("dp")
    tokens = P(("dp", "blk"))
    in_specs = (both, tokens, tokens, P(), one, one, rows, one, one, rows, one, one, one, rows, one, rows, one, both)
    out_specs = (both, both, one, one, rows, one, one, rows, one, one, one, rows, one, rows, one)
    return jax.shard_map(
        functools.partial(body, mesh.shape["dp"], mesh.shape["blk"]),
        mesh=mesh,
        in_specs=in_specs,
        out_specs=out_specs,
        check_vma=False,
    )
```

```python
import functools
import math

import jax
import jax.numpy as jnp
from jax import lax
from jax.experimental import pallas as pl
from jax.experimental.pallas import tpu as pltpu
from jax.sharding import PartitionSpec as P

EPSILON = 1e-05
MASKED = -1e30
BF16 = jnp.bfloat16
F32 = jnp.float32
MESH = pl.DeviceIdType.MESH
PLANE = 4
LANES = 128
VMEM_BYTES = 58 * 2**20
VMEM_BACK = 63 * 2**20


def matmul(left, right):
    return jnp.dot(left, right, preferred_element_type=F32)


def matmul_tn(left, right):
    return lax.dot_general(left, right, (((0,), (0,)), ((), ())), preferred_element_type=F32)


def matmul_nt(left, right):
    return lax.dot_general(left, right, (((1,), (1,)), ((), ())), preferred_element_type=F32)


def layer_norm(inputs, gain_vec, bias_vec):
    row_mean = jnp.mean(inputs, axis=-1, keepdims=True)
    centred = inputs - row_mean
    spread = jnp.mean(centred * centred, axis=-1, keepdims=True)
    return centred * lax.rsqrt(spread + EPSILON) * gain_vec + bias_vec


class Place:
    def __init__(self, n_dp, n_blk):
        self.n_dp, self.n_blk, self.length = n_dp, n_blk, n_dp // PLANE
        self.dp, self.c = lax.axis_index("dp"), lax.axis_index("blk")
        self.z, self.p = self.dp // PLANE, lax.rem(self.dp, PLANE)
        side, row = lax.rem(self.p, 2), self.p // 2
        self.flip_x, self.flip_y = self.p + 1 - 2 * side, self.p + 2 - 4 * row
        self.diag = PLANE - 1 - self.p

    def routes(self, zz):
        odd = lax.rem(zz, 2)
        return (
            self.flip_x * (1 - odd) + self.flip_y * odd,
            self.flip_x * odd + self.flip_y * (1 - odd),
        )

    def at(self, zz, pp):
        return (zz * PLANE + pp, self.c)

    def sibling(self, k):
        return (self.dp, lax.rem(self.c + k, self.n_blk))

    def apart(self, s, run):
        if s == 0:
            run(self.z)
            return

        @pl.loop(0, 2)
        def _(k):
            zz = self.z + s * (1 - 2 * k)
            pl.when((zz >= 0) & (zz < self.length))(lambda: run(zz))

    def up_down(self, run_up, run_down):
        pl.when(self.z < self.length - 1)(run_up)
        pl.when(self.z > 0)(run_down)

    def greet(self):
        barrier = pltpu.get_barrier_semaphore()

        def hello(device):
            pl.semaphore_signal(barrier, inc=1, device_id=device, device_id_type=MESH)

        hello(self.at(self.z, self.flip_x))
        hello(self.at(self.z, self.flip_y))
        hello(self.at(self.z, self.diag))
        for k in range(1, self.n_blk):
            hello(self.sibling(k))

        @pl.loop(1, self.length)
        def _(k):
            hello(self.at(lax.rem(self.z + k, self.length), self.p))

        pl.semaphore_wait(barrier, self.n_blk + self.length + 1)


def remote(src, dst, send_sem, recv_sem, device):
    return pltpu.make_async_remote_copy(
        src_ref=src,
        dst_ref=dst,
        send_sem=send_sem,
        recv_sem=recv_sem,
        device_id=device,
        device_id_type=MESH,
    )


class Gather:
    def __init__(self, place, unit, chunk, send, recv):
        self.place, self.chunk = place, chunk
        self.send = lambda kind, zz: send.at[unit, kind, zz]
        self.recv = lambda slot: recv.at[unit, slot]

    def copy(self, slot, kind, zz, device):
        piece = self.chunk(slot)
        return remote(piece, piece, self.send(kind, zz), self.recv(slot), device)

    def arrived(self, slot):
        self.copy(slot, 0, 0, self.place.sibling(1)).wait_recv()

    def line(self):
        pc = self.place
        pc.up_down(
            lambda: self.copy(pc.dp, 3, pc.z, pc.at(pc.z + 1, pc.p)).start(),
            lambda: self.copy(pc.dp, 4, pc.z, pc.at(pc.z - 1, pc.p)).start(),
        )

    def along(self, s):
        pc = self.place

        def pass_on(zz):
            slot = zz * PLANE + pc.p
            self.arrived(slot)
            below = jnp.where(zz < pc.z, 1, 0)
            onward = pc.z + 2 * below - 1
            more = (onward >= 0) & (onward < pc.length)
            pl.when(more)(lambda: self.copy(slot, 3, zz, pc.at(onward, pc.p)).start())

        pc.apart(s, pass_on)

    def ring(self, s):
        pc = self.place

        def both(zz):
            slot = zz * PLANE + pc.p
            self.copy(slot, 0, zz, pc.at(pc.z, pc.flip_x)).start()
            self.copy(slot, 1, zz, pc.at(pc.z, pc.flip_y)).start()

        pc.apart(s, both)

    def across(self, s):
        pc = self.place

        def turn(zz):
            near, far = pc.routes(zz)
            slot = zz * PLANE + near
            self.arrived(slot)
            self.copy(slot, 2, zz, pc.at(pc.z, far)).start()

        pc.apart(s, turn)

    def finish(self):
        pc = self.place

        @pl.loop(0, pc.length)
        def _(zz):
            self.arrived(zz * PLANE + pc.routes(zz)[1])
            self.arrived(zz * PLANE + pc.diag)

    def drain(self):
        pc = self.place

        def sent(kind, zz):
            self.copy(pc.dp, kind, zz, pc.sibling(1)).wait_send()

        @pl.loop(0, pc.length)
        def _(zz):
            sent(0, zz)
            sent(1, zz)
            sent(2, zz)
            pl.when((zz <= pc.z) & (pc.z < pc.length - 1))(lambda: sent(3, zz))
            pl.when((zz > pc.z) & (pc.z > 0))(lambda: sent(3, zz))

        pl.when(pc.z > 0)(lambda: sent(4, pc.z))


class RingGather:
    def __init__(self, place, unit, chunk, part, send, recv):
        self.place, self.chunk, self.part = place, chunk, part
        self.lift = lambda pp, zz: send.at[unit, pp, zz]
        self.side = lambda k: send.at[unit + 1, 0, k]
        self.recv = lambda slot: recv.at[unit, slot]
        self.other = recv.at[unit + 1, 0]

    def copy(self, piece, sem, recv, device):
        return remote(piece, piece, sem, recv, device)

    def arrived(self, slot):
        self.copy(self.chunk(slot), self.side(0), self.recv(slot), self.place.sibling(1)).wait_recv()

    def start(self):
        pc = self.place
        piece, recv = self.chunk(pc.dp), self.recv(pc.dp)
        self.copy(piece, self.side(0), recv, pc.at(pc.z, pc.flip_x)).start()
        self.copy(piece, self.side(1), recv, pc.at(pc.z, pc.flip_y)).start()

    def across(self):
        pc = self.place
        base = pc.z * PLANE
        self.arrived(base + pc.flip_x)
        half = self.part(base + pc.flip_x, 0)
        self.copy(half, self.side(2), self.recv(base + pc.flip_x), pc.at(pc.z, pc.flip_y)).start()
        self.arrived(base + pc.flip_y)
        half = self.part(base + pc.flip_y, 1)
        self.copy(half, self.side(3), self.other, pc.at(pc.z, pc.flip_x)).start()

    def rise(self):
        pc = self.place
        slot = pc.z * PLANE + pc.diag
        for i, recv in enumerate((self.recv(slot), self.other)):
            self.copy(self.part(slot, i), self.side(0), recv, pc.sibling(1)).wait_recv()

        @pl.loop(0, PLANE)
        def _(pp):
            at = pc.z * PLANE + pp
            piece = self.chunk(at)

            def to(sem, zz):
                self.copy(piece, sem, self.recv(at), pc.at(zz, pc.p)).start()

            pc.up_down(
                lambda: to(self.lift(pp, pc.z), pc.z + 1), lambda: to(self.lift(4, pp), pc.z - 1)
            )

    def along(self, s):
        pc = self.place

        def pass_on(zz):
            below = jnp.where(zz < pc.z, 1, 0)
            onward = pc.z + 2 * below - 1

            @pl.loop(0, PLANE)
            def _(pp):
                slot = zz * PLANE + pp
                self.arrived(slot)
                copy = self.copy(
                    self.chunk(slot), self.lift(pp, zz), self.recv(slot), pc.at(onward, pc.p)
                )
                pl.when((onward >= 0) & (onward < pc.length))(copy.start)

        pc.apart(s, pass_on)

    def drain(self):
        pc = self.place
        piece = self.chunk(pc.dp)

        def sent(sem, view=piece):
            self.copy(view, sem, self.recv(pc.dp), pc.sibling(1)).wait_send()

        sent(self.side(0))
        sent(self.side(1))
        sent(self.side(2), self.part(pc.dp, 0))
        sent(self.side(3), self.part(pc.dp, 1))

        @pl.loop(0, PLANE)
        def _(pp):
            @pl.loop(0, pc.length)
            def _(zz):
                pl.when((zz <= pc.z) & (pc.z < pc.length - 1))(lambda: sent(self.lift(pp, zz)))
                pl.when((zz > pc.z) & (pc.z > 0))(lambda: sent(self.lift(pp, zz)))

            pl.when(pc.z > 0)(lambda: sent(self.lift(4, pp)))


def gather_kernel(
    n_dp, n_blk, qkv, out, fc, proj, small, all_qkv, all_out, all_fc, all_proj, all_small, send, recv, local, side
):
    pc = Place(n_dp, n_blk)
    wide = out.shape[1]
    mine = pl.ds(pl.multiple_of(pc.c * wide, LANES), wide)
    parts = [
        (small, lambda slot: all_small.at[slot]),
        (qkv, lambda slot: all_qkv.at[slot]),
        (out, lambda slot: all_out.at[slot, :, mine]),
        (fc, lambda slot: all_fc.at[slot]),
        (proj, lambda slot: all_proj.at[slot]),
    ]
    for i, (own, chunk) in enumerate(parts):
        pltpu.make_async_copy(own, chunk(pc.dp), local.at[i]).start()
    pc.greet()
    for i, (own, chunk) in enumerate(parts):
        pltpu.make_async_copy(own, chunk(pc.dp), local.at[i]).wait()
    units = [Gather(pc, i, chunk, send, recv) for i, (_, chunk) in enumerate(parts)]
    steps = range(pc.length)
    for i, unit in enumerate(units):
        unit.line()
        for s in steps:
            if s:
                unit.along(s)
            unit.ring(s)
        if i > 0:
            for s in steps:
                units[i - 1].across(s)
            units[i - 1].finish()
    for s in steps:
        units[4].across(s)
    side_copies = []
    piece = all_out.at[:, :, mine]
    for k in range(1, n_blk):
        copy = remote(piece, piece, side.at[0, k], side.at[1, k], pc.sibling(k))
        copy.start()
        side_copies.append(copy)
    units[4].finish()
    for copy in side_copies:
        copy.wait()
    for unit in units:
        unit.drain()


class Scatter:
    def __init__(self, place, unit, chunk, bufs, send, recv, source=None):
        self.place, self.chunk, self.source = place, chunk, source or chunk
        self.diag, self.near, self.far, self.line = bufs
        self.kind = self.near.dtype
        self.send = lambda kind, zz: send.at[unit, kind, zz]
        self.recv = lambda kind, zz: recv.at[unit, kind, zz]

    def copy(self, src, dst, kind, zz, device):
        return remote(src, dst, self.send(kind, zz), self.recv(kind, zz), device)

    def arrived(self, piece, kind, zz):
        self.copy(piece, piece, kind, zz, self.place.sibling(1)).wait_recv()

    def start(self, near=True):
        pc = self.place
        steps = range(pc.length - 1, -1, -1)

        def first(zz):
            to = pc.at(pc.z, pc.routes(zz)[0])
            self.copy(self.source(zz * PLANE + pc.diag), self.diag.at[zz], 0, zz, to).start()

        for s in steps:
            pc.apart(s, first)
        if near:
            for s in steps:
                pc.apart(s, self.send_near)

    def send_near(self, zz):
        pc = self.place
        near = pc.routes(zz)[0]
        piece = self.source(zz * PLANE + near)
        self.copy(piece, self.near.at[zz], 1, zz, pc.at(pc.z, near)).start()

    def middle(self, s, near=False):
        pc = self.place

        def turn(zz):
            far = pc.routes(zz)[1]
            self.arrived(self.diag.at[zz], 0, zz)
            total = self.diag[zz].astype(F32) + self.chunk(zz * PLANE + far)[...].astype(F32)
            self.diag[zz] = total.astype(self.kind)
            self.copy(self.diag.at[zz], self.far.at[zz], 2, zz, pc.at(pc.z, far)).start()
            if near:
                self.send_near(zz)

        pc.apart(s, turn)

    def settle(self, s):
        pc = self.place

        def add(zz):
            self.arrived(self.near.at[zz], 1, zz)
            self.arrived(self.far.at[zz], 2, zz)
            total = self.near[zz].astype(F32) + self.far[zz].astype(F32)
            total += self.chunk(zz * PLANE + pc.p)[...].astype(F32)
            self.near[zz] = total.astype(self.kind)

        pc.apart(s, add)

    def along(self, s):
        pc = self.place

        def send_on(zz):
            to = pc.at(zz, pc.p)
            sems = self.send(3, zz), self.recv(3, pc.z)
            remote(self.near.at[zz], self.line.at[pc.z], *sems, to).start()

        pc.apart(s, send_on)

    def finish(self, total):
        pc = self.place
        total[...] = self.near[pc.z].astype(F32)

        @pl.loop(1, pc.length)
        def _(k):
            zz = lax.rem(pc.z + k, pc.length)
            self.arrived(self.line.at[zz], 3, zz)
            total[...] += self.line[zz].astype(F32)

    def drain(self):
        pc = self.place

        def sent(kind, zz):
            piece = self.near.at[zz]
            self.copy(piece, piece, kind, zz, pc.sibling(1)).wait_send()

        @pl.loop(0, pc.length)
        def _(zz):
            sent(0, zz)
            sent(1, zz)
            sent(2, zz)
            pl.when(zz != pc.z)(lambda: sent(3, zz))


class LineScatter:
    def __init__(self, place, unit, chunk, bufs, send, recv, source=None):
        self.place, self.chunk, self.source = place, chunk, source or chunk
        self.line, self.half, self.ring = bufs
        self.lift = lambda pp, zz: send.at[unit, pp, zz]
        self.drop = lambda kind, zz: recv.at[unit, kind, zz]
        self.side = lambda k: (send.at[unit + 1, 0, k], recv.at[unit + 1, 0, k])
        self.middle_row = self.half.shape[1]

    def arrived(self, piece, sem):
        remote(piece, piece, self.lift(0, 0), sem, self.place.sibling(1)).wait_recv()

    def along(self, s):
        pc = self.place

        def pass_on(zz):
            above = jnp.where(zz > pc.z, 1, 0)
            onward = pc.z + 2 * above - 1
            before = pc.z - 2 * above + 1
            at = zz if s > 1 else zz * above + pc.length * (1 - above)

            @pl.loop(0, PLANE)
            def _(pp):
                last = pp * (1 - above) + zz * above if s == 1 else zz
                kind = pp if s > 1 else pp * above + PLANE * (1 - above)
                sem = self.drop(kind, last)
                dst, to = self.line.at[pp, at], pc.at(onward, pc.p)
                own = self.chunk(zz * PLANE + pp)

                def plain():
                    first = self.source(zz * PLANE + pp)
                    remote(first, dst, self.lift(pp, zz), sem, to).start()

                def more():
                    piece = self.line.at[pp, zz]
                    self.arrived(piece, self.drop(pp, zz))
                    piece[...] = (piece[...].astype(F32) + own[...].astype(F32)).astype(BF16)
                    remote(piece, dst, self.lift(pp, zz), sem, to).start()

                inside = (before >= 0) & (before < pc.length)
                if s == pc.length - 1:
                    plain()
                else:
                    pl.when(inside)(more)
                    pl.when(jnp.logical_not(inside))(plain)

        pc.apart(s, pass_on)

    def settle(self):
        pc = self.place

        @pl.loop(0, PLANE)
        def _(pp):
            own = self.chunk(pc.z * PLANE + pp)
            piece, over = self.line.at[pp, pc.z], self.line.at[pp, pc.length]

            def below():
                self.arrived(piece, self.drop(pp, pc.z))
                piece[...] = (piece[...].astype(F32) + own[...].astype(F32)).astype(BF16)

            def bottom():
                piece[...] = own[...]

            def above():
                self.arrived(over, self.drop(PLANE, pp))
                piece[...] = (piece[...].astype(F32) + over[...].astype(F32)).astype(BF16)

            pl.when(pc.z > 0)(below)
            pl.when(pc.z == 0)(bottom)
            pl.when(pc.z < pc.length - 1)(above)

        for i, to in enumerate((pc.flip_x, pc.flip_y)):
            rows = pl.ds(i * self.middle_row, self.middle_row)
            piece = self.line.at[pc.diag, pc.z, rows]
            remote(piece, self.half.at[i], *self.side(i), pc.at(pc.z, to)).start()

    def turn(self):
        pc = self.place
        for i, (dest, to) in enumerate(((pc.flip_y, pc.flip_y), (pc.flip_x, pc.flip_x))):
            rows = pl.ds(i * self.middle_row, self.middle_row)
            self.arrived(self.half.at[i], self.side(i)[1])
            value = self.line[dest, pc.z, rows].astype(F32) + self.half[i].astype(F32)
            self.line[dest, pc.z, rows] = value.astype(BF16)
            piece = self.line.at[dest, pc.z]
            remote(piece, self.ring.at[1 - i], *self.side(3 - i), pc.at(pc.z, to)).start()

    def finish(self, total):
        pc = self.place
        value = self.line[pc.p, pc.z].astype(F32)
        for i in range(2):
            self.arrived(self.ring.at[i], self.side(2 + i)[1])
            value += self.ring[i].astype(F32)
        total[...] = value

    def drain(self):
        pc = self.place

        def sent(piece, sem):
            remote(piece, piece, sem, self.drop(0, 0), pc.sibling(1)).wait_send()

        for i in range(2):
            sent(self.half.at[i], self.side(i)[0])
            sent(self.ring.at[i], self.side(2 + i)[0])

        @pl.loop(0, PLANE)
        def _(pp):
            @pl.loop(0, pc.length)
            def _(zz):
                piece = self.line.at[pp, zz]
                pl.when(zz > pc.z)(lambda: sent(piece, self.lift(pp, zz)))
                pl.when(zz < pc.z)(lambda: sent(piece, self.lift(pp, zz)))


class SmallSum:
    def __init__(self, place, unit, chunks, bufs, send, recv):
        self.place, self.chunks = place, chunks
        self.ring, self.sums, self.line = bufs
        self.sems = lambda kind, k: (send.at[unit, kind, k], recv.at[unit, kind, k])

    def flat(self):
        pc = self.place
        dests = ((1, pc.flip_x), (2, pc.flip_y), (3, pc.diag))
        return [
            remote(self.chunks.at[to], self.ring.at[k - 1], *self.sems(0, k), pc.at(pc.z, to))
            for k, to in dests
        ]

    def start(self):
        for copy in self.flat():
            copy.start()

    def middle(self):
        pc = self.place
        for copy in self.flat():
            copy.wait()
        self.sums[...] = self.chunks[pc.p] + self.ring[0] + self.ring[1] + self.ring[2]

        @pl.loop(1, pc.length)
        def _(k):
            zz = lax.rem(pc.z + k, pc.length)
            send, recv = self.sems(1, zz)[0], self.sems(1, pc.z)[1]
            remote(self.sums.at[zz], self.line.at[pc.z], send, recv, pc.at(zz, pc.p)).start()

    def finish(self, total):
        pc = self.place
        total[...] = self.sums[pc.z]

        @pl.loop(1, pc.length)
        def _(k):
            zz = lax.rem(pc.z + k, pc.length)
            piece = self.line.at[zz]
            remote(piece, piece, *self.sems(1, zz), pc.sibling(1)).wait()
            total[...] += self.line[zz]


def scatter_kernel(n_dp, n_blk, *refs):
    grads, outs, rest = refs[:4], refs[4:8], refs[8:]
    bufs, totals, rest = rest[:16], rest[16:20], rest[20:]
    side_buf, send, recv, side, last = rest
    proj, fc, out, qkv = grads
    pc = Place(n_dp, n_blk)
    pc.greet()
    wide = out.shape[2] // n_blk

    def columns(core):
        return pl.ds(pl.multiple_of(core * wide, LANES), wide)

    chunks = [
        lambda slot: proj.at[slot],
        lambda slot: fc.at[slot],
        lambda slot: side_buf.at[0, slot],
        lambda slot: qkv.at[slot],
    ]
    units = [
        Scatter(pc, i, chunks[i], bufs[4 * i : 4 * i + 4], send, recv) for i in range(4)
    ]
    units[0].start()
    units[1].start()
    side_copies = []
    for k in range(1, n_blk):
        dev = pc.sibling(k)
        copy = remote(
            out.at[:, :, columns(dev[1])], side_buf.at[k], side.at[0, k], side.at[1, k], dev
        )
        copy.start()
        side_copies.append(copy)

    def side_sum():
        for copy in side_copies:
            copy.wait()

        @pl.loop(0, n_dp)
        def _(slot):
            total = out[slot, :, columns(pc.c)].astype(F32)
            for k in range(1, n_blk):
                total += side_buf[k, slot].astype(F32)
            side_buf[0, slot] = total.astype(BF16)

    pending = []

    def spread(i):
        units[i].finish(totals[i])
        total = totals[i]
        pieces = [(total, outs[i].at[pc.c])]
        for j, (src, dst) in enumerate(pieces):
            keep = pltpu.make_async_copy(src, dst, last.at[i, 0, 0])
            keep.start()
            pending.append(keep)
            for k in range(1, n_blk):
                copy = remote(src, dst, last.at[i, 0, k], last.at[i, 1, k], pc.sibling(k))
                copy.start()
                pending.append(copy)

    steps = range(pc.length - 1, -1, -1)

    def middle(i):
        for s in steps:
            units[i].middle(s)

    def settle(i):
        for s in steps:
            units[i].settle(s)
            if s:
                units[i].along(s)

    middle(0)
    side_sum()
    units[2].start()
    middle(1)
    units[3].start()
    settle(0)
    middle(2)
    settle(1)
    spread(0)
    middle(3)
    settle(2)
    settle(3)
    spread(1)
    spread(2)
    spread(3)
    for copy in pending:
        copy.wait()
    for unit in units:
        unit.drain()


def gather_weights(n_dp, n_blk, qkv, out, fc, proj, small):
    shards = (qkv, out, fc, proj, small)
    shapes = [
        jax.ShapeDtypeStruct((n_dp, a.shape[0], a.shape[1] * (n_blk if a is out else 1)), BF16)
        for a in shards
    ]
    length = n_dp // PLANE
    hbm = pl.BlockSpec(memory_space=pl.ANY)
    return pl.pallas_call(
        functools.partial(gather_kernel, n_dp, n_blk),
        out_shape=shapes,
        in_specs=[hbm] * 5,
        out_specs=[hbm] * 5,
        scratch_shapes=[
            pltpu.SemaphoreType.DMA((5, 5, length)),
            pltpu.SemaphoreType.DMA((5, n_dp)),
            pltpu.SemaphoreType.DMA((5,)),
            pltpu.SemaphoreType.DMA((2, n_blk)),
        ],
        compiler_params=pltpu.CompilerParams(
            collective_id=0, has_side_effects=True, vmem_limit_bytes=VMEM_BYTES
        ),
    )(*shards)


def scatter_grads(n_dp, n_blk, proj, fc, out, qkv):
    length = n_dp // PLANE
    grads = (proj, fc, out, qkv)
    sizes = [a.shape[1:] for a in grads]
    sizes[2] = (sizes[2][0], sizes[2][1] // n_blk)
    vmem = pl.BlockSpec(memory_space=pltpu.VMEM)
    scratch = []
    for size in sizes:
        scratch += [pltpu.VMEM((length,) + size, BF16)] * 4
    scratch += [pltpu.VMEM(size, F32) for size in sizes]
    scratch += [
        pltpu.VMEM((n_blk, n_dp) + sizes[2], BF16),
        pltpu.SemaphoreType.DMA((4, 5, length)),
        pltpu.SemaphoreType.DMA((4, 5, length)),
        pltpu.SemaphoreType.DMA((2, n_blk)),
        pltpu.SemaphoreType.DMA((4, 2, n_blk)),
    ]
    return pl.pallas_call(
        functools.partial(scatter_kernel, n_dp, n_blk),
        out_shape=[jax.ShapeDtypeStruct((n_blk,) + size, F32) for size in sizes],
        in_specs=[vmem] * 4,
        out_specs=[pl.BlockSpec(memory_space=pl.ANY)] * 4,
        scratch_shapes=scratch,
        compiler_params=pltpu.CompilerParams(
            collective_id=1, has_side_effects=True, vmem_limit_bytes=VMEM_BYTES
        ),
    )(*grads)


def lane_split(value, lane, first, base):
    for i in range(3):
        term = value.astype(BF16)
        base = jnp.where(lane == first + i, term, base)
        value = value - term.astype(F32)
    return base


def causal_tail(scores, block, axis, masked):
    key_axis, query_axis = (0, 1) if axis == 0 else (1, 0)
    tail_shape = (block, block)
    keep = lax.broadcasted_iota(jnp.int32, tail_shape, key_axis) <= lax.broadcasted_iota(
        jnp.int32, tail_shape, query_axis
    )
    size = scores.shape[axis]
    if size == block:
        return jnp.where(keep, scores, masked)
    head = lax.slice_in_dim(scores, 0, size - block, axis=axis)
    tail = jnp.where(keep, lax.slice_in_dim(scores, size - block, size, axis=axis), masked)
    return jnp.concatenate([head, tail], axis=axis)


def causal_all(scores, offset, axis, masked):
    key_axis, query_axis = (0, 1) if axis == 0 else (1, 0)
    keep = (
        lax.broadcasted_iota(jnp.int32, scores.shape, key_axis)
        <= lax.broadcasted_iota(jnp.int32, scores.shape, query_axis) + offset
    )
    return jnp.where(keep, scores, masked)


def query_blocks(total, block, run):
    count = total // block
    if count <= 4:
        for b in range(count):
            run(
                b * block,
                (b + 1) * block,
                lambda scores, axis, masked: causal_tail(scores, block, axis, masked),
            )
    else:

        @pl.loop(0, count)
        def _(b):
            first = pl.multiple_of(b * block, block)
            run(first, total, lambda scores, axis, masked: causal_all(scores, first, axis, masked))


def attend_kernel(block, scale, q_ref, k_ref, v_ref, key_aug, query_aug, slopes, out_ref, qx_ref):
    total = q_ref.shape[0]
    half = LANES // 2
    lane = lax.broadcasted_iota(jnp.int32, (1, LANES), 1)
    slope_rows = []
    for hh in range(2):
        base = half * (1 - hh)
        slope = jnp.full((1, LANES), slopes[hh], F32)
        row = lane_split(slope, lane, base, jnp.zeros((1, LANES), BF16))
        slope_rows.append(lane_split(slope, lane, base + 3, row))

    def run(first, keys, mask):
        rows = pl.ds(first, block)
        result = None
        for hh in range(2):
            own = (lane < half) if hh == 0 else (lane >= half)
            base = half * (1 - hh)
            aug = query_aug[rows, :] + slope_rows[hh]
            query = jnp.where(own, q_ref[rows, :] * BF16(scale), aug)
            key = jnp.where(own, k_ref[0:keys, :], key_aug[0:keys, :])
            value = jnp.where(own, v_ref[0:keys, :], BF16(1))
            scores = mask(matmul_nt(query, key), 1, MASKED)
            top = jnp.max(scores, axis=1, keepdims=True)
            weights = jnp.exp(scores - top).astype(BF16)
            sums = matmul(weights, value)
            log_total = top + jnp.log(sums[:, base : base + 1])
            qx_ref[0, hh, rows, :] = lane_split(-log_total, lane, base + 8, query)
            part = sums / pltpu.roll(sums, half, 1)
            result = part if hh == 0 else jnp.where(own, part, result)
        out_ref[rows, :] = result.astype(BF16)

    query_blocks(total, block, run)


def attend_back_kernel(
    block, scale, qx_ref, k_ref, v_ref, key_aug, out_ref, grad_ref, dq_ref, dk_ref, dv_ref, dk_acc, dv_acc
):
    total = k_ref.shape[0]
    half = LANES // 2
    lane = lax.broadcasted_iota(jnp.int32, (1, LANES), 1)
    dk_acc[...] = jnp.zeros_like(dk_acc)
    dv_acc[...] = jnp.zeros_like(dv_acc)

    def run(first, keys, mask):
        rows = pl.ds(first, block)
        grad = grad_ref[rows, :]
        product = grad.astype(F32) * out_ref[rows, :].astype(F32)
        dq = None
        dk = None
        dv = None
        for hh in range(2):
            own = (lane < half) if hh == 0 else (lane >= half)
            base = half * (1 - hh)
            query = qx_ref[0, hh, rows, :]
            key = jnp.where(own, k_ref[0:keys, :], key_aug[0:keys, :])
            delta = jnp.sum(jnp.where(own, product, 0.0), axis=1, keepdims=True)
            grad_own = jnp.where(own, grad, BF16(0))
            grad_aug = lane_split(-delta, lane, base, grad_own)
            value = jnp.where(own, v_ref[0:keys, :], BF16(1))
            weights = mask(jnp.exp(matmul_nt(key, query)), 0, 0.0)
            change = (weights * matmul_nt(value, grad_aug)).astype(BF16)
            key_own = jnp.where(own, key, BF16(0))
            query_own = jnp.where(own, query, BF16(0))
            dv_part = matmul(weights.astype(BF16), grad_own)
            dk_part = matmul(change, query_own)
            dq_part = matmul_tn(change, key_own)
            dv = dv_part if hh == 0 else dv + dv_part
            dk = dk_part if hh == 0 else dk + dk_part
            dq = dq_part if hh == 0 else dq + dq_part
        dq_ref[rows, :] = (dq * scale).astype(BF16)
        dk_acc[0:keys, :] += dk
        dv_acc[0:keys, :] += dv

    query_blocks(total, block, run)
    dk_ref[...] = dk_acc[...].astype(BF16)
    dv_ref[...] = dv_acc[...].astype(BF16)


def gelu_pair(u):
    k = math.sqrt(2.0 / math.pi)
    square = u * u
    t = jnp.tanh(k * u * (1.0 + 0.044715 * square))
    plus = 0.5 * (1.0 + t)
    slope = plus + (0.5 * k) * u * (1.0 - t * t) * (1.0 + 3 * 0.044715 * square)
    return u * plus, slope


def whole(ref, cols):
    value = ref[:, :, cols]
    return value.reshape(value.shape[0] * value.shape[1], value.shape[2])


def token_tables(pos_ref, row_ref, key_ref, query_ref, first):
    lane = lax.rem(lax.broadcasted_iota(jnp.int32, (1, LANES), 1), LANES // 2)
    for b in range(pos_ref.shape[0]):

        def column(ref):
            row = ref[b : b + 1, :].astype(F32)
            return jnp.transpose(jnp.broadcast_to(row, (LANES, LANES)))

        place, other = column(pos_ref), column(row_ref)
        high = jnp.floor(place * (1.0 / 256)) * 256
        key = jnp.where(lane < 3, high, place - high)
        key = jnp.where(lane == 6, 1.0 - other, key)
        key = jnp.where(lane == 7, other, key)
        key = jnp.where(lane < 8, key, jnp.where(lane < 11, 1.0, 0.0))
        query = jnp.where(lane == 6, other * MASKED, 0.0)
        query = jnp.where(lane == 7, (1.0 - other) * MASKED, query)
        rows = pl.ds(pl.multiple_of(first + b * LANES, LANES), LANES)
        key_ref[rows, :] = key.astype(BF16)
        query_ref[rows, :] = query.astype(BF16)


def forward_kernel(n_dp, n_blk, scale, *refs):
    (qkv, out, fc, proj, tokens, out_grad, pos, rows_id, slopes, fc_bias) = refs[:10]
    vectors, refs = refs[10:18], refs[18:]
    (w_qkv_o, w_out_o, w_fc_o, w_proj_o, vec_o, h1_o, mixed_o, heads_o, att_o, qx_o, mid_o, h2_o, hid_o, slope_o, dy_o, key_o, gp_o) = refs[:17]
    (w_qkv, w_out, w_fc, w_proj, vec, h1, mixed, heads, att, qx, mid, h2, hid, gslope, dy, key_aug, gp) = refs[17:34]
    (w_small, fcb, x_all, query_aug, f_qkv, f_out, f_fc, f_proj) = refs[34:42]
    send, recv, side, load, save_sem = refs[42:]
    pc = Place(n_dp, n_blk)
    sib = pc.sibling(1)
    rows_own, width = tokens.shape
    total = n_blk * rows_own
    wide = width // n_blk
    piece = f_proj.shape[0]
    tile = 256
    mine = pl.ds(pl.multiple_of(pc.c * rows_own, rows_own), rows_own)
    theirs = pl.ds(pl.multiple_of(sib[1] * rows_own, rows_own), rows_own)
    my_start = pl.multiple_of(pc.c * wide, LANES)
    my_cols = pl.ds(my_start, wide)
    saves = []

    def exchange(i, src, dst):
        copy = remote(src, dst, side.at[0, i], side.at[1, i], sib)
        copy.start()
        return copy

    def keep(i, src, dst):
        copy = pltpu.make_async_copy(src, dst, load.at[i])
        copy.start()
        return copy

    def save(i, src, dst):
        copy = pltpu.make_async_copy(src, dst, save_sem.at[i])
        copy.start()
        saves.append(copy)

    get_qkv = [
        keep(i, qkv.at[:, pl.ds(my_start + i * width, wide)], f_qkv.at[:, i * wide : (i + 1) * wide])
        for i in range(3)
    ]
    get_out = keep(3, out.at[:, my_cols], f_out)
    get_proj = keep(4, proj.at[pl.ds(pl.multiple_of(pc.c * piece, piece), piece)], f_proj)

    def fc_part(j):
        src = fc.at[:, pl.ds(pl.multiple_of((j * n_blk + pc.c) * piece, piece), piece)]
        dst = f_fc.at[:, pl.ds(pl.multiple_of(j * piece, piece), piece)]
        return pltpu.make_async_copy(src, dst, load.at[8 + j])

    pl.loop(0, n_dp)(lambda j: fc_part(j).start())
    get_x = keep(5, tokens, x_all.at[mine])
    pc.greet()
    first = [exchange(0, tokens, x_all.at[mine])]
    lane = lax.broadcasted_iota(jnp.int32, (1, LANES), 1)
    shard = width // n_dp
    own_part = lane // shard == lax.rem(pc.dp, LANES // shard)
    lines = []
    for ref in vectors:
        lines.append(jnp.where(own_part, jnp.concatenate([ref[...]] * (LANES // shard), axis=1), 0.0))
    lines.append(fc_bias[:, pl.ds(pl.multiple_of(pc.c * piece, piece), piece)])
    lines.append(jnp.zeros((16 - len(lines), LANES), F32))
    w_small[pc.dp] = jnp.concatenate(lines, axis=0).astype(BF16)
    cut = piece // 2
    quarter = cut // 2
    chunks = [
        lambda slot: w_small.at[slot],
        lambda slot: w_qkv.at[slot],
        lambda slot: w_out.at[slot, :, my_cols],
        lambda slot: w_fc.at[slot],
        lambda slot: w_proj.at[slot, cut:piece],
    ]
    u_small, u_qkv, u_out, u_fc, u_proj = [
        Gather(pc, i, chunk, send, recv) for i, chunk in enumerate(chunks)
    ]
    u_ring = RingGather(
        pc,
        5,
        lambda slot: w_proj.at[slot, 0:cut],
        lambda slot, i: w_proj.at[slot, i * quarter : (i + 1) * quarter],
        send,
        recv,
    )
    steps = range(1, pc.length)
    u_small.line()
    u_small.ring(0)
    for copy in get_qkv:
        copy.wait()
    w_qkv[pc.dp] = f_qkv[...].astype(BF16)
    u_qkv.line()
    u_qkv.ring(0)
    get_out.wait()
    w_out[pc.dp, :, my_cols] = f_out[...].astype(BF16)
    get_proj.wait()
    w_proj[pc.dp] = f_proj[...].astype(BF16)
    token_tables(pos, rows_id, key_aug, query_aug, pc.c * rows_own)
    first.append(exchange(1, key_aug.at[mine], key_aug.at[mine]))
    first.append(exchange(2, query_aug.at[mine], query_aug.at[mine]))
    u_small.along(1)
    u_small.ring(1)
    u_qkv.along(1)
    u_qkv.ring(1)
    for s in steps[1:]:
        u_small.along(s)
        u_small.ring(s)
    for s in range(pc.length):
        u_small.across(s)
    pl.loop(0, n_dp)(lambda j: fc_part(j).wait())
    w_fc[pc.dp] = f_fc[...].astype(BF16)
    later = [exchange(3, out_grad, dy.at[mine]), keep(6, out_grad, dy.at[mine])]
    u_small.finish()
    u_qkv.along(2)
    u_qkv.ring(2)
    u_out.line()
    get_x.wait()
    for copy in first:
        copy.wait()
    per = n_dp // (width // LANES)
    for t in range(width // LANES):
        rows = w_small[t * per].astype(F32)
        for k in range(1, per):
            rows += w_small[t * per + k].astype(F32)
        vec[:, t * LANES : (t + 1) * LANES] = rows
    for t in range(n_dp):
        fcb[:, t * LANES : (t + 1) * LANES] = w_small[t, 8:9, :].astype(F32)
    save(0, vec, vec_o)

    def first_norm(b):
        rows = pl.ds(pl.multiple_of(b * LANES, LANES), LANES)
        h1[rows, :] = layer_norm(x_all[rows, :].astype(F32), vec[0:1, :], vec[1:2, :]).astype(BF16)

    norm_blocks = total // LANES
    pl.loop(0, norm_blocks // 2)(first_norm)
    for s in steps[2:]:
        u_qkv.along(s)
        u_qkv.ring(s)
    u_fc.line()
    u_out.ring(0)
    pl.loop(norm_blocks // 2, norm_blocks)(first_norm)
    save(2, h1, h1_o)
    for s in range(pc.length):
        u_qkv.across(s)
    u_ring.start()
    for s in steps:
        u_out.along(s)
        u_out.ring(s)
    u_fc.along(1)
    u_qkv.finish()
    save(3, w_qkv, w_qkv_o)
    for third in range(3):
        for b in range(wide // tile):

            @pl.loop(0, total // 512)
            def _(m, third=third, b=b):
                rows = pl.ds(pl.multiple_of(m * 512, 512), 512)
                cols = pl.ds(third * wide + b * tile, tile)
                value = matmul(h1[rows, :], whole(w_qkv, cols))
                if third != 1:
                    at = pl.ds(my_start + b * tile, tile)
                    value += vec[pl.ds(2 + third // 2, 1), at]
                mixed[rows, cols] = value.astype(BF16)

        if third == 0:
            u_fc.along(2)
            for s in range(pc.length):
                u_out.across(s)
            u_ring.across()
    save(4, mixed, mixed_o)
    for s in steps[2:]:
        u_fc.along(s)
    for s in range(pc.length):
        u_fc.ring(s)
    u_proj.line()
    pairs = wide // LANES
    for j in range(pairs):
        cols = [pl.ds(i * wide + j * LANES, LANES) for i in range(3)]
        attend_kernel(
            tile,
            scale,
            mixed.at[:, cols[0]],
            mixed.at[:, cols[1]],
            mixed.at[:, cols[2]],
            key_aug,
            query_aug,
            [slopes[pc.c * 2 * pairs + 2 * j + hh] for hh in range(2)],
            heads.at[:, cols[0]],
            qx.at[pl.ds(j, 1)],
        )
        if j == 0:
            u_ring.rise()
        if j < pc.length - 1:
            u_proj.along(j + 1)
        if j == 1:
            u_fc.across(0)
        if j == 2:
            u_ring.along(1)
            u_fc.across(1)
            u_out.finish()
            part = w_out.at[:, :, my_cols]
            share = exchange(4, part, part)
    swap = exchange(5, heads.at[theirs], att.at[:, my_cols])
    stay = keep(7, heads.at[mine], att.at[:, my_cols])
    save(5, heads, heads_o)
    save(6, qx, qx_o)
    share.wait()
    save(7, w_out, w_out_o)
    swap.wait()
    stay.wait()
    save(8, att, att_o)

    @pl.loop(0, width // tile)
    def _(b):
        cols = pl.ds(pl.multiple_of(b * tile, tile), tile)
        value = matmul(att[...], whole(w_out, cols))
        mid[:, cols] = x_all[mine, cols].astype(F32) + value + vec[4:5, cols]

    u_fc.across(2)

    @pl.loop(0, rows_own // LANES)
    def _(b):
        rows = pl.ds(pl.multiple_of(b * LANES, LANES), LANES)
        into = pl.ds(pl.multiple_of(pc.c * rows_own + b * LANES, LANES), LANES)
        h2[into, :] = layer_norm(mid[rows, :], vec[5:6, :], vec[6:7, :]).astype(BF16)

    both = exchange(6, h2.at[mine], h2.at[mine])
    save(9, mid, mid_o)
    u_ring.along(2)
    for s in range(3, pc.length):
        u_fc.across(s)
    for s in range(pc.length):
        u_proj.ring(s)
    both.wait()
    save(10, h2, h2_o)
    u_fc.finish()
    save(11, w_fc, w_fc_o)

    def feed(b):
        cols = pl.ds(pl.multiple_of(b * tile, tile), tile)

        @pl.loop(0, total // 512)
        def _(m):
            rows = pl.ds(pl.multiple_of(m * 512, 512), 512)
            value = matmul(h2[rows, :], whole(w_fc, cols)) + fcb[:, cols]
            value, slope = gelu_pair(value)
            hid[rows, cols] = value.astype(BF16)
            gslope[rows, cols] = slope.astype(BF16)

    blocks = hid.shape[1] // tile
    pl.loop(0, blocks // 4)(feed)
    for s in range(3, pc.length):
        u_ring.along(s)
    u_proj.across(0)
    pl.loop(blocks // 4, blocks // 2)(feed)
    u_proj.across(1)
    pl.loop(blocks // 2, blocks)(feed)
    for s in range(2, pc.length):
        u_proj.across(s)
    save(12, hid, hid_o)
    save(13, gslope, slope_o)
    for copy in later:
        copy.wait()
    save(14, dy, dy_o)
    save(15, key_aug, key_o)
    slots = tile // piece

    def proj_grad(b):
        cols = pl.ds(pl.multiple_of(b * tile, tile), tile)
        for n in range(width // 512):
            value = matmul_tn(hid[:, cols], dy[:, n * 512 : (n + 1) * 512]).astype(BF16)
            gp[pl.ds(b * slots, slots), :, n * 512 : (n + 1) * 512] = value.reshape(slots, piece, 512)

    pl.loop(0, blocks // 2)(proj_grad)
    save(16, gp.at[: n_dp // 2], gp_o.at[: n_dp // 2])
    save(17, w_proj.at[:, :cut], w_proj_o.at[:, :cut])
    pl.loop(blocks // 2, blocks)(proj_grad)
    save(18, gp.at[n_dp // 2 :], gp_o.at[n_dp // 2 :])
    u_proj.finish()
    save(1, w_proj.at[:, cut:], w_proj_o.at[:, cut:])
    for copy in saves:
        copy.wait()
    for unit in (u_small, u_qkv, u_out, u_fc, u_proj, u_ring):
        unit.drain()


def forward(n_dp, n_blk, scale, qkv, out, fc, proj, tokens, out_grad, positions, row_ids, slopes, fc_bias, vectors):
    rows_own, width = tokens.shape
    total = n_blk * rows_own
    wide = width // n_blk
    pairs = wide // LANES
    piece = proj.shape[0] // n_blk
    ff = n_dp * piece
    shard, length = qkv.shape[0], n_dp // PLANE
    weights = [(shard, 3 * wide), (shard, width), (shard, ff), (piece, width)]
    outs = [((n_dp,) + w, BF16) for w in weights] + [
        ((16, width), F32),
        ((total, width), BF16),
        ((total, 3 * wide), BF16),
        ((total, wide), BF16),
        ((rows_own, width), BF16),
        ((pairs, 2, total, LANES), BF16),
        ((rows_own, width), F32),
        ((total, width), BF16),
        ((total, ff), BF16),
        ((total, ff), BF16),
        ((total, width), BF16),
        ((total, LANES), BF16),
        ((n_dp, piece, width), BF16),
    ]
    scratch = outs + [
        ((n_dp, 16, LANES), BF16),
        ((1, ff), F32),
        ((total, width), BF16),
        ((total, LANES), BF16),
        ((shard, 3 * wide), F32),
        ((shard, wide), F32),
        ((shard, ff), F32),
        ((piece, width), F32),
    ]
    hbm = pl.BlockSpec(memory_space=pl.ANY)
    vmem = pl.BlockSpec(memory_space=pltpu.VMEM)
    smem = pl.BlockSpec(memory_space=pltpu.SMEM)
    grid = (rows_own // LANES, LANES)
    small = [a.reshape(1, -1) for a in (fc_bias, *vectors)]
    return pl.pallas_call(
        functools.partial(forward_kernel, n_dp, n_blk, scale),
        out_shape=[jax.ShapeDtypeStruct(*o) for o in outs],
        in_specs=[hbm] * 6 + [vmem] * 2 + [smem] + [vmem] * len(small),
        out_specs=[hbm] * len(outs),
        scratch_shapes=[pltpu.VMEM(*s) for s in scratch]
        + [
            pltpu.SemaphoreType.DMA((7, 5, length)),
            pltpu.SemaphoreType.DMA((7, n_dp)),
            pltpu.SemaphoreType.DMA((2, 7)),
            pltpu.SemaphoreType.DMA((8 + n_dp,)),
            pltpu.SemaphoreType.DMA((19,)),
        ],
        compiler_params=pltpu.CompilerParams(
            collective_id=2, has_side_effects=True, vmem_limit_bytes=VMEM_BYTES
        ),
    )(qkv, out, fc, proj, tokens, out_grad, positions.reshape(grid), row_ids.reshape(grid), slopes, *small)


def normed_rows(rows):
    centred = rows - jnp.mean(rows, axis=-1, keepdims=True)
    inverse = lax.rsqrt(jnp.mean(centred * centred, axis=-1, keepdims=True) + EPSILON)
    return centred * inverse, inverse


def norm_back(rows, gain_vec, grad):
    unit, inverse = normed_rows(rows)
    m = grad * gain_vec
    shift = jnp.mean(m, axis=-1, keepdims=True)
    stretch = jnp.mean(m * unit, axis=-1, keepdims=True)
    return (m - shift - unit * stretch) * inverse, grad * unit


def column_sum(value):
    return jnp.sum(value, axis=0, keepdims=True)


def backward_kernel(n_dp, n_blk, scale, *refs):
    (w_qkv_h, w_out_h, w_fc_h, w_proj_h, vec, h1_h, mixed_h, heads_h, att_h, qx_h, mid_h, h2_h, hid_h, slope_h, dy_h, key_h, gp_h, tokens_h) = refs[:18]
    (layer_o, input_o, proj_o, fc_o, qkv_o, out_o, small_o) = refs[18:25]
    (P2, S, Y, F, H, A, M, T, O, Q, E, K, GP, side0, side1, R1, R2, R3, DH, SB, PF, acc_k, acc_v, VG, fcg, SG, small_in) = refs[25:52]
    bufs, small_bufs, rest = refs[52:68], refs[68:71], refs[71:]
    ring_bufs, rest = rest[:3], rest[3:]
    totals, rest = rest[:6], rest[6:]
    send, recv, xsem, load, last = rest
    pc = Place(n_dp, n_blk)
    sib = pc.sibling(1)
    rows_own, width = tokens_h.shape
    total = n_blk * rows_own
    wide = width // n_blk
    ff = A.shape[1]
    shard = width // n_dp
    piece = ff // n_dp
    tile = 256
    mine = pl.ds(pl.multiple_of(pc.c * rows_own, rows_own), rows_own)
    theirs = pl.ds(pl.multiple_of(sib[1] * rows_own, rows_own), rows_own)
    my_cols = pl.ds(pl.multiple_of(pc.c * wide, LANES), wide)
    their_cols = pl.ds(pl.multiple_of(sib[1] * wide, LANES), wide)

    def fetch(i, src, dst):
        copy = pltpu.make_async_copy(src, dst, load.at[i])
        copy.start()
        return copy

    def exchange(i, src, dst):
        copy = remote(src, dst, xsem.at[0, i], xsem.at[1, i], sib)
        copy.start()
        return copy

    def span(i, size=tile):
        return pl.ds(pl.multiple_of(i * size, size), size)

    get_proj = fetch(2, w_proj_h, P2)
    get_dy = fetch(3, dy_h, Y)
    get_slope = fetch(4, slope_h, S)
    get_gp = fetch(0, gp_h, GP)
    get_h2 = fetch(5, h2_h, H)
    get_mid = fetch(6, mid_h, M)
    get_fc = fetch(7, w_fc_h, F)
    get_att = fetch(8, att_h, T)
    get_out = fetch(9, w_out_h, O)
    get_qx = fetch(10, qx_h, Q)
    get_heads = fetch(11, heads_h, E)
    get_key = fetch(12, key_h, K)
    pc.greet()
    cut = piece // 2
    chunks = [
        lambda slot: GP.at[pl.ds(pl.multiple_of(slot * piece + cut, cut), cut)],
        lambda slot: A.at[span(slot, shard)],
        lambda slot: F.at[span(slot, shard), 0 : 3 * wide],
        lambda slot: side0.at[span(slot, shard)],
    ]

    def from_proj(ref, first):
        return lambda slot: ref.at[pl.ds(pl.multiple_of(slot * piece + first, cut), cut)]

    u_proj, u_fc, u_qkv, u_out = [
        Scatter(
            pc, i, chunks[i], bufs[4 * i : 4 * i + 4], send, recv, None if i else from_proj(gp_h, cut)
        )
        for i in range(4)
    ]
    u_small = SmallSum(pc, 4, SG, small_bufs, send, recv)
    u_line = LineScatter(pc, 5, from_proj(GP, 0), ring_bufs, send, recv, from_proj(gp_h, 0))
    length = pc.length
    far_first = range(length - 1, -1, -1)
    pending = []

    def give(i, src, dst):
        keep = pltpu.make_async_copy(src, dst, last.at[0, i])
        copy = remote(src, dst, last.at[1, i], last.at[2, i], sib)
        keep.start()
        copy.start()
        return keep, copy

    VG[...] = jnp.zeros_like(VG)
    u_line.along(length - 1)
    u_proj.start()
    get_proj.wait()
    get_dy.wait()
    get_slope.wait()

    def hidden_grads(b):
        cols = span(b)
        sums = None
        for m in range(total // 512):
            rows = pl.ds(m * 512, 512)
            value = S[rows, cols].astype(F32) * matmul_nt(Y[rows, :], P2[cols, :])
            value = value.astype(BF16)
            S[rows, cols] = value
            part = column_sum(value.astype(F32))
            sums = part if sums is None else sums + part
        fcg[:, cols] = sums

    blocks = ff // tile
    pl.loop(0, blocks // 2)(hidden_grads)
    get_gp.wait()
    for s in far_first[:2]:
        u_proj.middle(s)
    pl.loop(blocks // 2, blocks)(hidden_grads)
    for s in far_first[2:]:
        u_proj.middle(s)
    get_h2.wait()

    @pl.loop(0, width // tile)
    def _(b):
        for n in range(ff // 1024):
            cols = pl.ds(n * 1024, 1024)
            A[span(b), cols] = matmul_tn(H[:, span(b)], S[:, cols]).astype(BF16)

    u_fc.start()
    u_line.along(length - 2)
    get_qkv = [
        fetch(13, w_qkv_h.at[:, 0 : 2 * wide], P2.at[0:width]),
        fetch(14, w_qkv_h.at[:, 2 * wide :], P2.at[width : 2 * width, 0:wide]),
    ]
    get_mid.wait()
    get_fc.wait()

    @pl.loop(0, width // tile)
    def _(b):
        SB[:, span(b)] = matmul_nt(S[theirs, :], F[span(b), :]).astype(BF16)

    swap_two = exchange(1, SB, R2)
    for s in far_first[:2]:
        u_proj.settle(s)

    @pl.loop(0, width // tile)
    def _(b):
        PF[:, span(b)] = matmul_nt(S[mine, :], F[span(b), :])

    for s in far_first[2:]:
        u_proj.settle(s)
    swap_two.wait()
    get_h1 = fetch(16, h1_h, S.at[:, 0:width])
    get_kv = fetch(17, mixed_h.at[:, wide:], S.at[:, width : 2 * width])

    @pl.loop(0, rows_own // LANES)
    def _(b):
        rows = span(b, LANES)
        from_mine = pl.ds(pl.multiple_of(pc.c * rows_own + b * LANES, LANES), LANES)
        into = pl.ds(pl.multiple_of(sib[1] * rows_own + b * LANES, LANES), LANES)
        grad = PF[rows, :] + R2[rows, :].astype(F32)
        top = Y[from_mine, :].astype(F32)
        back, terms = norm_back(M[rows, :], vec[5:6, :], grad)
        value = top + back
        M[rows, :] = value
        branch = value.astype(BF16)
        Y[into, :] = branch
        VG[4:5, :] += column_sum(branch.astype(F32))
        VG[5:6, :] += column_sum(terms)
        VG[6:7, :] += column_sum(grad)
        VG[7:8, :] += column_sum(top)

    get_out.wait()

    @pl.loop(0, width // tile)
    def _(b):
        Y[mine, span(b)] = matmul_nt(Y[theirs, :], O[span(b), :]).astype(BF16)

    swap_heads = exchange(2, Y.at[mine, their_cols], DH.at[mine])
    stay_heads = fetch(18, Y.at[mine, my_cols], DH.at[mine])
    for s in range(length - 3, 0, -1):
        u_line.along(s)
    get_att.wait()

    @pl.loop(0, width // tile)
    def _(b):
        O[span(b), :] = matmul_tn(T[:, span(b)], Y[theirs, :]).astype(BF16)

    swap_side = exchange(3, O.at[:, their_cols], side1)
    get_tokens = fetch(19, tokens_h, T)
    get_qx.wait()
    get_heads.wait()
    get_key.wait()
    get_kv.wait()
    stay_heads.wait()
    swap_heads.wait()
    pairs = wide // LANES
    for j in range(pairs):
        cols = pl.ds(j * LANES, LANES)
        attend_back_kernel(
            tile,
            scale,
            Q.at[pl.ds(j, 1)],
            S.at[:, pl.ds(width + j * LANES, LANES)],
            S.at[:, pl.ds(width + wide + j * LANES, LANES)],
            K,
            E.at[:, cols],
            DH.at[:, cols],
            H.at[:, cols],
            H.at[:, pl.ds(wide + j * LANES, LANES)],
            P2.at[width : 2 * width, pl.ds(wide + j * LANES, LANES)],
            acc_k,
            acc_v,
        )
        if j == 0:
            swap_side.wait()

            @pl.loop(0, n_dp)
            def _(slot):
                rows = span(slot, shard)
                value = O[rows, my_cols].astype(F32) + side1[rows, :].astype(F32)
                side0[rows, :] = value.astype(BF16)

            u_out.start()
            for s in far_first[:2]:
                u_fc.middle(s)
        if j == 1:
            for s in far_first[2:]:
                u_fc.middle(s)
            for s in far_first[:-1]:
                u_proj.along(s)
        if j == 2:
            for s in far_first[:1]:
                u_fc.settle(s)
                u_fc.along(s)
            for s in far_first[:2]:
                u_out.middle(s)
        if j == 3:
            u_line.settle()
            for s in far_first[1:2]:
                u_fc.settle(s)
                u_fc.along(s)
            for s in far_first[2:]:
                u_out.middle(s)
    get_h1.wait()

    @pl.loop(0, width // tile)
    def _(b):
        F[span(b), 0 : 2 * wide] = matmul_tn(S[:, span(b)], H[...]).astype(BF16)
        value = matmul_tn(S[:, span(b)], P2[width : 2 * width, wide : 2 * wide])
        F[span(b), 2 * wide : 3 * wide] = value.astype(BF16)

    u_qkv.start(near=False)
    VG[2:3, my_cols] = column_sum(H[:, 0:wide].astype(F32))
    VG[3:4, my_cols] = column_sum(P2[width : 2 * width, wide : 2 * wide].astype(F32))
    get_hid = fetch(1, hid_h, S)
    for copy in get_qkv:
        copy.wait()

    def input_part(first, b):
        rows = pl.ds(pl.multiple_of(first, rows_own), rows_own)
        below = pl.ds(pl.multiple_of(width + first, rows_own), rows_own)
        after = pl.ds(pl.multiple_of(width + b * tile, tile), tile)
        part = matmul_nt(P2[below, wide : 2 * wide], P2[after, 0:wide])
        return part + matmul_nt(H[rows, :], P2[span(b), :])

    @pl.loop(0, width // tile)
    def _(b):
        SB[:, span(b)] = input_part(sib[1] * rows_own, b).astype(BF16)

    swap_one = exchange(4, SB, R3)
    for s in far_first[2:]:
        u_fc.settle(s)
        if s:
            u_fc.along(s)

    @pl.loop(0, width // tile)
    def _(b):
        PF[:, span(b)] = input_part(pc.c * rows_own, b)

    get_proj = fetch(2, w_proj_h, P2)
    get_tokens.wait()
    swap_one.wait()

    def last_norm(b):
        rows = span(b, LANES)
        grad = PF[rows, :] + R3[rows, :].astype(F32)
        back, terms = norm_back(T[rows, :].astype(F32), vec[0:1, :], grad)
        M[rows, :] += back
        VG[0:1, :] += column_sum(terms)
        VG[1:2, :] += column_sum(grad)

    norm_blocks = rows_own // LANES
    for s in far_first[:2]:
        u_qkv.middle(s, near=True)
    pl.loop(0, norm_blocks // 2)(last_norm)
    u_line.turn()
    for s in far_first[2:]:
        u_qkv.middle(s, near=True)
    pl.loop(norm_blocks // 2, norm_blocks)(last_norm)
    get_mid_again = fetch(21, mid_h, PF)
    put_input = pltpu.make_async_copy(M, input_o, load.at[20])
    put_input.start()
    per = n_dp // (width // LANES)
    for slot in range(n_dp):
        t = slot // per
        at = slot % PLANE, slot // PLANE
        SG[*at, 0:8, :] = VG[0:8, t * LANES : (t + 1) * LANES]
        SG[*at, 8:16, :] = jnp.broadcast_to(fcg[:, slot * LANES : (slot + 1) * LANES], (8, LANES))
    u_small.start()
    get_hid.wait()
    get_proj.wait()

    def layer_part(rows, b):
        return matmul(S[rows, :], P2[:, span(b)])

    @pl.loop(0, width // tile)
    def _(b):
        SB[:, span(b)] = layer_part(theirs, b).astype(BF16)

    swap_out = exchange(0, SB, R1)
    for s in far_first:
        u_out.settle(s)
        if s:
            u_out.along(s)
    get_mid_again.wait()

    @pl.loop(0, width // tile)
    def _(b):
        PF[:, span(b)] += layer_part(mine, b)

    for s in far_first[:2]:
        u_qkv.settle(s)
        u_qkv.along(s)
    u_small.middle()
    swap_out.wait()

    @pl.loop(0, rows_own // LANES)
    def _(b):
        rows = span(b, LANES)
        value = PF[rows, :] + R1[rows, :].astype(F32) + vec[7:8, :]
        R1[rows, :] = value.astype(BF16)

    put_layer = pltpu.make_async_copy(R1, layer_o, load.at[15])
    put_layer.start()
    u_fc.finish(totals[1])

    @pl.loop(0, n_dp)
    def _(j):
        dst = fc_o.at[:, pl.ds(pl.multiple_of((j * n_blk + pc.c) * piece, piece), piece)]
        give(1 + j, totals[1].at[:, span(j, piece)], dst)

    u_proj.finish(totals[0])
    at = pl.multiple_of(pc.c * piece + cut, cut)
    pending += give(0, totals[0], proj_o.at[pl.ds(at, cut)])
    u_line.finish(totals[5])
    pending += give(5 + n_dp, totals[5], proj_o.at[pl.ds(pl.multiple_of(pc.c * piece, cut), cut)])
    u_out.finish(totals[3])
    pending += give(4 + n_dp, totals[3], out_o.at[:, my_cols])
    for s in far_first[2:]:
        u_qkv.settle(s)
        if s:
            u_qkv.along(s)
    u_small.finish(totals[4])
    swap_small = exchange(5, totals[4], small_in)
    u_qkv.finish(totals[2])
    for j in range(3):
        at = pl.ds(pl.multiple_of(pc.c * wide, LANES) + j * width, wide)
        pending += give(1 + n_dp + j, totals[2].at[:, j * wide : (j + 1) * wide], qkv_o.at[:, at])
    swap_small.wait()
    low = jnp.where(pc.c == 0, totals[4][...], small_in[...])
    high = jnp.where(pc.c == 0, small_in[...], totals[4][...])
    small_o[0:8, :] = low[0:8] + high[0:8]
    small_o[8:16, :] = low[8:16]
    small_o[16:24, :] = high[8:16]

    @pl.loop(0, n_dp)
    def _(j):
        dst = fc_o.at[:, pl.ds(pl.multiple_of((j * n_blk + pc.c) * piece, piece), piece)]
        src = totals[1].at[:, span(j, piece)]
        pltpu.make_async_copy(src, dst, last.at[0, 1 + j]).wait()
        remote(src, dst, last.at[1, 1 + j], last.at[2, 1 + j], sib).wait()

    for copy in pending:
        copy.wait()
    put_layer.wait()
    put_input.wait()
    for unit in (u_proj, u_line, u_fc, u_qkv, u_out):
        unit.drain()


def backward(n_dp, n_blk, scale, saved, tokens):
    rows_own, width = tokens.shape
    total = n_blk * rows_own
    wide = width // n_blk
    w_proj = saved[3]
    ff = w_proj.shape[0]
    piece, shard, length = ff // n_dp, width // n_dp, n_dp // PLANE
    square, long, own = ((total, width), BF16), ((total, ff), BF16), ((rows_own, width), BF16)
    own_f32 = ((rows_own, width), F32)
    sizes = [
        ((piece // 2, width), BF16),
        ((shard, ff), BF16),
        ((shard, 3 * wide), BF16),
        ((shard, wide), BF16),
        ((16, LANES), F32),
    ]
    scratch = [((ff, width), BF16), long, square, long, square, long, own_f32, own]
    scratch += [((width, width), BF16), (saved[9].shape, BF16), ((total, wide), BF16)]
    scratch += [((total, LANES), BF16), ((ff, width), BF16)]
    scratch += [((width, wide), BF16)] * 2 + [own] * 3 + [((total, wide), BF16), own, own_f32]
    scratch += [((total, LANES), F32)] * 2 + [((8, width), F32), ((1, ff), F32)]
    scratch += [((PLANE, length, 16, LANES), F32), ((16, LANES), F32)]
    for size, kind in sizes[:4]:
        scratch += [((length,) + size, kind)] * 4
    one = ((length, 16, LANES), F32)
    scratch += [((PLANE - 1,) + one[0], F32), one, one]
    half, quarter = (piece // 2, width), (piece // 4, width)
    scratch += [((PLANE, length + 1) + half, BF16), ((2,) + quarter, BF16), ((2,) + half, BF16)]
    scratch += [(size, F32) for size, _ in sizes] + [(half, F32)]
    outs = [own, own_f32, ((n_blk * piece, width), F32), ((shard, n_blk * ff), F32)]
    outs += [((shard, 3 * width), F32), ((shard, width), F32), ((24, LANES), F32)]
    hbm = pl.BlockSpec(memory_space=pl.ANY)
    vmem = pl.BlockSpec(memory_space=pltpu.VMEM)
    return pl.pallas_call(
        functools.partial(backward_kernel, n_dp, n_blk, scale),
        out_shape=[jax.ShapeDtypeStruct(*o) for o in outs],
        in_specs=[vmem if i == 4 else hbm for i in range(18)],
        out_specs=[hbm] * 6 + [vmem],
        scratch_shapes=[pltpu.VMEM(*s) for s in scratch]
        + [
            pltpu.SemaphoreType.DMA((7, 5, length)),
            pltpu.SemaphoreType.DMA((7, 5, length)),
            pltpu.SemaphoreType.DMA((2, 6)),
            pltpu.SemaphoreType.DMA((22,)),
            pltpu.SemaphoreType.DMA((3, 6 + n_dp)),
        ],
        compiler_params=pltpu.CompilerParams(
            collective_id=3, has_side_effects=True, vmem_limit_bytes=VMEM_BACK
        ),
    )(*saved, tokens)


def results_kernel(n_dp, piece, layer, inputs, proj, fc, qkv, out, small, *refs):
    big, vectors, fc_bias = refs[:6], refs[6:14], refs[14]
    hold, fetched, stored = refs[15:21], refs[21], refs[22]
    sources = (layer, inputs, proj, fc, qkv, out)
    loads = [pltpu.make_async_copy(s, h, fetched.at[i]) for i, (s, h) in enumerate(zip(sources, hold))]
    stores = [pltpu.make_async_copy(h, d, stored.at[i]) for i, (h, d) in enumerate(zip(hold, big))]
    for load in loads:
        load.start()
    shard = vectors[0].shape[1]
    per = LANES // shard
    turn = lax.rem(lax.axis_index("dp"), per)
    rows = small[0:8, 0:shard]
    for k in range(1, per):
        rows = jnp.where(turn == k, small[0:8, k * shard : (k + 1) * shard], rows)
    for i, vector in enumerate(vectors):
        vector[...] = rows[i : i + 1]
    for k in range(2):
        fc_bias[:, k * piece : (k + 1) * piece] = small[8 + 8 * k : 9 + 8 * k, :]
    for load, store in zip(loads, stores):
        load.wait()
        store.start()
    for store in stores:
        store.wait()


def results(n_dp, piece, outs):
    big, small = outs[:6], outs[6]
    shapes = [jax.ShapeDtypeStruct(a.shape, a.dtype) for a in big]
    shard = big[5].shape[0]
    sizes = [shard] * 8 + [2 * piece]
    shapes += [jax.ShapeDtypeStruct((1, size), F32) for size in sizes]
    hbm = pl.BlockSpec(memory_space=pl.ANY)
    vmem = pl.BlockSpec(memory_space=pltpu.VMEM)
    got = pl.pallas_call(
        functools.partial(results_kernel, n_dp, piece),
        out_shape=shapes,
        in_specs=[hbm] * 6 + [vmem],
        out_specs=[hbm] * 6 + [vmem] * 9,
        scratch_shapes=[pltpu.VMEM(a.shape, a.dtype) for a in big]
        + [pltpu.SemaphoreType.DMA((6,)), pltpu.SemaphoreType.DMA((6,))],
        compiler_params=pltpu.CompilerParams(vmem_limit_bytes=VMEM_BYTES),
    )(*outs)
    return got[:6], [a.reshape(-1) for a in got[6:]]


def columns_spec(rows, first):
    return pl.BlockSpec((rows, LANES), lambda j: (0, first + j))


def attend_step(block, scale, q_ref, k_ref, v_ref, key_aug, query_aug, slopes, out_ref, qx_ref):
    j = pl.program_id(0)
    pair = [slopes[2 * j + hh] for hh in range(2)]
    attend_kernel(block, scale, q_ref, k_ref, v_ref, key_aug, query_aug, pair, out_ref, qx_ref)


def attend(qkv, key_aug, query_aug, slopes, scale):
    total, wide = qkv.shape[0], qkv.shape[1] // 3
    pairs = wide // LANES
    block = math.gcd(total, 256)
    whole = pl.BlockSpec((total, LANES), lambda j: (0, 0))
    return pl.pallas_call(
        functools.partial(attend_step, block, scale),
        grid=(pairs,),
        out_shape=[
            jax.ShapeDtypeStruct((total, wide), BF16),
            jax.ShapeDtypeStruct((pairs, 2, total, LANES), BF16),
        ],
        in_specs=[
            columns_spec(total, 0),
            columns_spec(total, pairs),
            columns_spec(total, 2 * pairs),
            whole,
            whole,
            pl.BlockSpec(memory_space=pltpu.SMEM),
        ],
        out_specs=[
            columns_spec(total, 0),
            pl.BlockSpec((1, 2, total, LANES), lambda j: (j, 0, 0, 0)),
        ],
        compiler_params=pltpu.CompilerParams(vmem_limit_bytes=VMEM_BYTES),
    )(qkv, qkv, qkv, key_aug, query_aug, slopes)


def attend_back(query_ext, qkv, key_aug, attended, grad, scale):
    total, wide = attended.shape
    pairs = wide // LANES
    block = math.gcd(total, 256)
    whole = pl.BlockSpec((total, LANES), lambda j: (0, 0))
    out = jax.ShapeDtypeStruct((total, wide), BF16)
    return pl.pallas_call(
        functools.partial(attend_back_kernel, block, scale),
        grid=(pairs,),
        out_shape=[out] * 3,
        in_specs=[
            pl.BlockSpec((1, 2, total, LANES), lambda j: (j, 0, 0, 0)),
            columns_spec(total, pairs),
            columns_spec(total, 2 * pairs),
            whole,
            columns_spec(total, 0),
            columns_spec(total, 0),
        ],
        out_specs=[columns_spec(total, 0)] * 3,
        scratch_shapes=[pltpu.VMEM((total, LANES), F32)] * 2,
        compiler_params=pltpu.CompilerParams(vmem_limit_bytes=VMEM_BYTES),
    )(query_ext, qkv, qkv, key_aug, attended, grad)


def attention_terms(positions, rows):
    high = (positions // 256) * 256
    low = positions - high
    first = rows == 0
    one = jnp.ones_like(positions)
    zero = jnp.zeros_like(positions)

    def table(columns):
        cols = jnp.stack([col.astype(F32) for col in columns], axis=1)
        cols = jnp.pad(cols, ((0, 0), (0, LANES // 2 - len(columns))))
        return jnp.concatenate([cols, cols], axis=1).astype(BF16)

    key_aug = table([high, high, high, low, low, low, first, ~first, one, one, one])
    other = jnp.where(first, 0.0, MASKED)
    query_aug = table([zero] * 6 + [other, jnp.where(first, MASKED, 0.0)])
    return key_aug, query_aug


def body(
    n_dp,
    n_blk,
    tokens,
    positions,
    row_ids,
    alibi_slope,
    ln1_gain,
    ln1_bias,
    qkv_weight,
    query_bias,
    value_bias,
    out_weight,
    out_bias,
    ln2_gain,
    ln2_bias,
    fc_weight,
    fc_bias,
    proj_weight,
    proj_bias,
    out_grad,
):
    local, width = tokens.shape
    heads = alibi_slope.shape[0]
    hidden_all = fc_weight.shape[1]
    scale = 1.0 / math.sqrt(width // heads)
    c = lax.axis_index("blk")
    dp = lax.axis_index("dp")
    wide = width // n_blk
    shard = width // n_dp
    piece = hidden_all // (n_dp * n_blk)
    total = n_blk * local

    def swap(a):
        return lax.ppermute(a, "blk", [(0, 1), (1, 0)])

    def blk_gather(a):
        if n_blk != 2:
            return lax.all_gather(a, "blk", axis=0, tiled=True)
        other = swap(a)
        return jnp.where(
            c == 0, jnp.concatenate([a, other], 0), jnp.concatenate([other, a], 0)
        )

    def blk_sum(a):
        if n_blk != 2:
            return lax.psum_scatter(a.astype(BF16), "blk", scatter_dimension=0, tiled=True).astype(F32)
        own = lax.dynamic_slice_in_dim(a, c * local, local, 0)
        other = lax.dynamic_slice_in_dim(a, (1 - c) * local, local, 0)
        return own + swap(other.astype(BF16)).astype(F32)

    def to_tokens(a):
        if n_blk != 2:
            moved = lax.all_to_all(a.reshape(n_blk, local, wide), "blk", 0, 0)
            return jnp.transpose(moved, (1, 0, 2)).reshape(local, width)
        own = lax.dynamic_slice_in_dim(a, c * local, local, 0)
        other = swap(lax.dynamic_slice_in_dim(a, (1 - c) * local, local, 0))
        return jnp.where(
            c == 0, jnp.concatenate([own, other], 1), jnp.concatenate([other, own], 1)
        )

    def to_heads(a):
        if n_blk != 2:
            moved = lax.all_to_all(
                jnp.transpose(a.reshape(local, n_blk, wide), (1, 0, 2)), "blk", 0, 0
            )
            return moved.reshape(total, wide)
        own = lax.dynamic_slice_in_dim(a, c * wide, wide, 1)
        other = swap(lax.dynamic_slice_in_dim(a, (1 - c) * wide, wide, 1))
        return jnp.where(
            c == 0, jnp.concatenate([own, other], 0), jnp.concatenate([other, own], 0)
        )

    def mine(a, axis, size):
        return lax.dynamic_slice_in_dim(a, c * size, size, axis)

    vectors = [ln1_gain, ln1_bias, query_bias, value_bias, out_bias, ln2_gain, ln2_bias, proj_bias]
    if n_blk == 2 and piece == LANES:
        weights = (qkv_weight, out_weight, fc_weight, proj_weight)
        saved = forward(
            n_dp, n_blk, scale, *weights, tokens, out_grad, positions, row_ids, alibi_slope, fc_bias, vectors
        )
        saved = [a if i == 9 else a.reshape(-1, a.shape[-1]) for i, a in enumerate(saved)]
        outs = backward(n_dp, n_blk, scale, saved, tokens)
        big, vectors = results(n_dp, piece, outs)
        layer_output, input_grad, proj_sum, fc_sum, qkv_sum, out_sum = big
        return (
            layer_output,
            input_grad,
            vectors[0],
            vectors[1],
            qkv_sum,
            vectors[2],
            vectors[3],
            out_sum,
            vectors[4],
            vectors[5],
            vectors[6],
            fc_sum,
            vectors[8],
            proj_sum,
            vectors[7],
        )

    qkv_own = jnp.concatenate(
        [mine(qkv_weight[:, i * width : (i + 1) * width], 1, wide) for i in range(3)], 1
    ).astype(BF16)
    out_own = mine(out_weight, 1, wide).astype(BF16)
    fc_own = mine(fc_weight.reshape(shard, n_dp, n_blk, piece), 2, 1).reshape(shard, n_dp * piece)
    proj_own = mine(proj_weight, 0, piece)
    vectors.append(mine(fc_bias, 0, piece))
    small = jnp.stack(
        [
            lax.dynamic_update_slice_in_dim(
                jnp.zeros((LANES,), F32), vec, lax.rem(dp * vec.shape[0], LANES), 0
            )
            for vec in vectors
        ]
    )
    small = jnp.pad(small, ((0, 16 - len(vectors)), (0, 0))).astype(BF16)
    inputs = tokens.astype(F32)
    grad_top = out_grad.astype(F32)
    shards = (qkv_own, out_own, fc_own.astype(BF16), proj_own.astype(BF16), small)
    full_qkv, full_out, full_fc, full_proj, full_small = gather_weights(
        n_dp, n_blk, *shards
    )
    weight_qkv = full_qkv.reshape(width, 3 * wide)
    weight_out = full_out.reshape(width, width)
    weight_fc = full_fc.reshape(width, n_dp * piece)
    weight_proj = full_proj.reshape(n_dp * piece, width)
    spread = full_small.astype(F32)

    def vector(i):
        size = vectors[i].shape[0]
        per = LANES // size
        rows = jnp.sum(spread[:, i].reshape(n_dp // per, per, LANES), axis=1)
        return rows.reshape(n_dp * size)

    gain_one, bias_one, bias_query, bias_value, bias_out, gain_two, bias_two, bias_proj, bias_fc = (
        vector(i) for i in range(len(vectors))
    )
    place = blk_gather(jnp.stack([positions, row_ids], axis=1))
    key_aug, query_aug = attention_terms(place[:, 0], place[:, 1])
    every_token = blk_gather(tokens).astype(F32)
    every_grad = blk_gather(out_grad)
    normed = layer_norm(every_token, gain_one, bias_one).astype(BF16)
    bias_qkv = jnp.concatenate(
        [mine(bias_query, 0, wide), jnp.zeros((wide,), F32), mine(bias_value, 0, wide)]
    )
    mixed = (matmul(normed, weight_qkv) + bias_qkv).astype(BF16)
    slopes = mine(alibi_slope, 0, heads // n_blk)
    attended_heads, query_ext = attend(mixed, key_aug, query_aug, slopes, scale)
    attended = to_tokens(attended_heads)
    middle = inputs + matmul(attended, weight_out) + bias_out
    normed_two = layer_norm(middle, gain_two, bias_two).astype(BF16)
    every_two = blk_gather(normed_two)
    hidden_pre = matmul(every_two, weight_fc) + bias_fc
    hidden_vals, gelu_slope = gelu_pair(hidden_pre)
    hidden = hidden_vals.astype(BF16)
    grad_proj_weight = matmul_tn(hidden, every_grad).astype(BF16)
    layer_output = (middle + blk_sum(matmul(hidden, weight_proj)) + bias_proj).astype(BF16)
    grad_proj_bias = jnp.sum(grad_top, axis=0)
    grad_pre = (gelu_slope * matmul_nt(every_grad, weight_proj)).astype(BF16)
    grad_fc_weight = matmul_tn(every_two, grad_pre).astype(BF16)
    grad_fc_bias = jnp.sum(grad_pre.astype(F32), axis=0)
    grad_normed_two = blk_sum(matmul_nt(grad_pre, weight_fc))
    _, norm_two_back = jax.vjp(layer_norm, middle, gain_two, bias_two)
    grad_mid_norm, grad_gain_two, grad_bias_two = norm_two_back(grad_normed_two)
    grad_middle = grad_top + grad_mid_norm
    grad_branch = grad_middle.astype(BF16)
    grad_out_weight = matmul_tn(attended, grad_branch).astype(BF16)
    grad_out_bias = jnp.sum(grad_branch.astype(F32), axis=0)
    grad_heads = to_heads(matmul_nt(grad_branch, weight_out).astype(BF16))
    grad_mixed = jnp.concatenate(
        attend_back(query_ext, mixed, key_aug, attended_heads, grad_heads, scale), axis=1
    )
    grad_qkv_weight = matmul_tn(normed, grad_mixed).astype(BF16)
    sums = jnp.sum(grad_mixed.astype(F32), axis=0)
    grad_normed = blk_sum(matmul_nt(grad_mixed, weight_qkv))
    _, norm_one_back = jax.vjp(layer_norm, inputs, gain_one, bias_one)
    grad_in_norm, grad_gain_one, grad_bias_one = norm_one_back(grad_normed)
    input_grad = grad_middle + grad_in_norm

    proj_sum, fc_sum, out_sum, qkv_sum = scatter_grads(
        n_dp,
        n_blk,
        grad_proj_weight.reshape(n_dp, piece, width),
        grad_fc_weight.reshape(n_dp, shard, n_dp * piece),
        grad_out_weight.reshape(n_dp, shard, width),
        grad_qkv_weight.reshape(n_dp, shard, 3 * wide),
    )

    def spread_out(vec, size):
        parts = vec.reshape(-1, 1, size)
        return jnp.where((jnp.arange(n_blk) == c)[None, :, None], parts, 0.0).reshape(-1)

    small_grads = [
        grad_gain_one,
        grad_bias_one,
        spread_out(sums[:wide], wide),
        spread_out(sums[2 * wide :], wide),
        grad_out_bias,
        grad_gain_two,
        grad_bias_two,
        grad_proj_bias,
        spread_out(grad_fc_bias, piece),
    ]
    small_sum = lax.psum(jnp.concatenate(small_grads), ("dp", "blk"))
    finals = []
    at = 0
    for vec in small_grads:
        size = vec.shape[0]
        finals.append(lax.dynamic_slice_in_dim(small_sum, at + dp * (size // n_dp), size // n_dp, 0))
        at += size
    g_gain1, g_bias1, g_query, g_value, g_out, g_gain2, g_bias2, g_proj, g_fc = finals
    final_qkv = jnp.transpose(qkv_sum.reshape(n_blk, shard, 3, wide), (1, 2, 0, 3))
    final_fc = jnp.transpose(fc_sum.reshape(n_blk, shard, n_dp, piece), (1, 2, 0, 3))
    return (
        layer_output,
        input_grad,
        g_gain1,
        g_bias1,
        final_qkv.reshape(shard, 3 * width),
        g_query,
        g_value,
        jnp.transpose(out_sum, (1, 0, 2)).reshape(shard, width),
        g_out,
        g_gain2,
        g_bias2,
        final_fc.reshape(shard, hidden_all),
        g_fc,
        proj_sum.reshape(n_blk * piece, width),
        g_proj,
    )


def solution(mesh):
    both, rows, one = P(("dp", "blk"), None), P("dp", None), P("dp")
    tokens = P(("dp", "blk"))
    in_specs = (both, tokens, tokens, P(), one, one, rows, one, one, rows, one, one, one, rows, one, rows, one, both)
    out_specs = (both, both, one, one, rows, one, one, rows, one, one, one, rows, one, rows, one)
    return jax.shard_map(
        functools.partial(body, mesh.shape["dp"], mesh.shape["blk"]),
        mesh=mesh,
        in_specs=in_specs,
        out_specs=out_specs,
        check_vma=False,
    )
```
